32 devices in a mesh: blk: 16 (over z, x, core), req: 2 (over y).
Axes of the slice: x: 2, y: 2, z: 4, core: 2. Of those that a mesh axis runs over, the one named last changes fastest.
Arguments:
- prefill_queries: bfloat16 [2, 512, 1024], P('req', 'blk'), may hold values from -6 to 6
- decode_queries: bfloat16 [32, 1024], P('req'), may hold values from -6 to 6
- new_prefill: bfloat16 [2, 512, 512], P('req', 'blk'), may hold values from -6 to 6
- new_decode: bfloat16 [32, 512], P('req'), may hold values from -6 to 6
- prefill_cache: bfloat16 [2, 2048, 512], P('req', 'blk'), may hold values from -5 to 5
- decode_cache: bfloat16 [32, 2048, 512], P('req', 'blk'), may hold values from -5 to 5
- prefill_offsets: int32 [2], P('req'), may hold values from 2 to 1536, as said below
- decode_lengths: int32 [32], P('req'), may hold values from 2 to 2047, as said below
- dealing: int32 [34], replicated, may hold values from 0 to 31, as said below
Outputs:
- prefill_out: bfloat16 [2, 512, 1024], P('req', 'blk')
- decode_out: bfloat16 [32, 1024], P('req')
- prefill_cache_out: bfloat16 [2, 2048, 512], P('req', 'blk')
- decode_cache_out: bfloat16 [32, 2048, 512], P('req', 'blk')
The draws below stay inside these ranges and needn't reach their ends.
Inputs may be any that keep to these rules, and one draw needn't show every extreme that they name: The block of prefill slot i fills positions prefill_offsets[i] to prefill_offsets[i] + 511; some slot has offset 2048 - 512. The new token of decode slot j goes to position decode_lengths[j]; some slot has length 2047. `dealing`: the first 2 entries are a permutation of 0 to 1, the other 32 a permutation of 0 to 31.
All inputs are finite; a program needn't handle non-finite values.
Results may differ from the reference program's by a relative error of at most 0.0085.
Values may be sent and summed in bfloat16 or wider, within the bound.
No kernel may reach another device: no remote copies, remote signals or barrier semaphores. Data moves between devices by JAX's collectives and lax.ppermute only.
A program may use at most 64 MiB of HBM per device.

```python
import jax
import jax.numpy as jnp
from jax import lax

QUERY_HEADS = 8
KEY_VALUE_HEADS = 2
HEAD_SIZE = 128
P_SIZE = 512
KVW = 512
CTX = 2048
NPRE = 2
NDEC = 32


def cache_draw(key, slots, salt):
    drawn = jax.random.truncated_normal(jax.random.fold_in(key, salt + 1), -4.0, 4.0, (slots, CTX, KVW), jnp.float32)
    return drawn.astype(jnp.bfloat16)


def draw_prefill_cache(key, part):
    return cache_draw(key, NPRE, 7)


def draw_decode_cache(key, part):
    return cache_draw(key, NDEC, 11)


def draw_prefill_queries(key, part):
    drawn = 2.0 * jax.random.truncated_normal(jax.random.fold_in(key, 31), -3.0, 3.0, (NPRE, P_SIZE, QUERY_HEADS * HEAD_SIZE), jnp.float32)
    return drawn.astype(jnp.bfloat16)


def draw_decode_queries(key, part):
    drawn = 2.0 * jax.random.truncated_normal(jax.random.fold_in(key, 33), -3.0, 3.0, (NDEC, QUERY_HEADS * HEAD_SIZE), jnp.float32)
    return drawn.astype(jnp.bfloat16)


def skewed_positions(key, count, upper, salt):
    first_draw = jax.random.randint(jax.random.fold_in(key, salt), (count,), 0, upper - 1)
    second_draw = jax.random.randint(jax.random.fold_in(key, salt + 1), (count,), 0, upper - 1)
    skewed = 2 + first_draw * second_draw // upper
    longest = jax.random.randint(jax.random.fold_in(key, salt + 2), (), 0, count)
    slots = jnp.arange(count)
    skewed = jnp.where(slots == longest, upper, skewed)
    return skewed.astype(jnp.int32)


def draw_prefill_offsets(key, part):
    return skewed_positions(key, NPRE, CTX - P_SIZE, 41)


def draw_decode_lengths(key, part):
    return skewed_positions(key, NDEC, CTX - 1, 45)


def draw_dealing(key, part):
    first_order = jax.random.permutation(jax.random.fold_in(key, 51), NPRE)
    second_order = jax.random.permutation(jax.random.fold_in(key, 52), NDEC)
    return jnp.concatenate([first_order, second_order]).astype(jnp.int32)


def block_levels(stream_key, dims, cuts, low, top_value):
    def one(position, blocks):
        draws = jax.random.uniform(jax.random.fold_in(jax.random.fold_in(stream_key, 6), position), (blocks,), jnp.float32, low / len(cuts), top_value / len(cuts))
        return jnp.repeat(jnp.exp(draws), dims[position] // blocks).reshape((-1,) + (1,) * (len(dims) - position - 1))

    factor_of = one(*cuts[0])
    for cut in cuts[1:]:
        factor_of = factor_of * one(*cut)
    return factor_of


def centred(stream_key, extent, scale, limit, shards=(), kind=jnp.bfloat16):
    factor_of = block_levels(stream_key, extent, shards, -0.22, 0.18) if shards else 1.0
    result = jax.random.normal(stream_key, extent, jnp.float32) * scale * factor_of
    return jnp.minimum(jnp.maximum(result, -limit), limit).astype(kind)


def setup_inputs(seed: int = 0) -> dict:
    streams_of = jax.random.split(jax.random.key(seed), 10)
    return {
        "prefill_queries": draw_prefill_queries(jax.random.fold_in(streams_of[9], 71), 0),
        "decode_queries": draw_decode_queries(jax.random.fold_in(streams_of[9], 71), 0),
        "new_prefill": centred(streams_of[2], (NPRE, P_SIZE, KVW), 1.0, 6.0, ((0, 2), (1, 16))),
        "new_decode": centred(streams_of[3], (NDEC, KVW), 1.0, 6.0, ((0, 2),)),
        "prefill_cache": draw_prefill_cache(jax.random.fold_in(streams_of[9], 71), 0),
        "decode_cache": draw_decode_cache(jax.random.fold_in(streams_of[9], 71), 0),
        "prefill_offsets": draw_prefill_offsets(jax.random.fold_in(streams_of[9], 71), 0),
        "decode_lengths": draw_decode_lengths(jax.random.fold_in(streams_of[9], 71), 0),
        "dealing": draw_dealing(jax.random.fold_in(streams_of[9], 71), 0),
    }


masked_fill = -1e30


def heads_attend(query_rows, cache_table, limits):
    row_total = query_rows.shape[0]
    grouped_queries = query_rows.astype(jnp.float32).reshape(row_total, KEY_VALUE_HEADS, QUERY_HEADS // KEY_VALUE_HEADS, HEAD_SIZE)
    key_portion = cache_table[:, :KEY_VALUE_HEADS * HEAD_SIZE].astype(jnp.float32).reshape(-1, KEY_VALUE_HEADS, HEAD_SIZE)
    value_portion = cache_table[:, KEY_VALUE_HEADS * HEAD_SIZE:].astype(jnp.float32).reshape(-1, KEY_VALUE_HEADS, HEAD_SIZE)
    scores = jnp.einsum("rgqd,cgd->gqrc", grouped_queries, key_portion) * (HEAD_SIZE ** -0.5)
    visible = jnp.arange(cache_table.shape[0], dtype=jnp.int32)[None, :] <= limits[:, None]
    scores = jnp.where(visible, scores, masked_fill)
    maxima = jnp.max(scores, axis=-1, keepdims=True)
    exponent = jnp.where(visible, jnp.exp(scores - maxima), 0.0)
    totals = jnp.sum(exponent, axis=-1)
    rounded = lax.optimization_barrier(exponent.astype(jnp.bfloat16)).astype(jnp.float32)
    weighted = jnp.einsum("gqrc,cgd->gqrd", rounded, value_portion)
    normed = weighted / totals[..., None]
    return jnp.transpose(normed, (2, 0, 1, 3)).reshape(row_total, QUERY_HEADS * HEAD_SIZE).astype(jnp.bfloat16)


def reference(prefill_queries, decode_queries, new_prefill, new_decode, prefill_cache, decode_cache, prefill_offsets, decode_lengths, dealing):
    positions = jnp.arange(CTX, dtype=jnp.int32)
    relative = positions[None, :] - prefill_offsets[:, None]
    picked = jax.vmap(lambda source_rows, row_index: source_rows[row_index])(new_prefill, jnp.clip(relative, 0, P_SIZE - 1).astype(jnp.int32))
    inside = (relative >= 0) & (relative < P_SIZE)
    prefill_cache_out = jnp.where(inside[:, :, None], picked, prefill_cache)
    written = positions[None, :] == decode_lengths[:, None]
    decode_cache_out = jnp.where(written[:, :, None], new_decode[:, None, :], decode_cache)
    prefill_limits = prefill_offsets[:, None] + jnp.arange(P_SIZE, dtype=jnp.int32)[None, :]
    prefill_attn = lax.map(lambda operands: heads_attend(operands[0], operands[1], operands[2]), (prefill_queries, prefill_cache_out, prefill_limits))
    decode_attn = lax.map(lambda operands: heads_attend(operands[0], operands[1], operands[2]), (decode_queries[:, None, :], decode_cache_out, decode_lengths[:, None]))
    decode_attn = decode_attn.reshape(NDEC, QUERY_HEADS * HEAD_SIZE)
    prefill_out = jnp.zeros_like(prefill_attn).at[dealing[:NPRE]].set(prefill_attn)
    decode_out = jnp.zeros_like(decode_attn).at[dealing[NPRE:]].set(decode_attn)
    return (prefill_out, decode_out, prefill_cache_out, decode_cache_out)
```

```python
import functools

import jax
import jax.numpy as jnp
from jax import lax
from jax.experimental import pallas as pl
from jax.experimental.pallas import tpu as pltpu
from jax.sharding import PartitionSpec as P

QUERY_HEADS = 8
KEY_VALUE_HEADS = 2
HEAD_SIZE = 128
GROUP = QUERY_HEADS // KEY_VALUE_HEADS
QW = QUERY_HEADS * HEAD_SIZE
KW = KEY_VALUE_HEADS * HEAD_SIZE
GW = GROUP * HEAD_SIZE
STATS = 128
QUAD = 4
SCALE = HEAD_SIZE**-0.5
MASKED = -1e30
FLOOR = -1e20
F32 = jnp.float32
BF16 = jnp.bfloat16

VMEM = pl.BlockSpec(memory_space=pltpu.VMEM)
SMEM = pl.BlockSpec(memory_space=pltpu.SMEM)


def dot_t(a, b):
    return lax.dot_general(a, b, (((1,), (1,)), ((), ())), preferred_element_type=F32)


def dot(a, b):
    return lax.dot_general(a, b, (((1,), (0,)), ((), ())), preferred_element_type=F32)


def split3(value):
    high = value.astype(BF16).astype(F32)
    rest = value - high
    middle = rest.astype(BF16).astype(F32)
    return high, middle, rest - middle


def stats_block(columns, rows):
    lane = lax.broadcasted_iota(jnp.int32, (rows, STATS), 1)
    count = len(columns)
    out = jnp.zeros((rows, STATS), F32)
    for head, column in enumerate(columns):
        for term, part in enumerate(split3(column)):
            out = jnp.where(lane == term * count + head, part, out)
    return out.astype(BF16)


def spread_matrix(heads):
    lane = lax.broadcasted_iota(jnp.int32, (STATS, heads * HEAD_SIZE), 0)
    head = lax.broadcasted_iota(jnp.int32, (STATS, heads * HEAD_SIZE), 1) // HEAD_SIZE
    hit = (lane == head) | (lane == head + heads) | (lane == head + 2 * heads)
    return jnp.where(hit, 1.0, 0.0).astype(BF16)


def join(parts, heads):
    width = heads * HEAD_SIZE
    spread = spread_matrix(heads)
    logs = [dot(part[:, width:], spread) for part in parts]
    top = functools.reduce(jnp.maximum, logs)
    scales = [jnp.exp(log - top) for log in logs]
    total = functools.reduce(jnp.add, scales)
    summed = functools.reduce(
        jnp.add, [scale * part[:, :width].astype(F32) for scale, part in zip(scales, parts)]
    )
    return (summed / total).astype(BF16)


def decode_kernel(step_slots, len_ref, q_ref, new_ref, cache_ref, out_ref, part_ref, acc, top, tot):
    step = pl.program_id(0)
    slots = q_ref.shape[0]
    ctx = cache_ref.shape[1]
    rows = GROUP * slots
    base = lax.axis_index("blk") * ctx
    row_slot = lax.broadcasted_iota(jnp.int32, (rows, ctx), 0) % slots
    column = lax.broadcasted_iota(jnp.int32, (rows, ctx), 1)
    cache_row = lax.broadcasted_iota(jnp.int32, (ctx, cache_ref.shape[2]), 0)

    @pl.when(step == 0)
    def _():
        acc[...] = jnp.zeros_like(acc)
        top[...] = jnp.zeros_like(top)
        tot[...] = jnp.zeros_like(tot)

    limit = jnp.full((rows, ctx), -1, jnp.int32)
    for s in range(step_slots):
        slot = step * step_slots + s
        relative = len_ref[slot] - base
        new_row = new_ref[slot]
        out_ref[s] = jnp.where(cache_row == relative, new_row, cache_ref[s])
        limit = jnp.where(row_slot == slot, relative, limit)
    visible = column <= limit
    inside = (row_slot >= step * step_slots) & (row_slot < (step + 1) * step_slots)
    for g in range(KEY_VALUE_HEADS):
        query = jnp.concatenate(
            [q_ref[:, pl.ds((g * GROUP + h) * HEAD_SIZE, HEAD_SIZE)] for h in range(GROUP)], axis=0
        )
        scores = jnp.full((rows, ctx), MASKED, F32)
        for s in range(step_slots):
            key = out_ref[s, :, pl.ds(g * HEAD_SIZE, HEAD_SIZE)]
            scores = jnp.where(row_slot == step * step_slots + s, dot_t(query, key), scores)
        scores = jnp.where(visible, scores * SCALE, MASKED)
        maxima = jnp.maximum(jnp.max(scores, axis=1, keepdims=True), FLOOR)
        weights = jnp.exp(scores - maxima)
        totals = jnp.sum(weights, axis=1, keepdims=True)
        rounded = weights.astype(BF16)
        total_sum = acc[g]
        for s in range(step_slots):
            value = out_ref[s, :, pl.ds(KW + g * HEAD_SIZE, HEAD_SIZE)]
            picked = jnp.where(row_slot == step * step_slots + s, rounded, jnp.zeros_like(rounded))
            total_sum += dot(picked, value)
        acc[g] = total_sum
        top[g] = jnp.where(inside, maxima, top[g])
        tot[g] = jnp.where(inside, totals, tot[g])

    @pl.when(step == pl.num_programs(0) - 1)
    def _():
        for g in range(KEY_VALUE_HEADS):
            totals = tot[g]
            seen = totals > 0.0
            normed = acc[g] / jnp.where(seen, totals, 1.0)
            logs = jnp.where(seen, top[g] + jnp.log(jnp.where(seen, totals, 1.0)), MASKED)
            columns = []
            for h in range(GROUP):
                part = pl.ds(h * HEAD_SIZE, HEAD_SIZE)
                part_ref[g, :, part] = normed[h * slots : (h + 1) * slots].astype(BF16)
                columns.append(logs[h * slots : (h + 1) * slots, :1])
            part_ref[g, :, pl.ds(GW, STATS)] = stats_block(columns, slots)


def decode_partials(lengths, queries, new_rows, cache):
    slots, ctx, width = cache.shape
    step_slots = 4
    rows = GROUP * slots
    whole = lambda *shape: pl.BlockSpec(shape, lambda i: (0,) * len(shape))
    block = pl.BlockSpec((step_slots, ctx, width), lambda i: (i, 0, 0))
    return pl.pallas_call(
        functools.partial(decode_kernel, step_slots),
        grid=(slots // step_slots,),
        in_specs=[SMEM, whole(slots, QW), whole(slots, 1, width), block],
        out_specs=[block, whole(KEY_VALUE_HEADS, slots, GW + STATS)],
        out_shape=[
            jax.ShapeDtypeStruct(cache.shape, BF16),
            jax.ShapeDtypeStruct((KEY_VALUE_HEADS, slots, GW + STATS), BF16),
        ],
        scratch_shapes=[pltpu.VMEM((KEY_VALUE_HEADS, rows, HEAD_SIZE), F32)] * 3,
        compiler_params=pltpu.CompilerParams(vmem_limit_bytes=16 << 20),
        cost_estimate=pl.CostEstimate(
            flops=4 * slots * ctx * QW, bytes_accessed=2 * cache.size * 2, transcendentals=slots * ctx * 8
        ),
        name="decode_partials",
    )(lengths, queries, new_rows[:, None, :], cache)


def prefill_kernel(hi_count, ctx, off_ref, *refs):
    packs, tables, outs = refs[:hi_count], refs[hi_count : hi_count + QUAD], refs[hi_count + QUAD :]
    tokens = packs[0].shape[0]
    span = tables[0].shape[0]
    me = lax.axis_index("blk")
    hi, quad = me // QUAD, me % QUAD
    offset = off_ref[0]
    pieces = []
    for k in range(QUAD):
        holder = hi * QUAD + (quad ^ k)
        index = lax.broadcasted_iota(jnp.int32, (1, span), 1)
        old = jnp.where(holder * ctx + index < offset, -1, 1 << 30)
        pieces.append(jnp.where(index < ctx, old, holder * tokens + index - ctx))
    key_mark = jnp.concatenate(pieces, axis=1)
    in_block = lax.broadcasted_iota(jnp.int32, (GROUP * tokens, 1), 0) % tokens
    for g in range(KEY_VALUE_HEADS):
        keys = jnp.concatenate([t[:, pl.ds(g * HEAD_SIZE, HEAD_SIZE)] for t in tables], axis=0)
        values = jnp.concatenate([t[:, pl.ds(KW + g * HEAD_SIZE, HEAD_SIZE)] for t in tables], axis=0)
        for k in range(hi_count):
            token = ((hi ^ k) * QUAD + quad) * tokens + in_block
            query = jnp.concatenate(
                [packs[k][:, pl.ds((g * GROUP + h) * HEAD_SIZE, HEAD_SIZE)] for h in range(GROUP)], axis=0
            )
            scores = jnp.where(key_mark <= token, dot_t(query, keys) * SCALE, MASKED)
            maxima = jnp.maximum(jnp.max(scores, axis=1, keepdims=True), FLOOR)
            weights = jnp.exp(scores - maxima)
            totals = jnp.sum(weights, axis=1, keepdims=True)
            summed = dot(weights.astype(BF16), values)
            seen = totals > 0.0
            safe = jnp.where(seen, totals, 1.0)
            normed = (summed / safe).astype(BF16)
            logs = jnp.where(seen, maxima + jnp.log(safe), MASKED)
            for h in range(GROUP):
                part = slice(h * tokens, (h + 1) * tokens)
                outs[k][:, pl.ds((g * GROUP + h) * HEAD_SIZE, HEAD_SIZE)] = normed[part]
            lane = lax.broadcasted_iota(jnp.int32, (tokens, STATS), 1)
            block = jnp.zeros((tokens, STATS), F32) if g == 0 else outs[k][:, pl.ds(QW, STATS)].astype(F32)
            for h in range(GROUP):
                for term, value in enumerate(split3(logs[h * tokens : (h + 1) * tokens])):
                    block = jnp.where(lane == term * QUERY_HEADS + g * GROUP + h, value, block)
            outs[k][:, pl.ds(QW, STATS)] = block.astype(BF16)


def prefill_partials(offset, packs, tables, ctx):
    tokens = packs[0].shape[0]
    span = tables[0].shape[0]
    pairs = len(packs) * tokens * QUAD * span
    return pl.pallas_call(
        functools.partial(prefill_kernel, len(packs), ctx),
        in_specs=[SMEM] + [VMEM] * (len(packs) + len(tables)),
        out_specs=[VMEM] * len(packs),
        out_shape=[jax.ShapeDtypeStruct((tokens, QW + STATS), BF16)] * len(packs),
        compiler_params=pltpu.CompilerParams(vmem_limit_bytes=32 << 20),
        cost_estimate=pl.CostEstimate(
            flops=4 * pairs * QW, bytes_accessed=4 << 20, transcendentals=pairs * QUERY_HEADS
        ),
        name="prefill_partials",
    )(offset, *packs, *tables)


def join_prefill_kernel(*refs):
    refs[-1][...] = join([ref[...] for ref in refs[:-1]], QUERY_HEADS)


def join_prefill(parts):
    return pl.pallas_call(
        join_prefill_kernel,
        in_specs=[VMEM] * len(parts),
        out_specs=VMEM,
        out_shape=jax.ShapeDtypeStruct((parts[0].shape[0], QW), BF16),
        compiler_params=pltpu.CompilerParams(vmem_limit_bytes=16 << 20),
        name="join_prefill",
    )(*parts)


def join_decode_kernel(part_ref, out_ref):
    out_ref[...] = join([part_ref[i] for i in range(part_ref.shape[0])], GROUP)


def join_decode(parts):
    return pl.pallas_call(
        join_decode_kernel,
        in_specs=[VMEM],
        out_specs=VMEM,
        out_shape=jax.ShapeDtypeStruct((parts.shape[1], GW), BF16),
        compiler_params=pltpu.CompilerParams(vmem_limit_bytes=16 << 20),
        name="join_decode",
    )(parts)


def update_kernel(hi_count, off_ref, cache_ref, *refs):
    packs, tables, others, out_ref = (
        refs[:hi_count],
        refs[hi_count : hi_count + QUAD],
        refs[hi_count + QUAD : -1],
        refs[-1],
    )
    ctx = cache_ref.shape[0]
    tokens = packs[0].shape[0]
    me = lax.axis_index("blk")
    hi, quad = me // QUAD, me % QUAD
    blocks = []
    for k in range(hi_count):
        for j in range(QUAD):
            if j == 0:
                blocks.append(packs[k][:, pl.ds(QW, 2 * KW)])
            elif k == 0:
                blocks.append(tables[j][pl.ds(ctx, tokens), :])
            else:
                blocks.append(others[j - 1][pl.ds((k - 1) * tokens, tokens), :])
    rows = jnp.concatenate(blocks, axis=0)
    count = rows.shape[0]
    index = lax.broadcasted_iota(jnp.int32, (1, count), 1)
    block = index // tokens
    token = ((hi ^ (block // QUAD)) * QUAD + (quad ^ (block % QUAD))) * tokens + index % tokens
    wanted = me * ctx + lax.broadcasted_iota(jnp.int32, (ctx, 1), 0) - off_ref[0]
    picked = dot(jnp.where(wanted == token, 1.0, 0.0).astype(BF16), rows).astype(BF16)
    inside = jnp.broadcast_to((wanted >= 0) & (wanted < count), out_ref.shape)
    out_ref[...] = jnp.where(inside, picked, cache_ref[...])


def update_cache(offset, cache, packs, tables, others):
    return pl.pallas_call(
        functools.partial(update_kernel, len(packs)),
        in_specs=[SMEM] + [VMEM] * (1 + len(packs) + len(tables) + len(others)),
        out_specs=VMEM,
        out_shape=jax.ShapeDtypeStruct(cache.shape, BF16),
        compiler_params=pltpu.CompilerParams(vmem_limit_bytes=16 << 20),
        name="update_cache",
    )(offset, cache, *packs, *tables, *others)


def per_device(
    prefill_queries,
    decode_queries,
    new_prefill,
    new_decode,
    prefill_cache,
    decode_cache,
    prefill_offsets,
    decode_lengths,
    dealing,
):
    blk = lax.axis_size("blk")
    req = lax.axis_size("req")
    hi_count = blk // QUAD
    ctx = prefill_cache.shape[1]
    slots = decode_cache.shape[0]
    group = lax.axis_index("req")

    def over_quad(array, k):
        return lax.ppermute(array, "blk", [(i, i ^ k) for i in range(blk)])

    def over_hi(array, k):
        return lax.ppermute(array, "blk", [(i, i ^ (k * QUAD)) for i in range(blk)])

    table = jnp.concatenate([prefill_cache[0], new_prefill[0]], axis=0)
    pack = jnp.concatenate([prefill_queries[0], new_prefill[0]], axis=1)
    packs = [pack] + [over_hi(pack, k) for k in range(1, hi_count)]
    tables = [table] + [over_quad(table, k) for k in range(1, QUAD)]

    decode_cache_out, decode_part = decode_partials(decode_lengths, decode_queries, new_decode, decode_cache)
    pieces = KEY_VALUE_HEADS * slots // blk
    decode_part = decode_part.reshape(blk, pieces, GW + STATS)
    decode_parts = lax.all_to_all(decode_part, "blk", split_axis=0, concat_axis=0, tiled=True)

    parts = prefill_partials(prefill_offsets, packs, tables, ctx)
    arrived = [over_hi(parts[k], k) for k in range(1, hi_count)]

    decode_piece = join_decode(decode_parts)
    everywhere = jnp.broadcast_to(decode_piece[None], (req * blk, pieces, GW))
    gathered = lax.all_to_all(everywhere, ("req", "blk"), split_axis=0, concat_axis=0, tiled=True)

    new_rows = jnp.concatenate([p[:, QW:] for p in packs[1:]], axis=0)
    others = [over_quad(new_rows, k) for k in range(1, QUAD)]
    prefill_cache_out = update_cache(prefill_offsets, prefill_cache[0], packs, tables, others)[None]

    attended = join_prefill([parts[0]] + arrived)
    if req == 2:
        other = lax.ppermute(attended, "req", [(0, 1), (1, 0)])
        prefill_out = jnp.where(dealing[group] == group, attended, other)[None]
    else:
        spread = lax.all_gather(attended, "req", axis=0)
        source = jnp.argmax(dealing[:req] == group)
        prefill_out = lax.dynamic_index_in_dim(spread, source, 0, True)

    gathered = gathered.reshape(req, KEY_VALUE_HEADS, slots, GW)
    own = group * slots + jnp.arange(slots, dtype=jnp.int32)
    chosen = (dealing[req:][None, :] == own[:, None]).astype(BF16)
    decode_out = jnp.einsum(
        "ors,rgsf->ogf", chosen.reshape(slots, req, slots), gathered, preferred_element_type=F32
    )
    decode_out = decode_out.reshape(slots, QW).astype(BF16)
    return (prefill_out, decode_out, prefill_cache_out, decode_cache_out)


def solution(mesh):
    in_specs = (
        P("req", "blk", None),
        P("req", None),
        P("req", "blk", None),
        P("req", None),
        P("req", "blk", None),
        P("req", "blk", None),
        P("req"),
        P("req"),
        P(),
    )
    out_specs = (
        P("req", "blk", None),
        P("req", None),
        P("req", "blk", None),
        P("req", "blk", None),
    )
    return jax.shard_map(
        per_device, mesh=mesh, in_specs=in_specs, out_specs=out_specs, check_vma=False
    )
```

```python
import functools

import jax
import jax.numpy as jnp
from jax import lax
from jax.experimental import pallas as pl
from jax.experimental.pallas import tpu as pltpu
from jax.sharding import PartitionSpec as P

QUERY_HEADS = 8
KEY_VALUE_HEADS = 2
HEAD_SIZE = 128
GROUP = QUERY_HEADS // KEY_VALUE_HEADS
QW = QUERY_HEADS * HEAD_SIZE
KW = KEY_VALUE_HEADS * HEAD_SIZE
GW = GROUP * HEAD_SIZE
STATS = 128
QUAD = 4
SCALE = HEAD_SIZE**-0.5
MASKED = -1e30
FLOOR = -1e20
F32 = jnp.float32
BF16 = jnp.bfloat16

BLK = ("hi", "quad")
KVW = 2 * KW
CHUNKS = 4
TILE = 16

ANY = pl.BlockSpec(memory_space=pl.ANY)
HBM = pl.BlockSpec(memory_space=pltpu.HBM)
VMEM = pl.BlockSpec(memory_space=pltpu.VMEM)
SMEM = pl.BlockSpec(memory_space=pltpu.SMEM)


def dot_t(a, b):
    return lax.dot_general(a, b, (((1,), (1,)), ((), ())), preferred_element_type=F32)


def dot(a, b):
    return lax.dot_general(a, b, (((1,), (0,)), ((), ())), preferred_element_type=F32)


def split3(value):
    high = value.astype(BF16).astype(F32)
    rest = value - high
    middle = rest.astype(BF16).astype(F32)
    return high, middle, rest - middle


def stats_block(columns, rows):
    lane = lax.broadcasted_iota(jnp.int32, (rows, STATS), 1)
    count = len(columns)
    out = jnp.zeros((rows, STATS), F32)
    for head, column in enumerate(columns):
        for term, part in enumerate(split3(column)):
            out = jnp.where(lane == term * count + head, part, out)
    return out.astype(BF16)


def spread_matrix(heads):
    lane = lax.broadcasted_iota(jnp.int32, (STATS, heads * HEAD_SIZE), 0)
    head = lax.broadcasted_iota(jnp.int32, (STATS, heads * HEAD_SIZE), 1) // HEAD_SIZE
    hit = (lane == head) | (lane == head + heads) | (lane == head + 2 * heads)
    return jnp.where(hit, 1.0, 0.0).astype(BF16)


def join(parts, heads):
    width = heads * HEAD_SIZE
    spread = spread_matrix(heads)
    logs = [dot(part[:, width:], spread) for part in parts]
    top = functools.reduce(jnp.maximum, logs)
    scales = [jnp.exp(log - top) for log in logs]
    total = functools.reduce(jnp.add, scales)
    summed = functools.reduce(
        jnp.add, [scale * part[:, :width].astype(F32) for scale, part in zip(scales, parts)]
    )
    return (summed / total).astype(BF16)


def decode_kernel(
    len_hbm, q_hbm, new_hbm, cache_hbm, out_hbm, part_ref, lens, query_ref, new_ref, table, sems
):
    slots, ctx, _ = table.shape
    rows = GROUP * slots
    chunk = slots // CHUNKS
    base = lax.axis_index(BLK) * ctx
    small = [
        pltpu.make_async_copy(len_hbm, lens, sems.at[0]),
        pltpu.make_async_copy(q_hbm, query_ref, sems.at[1]),
        pltpu.make_async_copy(new_hbm, new_ref, sems.at[2]),
    ]
    loads, stores = [], []
    for c in range(CHUNKS):
        part = pl.ds(c * chunk, chunk)
        loads.append(pltpu.make_async_copy(cache_hbm.at[part], table.at[part], sems.at[3 + c]))
        stores.append(pltpu.make_async_copy(table.at[part], out_hbm.at[part], sems.at[3 + CHUNKS + c]))
    for copy in small + loads:
        copy.start()
    for copy in small:
        copy.wait()
    row_slot = lax.broadcasted_iota(jnp.int32, (rows, ctx), 0) % slots
    column = lax.broadcasted_iota(jnp.int32, (rows, ctx), 1)
    in_tile = lax.broadcasted_iota(jnp.int32, (TILE, KVW), 0)
    limit = jnp.full((rows, ctx), -1, jnp.int32)
    queries = [
        jnp.concatenate(
            [query_ref[:, pl.ds((g * GROUP + h) * HEAD_SIZE, HEAD_SIZE)] for h in range(GROUP)], axis=0
        )
        for g in range(KEY_VALUE_HEADS)
    ]
    scores = [jnp.zeros((rows, ctx), F32) for _ in range(KEY_VALUE_HEADS)]
    for c in range(CHUNKS):
        loads[c].wait()
        for s in range(c * chunk, (c + 1) * chunk):
            relative = lens[s] - base
            limit = jnp.where(row_slot == s, relative, limit)

            @pl.when((relative >= 0) & (relative < ctx))
            def _():
                start = pl.multiple_of(relative // TILE * TILE, TILE)
                tile = table[s, pl.ds(start, TILE), :]
                table[s, pl.ds(start, TILE), :] = jnp.where(
                    in_tile == relative - start, new_ref[s : s + 1, :], tile
                )

        stores[c].start()
        for s in range(c * chunk, (c + 1) * chunk):
            for g in range(KEY_VALUE_HEADS):
                key = table[s, :, pl.ds(g * HEAD_SIZE, HEAD_SIZE)]
                scores[g] = jnp.where(row_slot == s, dot_t(queries[g], key), scores[g])
    visible = column <= limit
    for g in range(KEY_VALUE_HEADS):
        masked = jnp.where(visible, scores[g] * SCALE, MASKED)
        maxima = jnp.maximum(jnp.max(masked, axis=1, keepdims=True), FLOOR)
        weights = jnp.exp(masked - maxima)
        totals = jnp.sum(weights, axis=1, keepdims=True)
        summed = jnp.zeros((rows, HEAD_SIZE), F32)
        for s in range(slots):
            value = table[s, :, pl.ds(KW + g * HEAD_SIZE, HEAD_SIZE)]
            picked = jnp.where(row_slot == s, weights, 0.0).astype(BF16)
            summed += dot(picked, value)
        seen = totals > 0.0
        safe = jnp.where(seen, totals, 1.0)
        normed = (summed / safe).astype(BF16)
        logs = jnp.where(seen, maxima + jnp.log(safe), MASKED)
        columns = []
        for h in range(GROUP):
            part = slice(h * slots, (h + 1) * slots)
            part_ref[g, :, pl.ds(h * HEAD_SIZE, HEAD_SIZE)] = normed[part]
            columns.append(logs[part])
        part_ref[g, :, pl.ds(GW, STATS)] = stats_block(columns, slots)
    for copy in stores:
        copy.wait()


def decode_partials(lengths, queries, new_rows, cache):
    slots, ctx, width = cache.shape
    return pl.pallas_call(
        decode_kernel,
        in_specs=[HBM] * 4,
        out_specs=[HBM, VMEM],
        out_shape=[
            jax.ShapeDtypeStruct(cache.shape, BF16),
            jax.ShapeDtypeStruct((KEY_VALUE_HEADS, slots, GW + STATS), BF16),
        ],
        scratch_shapes=[
            pltpu.SMEM(lengths.shape, jnp.int32),
            pltpu.VMEM(queries.shape, BF16),
            pltpu.VMEM(new_rows.shape, BF16),
            pltpu.VMEM(cache.shape, BF16),
            pltpu.SemaphoreType.DMA((3 + 2 * CHUNKS,)),
        ],
        compiler_params=pltpu.CompilerParams(vmem_limit_bytes=16 << 20),
        cost_estimate=pl.CostEstimate(
            flops=4 * slots * ctx * QW, bytes_accessed=2 * cache.size * 2, transcendentals=slots * ctx * 8
        ),
        name="decode_partials",
    )(lengths, queries, new_rows, cache)


def prepare_kernel(q_hbm, new_hbm, cache_hbm, pack_ref, table_ref, sems):
    ctx, tokens = cache_hbm.shape[1], new_hbm.shape[1]
    copies = []
    for k in range(pack_ref.shape[0]):
        copies.append((q_hbm.at[0], pack_ref.at[k, :, pl.ds(0, QW)]))
        copies.append((new_hbm.at[0], pack_ref.at[k, :, pl.ds(QW, KVW)]))
    for k in range(QUAD):
        copies.append((cache_hbm.at[0], table_ref.at[k, pl.ds(0, ctx), :]))
        copies.append((new_hbm.at[0], table_ref.at[k, pl.ds(ctx, tokens), :]))
    copies = [pltpu.make_async_copy(a, b, sems.at[i]) for i, (a, b) in enumerate(copies)]
    for copy in copies:
        copy.start()
    for copy in copies:
        copy.wait()


def prepare(queries, new_rows, cache, hi_count):
    tokens, ctx = queries.shape[1], cache.shape[1]
    return pl.pallas_call(
        prepare_kernel,
        in_specs=[HBM] * 3,
        out_specs=[ANY] * 2,
        out_shape=[
            jax.ShapeDtypeStruct((hi_count, tokens, QW + KVW), BF16),
            jax.ShapeDtypeStruct((QUAD, ctx + tokens, KVW), BF16),
        ],
        scratch_shapes=[pltpu.SemaphoreType.DMA((2 * hi_count + 2 * QUAD,))],
        name="prepare",
    )(queries, new_rows, cache)


def prefill_kernel(ctx, off_ref, packs, tables, outs, news):
    hi_count, tokens, _ = packs.shape
    span = tables.shape[1]
    quad = lax.axis_index("quad")
    offset = off_ref[0]
    hi = lax.axis_index("hi")
    pieces = []
    for k in range(QUAD):
        holder = hi * QUAD + k
        index = lax.broadcasted_iota(jnp.int32, (1, span), 1)
        old = jnp.where(holder * ctx + index < offset, -1, 1 << 30)
        pieces.append(jnp.where(index < ctx, old, holder * tokens + index - ctx))
    key_mark = jnp.concatenate(pieces, axis=1)
    in_block = lax.broadcasted_iota(jnp.int32, (GROUP * tokens, 1), 0) % tokens
    for k in range(hi_count):
        for j in range(QUAD):
            news[j, pl.ds(k * tokens, tokens), :] = packs[k, :, pl.ds(QW, KVW)]
    for g in range(KEY_VALUE_HEADS):
        keys = jnp.concatenate([tables[k, :, pl.ds(g * HEAD_SIZE, HEAD_SIZE)] for k in range(QUAD)], axis=0)
        values = jnp.concatenate(
            [tables[k, :, pl.ds(KW + g * HEAD_SIZE, HEAD_SIZE)] for k in range(QUAD)], axis=0
        )
        for k in range(hi_count):
            token = (k * QUAD + quad) * tokens + in_block
            query = jnp.concatenate(
                [packs[k, :, pl.ds((g * GROUP + h) * HEAD_SIZE, HEAD_SIZE)] for h in range(GROUP)], axis=0
            )
            scores = jnp.where(key_mark <= token, dot_t(query, keys) * SCALE, MASKED)
            maxima = jnp.maximum(jnp.max(scores, axis=1, keepdims=True), FLOOR)
            weights = jnp.exp(scores - maxima)
            totals = jnp.sum(weights, axis=1, keepdims=True)
            summed = dot(weights.astype(BF16), values)
            seen = totals > 0.0
            safe = jnp.where(seen, totals, 1.0)
            normed = (summed / safe).astype(BF16)
            logs = jnp.where(seen, maxima + jnp.log(safe), MASKED)
            for h in range(GROUP):
                part = slice(h * tokens, (h + 1) * tokens)
                outs[k, :, pl.ds((g * GROUP + h) * HEAD_SIZE, HEAD_SIZE)] = normed[part]
            lane = lax.broadcasted_iota(jnp.int32, (tokens, STATS), 1)
            block = jnp.zeros((tokens, STATS), F32) if g == 0 else outs[k, :, pl.ds(QW, STATS)].astype(F32)
            for h in range(GROUP):
                for term, value in enumerate(split3(logs[h * tokens : (h + 1) * tokens])):
                    block = jnp.where(lane == term * QUERY_HEADS + g * GROUP + h, value, block)
            outs[k, :, pl.ds(QW, STATS)] = block.astype(BF16)


def prefill_partials(offset, packs, tables, ctx):
    hi_count, tokens, _ = packs.shape
    span = tables.shape[1]
    pairs = hi_count * tokens * QUAD * span
    return pl.pallas_call(
        functools.partial(prefill_kernel, ctx),
        in_specs=[SMEM, VMEM, VMEM],
        out_specs=[VMEM, VMEM],
        out_shape=[
            jax.ShapeDtypeStruct((hi_count, tokens, QW + STATS), BF16),
            jax.ShapeDtypeStruct((QUAD, hi_count * tokens, KVW), BF16),
        ],
        compiler_params=pltpu.CompilerParams(vmem_limit_bytes=32 << 20),
        cost_estimate=pl.CostEstimate(
            flops=4 * pairs * QW, bytes_accessed=4 << 20, transcendentals=pairs * QUERY_HEADS
        ),
        name="prefill_partials",
    )(offset, packs, tables)


def join_kernel(heads, part_ref, out_ref):
    out_ref[...] = join([part_ref[i] for i in range(part_ref.shape[0])], heads)


def join_parts(parts, heads, name):
    return pl.pallas_call(
        functools.partial(join_kernel, heads),
        in_specs=[VMEM],
        out_specs=VMEM,
        out_shape=jax.ShapeDtypeStruct((parts.shape[1], heads * HEAD_SIZE), BF16),
        compiler_params=pltpu.CompilerParams(vmem_limit_bytes=16 << 20),
        name=name,
    )(parts)


def update_kernel(tokens, off_ref, cache_ref, news, out_ref):
    ctx = cache_ref.shape[0]
    rows = jnp.concatenate([news[j] for j in range(QUAD)], axis=0)
    count = rows.shape[0]
    index = lax.broadcasted_iota(jnp.int32, (1, count), 1)
    block = index // tokens
    hi_count = count // (QUAD * tokens)
    token = ((block % hi_count) * QUAD + block // hi_count) * tokens + index % tokens
    wanted = lax.axis_index(BLK) * ctx + lax.broadcasted_iota(jnp.int32, (ctx, 1), 0) - off_ref[0]
    picked = dot(jnp.where(wanted == token, 1.0, 0.0).astype(BF16), rows).astype(BF16)
    inside = jnp.broadcast_to((wanted >= 0) & (wanted < count), out_ref.shape)
    out_ref[...] = jnp.where(inside, picked, cache_ref[...])


def update_cache(offset, cache, news, tokens):
    return pl.pallas_call(
        functools.partial(update_kernel, tokens),
        in_specs=[SMEM, VMEM, VMEM],
        out_specs=VMEM,
        out_shape=jax.ShapeDtypeStruct(cache.shape, BF16),
        compiler_params=pltpu.CompilerParams(vmem_limit_bytes=16 << 20),
        name="update_cache",
    )(offset, cache, news)


def exchange(array, axis):
    return lax.all_to_all(array, axis, split_axis=0, concat_axis=0, tiled=True)


def per_device(
    prefill_queries,
    decode_queries,
    new_prefill,
    new_decode,
    prefill_cache,
    decode_cache,
    prefill_offsets,
    decode_lengths,
    dealing,
):
    hi_count = lax.axis_size("hi")
    blk = hi_count * QUAD
    req = lax.axis_size("req")
    ctx = prefill_cache.shape[1]
    tokens = prefill_queries.shape[1]
    slots = decode_cache.shape[0]
    group = lax.axis_index("req")

    pack, table = prepare(prefill_queries, new_prefill, prefill_cache, hi_count)
    packs = exchange(pack, "hi")
    tables = exchange(table, "quad")

    decode_cache_out, decode_part = decode_partials(decode_lengths, decode_queries, new_decode, decode_cache)
    pieces = KEY_VALUE_HEADS * slots // blk
    decode_parts = exchange(decode_part.reshape(blk, pieces, GW + STATS), BLK)

    parts, news = prefill_partials(prefill_offsets, packs, tables, ctx)
    arrived = exchange(parts, "hi")

    decode_parts, news, parts = lax.optimization_barrier((decode_parts, news, parts))
    decode_piece = join_parts(decode_parts, GROUP, "join_decode")
    everywhere = jnp.broadcast_to(decode_piece[None], (req * blk, pieces, GW))
    gathered = exchange(everywhere, ("req",) + BLK)

    prefill_cache_out = update_cache(prefill_offsets, prefill_cache[0], exchange(news, "quad"), tokens)[None]

    attended = join_parts(arrived, QUERY_HEADS, "join_prefill")
    if req == 2:
        other = lax.ppermute(attended, "req", [(0, 1), (1, 0)])
        prefill_out = jnp.where(dealing[group] == group, attended, other)[None]
    else:
        spread = lax.all_gather(attended, "req", axis=0)
        source = jnp.argmax(dealing[:req] == group)
        prefill_out = lax.dynamic_index_in_dim(spread, source, 0, True)

    gathered = gathered.reshape(req, KEY_VALUE_HEADS, slots, GW)
    own = group * slots + jnp.arange(slots, dtype=jnp.int32)
    chosen = (dealing[req:][None, :] == own[:, None]).astype(BF16)
    decode_out = jnp.einsum(
        "ors,rgsf->ogf", chosen.reshape(slots, req, slots), gathered, preferred_element_type=F32
    )
    decode_out = decode_out.reshape(slots, QW).astype(BF16)
    return (prefill_out, decode_out, prefill_cache_out, decode_cache_out)


def solution(mesh):
    blk, req = mesh.shape["blk"], mesh.shape["req"]
    mesh = jax.sharding.Mesh(mesh.devices.reshape(blk // QUAD, QUAD, req), ("hi", "quad", "req"))
    in_specs = (
        P("req", BLK, None),
        P("req", None),
        P("req", BLK, None),
        P("req", None),
        P("req", BLK, None),
        P("req", BLK, None),
        P("req"),
        P("req"),
        P(),
    )
    out_specs = (
        P("req", BLK, None),
        P("req", None),
        P("req", BLK, None),
        P("req", BLK, None),
    )
    return jax.shard_map(
        per_device, mesh=mesh, in_specs=in_specs, out_specs=out_specs, check_vma=False
    )
```

```python
import functools

import jax
import jax.numpy as jnp
from jax import lax
from jax.experimental import pallas as pl
from jax.experimental.pallas import tpu as pltpu
from jax.sharding import PartitionSpec as P

QUERY_HEADS = 8
KEY_VALUE_HEADS = 2
HEAD_SIZE = 128
GROUP = QUERY_HEADS // KEY_VALUE_HEADS
QW = QUERY_HEADS * HEAD_SIZE
KW = KEY_VALUE_HEADS * HEAD_SIZE
STATS = 128
QUAD = 4
SCALE = HEAD_SIZE**-0.5
MASKED = -1e30
FLOOR = -1e20
F32 = jnp.float32
BF16 = jnp.bfloat16

KVW = 2 * KW
CHUNKS = 4
TILE = 16

HBM = pl.BlockSpec(memory_space=pltpu.HBM)
VMEM = pl.BlockSpec(memory_space=pltpu.VMEM)


def dot_t(a, b):
    return lax.dot_general(a, b, (((1,), (1,)), ((), ())), preferred_element_type=F32)


def dot(a, b):
    return lax.dot_general(a, b, (((1,), (0,)), ((), ())), preferred_element_type=F32)


def split3(value):
    high = value.astype(BF16).astype(F32)
    rest = value - high
    middle = rest.astype(BF16).astype(F32)
    return high, middle, rest - middle


def stats_block(columns, rows):
    lane = lax.broadcasted_iota(jnp.int32, (rows, STATS), 1)
    count = len(columns)
    out = jnp.zeros((rows, STATS), F32)
    for head, column in enumerate(columns):
        for term, part in enumerate(split3(column)):
            out = jnp.where(lane == term * count + head, part, out)
    return out.astype(BF16)


def spread_matrix(heads):
    lane = lax.broadcasted_iota(jnp.int32, (STATS, heads * HEAD_SIZE), 0)
    head = lax.broadcasted_iota(jnp.int32, (STATS, heads * HEAD_SIZE), 1) // HEAD_SIZE
    hit = (lane == head) | (lane == head + heads) | (lane == head + 2 * heads)
    return jnp.where(hit, 1.0, 0.0).astype(BF16)


def join(parts):
    spread = spread_matrix(QUERY_HEADS)
    logs = [dot(part[:, QW:], spread) for part in parts]
    top = functools.reduce(jnp.maximum, logs)
    scales = [jnp.exp(log - top) for log in logs]
    total = functools.reduce(jnp.add, scales)
    summed = functools.reduce(
        jnp.add, [scale * part[:, :QW].astype(F32) for scale, part in zip(scales, parts)]
    )
    return (summed / total).astype(BF16), top + jnp.log(total)


def source_group(j):
    return lax.axis_index("req") ^ j if lax.axis_size("req") == 2 else j


def decode_kernel(
    len_hbm,
    off_hbm,
    deal_hbm,
    q_hbm,
    new_hbm,
    cache_hbm,
    out_hbm,
    part_ref,
    off_ref,
    route_ref,
    lens,
    off,
    deal,
    query_ref,
    new_ref,
    table,
    sems,
):
    slots, ctx, _ = table.shape
    rows = GROUP * slots
    chunk = slots // CHUNKS
    base = lax.axis_index("blk") * ctx
    small = [(len_hbm, lens), (off_hbm, off), (deal_hbm, deal), (q_hbm, query_ref), (new_hbm, new_ref)]
    small = [pltpu.make_async_copy(a, b, sems.at[i]) for i, (a, b) in enumerate(small)]
    loads, stores = [], []
    for c in range(CHUNKS):
        part = pl.ds(c * chunk, chunk)
        loads.append(pltpu.make_async_copy(cache_hbm.at[part], table.at[part], sems.at[5 + c]))
        stores.append(pltpu.make_async_copy(table.at[part], out_hbm.at[part], sems.at[5 + CHUNKS + c]))
    for copy in small + loads:
        copy.start()
    for copy in small:
        copy.wait()
    off_ref[...] = jnp.full(off_ref.shape, off[0], jnp.int32)
    group = lax.axis_index("req")
    req = route_ref.shape[0]
    out_row = lax.broadcasted_iota(jnp.int32, (slots, HEAD_SIZE), 0)
    out_lane = lax.broadcasted_iota(jnp.int32, (slots, HEAD_SIZE), 1)
    for j in range(req):
        source = source_group(j)
        chosen = jnp.zeros((slots, HEAD_SIZE), F32)
        for s in range(slots):
            place = deal[req + source * slots + s] - group * slots
            chosen = jnp.where((out_lane == s) & (out_row == place), 1.0, chosen)
        route_ref[j, pl.ds(0, slots), :] = chosen
        mine = (deal[source] == group).astype(F32)
        route_ref[j, pl.ds(slots, 8), :] = jnp.full((8, HEAD_SIZE), mine, F32)
    row_slot = lax.broadcasted_iota(jnp.int32, (rows, ctx), 0) % slots
    column = lax.broadcasted_iota(jnp.int32, (rows, ctx), 1)
    in_tile = lax.broadcasted_iota(jnp.int32, (TILE, KVW), 0)
    limit = jnp.full((rows, ctx), -1, jnp.int32)
    queries = [
        jnp.concatenate(
            [query_ref[:, pl.ds((g * GROUP + h) * HEAD_SIZE, HEAD_SIZE)] for h in range(GROUP)], axis=0
        )
        for g in range(KEY_VALUE_HEADS)
    ]
    scores = [jnp.zeros((rows, ctx), F32) for _ in range(KEY_VALUE_HEADS)]
    for c in range(CHUNKS):
        loads[c].wait()
        for s in range(c * chunk, (c + 1) * chunk):
            relative = lens[s] - base
            limit = jnp.where(row_slot == s, relative, limit)

            @pl.when((relative >= 0) & (relative < ctx))
            def _():
                start = pl.multiple_of(relative // TILE * TILE, TILE)
                tile = table[s, pl.ds(start, TILE), :]
                table[s, pl.ds(start, TILE), :] = jnp.where(
                    in_tile == relative - start, new_ref[s : s + 1, :], tile
                )

        stores[c].start()
        for s in range(c * chunk, (c + 1) * chunk):
            for g in range(KEY_VALUE_HEADS):
                key = table[s, :, pl.ds(g * HEAD_SIZE, HEAD_SIZE)]
                scores[g] = jnp.where(row_slot == s, dot_t(queries[g], key), scores[g])
    visible = column <= limit
    columns = []
    for g in range(KEY_VALUE_HEADS):
        masked = jnp.where(visible, scores[g] * SCALE, MASKED)
        maxima = jnp.maximum(jnp.max(masked, axis=1, keepdims=True), FLOOR)
        weights = jnp.exp(masked - maxima)
        totals = jnp.sum(weights, axis=1, keepdims=True)
        summed = jnp.zeros((rows, HEAD_SIZE), F32)
        for s in range(slots):
            value = table[s, :, pl.ds(KW + g * HEAD_SIZE, HEAD_SIZE)]
            picked = jnp.where(row_slot == s, weights, 0.0).astype(BF16)
            summed += dot(picked, value)
        seen = totals > 0.0
        safe = jnp.where(seen, totals, 1.0)
        normed = (summed / safe).astype(BF16)
        logs = jnp.where(seen, maxima + jnp.log(safe), MASKED)
        for h in range(GROUP):
            part = slice(h * slots, (h + 1) * slots)
            part_ref[:, pl.ds((g * GROUP + h) * HEAD_SIZE, HEAD_SIZE)] = normed[part]
            columns.append(logs[part])
    part_ref[:, pl.ds(QW, STATS)] = stats_block(columns, slots)
    for copy in stores:
        copy.wait()


def decode_partials(lengths, offset, dealing, queries, new_rows, cache, req):
    slots, ctx, width = cache.shape
    return pl.pallas_call(
        decode_kernel,
        in_specs=[HBM] * 6,
        out_specs=[HBM, VMEM, VMEM, VMEM],
        out_shape=[
            jax.ShapeDtypeStruct(cache.shape, BF16),
            jax.ShapeDtypeStruct((slots, QW + STATS), BF16),
            jax.ShapeDtypeStruct((8, HEAD_SIZE), jnp.int32),
            jax.ShapeDtypeStruct((req, slots + 8, HEAD_SIZE), F32),
        ],
        scratch_shapes=[
            pltpu.SMEM(lengths.shape, jnp.int32),
            pltpu.SMEM(offset.shape, jnp.int32),
            pltpu.SMEM(dealing.shape, jnp.int32),
            pltpu.VMEM(queries.shape, BF16),
            pltpu.VMEM(new_rows.shape, BF16),
            pltpu.VMEM(cache.shape, BF16),
            pltpu.SemaphoreType.DMA((5 + 2 * CHUNKS,)),
        ],
        compiler_params=pltpu.CompilerParams(vmem_limit_bytes=16 << 20),
        cost_estimate=pl.CostEstimate(
            flops=4 * slots * ctx * QW, bytes_accessed=2 * cache.size * 2, transcendentals=slots * ctx * 8
        ),
        name="decode_partials",
    )(lengths, offset, dealing, queries, new_rows, cache)


def prepare_kernel(q_hbm, new_hbm, cache_hbm, pack_ref, table_ref, sems):
    ctx, tokens = cache_hbm.shape[1], new_hbm.shape[1]
    copies = [
        (q_hbm.at[0], pack_ref.at[:, pl.ds(0, QW)]),
        (new_hbm.at[0], pack_ref.at[:, pl.ds(QW, KVW)]),
        (cache_hbm.at[0], table_ref.at[pl.ds(0, ctx), :]),
        (new_hbm.at[0], table_ref.at[pl.ds(ctx, tokens), :]),
    ]
    copies = [pltpu.make_async_copy(a, b, sems.at[i]) for i, (a, b) in enumerate(copies)]
    for copy in copies:
        copy.start()
    for copy in copies:
        copy.wait()


def prepare(queries, new_rows, cache):
    tokens, ctx = queries.shape[1], cache.shape[1]
    return pl.pallas_call(
        prepare_kernel,
        in_specs=[HBM] * 3,
        out_specs=[VMEM] * 2,
        out_shape=[
            jax.ShapeDtypeStruct((tokens, QW + KVW), BF16),
            jax.ShapeDtypeStruct((ctx + tokens, KVW), BF16),
        ],
        scratch_shapes=[pltpu.SemaphoreType.DMA((4,))],
        name="prepare",
    )(queries, new_rows, cache)


def prefill_kernel(hi_count, ctx, off_ref, *refs):
    packs, tables, decodes = refs[:hi_count], refs[hi_count : hi_count + QUAD], refs[hi_count + QUAD : -hi_count - 1]
    outs, news = refs[-hi_count - 1 : -1], refs[-1]
    tokens = packs[0].shape[0]
    slots = decodes[0].shape[0]
    span = tables[0].shape[0]
    me = lax.axis_index("blk")
    hi, quad = me // QUAD, me % QUAD
    offset = off_ref[:1, :1]
    pieces = []
    for k in range(QUAD):
        holder = hi * QUAD + (quad ^ k)
        index = lax.broadcasted_iota(jnp.int32, (1, span), 1)
        old = jnp.where(holder * ctx + index < offset, -1, 1 << 30)
        pieces.append(jnp.where(index < ctx, old, holder * tokens + index - ctx))
    key_mark = jnp.concatenate(pieces, axis=1)
    in_block = lax.broadcasted_iota(jnp.int32, (GROUP * tokens, 1), 0) % tokens
    for k in range(1, hi_count):
        news[pl.ds((k - 1) * tokens, tokens), :] = packs[k][:, pl.ds(QW, KVW)]
    lane = lax.broadcasted_iota(jnp.int32, (tokens, STATS), 1)
    stats = [jnp.zeros((tokens, STATS), F32) for _ in range(hi_count)]
    for g in range(KEY_VALUE_HEADS):
        keys = jnp.concatenate([t[:, pl.ds(g * HEAD_SIZE, HEAD_SIZE)] for t in tables], axis=0)
        values = jnp.concatenate([t[:, pl.ds(KW + g * HEAD_SIZE, HEAD_SIZE)] for t in tables], axis=0)
        for k in range(hi_count):
            token = ((hi ^ k) * QUAD + quad) * tokens + in_block
            query = jnp.concatenate(
                [packs[k][:, pl.ds((g * GROUP + h) * HEAD_SIZE, HEAD_SIZE)] for h in range(GROUP)], axis=0
            )
            scores = jnp.where(key_mark <= token, dot_t(query, keys) * SCALE, MASKED)
            maxima = jnp.maximum(jnp.max(scores, axis=1, keepdims=True), FLOOR)
            weights = jnp.exp(scores - maxima)
            totals = jnp.sum(weights, axis=1, keepdims=True)
            summed = dot(weights.astype(BF16), values)
            seen = totals > 0.0
            safe = jnp.where(seen, totals, 1.0)
            normed = (summed / safe).astype(BF16)
            logs = jnp.where(seen, maxima + jnp.log(safe), MASKED)
            for h in range(GROUP):
                part = slice(h * tokens, (h + 1) * tokens)
                outs[k][pl.ds(0, tokens), pl.ds((g * GROUP + h) * HEAD_SIZE, HEAD_SIZE)] = normed[part]
                for term, value in enumerate(split3(logs[part])):
                    stats[k] = jnp.where(lane == term * QUERY_HEADS + g * GROUP + h, value, stats[k])
    joined, logs = join([d[...] for d in decodes])
    joined_stats = stats_block([logs[:, h * HEAD_SIZE : h * HEAD_SIZE + 1] for h in range(QUERY_HEADS)], slots)
    for k in range(hi_count):
        outs[k][pl.ds(0, tokens), pl.ds(QW, STATS)] = stats[k].astype(BF16)
        outs[k][pl.ds(tokens, slots), pl.ds(0, QW)] = joined
        outs[k][pl.ds(tokens, slots), pl.ds(QW, STATS)] = joined_stats


def prefill_partials(offset, packs, tables, decodes, ctx):
    tokens = packs[0].shape[0]
    slots = decodes[0].shape[0]
    pairs = len(packs) * tokens * QUAD * tables[0].shape[0]
    return pl.pallas_call(
        functools.partial(prefill_kernel, len(packs), ctx),
        in_specs=[VMEM] * (1 + len(packs) + len(tables) + len(decodes)),
        out_specs=[VMEM] * (len(packs) + 1),
        out_shape=[jax.ShapeDtypeStruct((tokens + slots, QW + STATS), BF16)] * len(packs)
        + [jax.ShapeDtypeStruct(((len(packs) - 1) * tokens, KVW), BF16)],
        compiler_params=pltpu.CompilerParams(vmem_limit_bytes=32 << 20),
        cost_estimate=pl.CostEstimate(
            flops=4 * pairs * QW, bytes_accessed=4 << 20, transcendentals=pairs * QUERY_HEADS
        ),
        name="prefill_partials",
    )(offset, *packs, *tables, *decodes)


def join_kernel(*refs):
    refs[-1][...] = join([ref[...] for ref in refs[:-1]])[0]


def join_parts(parts):
    return pl.pallas_call(
        join_kernel,
        in_specs=[VMEM] * len(parts),
        out_specs=VMEM,
        out_shape=jax.ShapeDtypeStruct((parts[0].shape[0], QW), BF16),
        compiler_params=pltpu.CompilerParams(vmem_limit_bytes=16 << 20),
        name="join_parts",
    )(*parts)


def update_kernel(hi_count, off_ref, cache_hbm, *refs):
    packs, tables, others = refs[:hi_count], refs[hi_count : hi_count + QUAD], refs[hi_count + QUAD : -3]
    out_ref, cache_ref, sem = refs[-3:]
    load = pltpu.make_async_copy(cache_hbm.at[0], cache_ref, sem)
    load.start()
    ctx = cache_ref.shape[0]
    tokens = packs[0].shape[0]
    me = lax.axis_index("blk")
    hi, quad = me // QUAD, me % QUAD
    blocks = []
    for k in range(hi_count):
        for j in range(QUAD):
            if j == 0:
                blocks.append(packs[k][:, pl.ds(QW, KVW)])
            elif k == 0:
                blocks.append(tables[j][pl.ds(ctx, tokens), :])
            else:
                blocks.append(others[j - 1][pl.ds((k - 1) * tokens, tokens), :])
    rows = jnp.concatenate(blocks, axis=0)
    count = rows.shape[0]
    index = lax.broadcasted_iota(jnp.int32, (1, count), 1)
    block = index // tokens
    token = ((hi ^ (block // QUAD)) * QUAD + (quad ^ (block % QUAD))) * tokens + index % tokens
    wanted = me * ctx + lax.broadcasted_iota(jnp.int32, (ctx, 1), 0) - off_ref[:1, :1]
    picked = dot(jnp.where(wanted == token, 1.0, 0.0).astype(BF16), rows).astype(BF16)
    inside = jnp.broadcast_to((wanted >= 0) & (wanted < count), cache_ref.shape)
    load.wait()
    out_ref[0] = jnp.where(inside, picked, cache_ref[...])


def update_cache(offset, cache, packs, tables, others):
    return pl.pallas_call(
        functools.partial(update_kernel, len(packs)),
        in_specs=[VMEM, HBM] + [VMEM] * (len(packs) + len(tables) + len(others)),
        out_specs=VMEM,
        out_shape=jax.ShapeDtypeStruct(cache.shape, BF16),
        scratch_shapes=[pltpu.VMEM(cache.shape[1:], BF16), pltpu.SemaphoreType.DMA],
        compiler_params=pltpu.CompilerParams(vmem_limit_bytes=16 << 20),
        name="update_cache",
    )(offset, cache, *packs, *tables, *others)


def route_kernel(count, route_ref, *refs):
    held, (pre_ref, dec_ref) = refs[:-2], refs[-2:]
    if len(held) < count:
        held = [held[0].at[j] for j in range(count)]
    tokens, slots = pre_ref.shape[1], dec_ref.shape[0]
    prefill = jnp.zeros(pre_ref.shape[1:], F32)
    decode = jnp.zeros(dec_ref.shape, F32)
    for j in range(count):
        flag = route_ref[j, pl.ds(slots, 1), pl.ds(0, 1)]
        prefill += flag * held[j][pl.ds(0, tokens), :].astype(F32)
        chosen = route_ref[j, pl.ds(0, slots), pl.ds(0, slots)].astype(BF16)
        decode += dot(chosen, held[j][pl.ds(tokens, slots), :])
    pre_ref[0] = prefill.astype(BF16)
    dec_ref[...] = decode.astype(BF16)


def route_outputs(route, held, tokens, slots):
    return pl.pallas_call(
        functools.partial(route_kernel, route.shape[0]),
        in_specs=[VMEM] * (1 + len(held)),
        out_specs=[VMEM] * 2,
        out_shape=[
            jax.ShapeDtypeStruct((1, tokens, QW), BF16),
            jax.ShapeDtypeStruct((slots, QW), BF16),
        ],
        compiler_params=pltpu.CompilerParams(vmem_limit_bytes=16 << 20),
        name="route_outputs",
    )(route, *held)


def per_device(
    prefill_queries,
    decode_queries,
    new_prefill,
    new_decode,
    prefill_cache,
    decode_cache,
    prefill_offsets,
    decode_lengths,
    dealing,
):
    blk = lax.axis_size("blk")
    req = lax.axis_size("req")
    hi_count = blk // QUAD
    ctx = prefill_cache.shape[1]
    tokens = prefill_queries.shape[1]
    slots = decode_cache.shape[0]

    def swap(array, distance):
        return lax.ppermute(array, "blk", [(i, i ^ distance) for i in range(blk)])

    def over_quad(array):
        beside, across = swap(array, 1), swap(array, 2)
        return [beside, across, swap(across, 1)]

    pack, table = prepare(prefill_queries, new_prefill, prefill_cache)
    packs = [pack] + [swap(pack, k * QUAD) for k in range(1, hi_count)]
    tables = [table] + over_quad(table)

    decode_cache_out, decode_part, offset, route = decode_partials(
        decode_lengths, prefill_offsets, dealing, decode_queries, new_decode, decode_cache, req
    )
    decodes = [decode_part] + [swap(decode_part, k) for k in range(1, QUAD)]

    *parts, news = prefill_partials(offset, packs, tables, decodes, ctx)
    arrived = [parts[0]] + [swap(parts[k], k * QUAD) for k in range(1, hi_count)]
    attended = join_parts(arrived)

    prefill_cache_out = update_cache(offset, prefill_cache, packs, tables, over_quad(news))

    if req == 2:
        held = [attended, lax.ppermute(attended, "req", [(0, 1), (1, 0)])]
    else:
        held = [lax.all_gather(attended, "req", axis=0)]
    prefill_out, decode_out = route_outputs(route, held, tokens, slots)
    return (prefill_out, decode_out, prefill_cache_out, decode_cache_out)


def solution(mesh):
    in_specs = (
        P("req", "blk", None),
        P("req", None),
        P("req", "blk", None),
        P("req", None),
        P("req", "blk", None),
        P("req", "blk", None),
        P("req"),
        P("req"),
        P(),
    )
    out_specs = (
        P("req", "blk", None),
        P("req", None),
        P("req", "blk", None),
        P("req", "blk", None),
    )
    return jax.shard_map(
        per_device, mesh=mesh, in_specs=in_specs, out_specs=out_specs, check_vma=False
    )
```

```python
import functools

import jax
import jax.numpy as jnp
from jax import lax
from jax.experimental import pallas as pl
from jax.experimental.pallas import tpu as pltpu
from jax.sharding import PartitionSpec as P

QUERY_HEADS = 8
KEY_VALUE_HEADS = 2
HEAD_SIZE = 128
GROUP = QUERY_HEADS // KEY_VALUE_HEADS
QW = QUERY_HEADS * HEAD_SIZE
KW = KEY_VALUE_HEADS * HEAD_SIZE
STATS = 128
QUAD = 4
KEY_SET = 8
SCALE = HEAD_SIZE**-0.5
MASKED = -1e30
FLOOR = -1e20
F32 = jnp.float32
BF16 = jnp.bfloat16

KVW = 2 * KW
BLK = ("hi", "quad")
CHUNKS = 4
TILE = 16

HBM = pl.BlockSpec(memory_space=pltpu.HBM)
VMEM = pl.BlockSpec(memory_space=pltpu.VMEM)


def dot_t(a, b):
    return lax.dot_general(a, b, (((1,), (1,)), ((), ())), preferred_element_type=F32)


def dot(a, b):
    return lax.dot_general(a, b, (((1,), (0,)), ((), ())), preferred_element_type=F32)


def split3(value):
    high = value.astype(BF16).astype(F32)
    rest = value - high
    middle = rest.astype(BF16).astype(F32)
    return high, middle, rest - middle


def stats_block(columns, rows):
    lane = lax.broadcasted_iota(jnp.int32, (rows, STATS), 1)
    count = len(columns)
    out = jnp.zeros((rows, STATS), F32)
    for head, column in enumerate(columns):
        for term, part in enumerate(split3(column)):
            out = jnp.where(lane == term * count + head, part, out)
    return out.astype(BF16)


def spread_matrix(heads):
    lane = lax.broadcasted_iota(jnp.int32, (STATS, heads * HEAD_SIZE), 0)
    head = lax.broadcasted_iota(jnp.int32, (STATS, heads * HEAD_SIZE), 1) // HEAD_SIZE
    hit = (lane == head) | (lane == head + heads) | (lane == head + 2 * heads)
    return jnp.where(hit, 1.0, 0.0).astype(BF16)


def join(parts):
    spread = spread_matrix(QUERY_HEADS)
    logs = [dot(part[:, QW:], spread) for part in parts]
    top = functools.reduce(jnp.maximum, logs)
    scales = [jnp.exp(log - top) for log in logs]
    total = functools.reduce(jnp.add, scales)
    summed = functools.reduce(
        jnp.add, [scale * part[:, :QW].astype(F32) for scale, part in zip(scales, parts)]
    )
    return (summed / total).astype(BF16), top + jnp.log(total)


def source_group(j):
    return lax.axis_index("req") ^ j if lax.axis_size("req") == 2 else j


def decode_kernel(
    len_hbm,
    off_hbm,
    deal_hbm,
    q_hbm,
    new_hbm,
    cache_hbm,
    pre_new_hbm,
    pre_cache_hbm,
    out_hbm,
    shared_ref,
    off_ref,
    route_ref,
    lens,
    off,
    deal,
    query_ref,
    new_ref,
    table,
    sems,
):
    slots, ctx, _ = table.shape
    rows = GROUP * slots
    chunk = slots // CHUNKS
    base = lax.axis_index(BLK) * ctx
    tokens = pre_new_hbm.shape[1]
    first = ctx + tokens
    small = [
        (len_hbm, lens),
        (off_hbm, off),
        (deal_hbm, deal),
        (q_hbm, query_ref),
        (new_hbm, new_ref),
        (pre_cache_hbm.at[0], shared_ref.at[pl.ds(0, ctx), :]),
        (pre_new_hbm.at[0], shared_ref.at[pl.ds(ctx, tokens), :]),
    ]
    small = [pltpu.make_async_copy(a, b, sems.at[i]) for i, (a, b) in enumerate(small)]
    loads, stores = [], []
    for c in range(CHUNKS):
        part = pl.ds(c * chunk, chunk)
        loads.append(pltpu.make_async_copy(cache_hbm.at[part], table.at[part], sems.at[7 + c]))
        stores.append(pltpu.make_async_copy(table.at[part], out_hbm.at[part], sems.at[7 + CHUNKS + c]))
    for copy in small + loads:
        copy.start()
    for copy in small:
        copy.wait()
    off_ref[...] = jnp.full(off_ref.shape, off[0], jnp.int32)
    group = lax.axis_index("req")
    req = route_ref.shape[0]
    out_row = lax.broadcasted_iota(jnp.int32, (slots, HEAD_SIZE), 0)
    out_lane = lax.broadcasted_iota(jnp.int32, (slots, HEAD_SIZE), 1)
    for j in range(req):
        source = source_group(j)
        chosen = jnp.zeros((slots, HEAD_SIZE), F32)
        for s in range(slots):
            place = deal[req + source * slots + s] - group * slots
            chosen = jnp.where((out_lane == s) & (out_row == place), 1.0, chosen)
        route_ref[j, pl.ds(0, slots), :] = chosen
        mine = (deal[source] == group).astype(F32)
        route_ref[j, pl.ds(slots, 8), :] = jnp.full((8, HEAD_SIZE), mine, F32)
    row_slot = lax.broadcasted_iota(jnp.int32, (rows, ctx), 0) % slots
    column = lax.broadcasted_iota(jnp.int32, (rows, ctx), 1)
    in_tile = lax.broadcasted_iota(jnp.int32, (TILE, KVW), 0)
    limit = jnp.full((rows, ctx), -1, jnp.int32)
    queries = [
        jnp.concatenate(
            [query_ref[:, pl.ds((g * GROUP + h) * HEAD_SIZE, HEAD_SIZE)] for h in range(GROUP)], axis=0
        )
        for g in range(KEY_VALUE_HEADS)
    ]
    scores = [jnp.zeros((rows, ctx), F32) for _ in range(KEY_VALUE_HEADS)]
    for c in range(CHUNKS):
        loads[c].wait()
        for s in range(c * chunk, (c + 1) * chunk):
            relative = lens[s] - base
            limit = jnp.where(row_slot == s, relative, limit)

            @pl.when((relative >= 0) & (relative < ctx))
            def _():
                start = pl.multiple_of(relative // TILE * TILE, TILE)
                tile = table[s, pl.ds(start, TILE), :]
                table[s, pl.ds(start, TILE), :] = jnp.where(
                    in_tile == relative - start, new_ref[s : s + 1, :], tile
                )

        stores[c].start()
        for s in range(c * chunk, (c + 1) * chunk):
            for g in range(KEY_VALUE_HEADS):
                key = table[s, :, pl.ds(g * HEAD_SIZE, HEAD_SIZE)]
                scores[g] = jnp.where(row_slot == s, dot_t(queries[g], key), scores[g])
    visible = column <= limit
    columns = []
    for g in range(KEY_VALUE_HEADS):
        masked = jnp.where(visible, scores[g] * SCALE, MASKED)
        maxima = jnp.maximum(jnp.max(masked, axis=1, keepdims=True), FLOOR)
        weights = jnp.exp(masked - maxima)
        totals = jnp.sum(weights, axis=1, keepdims=True)
        summed = jnp.zeros((rows, HEAD_SIZE), F32)
        for s in range(slots):
            value = table[s, :, pl.ds(KW + g * HEAD_SIZE, HEAD_SIZE)]
            picked = jnp.where(row_slot == s, weights, 0.0).astype(BF16)
            summed += dot(picked, value)
        seen = totals > 0.0
        safe = jnp.where(seen, totals, 1.0)
        normed = (summed / safe).astype(BF16)
        logs = jnp.where(seen, maxima + jnp.log(safe), MASKED)
        for h in range(GROUP):
            part = slice(h * slots, (h + 1) * slots)
            shared_ref[pl.ds(first + g * slots, slots), pl.ds(h * HEAD_SIZE, HEAD_SIZE)] = normed[part]
            columns.append(logs[part])
    last = pl.ds(first + KEY_VALUE_HEADS * slots, slots)
    shared_ref[last, pl.ds(0, STATS)] = stats_block(columns, slots)
    shared_ref[last, pl.ds(STATS, KVW - STATS)] = jnp.zeros((slots, KVW - STATS), BF16)
    for copy in stores:
        copy.wait()


def decode_partials(lengths, offset, dealing, queries, new_rows, cache, pre_new, pre_cache, req):
    slots, ctx, width = cache.shape
    rows = ctx + pre_new.shape[1] + (KEY_VALUE_HEADS + 1) * slots
    return pl.pallas_call(
        decode_kernel,
        in_specs=[HBM] * 8,
        out_specs=[HBM, VMEM, VMEM, VMEM],
        out_shape=[
            jax.ShapeDtypeStruct(cache.shape, BF16),
            jax.ShapeDtypeStruct((rows, KVW), BF16),
            jax.ShapeDtypeStruct((8, HEAD_SIZE), jnp.int32),
            jax.ShapeDtypeStruct((req, slots + 8, HEAD_SIZE), F32),
        ],
        scratch_shapes=[
            pltpu.SMEM(lengths.shape, jnp.int32),
            pltpu.SMEM(offset.shape, jnp.int32),
            pltpu.SMEM(dealing.shape, jnp.int32),
            pltpu.VMEM(queries.shape, BF16),
            pltpu.VMEM(new_rows.shape, BF16),
            pltpu.VMEM(cache.shape, BF16),
            pltpu.SemaphoreType.DMA((7 + 2 * CHUNKS,)),
        ],
        cost_estimate=pl.CostEstimate(
            flops=4 * slots * ctx * QW, bytes_accessed=2 * cache.size * 2, transcendentals=slots * ctx * 8
        ),
        name="decode_partials",
    )(lengths, offset, dealing, queries, new_rows, cache, pre_new, pre_cache)


def prefill_kernel(query_count, ctx, slots, off_ref, *refs):
    packs, tables, outs = refs[:query_count], refs[query_count:-query_count], refs[-query_count:]
    packs = [packs[0].at[0]] + list(packs[1:])
    tokens = packs[0].shape[0]
    span = ctx + tokens
    me = lax.axis_index(BLK)
    offset = off_ref[:1, :1]
    pieces = []
    for k in range(KEY_SET):
        holder = me ^ k
        index = lax.broadcasted_iota(jnp.int32, (1, span), 1)
        old = jnp.where(holder * ctx + index < offset, -1, 1 << 30)
        pieces.append(jnp.where(index < ctx, old, holder * tokens + index - ctx))
    key_mark = jnp.concatenate(pieces, axis=1)
    in_block = lax.broadcasted_iota(jnp.int32, (GROUP * tokens, 1), 0) % tokens
    lane = lax.broadcasted_iota(jnp.int32, (tokens, STATS), 1)
    stats = [jnp.zeros((tokens, STATS), F32) for _ in range(query_count)]
    for g in range(KEY_VALUE_HEADS):
        keys = jnp.concatenate([t[pl.ds(0, span), pl.ds(g * HEAD_SIZE, HEAD_SIZE)] for t in tables], axis=0)
        values = jnp.concatenate([t[pl.ds(0, span), pl.ds(KW + g * HEAD_SIZE, HEAD_SIZE)] for t in tables], axis=0)
        for k in range(query_count):
            token = (me ^ (k * KEY_SET)) * tokens + in_block
            query = jnp.concatenate(
                [packs[k][:, pl.ds((g * GROUP + h) * HEAD_SIZE, HEAD_SIZE)] for h in range(GROUP)], axis=0
            )
            scores = jnp.where(key_mark <= token, dot_t(query, keys) * SCALE, MASKED)
            maxima = jnp.maximum(jnp.max(scores, axis=1, keepdims=True), FLOOR)
            weights = jnp.exp(scores - maxima)
            totals = jnp.sum(weights, axis=1, keepdims=True)
            summed = dot(weights.astype(BF16), values)
            seen = totals > 0.0
            safe = jnp.where(seen, totals, 1.0)
            normed = (summed / safe).astype(BF16)
            logs = jnp.where(seen, maxima + jnp.log(safe), MASKED)
            for h in range(GROUP):
                part = slice(h * tokens, (h + 1) * tokens)
                outs[k][pl.ds(0, tokens), pl.ds((g * GROUP + h) * HEAD_SIZE, HEAD_SIZE)] = normed[part]
                for term, value in enumerate(split3(logs[part])):
                    stats[k] = jnp.where(lane == term * QUERY_HEADS + g * GROUP + h, value, stats[k])
    decodes = [
        jnp.concatenate(
            [t[pl.ds(span + g * slots, slots), :] for g in range(KEY_VALUE_HEADS)]
            + [t[pl.ds(span + KEY_VALUE_HEADS * slots, slots), pl.ds(0, STATS)]],
            axis=1,
        )
        for t in tables
    ]
    joined, logs = join(decodes)
    joined_stats = stats_block([logs[:, h * HEAD_SIZE : h * HEAD_SIZE + 1] for h in range(QUERY_HEADS)], slots)
    for k in range(query_count):
        outs[k][pl.ds(0, tokens), pl.ds(QW, STATS)] = stats[k].astype(BF16)
        outs[k][pl.ds(tokens, slots), pl.ds(0, QW)] = joined
        outs[k][pl.ds(tokens, slots), pl.ds(QW, STATS)] = joined_stats


def prefill_partials(offset, packs, tables, ctx, slots):
    tokens = packs[0].shape[1]
    pairs = len(packs) * tokens * KEY_SET * (ctx + tokens)
    return pl.pallas_call(
        functools.partial(prefill_kernel, len(packs), ctx, slots),
        in_specs=[VMEM] * (1 + len(packs) + len(tables)),
        out_specs=[VMEM] * len(packs),
        out_shape=[jax.ShapeDtypeStruct((tokens + slots, QW + STATS), BF16)] * len(packs),
        compiler_params=pltpu.CompilerParams(vmem_limit_bytes=32 << 20),
        cost_estimate=pl.CostEstimate(
            flops=4 * pairs * QW, bytes_accessed=4 << 20, transcendentals=pairs * QUERY_HEADS
        ),
        name="prefill_partials",
    )(offset, *packs, *tables)


def join_kernel(*refs):
    refs[-1][...] = join([ref[...] for ref in refs[:-1]])[0]


def join_parts(parts):
    return pl.pallas_call(
        join_kernel,
        in_specs=[VMEM] * len(parts),
        out_specs=VMEM,
        out_shape=jax.ShapeDtypeStruct((parts[0].shape[0], QW), BF16),
        compiler_params=pltpu.CompilerParams(vmem_limit_bytes=16 << 20),
        name="join_parts",
    )(*parts)


def update_kernel(tokens, off_ref, cache_hbm, news, out_ref, cache_ref, sem):
    load = pltpu.make_async_copy(cache_hbm.at[0], cache_ref, sem)
    load.start()
    ctx = cache_ref.shape[0]
    count = news.shape[0]
    hi_count = count // (QUAD * tokens)
    index = lax.broadcasted_iota(jnp.int32, (1, count), 1)
    block = index // tokens
    token = ((block % hi_count) * QUAD + block // hi_count) * tokens + index % tokens
    wanted = lax.axis_index(BLK) * ctx + lax.broadcasted_iota(jnp.int32, (ctx, 1), 0) - off_ref[:1, :1]
    picked = dot(jnp.where(wanted == token, 1.0, 0.0).astype(BF16), news[...]).astype(BF16)
    inside = jnp.broadcast_to((wanted >= 0) & (wanted < count), cache_ref.shape)
    load.wait()
    out_ref[0] = jnp.where(inside, picked, cache_ref[...])


def update_cache(offset, cache, news, tokens):
    return pl.pallas_call(
        functools.partial(update_kernel, tokens),
        in_specs=[VMEM, HBM, VMEM],
        out_specs=VMEM,
        out_shape=jax.ShapeDtypeStruct(cache.shape, BF16),
        scratch_shapes=[pltpu.VMEM(cache.shape[1:], BF16), pltpu.SemaphoreType.DMA],
        compiler_params=pltpu.CompilerParams(vmem_limit_bytes=16 << 20),
        name="update_cache",
    )(offset, cache, news)


def route_kernel(count, route_ref, *refs):
    held, (pre_ref, dec_ref) = refs[:-2], refs[-2:]
    if len(held) < count:
        held = [held[0].at[j] for j in range(count)]
    tokens, slots = pre_ref.shape[1], dec_ref.shape[0]
    prefill = jnp.zeros(pre_ref.shape[1:], F32)
    decode = jnp.zeros(dec_ref.shape, F32)
    for j in range(count):
        flag = route_ref[j, pl.ds(slots, 1), pl.ds(0, 1)]
        prefill += flag * held[j][pl.ds(0, tokens), :].astype(F32)
        chosen = route_ref[j, pl.ds(0, slots), pl.ds(0, slots)].astype(BF16)
        decode += dot(chosen, held[j][pl.ds(tokens, slots), :])
    pre_ref[0] = prefill.astype(BF16)
    dec_ref[...] = decode.astype(BF16)


def route_outputs(route, held, tokens, slots):
    return pl.pallas_call(
        functools.partial(route_kernel, route.shape[0]),
        in_specs=[VMEM] * (1 + len(held)),
        out_specs=[VMEM] * 2,
        out_shape=[
            jax.ShapeDtypeStruct((1, tokens, QW), BF16),
            jax.ShapeDtypeStruct((slots, QW), BF16),
        ],
        compiler_params=pltpu.CompilerParams(vmem_limit_bytes=16 << 20),
        name="route_outputs",
    )(route, *held)


def per_device(
    prefill_queries,
    decode_queries,
    new_prefill,
    new_decode,
    prefill_cache,
    decode_cache,
    prefill_offsets,
    decode_lengths,
    dealing,
):
    blk = lax.axis_size(BLK)
    req = lax.axis_size("req")
    ctx = prefill_cache.shape[1]
    tokens = prefill_queries.shape[1]
    slots = decode_cache.shape[0]

    def swap(array, distance):
        return lax.ppermute(array, BLK, [(i, i ^ distance) for i in range(blk)])

    packs = [prefill_queries] + [swap(prefill_queries[0], k) for k in range(KEY_SET, blk, KEY_SET)]
    news = lax.all_gather(new_prefill[0], "hi", axis=0, tiled=True)
    news = lax.all_gather(news, "quad", axis=0, tiled=True)

    decode_cache_out, table, offset, route = decode_partials(
        decode_lengths,
        prefill_offsets,
        dealing,
        decode_queries,
        new_decode,
        decode_cache,
        new_prefill,
        prefill_cache,
        req,
    )
    lanes = [table] + [swap(table, k) for k in range(2, KEY_SET, 2)]
    tables = [t for lane in lanes for t in (lane, swap(lane, 1))]

    parts = prefill_partials(offset, packs, tables, ctx, slots)
    attended = join_parts([parts[0]] + [swap(part, k * KEY_SET) for k, part in enumerate(parts) if k])

    prefill_cache_out = update_cache(offset, prefill_cache, news, tokens)

    if req == 2:
        held = [attended, lax.ppermute(attended, "req", [(0, 1), (1, 0)])]
    else:
        held = [lax.all_gather(attended, "req", axis=0)]
    prefill_out, decode_out = route_outputs(route, held, tokens, slots)
    return (prefill_out, decode_out, prefill_cache_out, decode_cache_out)


def solution(mesh):
    blk, req = mesh.shape["blk"], mesh.shape["req"]
    mesh = jax.sharding.Mesh(mesh.devices.reshape(blk // QUAD, QUAD, req), ("hi", "quad", "req"))
    in_specs = (
        P("req", BLK, None),
        P("req", None),
        P("req", BLK, None),
        P("req", None),
        P("req", BLK, None),
        P("req", BLK, None),
        P("req"),
        P("req"),
        P(),
    )
    out_specs = (
        P("req", BLK, None),
        P("req", None),
        P("req", BLK, None),
        P("req", BLK, None),
    )
    return jax.shard_map(
        per_device, mesh=mesh, in_specs=in_specs, out_specs=out_specs, check_vma=False
    )
```

```python
import functools

import jax
import jax.numpy as jnp
from jax import lax
from jax.experimental import pallas as pl
from jax.experimental.pallas import tpu as pltpu
from jax.sharding import PartitionSpec as P

QUERY_HEADS = 8
KEY_VALUE_HEADS = 2
HEAD_SIZE = 128
GROUP = QUERY_HEADS // KEY_VALUE_HEADS
QW = QUERY_HEADS * HEAD_SIZE
KW = KEY_VALUE_HEADS * HEAD_SIZE
STATS = 128
QUAD = 4
KEY_SET = 8
SCALE = HEAD_SIZE**-0.5
MASKED = -1e30
FLOOR = -1e20
F32 = jnp.float32
BF16 = jnp.bfloat16

KVW = 2 * KW
BLK = ("hi", "quad")
CHUNKS = 4
TILE = 16

HBM = pl.BlockSpec(memory_space=pltpu.HBM)
SMEM = pl.BlockSpec(memory_space=pltpu.SMEM)
VMEM = pl.BlockSpec(memory_space=pltpu.VMEM)


def dot_t(a, b):
    return lax.dot_general(a, b, (((1,), (1,)), ((), ())), preferred_element_type=F32)


def dot(a, b):
    return lax.dot_general(a, b, (((1,), (0,)), ((), ())), preferred_element_type=F32)


def split3(value):
    high = value.astype(BF16).astype(F32)
    rest = value - high
    middle = rest.astype(BF16).astype(F32)
    return high, middle, rest - middle


def stats_block(columns, rows):
    lane = lax.broadcasted_iota(jnp.int32, (rows, STATS), 1)
    count = len(columns)
    out = jnp.zeros((rows, STATS), F32)
    for head, column in enumerate(columns):
        for term, part in enumerate(split3(column)):
            out = jnp.where(lane == term * count + head, part, out)
    return out.astype(BF16)


def spread_matrix(heads):
    lane = lax.broadcasted_iota(jnp.int32, (STATS, heads * HEAD_SIZE), 0)
    head = lax.broadcasted_iota(jnp.int32, (STATS, heads * HEAD_SIZE), 1) // HEAD_SIZE
    hit = (lane == head) | (lane == head + heads) | (lane == head + 2 * heads)
    return jnp.where(hit, 1.0, 0.0).astype(BF16)


def join(parts):
    spread = spread_matrix(QUERY_HEADS)
    logs = [dot(part[:, QW:], spread) for part in parts]
    top = functools.reduce(jnp.maximum, logs)
    scales = [jnp.exp(log - top) for log in logs]
    total = functools.reduce(jnp.add, scales)
    summed = functools.reduce(
        jnp.add, [scale * part[:, :QW].astype(F32) for scale, part in zip(scales, parts)]
    )
    return (summed / total).astype(BF16), top + jnp.log(total)


def source_group(j):
    return lax.axis_index("req") ^ j if lax.axis_size("req") == 2 else j


def decode_kernel(
    len_hbm,
    deal_hbm,
    q_hbm,
    new_hbm,
    cache_hbm,
    pre_q_hbm,
    pre_new_hbm,
    pre_cache_hbm,
    out_hbm,
    shared_ref,
    pre_q_ref,
    route_ref,
    lens,
    deal,
    query_ref,
    new_ref,
    table,
    sems,
):
    slots, ctx, _ = table.shape
    rows = GROUP * slots
    chunk = slots // CHUNKS
    base = lax.axis_index(BLK) * ctx
    tokens = pre_new_hbm.shape[1]
    first = ctx + tokens
    small = [
        (len_hbm, lens),
        (deal_hbm, deal),
        (q_hbm, query_ref),
        (new_hbm, new_ref),
        (pre_q_hbm.at[0], pre_q_ref),
        (pre_cache_hbm.at[0], shared_ref.at[pl.ds(0, ctx), :]),
        (pre_new_hbm.at[0], shared_ref.at[pl.ds(ctx, tokens), :]),
    ]
    small = [pltpu.make_async_copy(a, b, sems.at[i]) for i, (a, b) in enumerate(small)]
    loads, stores = [], []
    for c in range(CHUNKS):
        part = pl.ds(c * chunk, chunk)
        loads.append(pltpu.make_async_copy(cache_hbm.at[part], table.at[part], sems.at[7 + c]))
        stores.append(pltpu.make_async_copy(table.at[part], out_hbm.at[part], sems.at[7 + CHUNKS + c]))
    for copy in small + loads:
        copy.start()
    for copy in small:
        copy.wait()
    group = lax.axis_index("req")
    req = route_ref.shape[0]
    out_row = lax.broadcasted_iota(jnp.int32, (slots, HEAD_SIZE), 0)
    out_lane = lax.broadcasted_iota(jnp.int32, (slots, HEAD_SIZE), 1)
    for j in range(req):
        source = source_group(j)
        chosen = jnp.zeros((slots, HEAD_SIZE), F32)
        for s in range(slots):
            place = deal[req + source * slots + s] - group * slots
            chosen = jnp.where((out_lane == s) & (out_row == place), 1.0, chosen)
        route_ref[j, pl.ds(0, slots), :] = chosen
        mine = (deal[source] == group).astype(F32)
        route_ref[j, pl.ds(slots, 8), :] = jnp.full((8, HEAD_SIZE), mine, F32)
    row_slot = lax.broadcasted_iota(jnp.int32, (rows, ctx), 0) % slots
    column = lax.broadcasted_iota(jnp.int32, (rows, ctx), 1)
    in_tile = lax.broadcasted_iota(jnp.int32, (TILE, KVW), 0)
    limit = jnp.full((rows, ctx), -1, jnp.int32)
    queries = [
        jnp.concatenate(
            [query_ref[:, pl.ds((g * GROUP + h) * HEAD_SIZE, HEAD_SIZE)] for h in range(GROUP)], axis=0
        )
        for g in range(KEY_VALUE_HEADS)
    ]
    scores = [jnp.zeros((rows, ctx), F32) for _ in range(KEY_VALUE_HEADS)]
    for c in range(CHUNKS):
        loads[c].wait()
        for s in range(c * chunk, (c + 1) * chunk):
            relative = lens[s] - base
            limit = jnp.where(row_slot == s, relative, limit)

            @pl.when((relative >= 0) & (relative < ctx))
            def _():
                start = pl.multiple_of(relative // TILE * TILE, TILE)
                tile = table[s, pl.ds(start, TILE), :]
                table[s, pl.ds(start, TILE), :] = jnp.where(
                    in_tile == relative - start, new_ref[s : s + 1, :], tile
                )

        stores[c].start()
        for s in range(c * chunk, (c + 1) * chunk):
            for g in range(KEY_VALUE_HEADS):
                key = table[s, :, pl.ds(g * HEAD_SIZE, HEAD_SIZE)]
                scores[g] = jnp.where(row_slot == s, dot_t(queries[g], key), scores[g])
    visible = column <= limit
    columns = []
    for g in range(KEY_VALUE_HEADS):
        masked = jnp.where(visible, scores[g] * SCALE, MASKED)
        maxima = jnp.maximum(jnp.max(masked, axis=1, keepdims=True), FLOOR)
        weights = jnp.exp(masked - maxima)
        totals = jnp.sum(weights, axis=1, keepdims=True)
        summed = jnp.zeros((rows, HEAD_SIZE), F32)
        for s in range(slots):
            value = table[s, :, pl.ds(KW + g * HEAD_SIZE, HEAD_SIZE)]
            picked = jnp.where(row_slot == s, weights, 0.0).astype(BF16)
            summed += dot(picked, value)
        seen = totals > 0.0
        safe = jnp.where(seen, totals, 1.0)
        normed = (summed / safe).astype(BF16)
        logs = jnp.where(seen, maxima + jnp.log(safe), MASKED)
        for h in range(GROUP):
            part = slice(h * slots, (h + 1) * slots)
            shared_ref[pl.ds(first + g * slots, slots), pl.ds(h * HEAD_SIZE, HEAD_SIZE)] = normed[part]
            columns.append(logs[part])
    last = pl.ds(first + KEY_VALUE_HEADS * slots, slots)
    shared_ref[last, pl.ds(0, STATS)] = stats_block(columns, slots)
    shared_ref[last, pl.ds(STATS, KVW - STATS)] = jnp.zeros((slots, KVW - STATS), BF16)
    for copy in stores:
        copy.wait()


def decode_partials(lengths, dealing, queries, new_rows, cache, pre_queries, pre_new, pre_cache, req):
    slots, ctx, width = cache.shape
    rows = ctx + pre_new.shape[1] + (KEY_VALUE_HEADS + 1) * slots
    inputs = (lengths, dealing, queries, new_rows, cache, pre_queries, pre_new, pre_cache)
    return pl.pallas_call(
        decode_kernel,
        in_specs=[HBM] * len(inputs),
        out_specs=[HBM, VMEM, VMEM, VMEM],
        out_shape=[
            pltpu.HBM(cache.shape, BF16),
            pltpu.VMEM((rows, KVW), BF16),
            pltpu.VMEM(pre_queries.shape[1:], BF16),
            pltpu.VMEM((req, slots + 8, HEAD_SIZE), F32),
        ],
        scratch_shapes=[
            pltpu.SMEM(lengths.shape, jnp.int32),
            pltpu.SMEM(dealing.shape, jnp.int32),
            pltpu.VMEM(queries.shape, BF16),
            pltpu.VMEM(new_rows.shape, BF16),
            pltpu.VMEM(cache.shape, BF16),
            pltpu.SemaphoreType.DMA((7 + 2 * CHUNKS,)),
        ],
        compiler_params=pltpu.CompilerParams(vmem_limit_bytes=16 << 20),
        cost_estimate=pl.CostEstimate(
            flops=4 * slots * ctx * QW, bytes_accessed=2 * cache.size * 2, transcendentals=slots * ctx * 8
        ),
        name="decode_partials",
    )(*[pltpu.with_memory_space_constraint(x, pltpu.HBM) for x in inputs])


def prefill_kernel(query_count, ctx, slots, off_ref, *refs):
    packs, tables, outs = refs[:query_count], refs[query_count:-query_count], refs[-query_count:]
    tokens = packs[0].shape[0]
    span = ctx + tokens
    me = lax.axis_index(BLK)
    offset = off_ref[0]
    pieces = []
    for k in range(KEY_SET):
        holder = me ^ k
        index = lax.broadcasted_iota(jnp.int32, (1, span), 1)
        old = jnp.where(holder * ctx + index < offset, -1, 1 << 30)
        pieces.append(jnp.where(index < ctx, old, holder * tokens + index - ctx))
    key_mark = jnp.concatenate(pieces, axis=1)
    in_block = lax.broadcasted_iota(jnp.int32, (GROUP * tokens, 1), 0) % tokens
    lane = lax.broadcasted_iota(jnp.int32, (tokens, STATS), 1)
    stats = [jnp.zeros((tokens, STATS), F32) for _ in range(query_count)]
    for g in range(KEY_VALUE_HEADS):
        keys = jnp.concatenate([t[pl.ds(0, span), pl.ds(g * HEAD_SIZE, HEAD_SIZE)] for t in tables], axis=0)
        values = jnp.concatenate([t[pl.ds(0, span), pl.ds(KW + g * HEAD_SIZE, HEAD_SIZE)] for t in tables], axis=0)
        for k in range(query_count):
            token = (me ^ (k * KEY_SET)) * tokens + in_block
            query = jnp.concatenate(
                [packs[k][:, pl.ds((g * GROUP + h) * HEAD_SIZE, HEAD_SIZE)] for h in range(GROUP)], axis=0
            )
            scores = jnp.where(key_mark <= token, dot_t(query, keys) * SCALE, MASKED)
            maxima = jnp.maximum(jnp.max(scores, axis=1, keepdims=True), FLOOR)
            weights = jnp.exp(scores - maxima)
            totals = jnp.sum(weights, axis=1, keepdims=True)
            summed = dot(weights.astype(BF16), values)
            seen = totals > 0.0
            safe = jnp.where(seen, totals, 1.0)
            normed = (summed / safe).astype(BF16)
            logs = jnp.where(seen, maxima + jnp.log(safe), MASKED)
            for h in range(GROUP):
                part = slice(h * tokens, (h + 1) * tokens)
                outs[k][pl.ds(0, tokens), pl.ds((g * GROUP + h) * HEAD_SIZE, HEAD_SIZE)] = normed[part]
                for term, value in enumerate(split3(logs[part])):
                    stats[k] = jnp.where(lane == term * QUERY_HEADS + g * GROUP + h, value, stats[k])
    decodes = [
        jnp.concatenate(
            [t[pl.ds(span + g * slots, slots), :] for g in range(KEY_VALUE_HEADS)]
            + [t[pl.ds(span + KEY_VALUE_HEADS * slots, slots), pl.ds(0, STATS)]],
            axis=1,
        )
        for t in tables
    ]
    joined, logs = join(decodes)
    joined_stats = stats_block([logs[:, h * HEAD_SIZE : h * HEAD_SIZE + 1] for h in range(QUERY_HEADS)], slots)
    for k in range(query_count):
        outs[k][pl.ds(0, tokens), pl.ds(QW, STATS)] = stats[k].astype(BF16)
        outs[k][pl.ds(tokens, slots), pl.ds(0, QW)] = joined
        outs[k][pl.ds(tokens, slots), pl.ds(QW, STATS)] = joined_stats


def prefill_partials(offset, packs, tables, ctx, slots):
    tokens = packs[0].shape[0]
    pairs = len(packs) * tokens * KEY_SET * (ctx + tokens)
    return pl.pallas_call(
        functools.partial(prefill_kernel, len(packs), ctx, slots),
        in_specs=[SMEM] + [VMEM] * (len(packs) + len(tables)),
        out_specs=[VMEM] * len(packs),
        out_shape=[jax.ShapeDtypeStruct((tokens + slots, QW + STATS), BF16)] * len(packs),
        compiler_params=pltpu.CompilerParams(vmem_limit_bytes=32 << 20),
        cost_estimate=pl.CostEstimate(
            flops=4 * pairs * QW, bytes_accessed=4 << 20, transcendentals=pairs * QUERY_HEADS
        ),
        name="prefill_partials",
    )(offset, *packs, *tables)


def join_kernel(*refs):
    refs[-1][...] = join([ref[...] for ref in refs[:-1]])[0]


def join_parts(parts):
    return pl.pallas_call(
        join_kernel,
        in_specs=[VMEM] * len(parts),
        out_specs=VMEM,
        out_shape=jax.ShapeDtypeStruct((parts[0].shape[0], QW), BF16),
        compiler_params=pltpu.CompilerParams(vmem_limit_bytes=16 << 20),
        name="join_parts",
    )(*parts)


def update_kernel(off_ref, cache_hbm, *refs):
    tables, news, (out_ref, cache_ref, sem) = refs[:KEY_SET], refs[KEY_SET:-3], refs[-3:]
    load = pltpu.make_async_copy(cache_hbm.at[0], cache_ref, sem)
    load.start()
    ctx = cache_ref.shape[0]
    tokens = news[0].shape[0] // (KEY_SET // 2)
    me = lax.axis_index(BLK)
    rows = jnp.concatenate([t[pl.ds(ctx, tokens), :] for t in tables] + [n[...] for n in news], axis=0)
    count = rows.shape[0]
    index = lax.broadcasted_iota(jnp.int32, (1, count), 1)
    block = index // tokens
    inner = block % KEY_SET
    turned = inner % (KEY_SET // 2) * 2 + inner // (KEY_SET // 2)
    distance = jnp.where(block < KEY_SET, block, block // KEY_SET * KEY_SET + turned)
    token = (me ^ distance) * tokens + index % tokens
    wanted = me * ctx + lax.broadcasted_iota(jnp.int32, (ctx, 1), 0) - off_ref[0]
    picked = dot(jnp.where(wanted == token, 1.0, 0.0).astype(BF16), rows).astype(BF16)
    inside = jnp.broadcast_to((wanted >= 0) & (wanted < count), cache_ref.shape)
    load.wait()
    out_ref[0] = jnp.where(inside, picked, cache_ref[...])


def update_cache(offset, cache, tables, news):
    return pl.pallas_call(
        update_kernel,
        in_specs=[SMEM, HBM] + [VMEM] * (len(tables) + len(news)),
        out_specs=VMEM,
        out_shape=jax.ShapeDtypeStruct(cache.shape, BF16),
        scratch_shapes=[pltpu.VMEM(cache.shape[1:], BF16), pltpu.SemaphoreType.DMA],
        compiler_params=pltpu.CompilerParams(vmem_limit_bytes=16 << 20),
        name="update_cache",
    )(offset, pltpu.with_memory_space_constraint(cache, pltpu.HBM), *tables, *news)


def route_kernel(count, route_ref, *refs):
    held, (pre_ref, dec_ref) = refs[:-2], refs[-2:]
    if len(held) < count:
        held = [held[0].at[j] for j in range(count)]
    tokens, slots = pre_ref.shape[1], dec_ref.shape[0]
    prefill = jnp.zeros(pre_ref.shape[1:], F32)
    decode = jnp.zeros(dec_ref.shape, F32)
    for j in range(count):
        flag = route_ref[j, pl.ds(slots, 1), pl.ds(0, 1)]
        prefill += flag * held[j][pl.ds(0, tokens), :].astype(F32)
        chosen = route_ref[j, pl.ds(0, slots), pl.ds(0, slots)].astype(BF16)
        decode += dot(chosen, held[j][pl.ds(tokens, slots), :])
    pre_ref[0] = prefill.astype(BF16)
    dec_ref[...] = decode.astype(BF16)


def route_outputs(route, held, tokens, slots):
    return pl.pallas_call(
        functools.partial(route_kernel, route.shape[0]),
        in_specs=[VMEM] * (1 + len(held)),
        out_specs=[VMEM] * 2,
        out_shape=[
            jax.ShapeDtypeStruct((1, tokens, QW), BF16),
            jax.ShapeDtypeStruct((slots, QW), BF16),
        ],
        compiler_params=pltpu.CompilerParams(vmem_limit_bytes=16 << 20),
        name="route_outputs",
    )(route, *held)


def per_device(
    prefill_queries,
    decode_queries,
    new_prefill,
    new_decode,
    prefill_cache,
    decode_cache,
    prefill_offsets,
    decode_lengths,
    dealing,
):
    blk = lax.axis_size(BLK)
    req = lax.axis_size("req")
    ctx = prefill_cache.shape[1]
    tokens = prefill_queries.shape[1]
    slots = decode_cache.shape[0]

    def swap(array, distance):
        return lax.ppermute(array, BLK, [(i, i ^ distance) for i in range(blk)])

    others = range(KEY_SET, blk, KEY_SET)
    packs = [swap(prefill_queries[0], k) for k in others]
    decode_cache_out, table, queries, route = decode_partials(
        decode_lengths,
        dealing,
        decode_queries,
        new_decode,
        decode_cache,
        prefill_queries,
        new_prefill,
        prefill_cache,
        req,
    )
    lanes = [table] + [swap(table, k) for k in range(2, KEY_SET, 2)]
    lanes[1], *packs = lax.optimization_barrier((lanes[1], *packs))
    tables = [t for lane in lanes for t in (lane, swap(lane, 1))]

    news = jnp.concatenate([lane[ctx : ctx + tokens] for lane in lanes], axis=0)
    news = [swap(news, k) for k in others]

    parts = prefill_partials(prefill_offsets, [queries] + packs, tables, ctx, slots)
    attended = join_parts([parts[0]] + [swap(part, k * KEY_SET) for k, part in enumerate(parts) if k])

    news, _ = lax.optimization_barrier((news, parts[0]))
    news = [n for near in news for n in (near, swap(near, 1))]
    prefill_cache_out = update_cache(prefill_offsets, prefill_cache, tables, news)

    if req == 2:
        held = [attended, lax.ppermute(attended, "req", [(0, 1), (1, 0)])]
    else:
        held = [lax.all_gather(attended, "req", axis=0)]
    prefill_out, decode_out = route_outputs(route, held, tokens, slots)
    return (prefill_out, decode_out, prefill_cache_out, decode_cache_out)


def solution(mesh):
    blk, req = mesh.shape["blk"], mesh.shape["req"]
    mesh = jax.sharding.Mesh(mesh.devices.reshape(blk // QUAD, QUAD, req), ("hi", "quad", "req"))
    in_specs = (
        P("req", BLK, None),
        P("req", None),
        P("req", BLK, None),
        P("req", None),
        P("req", BLK, None),
        P("req", BLK, None),
        P("req"),
        P("req"),
        P(),
    )
    out_specs = (
        P("req", BLK, None),
        P("req", None),
        P("req", BLK, None),
        P("req", BLK, None),
    )
    return jax.shard_map(
        per_device, mesh=mesh, in_specs=in_specs, out_specs=out_specs, check_vma=False
    )
```

```python
import functools

import jax
import jax.numpy as jnp
from jax import lax
from jax.experimental import pallas as pl
from jax.experimental.pallas import tpu as pltpu
from jax.sharding import PartitionSpec as P

QUERY_HEADS = 8
KEY_VALUE_HEADS = 2
HEAD_SIZE = 128
GROUP = QUERY_HEADS // KEY_VALUE_HEADS
QW = QUERY_HEADS * HEAD_SIZE
KW = KEY_VALUE_HEADS * HEAD_SIZE
STATS = 128
QUAD = 4
KEY_SET = 8
SCALE = HEAD_SIZE**-0.5
MASKED = -1e30
FLOOR = -1e20
F32 = jnp.float32
BF16 = jnp.bfloat16

KVW = 2 * KW
BLK = ("hi", "quad")
CHUNKS = 4
TILE = 16

HBM = pl.BlockSpec(memory_space=pltpu.HBM)
VMEM = pl.BlockSpec(memory_space=pltpu.VMEM)


def dot_t(a, b):
    return lax.dot_general(a, b, (((1,), (1,)), ((), ())), preferred_element_type=F32)


def dot(a, b):
    return lax.dot_general(a, b, (((1,), (0,)), ((), ())), preferred_element_type=F32)


def split3(value):
    high = value.astype(BF16).astype(F32)
    rest = value - high
    middle = rest.astype(BF16).astype(F32)
    return high, middle, rest - middle


def stats_block(columns, rows):
    lane = lax.broadcasted_iota(jnp.int32, (rows, STATS), 1)
    count = len(columns)
    out = jnp.zeros((rows, STATS), F32)
    for head, column in enumerate(columns):
        for term, part in enumerate(split3(column)):
            out = jnp.where(lane == term * count + head, part, out)
    return out.astype(BF16)


def spread_matrix(heads):
    lane = lax.broadcasted_iota(jnp.int32, (STATS, heads * HEAD_SIZE), 0)
    head = lax.broadcasted_iota(jnp.int32, (STATS, heads * HEAD_SIZE), 1) // HEAD_SIZE
    hit = (lane == head) | (lane == head + heads) | (lane == head + 2 * heads)
    return jnp.where(hit, 1.0, 0.0).astype(BF16)


def join(parts):
    spread = spread_matrix(QUERY_HEADS)
    logs = [dot(part[:, QW:], spread) for part in parts]
    top = functools.reduce(jnp.maximum, logs)
    scales = [jnp.exp(log - top) for log in logs]
    total = functools.reduce(jnp.add, scales)
    summed = functools.reduce(
        jnp.add, [scale * part[:, :QW].astype(F32) for scale, part in zip(scales, parts)]
    )
    return (summed / total).astype(BF16), top + jnp.log(total)


def source_group(j):
    return lax.axis_index("req") ^ j if lax.axis_size("req") == 2 else j


def decode_kernel(
    len_hbm,
    deal_hbm,
    q_hbm,
    new_hbm,
    cache_hbm,
    pre_q_hbm,
    pre_new_hbm,
    pre_cache_hbm,
    out_hbm,
    shared_ref,
    pre_q_ref,
    route_ref,
    lens,
    deal,
    query_ref,
    new_ref,
    table,
    sems,
):
    slots, ctx, _ = table.shape
    rows = GROUP * slots
    chunk = slots // CHUNKS
    base = lax.axis_index(BLK) * ctx
    tokens = pre_new_hbm.shape[1]
    first = ctx + tokens
    small = [
        (len_hbm, lens),
        (deal_hbm, deal),
        (q_hbm, query_ref),
        (new_hbm, new_ref),
        (pre_q_hbm.at[0], pre_q_ref),
        (pre_cache_hbm.at[0], shared_ref.at[pl.ds(0, ctx), :]),
        (pre_new_hbm.at[0], shared_ref.at[pl.ds(ctx, tokens), :]),
    ]
    small = [pltpu.make_async_copy(a, b, sems.at[i]) for i, (a, b) in enumerate(small)]
    loads, stores = [], []
    for c in range(CHUNKS):
        part = pl.ds(c * chunk, chunk)
        loads.append(pltpu.make_async_copy(cache_hbm.at[part], table.at[part], sems.at[7 + c]))
        stores.append(pltpu.make_async_copy(table.at[part], out_hbm.at[part], sems.at[7 + CHUNKS + c]))
    for copy in small + loads:
        copy.start()
    for copy in small:
        copy.wait()
    group = lax.axis_index("req")
    req = route_ref.shape[0]
    out_row = lax.broadcasted_iota(jnp.int32, (slots, HEAD_SIZE), 0)
    out_lane = lax.broadcasted_iota(jnp.int32, (slots, HEAD_SIZE), 1)
    for j in range(req):
        source = source_group(j)
        chosen = jnp.zeros((slots, HEAD_SIZE), F32)
        for s in range(slots):
            place = deal[req + source * slots + s] - group * slots
            chosen = jnp.where((out_lane == s) & (out_row == place), 1.0, chosen)
        route_ref[j, pl.ds(0, slots), :] = chosen
        mine = (deal[source] == group).astype(F32)
        route_ref[j, pl.ds(slots, 8), :] = jnp.full((8, HEAD_SIZE), mine, F32)
    row_slot = lax.broadcasted_iota(jnp.int32, (rows, ctx), 0) % slots
    column = lax.broadcasted_iota(jnp.int32, (rows, ctx), 1)
    in_tile = lax.broadcasted_iota(jnp.int32, (TILE, KVW), 0)
    limit = jnp.full((rows, ctx), -1, jnp.int32)
    queries = [
        jnp.concatenate(
            [query_ref[:, pl.ds((g * GROUP + h) * HEAD_SIZE, HEAD_SIZE)] for h in range(GROUP)], axis=0
        )
        for g in range(KEY_VALUE_HEADS)
    ]
    scores = [jnp.zeros((rows, ctx), F32) for _ in range(KEY_VALUE_HEADS)]
    for c in range(CHUNKS):
        loads[c].wait()
        for s in range(c * chunk, (c + 1) * chunk):
            relative = lens[s] - base
            limit = jnp.where(row_slot == s, relative, limit)

            @pl.when((relative >= 0) & (relative < ctx))
            def _():
                start = pl.multiple_of(relative // TILE * TILE, TILE)
                tile = table[s, pl.ds(start, TILE), :]
                table[s, pl.ds(start, TILE), :] = jnp.where(
                    in_tile == relative - start, new_ref[s : s + 1, :], tile
                )

        stores[c].start()
        for g in range(KEY_VALUE_HEADS):
            key = table[pl.ds(c * chunk, chunk), :, pl.ds(g * HEAD_SIZE, HEAD_SIZE)]
            wide = dot_t(queries[g], key.reshape(chunk * ctx, HEAD_SIZE))
            for s in range(chunk):
                part = wide[:, s * ctx : (s + 1) * ctx]
                scores[g] = jnp.where(row_slot == c * chunk + s, part, scores[g])
    visible = column <= limit
    columns = []
    for g in range(KEY_VALUE_HEADS):
        masked = jnp.where(visible, scores[g] * SCALE, MASKED)
        maxima = jnp.maximum(jnp.max(masked, axis=1, keepdims=True), FLOOR)
        weights = jnp.exp(masked - maxima)
        totals = jnp.sum(weights, axis=1, keepdims=True)
        summed = jnp.zeros((rows, HEAD_SIZE), F32)
        for c in range(CHUNKS):
            value = table[pl.ds(c * chunk, chunk), :, pl.ds(KW + g * HEAD_SIZE, HEAD_SIZE)]
            picked = [jnp.where(row_slot == c * chunk + s, weights, 0.0) for s in range(chunk)]
            picked = jnp.concatenate(picked, axis=1).astype(BF16)
            summed += dot(picked, value.reshape(chunk * ctx, HEAD_SIZE))
        seen = totals > 0.0
        safe = jnp.where(seen, totals, 1.0)
        normed = (summed / safe).astype(BF16)
        logs = jnp.where(seen, maxima + jnp.log(safe), MASKED)
        for h in range(GROUP):
            part = slice(h * slots, (h + 1) * slots)
            shared_ref[pl.ds(first + g * slots, slots), pl.ds(h * HEAD_SIZE, HEAD_SIZE)] = normed[part]
            columns.append(logs[part])
    last = pl.ds(first + KEY_VALUE_HEADS * slots, slots)
    shared_ref[last, pl.ds(0, STATS)] = stats_block(columns, slots)
    shared_ref[last, pl.ds(STATS, KVW - STATS)] = jnp.zeros((slots, KVW - STATS), BF16)
    for copy in stores:
        copy.wait()


def decode_partials(lengths, dealing, queries, new_rows, cache, pre_queries, pre_new, pre_cache, req, extra):
    slots, ctx, width = cache.shape
    rows = ctx + pre_new.shape[1] + (KEY_VALUE_HEADS + 1) * slots + extra
    inputs = (lengths, dealing, queries, new_rows, cache, pre_queries, pre_new, pre_cache)
    return pl.pallas_call(
        decode_kernel,
        in_specs=[HBM] * len(inputs),
        out_specs=[HBM, VMEM, VMEM, VMEM],
        out_shape=[
            pltpu.HBM(cache.shape, BF16),
            pltpu.VMEM((rows, KVW), BF16),
            pltpu.VMEM(pre_queries.shape[1:], BF16),
            pltpu.VMEM((req, slots + 8, HEAD_SIZE), F32),
        ],
        scratch_shapes=[
            pltpu.SMEM(lengths.shape, jnp.int32),
            pltpu.SMEM(dealing.shape, jnp.int32),
            pltpu.VMEM(queries.shape, BF16),
            pltpu.VMEM(new_rows.shape, BF16),
            pltpu.VMEM(cache.shape, BF16),
            pltpu.SemaphoreType.DMA((7 + 2 * CHUNKS,)),
        ],
        compiler_params=pltpu.CompilerParams(vmem_limit_bytes=16 << 20),
        cost_estimate=pl.CostEstimate(
            flops=4 * slots * ctx * QW, bytes_accessed=2 * cache.size * 2, transcendentals=slots * ctx * 8
        ),
        name="decode_partials",
    )(*[pltpu.with_memory_space_constraint(x, pltpu.HBM) for x in inputs])


def prefill_kernel(query_count, ctx, slots, off_ref, *refs):
    packs, tables, outs = refs[:query_count], refs[query_count:-query_count], refs[-query_count:]
    tokens = packs[0].shape[0]
    span = ctx + tokens
    me = lax.axis_index(BLK)
    offset = off_ref[:1, :1]
    pieces = []
    for k in range(KEY_SET):
        holder = me ^ k
        index = lax.broadcasted_iota(jnp.int32, (1, span), 1)
        old = jnp.where(holder * ctx + index < offset, -1, 1 << 30)
        pieces.append(jnp.where(index < ctx, old, holder * tokens + index - ctx))
    key_mark = jnp.concatenate(pieces, axis=1)
    in_block = lax.broadcasted_iota(jnp.int32, (GROUP * tokens, 1), 0) % tokens
    lane = lax.broadcasted_iota(jnp.int32, (tokens, STATS), 1)
    stats = [jnp.zeros((tokens, STATS), F32) for _ in range(query_count)]
    for g in range(KEY_VALUE_HEADS):
        keys = jnp.concatenate([t[pl.ds(0, span), pl.ds(g * HEAD_SIZE, HEAD_SIZE)] for t in tables], axis=0)
        values = jnp.concatenate([t[pl.ds(0, span), pl.ds(KW + g * HEAD_SIZE, HEAD_SIZE)] for t in tables], axis=0)
        for k in range(query_count):
            token = (me ^ (k * KEY_SET)) * tokens + in_block
            query = jnp.concatenate(
                [packs[k][:, pl.ds((g * GROUP + h) * HEAD_SIZE, HEAD_SIZE)] for h in range(GROUP)], axis=0
            )
            scores = jnp.where(key_mark <= token, dot_t(query, keys) * SCALE, MASKED)
            maxima = jnp.maximum(jnp.max(scores, axis=1, keepdims=True), FLOOR)
            weights = jnp.exp(scores - maxima)
            totals = jnp.sum(weights, axis=1, keepdims=True)
            summed = dot(weights.astype(BF16), values)
            seen = totals > 0.0
            safe = jnp.where(seen, totals, 1.0)
            normed = (summed / safe).astype(BF16)
            logs = jnp.where(seen, maxima + jnp.log(safe), MASKED)
            for h in range(GROUP):
                part = slice(h * tokens, (h + 1) * tokens)
                outs[k][pl.ds(0, tokens), pl.ds((g * GROUP + h) * HEAD_SIZE, HEAD_SIZE)] = normed[part]
                for term, value in enumerate(split3(logs[part])):
                    stats[k] = jnp.where(lane == term * QUERY_HEADS + g * GROUP + h, value, stats[k])
    decodes = [
        jnp.concatenate(
            [t[pl.ds(span + g * slots, slots), :] for g in range(KEY_VALUE_HEADS)]
            + [t[pl.ds(span + KEY_VALUE_HEADS * slots, slots), pl.ds(0, STATS)]],
            axis=1,
        )
        for t in tables
    ]
    joined, logs = join(decodes)
    joined_stats = stats_block([logs[:, h * HEAD_SIZE : h * HEAD_SIZE + 1] for h in range(QUERY_HEADS)], slots)
    for k in range(query_count):
        outs[k][pl.ds(0, tokens), pl.ds(QW, STATS)] = stats[k].astype(BF16)
        outs[k][pl.ds(tokens, slots), pl.ds(0, QW)] = joined
        outs[k][pl.ds(tokens, slots), pl.ds(QW, STATS)] = joined_stats


def prefill_partials(offset, packs, tables, ctx, slots):
    tokens = packs[0].shape[0]
    pairs = len(packs) * tokens * KEY_SET * (ctx + tokens)
    return pl.pallas_call(
        functools.partial(prefill_kernel, len(packs), ctx, slots),
        in_specs=[VMEM] * (1 + len(packs) + len(tables)),
        out_specs=[VMEM] * len(packs),
        out_shape=[jax.ShapeDtypeStruct((tokens + slots, QW + STATS), BF16)] * len(packs),
        compiler_params=pltpu.CompilerParams(vmem_limit_bytes=32 << 20),
        cost_estimate=pl.CostEstimate(
            flops=4 * pairs * QW, bytes_accessed=4 << 20, transcendentals=pairs * QUERY_HEADS
        ),
        name="prefill_partials",
    )(offset, *packs, *tables)


def join_kernel(*refs):
    refs[-1][...] = join([ref[...] for ref in refs[:-1]])[0]


def join_parts(parts):
    return pl.pallas_call(
        join_kernel,
        in_specs=[VMEM] * len(parts),
        out_specs=VMEM,
        out_shape=jax.ShapeDtypeStruct((parts[0].shape[0], QW), BF16),
        compiler_params=pltpu.CompilerParams(vmem_limit_bytes=16 << 20),
        name="join_parts",
    )(*parts)


def update_kernel(tokens, extra, off_ref, cache_hbm, *refs):
    tables, (out_ref, cache_ref, sem) = refs[:KEY_SET], refs[-3:]
    load = pltpu.make_async_copy(cache_hbm.at[0], cache_ref, sem)
    load.start()
    ctx, total = cache_ref.shape[0], tables[0].shape[0]
    me = lax.axis_index(BLK)
    starts = [ctx] + list(range(total - extra, total, tokens))
    rows = jnp.concatenate([t[pl.ds(start, tokens), :] for start in starts for t in tables], axis=0)
    count = rows.shape[0]
    index = lax.broadcasted_iota(jnp.int32, (1, count), 1)
    token = (me ^ (index // tokens)) * tokens + index % tokens
    wanted = me * ctx + lax.broadcasted_iota(jnp.int32, (ctx, 1), 0) - off_ref[:1, :1]
    picked = dot(jnp.where(wanted == token, 1.0, 0.0).astype(BF16), rows).astype(BF16)
    inside = jnp.broadcast_to((wanted >= 0) & (wanted < count), cache_ref.shape)
    load.wait()
    out_ref[0] = jnp.where(inside, picked, cache_ref[...])


def update_cache(offset, cache, tables, tokens, extra):
    return pl.pallas_call(
        functools.partial(update_kernel, tokens, extra),
        in_specs=[VMEM, HBM] + [VMEM] * len(tables),
        out_specs=VMEM,
        out_shape=jax.ShapeDtypeStruct(cache.shape, BF16),
        scratch_shapes=[pltpu.VMEM(cache.shape[1:], BF16), pltpu.SemaphoreType.DMA],
        compiler_params=pltpu.CompilerParams(vmem_limit_bytes=16 << 20),
        name="update_cache",
    )(offset, pltpu.with_memory_space_constraint(cache, pltpu.HBM), *tables)


def route_kernel(count, route_ref, *refs):
    held, (pre_ref, dec_ref) = refs[:-2], refs[-2:]
    if len(held) < count:
        held = [held[0].at[j] for j in range(count)]
    tokens, slots = pre_ref.shape[1], dec_ref.shape[0]
    prefill = jnp.zeros(pre_ref.shape[1:], F32)
    decode = jnp.zeros(dec_ref.shape, F32)
    for j in range(count):
        flag = route_ref[j, pl.ds(slots, 1), pl.ds(0, 1)]
        prefill += flag * held[j][pl.ds(0, tokens), :].astype(F32)
        chosen = route_ref[j, pl.ds(0, slots), pl.ds(0, slots)].astype(BF16)
        decode += dot(chosen, held[j][pl.ds(tokens, slots), :])
    pre_ref[0] = prefill.astype(BF16)
    dec_ref[...] = decode.astype(BF16)


def route_outputs(route, held, tokens, slots):
    return pl.pallas_call(
        functools.partial(route_kernel, route.shape[0]),
        in_specs=[VMEM] * (1 + len(held)),
        out_specs=[VMEM] * 2,
        out_shape=[
            jax.ShapeDtypeStruct((1, tokens, QW), BF16),
            jax.ShapeDtypeStruct((slots, QW), BF16),
        ],
        compiler_params=pltpu.CompilerParams(vmem_limit_bytes=16 << 20),
        name="route_outputs",
    )(route, *held)


def per_device(
    prefill_queries,
    decode_queries,
    new_prefill,
    new_decode,
    prefill_cache,
    decode_cache,
    prefill_offsets,
    decode_lengths,
    dealing,
):
    blk = lax.axis_size(BLK)
    req = lax.axis_size("req")
    ctx = prefill_cache.shape[1]
    tokens = prefill_queries.shape[1]
    slots = decode_cache.shape[0]

    def swap(array, distance):
        return lax.ppermute(array, BLK, [(i, i ^ distance) for i in range(blk)])

    others = range(KEY_SET, blk, KEY_SET)
    extra = len(others) * tokens
    far_rows = [swap(new_prefill[0], k) for k in others]
    packs = [swap(prefill_queries[0], k) for k in others]
    decode_cache_out, table, queries, route = decode_partials(
        decode_lengths,
        dealing,
        decode_queries,
        new_decode,
        decode_cache,
        prefill_queries,
        new_prefill,
        prefill_cache,
        req,
        extra,
    )
    far_rows, packs, table = lax.optimization_barrier((far_rows, packs, table))
    for i, rows in enumerate(far_rows):
        table = lax.dynamic_update_slice(table, rows, (table.shape[0] - extra + i * tokens, 0))
    lanes = [table] + [swap(table, k) for k in range(2, KEY_SET, 2)]
    offset = jnp.full((8, HEAD_SIZE), prefill_offsets[0], jnp.int32)
    lanes[1], offset = lax.optimization_barrier((lanes[1], offset))
    for i in range(2, len(lanes)):
        lanes[i], _ = lax.optimization_barrier((lanes[i], lanes[i - 1]))
    tables = [t for lane in lanes for t in (lane, swap(lane, 1))]

    parts = prefill_partials(offset, [queries] + packs, tables, ctx, slots)
    attended = join_parts([parts[0]] + [swap(part, k * KEY_SET) for k, part in enumerate(parts) if k])

    prefill_cache_out = update_cache(offset, prefill_cache, tables, tokens, extra)

    if req == 2:
        held = [attended, lax.ppermute(attended, "req", [(0, 1), (1, 0)])]
    else:
        held = [lax.all_gather(attended, "req", axis=0)]
    prefill_out, decode_out = route_outputs(route, held, tokens, slots)
    return (prefill_out, decode_out, prefill_cache_out, decode_cache_out)


def solution(mesh):
    blk, req = mesh.shape["blk"], mesh.shape["req"]
    mesh = jax.sharding.Mesh(mesh.devices.reshape(blk // QUAD, QUAD, req), ("hi", "quad", "req"))
    in_specs = (
        P("req", BLK, None),
        P("req", None),
        P("req", BLK, None),
        P("req", None),
        P("req", BLK, None),
        P("req", BLK, None),
        P("req"),
        P("req"),
        P(),
    )
    out_specs = (
        P("req", BLK, None),
        P("req", None),
        P("req", BLK, None),
        P("req", BLK, None),
    )
    return jax.shard_map(
        per_device, mesh=mesh, in_specs=in_specs, out_specs=out_specs, check_vma=False
    )
```

```python
import functools

import jax
import jax.numpy as jnp
from jax import lax
from jax.experimental import pallas as pl
from jax.experimental.pallas import tpu as pltpu
from jax.sharding import PartitionSpec as P

QUERY_HEADS = 8
KEY_VALUE_HEADS = 2
HEAD_SIZE = 128
GROUP = QUERY_HEADS // KEY_VALUE_HEADS
QW = QUERY_HEADS * HEAD_SIZE
KW = KEY_VALUE_HEADS * HEAD_SIZE
STATS = 128
QUAD = 4
KEY_SET = 8
SCALE = HEAD_SIZE**-0.5
MASKED = -1e30
FLOOR = -1e20
F32 = jnp.float32
BF16 = jnp.bfloat16

KVW = 2 * KW
BLK = ("hi", "quad")
CHUNKS = 4
TILE = 16

HBM = pl.BlockSpec(memory_space=pltpu.HBM)
VMEM = pl.BlockSpec(memory_space=pltpu.VMEM)


def dot_t(a, b):
    return lax.dot_general(a, b, (((1,), (1,)), ((), ())), preferred_element_type=F32)


def dot(a, b):
    return lax.dot_general(a, b, (((1,), (0,)), ((), ())), preferred_element_type=F32)


def split3(value):
    high = value.astype(BF16).astype(F32)
    rest = value - high
    middle = rest.astype(BF16).astype(F32)
    return high, middle, rest - middle


def stats_block(columns, rows):
    lane = lax.broadcasted_iota(jnp.int32, (rows, STATS), 1)
    count = len(columns)
    out = jnp.zeros((rows, STATS), F32)
    for head, column in enumerate(columns):
        for term, part in enumerate(split3(column)):
            out = jnp.where(lane == term * count + head, part, out)
    return out.astype(BF16)


def spread_matrix(heads):
    lane = lax.broadcasted_iota(jnp.int32, (STATS, heads * HEAD_SIZE), 0)
    head = lax.broadcasted_iota(jnp.int32, (STATS, heads * HEAD_SIZE), 1) // HEAD_SIZE
    hit = (lane == head) | (lane == head + heads) | (lane == head + 2 * heads)
    return jnp.where(hit, 1.0, 0.0).astype(BF16)


def join(parts):
    spread = spread_matrix(QUERY_HEADS)
    logs = [dot(part[:, QW:], spread) for part in parts]
    top = functools.reduce(jnp.maximum, logs)
    scales = [jnp.exp(log - top) for log in logs]
    total = functools.reduce(jnp.add, scales)
    summed = functools.reduce(
        jnp.add, [scale * part[:, :QW].astype(F32) for scale, part in zip(scales, parts)]
    )
    return (summed / total).astype(BF16), top + jnp.log(total)


def source_group(j):
    return lax.axis_index("req") ^ j if lax.axis_size("req") == 2 else j


def decode_kernel(
    len_hbm,
    deal_hbm,
    q_hbm,
    new_hbm,
    cache_hbm,
    pre_q_hbm,
    pre_new_hbm,
    pre_cache_hbm,
    out_hbm,
    shared_ref,
    pre_q_ref,
    route_ref,
    lens,
    deal,
    query_ref,
    new_ref,
    table,
    sems,
):
    slots, ctx, _ = table.shape
    rows = GROUP * slots
    chunk = slots // CHUNKS
    base = lax.axis_index(BLK) * ctx
    tokens = pre_new_hbm.shape[1]
    first = ctx + tokens
    small = [
        (len_hbm, lens),
        (deal_hbm, deal),
        (q_hbm, query_ref),
        (new_hbm, new_ref),
        (pre_q_hbm.at[0], pre_q_ref),
        (pre_cache_hbm.at[0], shared_ref.at[pl.ds(0, ctx), :]),
        (pre_new_hbm.at[0], shared_ref.at[pl.ds(ctx, tokens), :]),
    ]
    small = [pltpu.make_async_copy(a, b, sems.at[i]) for i, (a, b) in enumerate(small)]
    loads, stores = [], []
    for c in range(CHUNKS):
        part = pl.ds(c * chunk, chunk)
        loads.append(pltpu.make_async_copy(cache_hbm.at[part], table.at[part], sems.at[7 + c]))
        stores.append(pltpu.make_async_copy(table.at[part], out_hbm.at[part], sems.at[7 + CHUNKS + c]))
    for copy in small + loads:
        copy.start()
    for copy in small:
        copy.wait()
    group = lax.axis_index("req")
    req = route_ref.shape[0]
    out_row = lax.broadcasted_iota(jnp.int32, (slots, HEAD_SIZE), 0)
    out_lane = lax.broadcasted_iota(jnp.int32, (slots, HEAD_SIZE), 1)
    for j in range(req):
        source = source_group(j)
        chosen = jnp.zeros((slots, HEAD_SIZE), F32)
        for s in range(slots):
            place = deal[req + source * slots + s] - group * slots
            chosen = jnp.where((out_lane == s) & (out_row == place), 1.0, chosen)
        route_ref[j, pl.ds(0, slots), :] = chosen
        mine = (deal[source] == group).astype(F32)
        route_ref[j, pl.ds(slots, 8), :] = jnp.full((8, HEAD_SIZE), mine, F32)
    row_slot = lax.broadcasted_iota(jnp.int32, (rows, ctx), 0) % slots
    column = lax.broadcasted_iota(jnp.int32, (rows, ctx), 1)
    in_tile = lax.broadcasted_iota(jnp.int32, (TILE, KVW), 0)
    limit = jnp.full((rows, ctx), -1, jnp.int32)
    queries = [
        jnp.concatenate(
            [query_ref[:, pl.ds((g * GROUP + h) * HEAD_SIZE, HEAD_SIZE)] for h in range(GROUP)], axis=0
        )
        for g in range(KEY_VALUE_HEADS)
    ]
    scores = [jnp.zeros((rows, ctx), F32) for _ in range(KEY_VALUE_HEADS)]
    for c in range(CHUNKS):
        loads[c].wait()
        for s in range(c * chunk, (c + 1) * chunk):
            relative = lens[s] - base
            limit = jnp.where(row_slot == s, relative, limit)

            @pl.when((relative >= 0) & (relative < ctx))
            def _():
                start = pl.multiple_of(relative // TILE * TILE, TILE)
                tile = table[s, pl.ds(start, TILE), :]
                table[s, pl.ds(start, TILE), :] = jnp.where(
                    in_tile == relative - start, new_ref[s : s + 1, :], tile
                )

        stores[c].start()
        for g in range(KEY_VALUE_HEADS):
            key = table[pl.ds(c * chunk, chunk), :, pl.ds(g * HEAD_SIZE, HEAD_SIZE)]
            wide = dot_t(queries[g], key.reshape(chunk * ctx, HEAD_SIZE))
            for s in range(chunk):
                part = wide[:, s * ctx : (s + 1) * ctx]
                scores[g] = jnp.where(row_slot == c * chunk + s, part, scores[g])
    visible = column <= limit
    columns = []
    for g in range(KEY_VALUE_HEADS):
        masked = jnp.where(visible, scores[g] * SCALE, MASKED)
        maxima = jnp.maximum(jnp.max(masked, axis=1, keepdims=True), FLOOR)
        weights = jnp.exp(masked - maxima)
        totals = jnp.sum(weights, axis=1, keepdims=True)
        summed = jnp.zeros((rows, HEAD_SIZE), F32)
        for c in range(CHUNKS):
            value = table[pl.ds(c * chunk, chunk), :, pl.ds(KW + g * HEAD_SIZE, HEAD_SIZE)]
            picked = [jnp.where(row_slot == c * chunk + s, weights, 0.0) for s in range(chunk)]
            picked = jnp.concatenate(picked, axis=1).astype(BF16)
            summed += dot(picked, value.reshape(chunk * ctx, HEAD_SIZE))
        seen = totals > 0.0
        safe = jnp.where(seen, totals, 1.0)
        normed = (summed / safe).astype(BF16)
        logs = jnp.where(seen, maxima + jnp.log(safe), MASKED)
        for h in range(GROUP):
            part = slice(h * slots, (h + 1) * slots)
            shared_ref[pl.ds(first + g * slots, slots), pl.ds(h * HEAD_SIZE, HEAD_SIZE)] = normed[part]
            columns.append(logs[part])
    last = pl.ds(first + KEY_VALUE_HEADS * slots, slots)
    shared_ref[last, pl.ds(0, STATS)] = stats_block(columns, slots)
    shared_ref[last, pl.ds(STATS, KVW - STATS)] = jnp.zeros((slots, KVW - STATS), BF16)
    for copy in stores:
        copy.wait()


def decode_partials(lengths, dealing, queries, new_rows, cache, pre_queries, pre_new, pre_cache, req):
    slots, ctx, width = cache.shape
    rows = ctx + pre_new.shape[1] + (KEY_VALUE_HEADS + 1) * slots
    inputs = (lengths, dealing, queries, new_rows, cache, pre_queries, pre_new, pre_cache)
    return pl.pallas_call(
        decode_kernel,
        in_specs=[HBM] * len(inputs),
        out_specs=[HBM, VMEM, VMEM, VMEM],
        out_shape=[
            pltpu.HBM(cache.shape, BF16),
            pltpu.VMEM((rows, KVW), BF16),
            pltpu.VMEM(pre_queries.shape[1:], BF16),
            pltpu.VMEM((req, slots + 8, HEAD_SIZE), F32),
        ],
        scratch_shapes=[
            pltpu.SMEM(lengths.shape, jnp.int32),
            pltpu.SMEM(dealing.shape, jnp.int32),
            pltpu.VMEM(queries.shape, BF16),
            pltpu.VMEM(new_rows.shape, BF16),
            pltpu.VMEM(cache.shape, BF16),
            pltpu.SemaphoreType.DMA((7 + 2 * CHUNKS,)),
        ],
        compiler_params=pltpu.CompilerParams(vmem_limit_bytes=16 << 20),
        cost_estimate=pl.CostEstimate(
            flops=4 * slots * ctx * QW, bytes_accessed=2 * cache.size * 2, transcendentals=slots * ctx * 8
        ),
        name="decode_partials",
    )(*[pltpu.with_memory_space_constraint(x, pltpu.HBM) for x in inputs])


def prefill_kernel(query_count, ctx, slots, off_ref, *refs):
    packs, tables, outs = refs[:query_count], refs[query_count:-query_count], refs[-query_count:]
    tokens = packs[0].shape[0]
    span = ctx + tokens
    me = lax.axis_index(BLK)
    offset = off_ref[:1, :1]
    pieces = []
    for k in range(KEY_SET):
        holder = me ^ k
        index = lax.broadcasted_iota(jnp.int32, (1, span), 1)
        old = jnp.where(holder * ctx + index < offset, -1, 1 << 30)
        pieces.append(jnp.where(index < ctx, old, holder * tokens + index - ctx))
    key_mark = jnp.concatenate(pieces, axis=1)
    in_block = lax.broadcasted_iota(jnp.int32, (GROUP * tokens, 1), 0) % tokens
    lane = lax.broadcasted_iota(jnp.int32, (tokens, STATS), 1)
    stats = [jnp.zeros((tokens, STATS), F32) for _ in range(query_count)]
    for g in range(KEY_VALUE_HEADS):
        keys = jnp.concatenate([t[pl.ds(0, span), pl.ds(g * HEAD_SIZE, HEAD_SIZE)] for t in tables], axis=0)
        values = jnp.concatenate([t[pl.ds(0, span), pl.ds(KW + g * HEAD_SIZE, HEAD_SIZE)] for t in tables], axis=0)
        for k in range(query_count):
            token = (me ^ (k * KEY_SET)) * tokens + in_block
            query = jnp.concatenate(
                [packs[k][:, pl.ds((g * GROUP + h) * HEAD_SIZE, HEAD_SIZE)] for h in range(GROUP)], axis=0
            )
            scores = jnp.where(key_mark <= token, dot_t(query, keys) * SCALE, MASKED)
            maxima = jnp.maximum(jnp.max(scores, axis=1, keepdims=True), FLOOR)
            weights = jnp.exp(scores - maxima)
            totals = jnp.sum(weights, axis=1, keepdims=True)
            summed = dot(weights.astype(BF16), values)
            seen = totals > 0.0
            safe = jnp.where(seen, totals, 1.0)
            normed = (summed / safe).astype(BF16)
            logs = jnp.where(seen, maxima + jnp.log(safe), MASKED)
            for h in range(GROUP):
                part = slice(h * tokens, (h + 1) * tokens)
                outs[k][pl.ds(0, tokens), pl.ds((g * GROUP + h) * HEAD_SIZE, HEAD_SIZE)] = normed[part]
                for term, value in enumerate(split3(logs[part])):
                    stats[k] = jnp.where(lane == term * QUERY_HEADS + g * GROUP + h, value, stats[k])
    decodes = [
        jnp.concatenate(
            [t[pl.ds(span + g * slots, slots), :] for g in range(KEY_VALUE_HEADS)]
            + [t[pl.ds(span + KEY_VALUE_HEADS * slots, slots), pl.ds(0, STATS)]],
            axis=1,
        )
        for t in tables
    ]
    joined, logs = join(decodes)
    joined_stats = stats_block([logs[:, h * HEAD_SIZE : h * HEAD_SIZE + 1] for h in range(QUERY_HEADS)], slots)
    for k in range(query_count):
        outs[k][pl.ds(0, tokens), pl.ds(QW, STATS)] = stats[k].astype(BF16)
        outs[k][pl.ds(tokens, slots), pl.ds(0, QW)] = joined
        outs[k][pl.ds(tokens, slots), pl.ds(QW, STATS)] = joined_stats


def prefill_partials(offset, packs, tables, ctx, slots):
    tokens = packs[0].shape[0]
    pairs = len(packs) * tokens * KEY_SET * (ctx + tokens)
    return pl.pallas_call(
        functools.partial(prefill_kernel, len(packs), ctx, slots),
        in_specs=[VMEM] * (1 + len(packs) + len(tables)),
        out_specs=[VMEM] * len(packs),
        out_shape=[jax.ShapeDtypeStruct((tokens + slots, QW + STATS), BF16)] * len(packs),
        compiler_params=pltpu.CompilerParams(vmem_limit_bytes=32 << 20),
        cost_estimate=pl.CostEstimate(
            flops=4 * pairs * QW, bytes_accessed=4 << 20, transcendentals=pairs * QUERY_HEADS
        ),
        name="prefill_partials",
    )(offset, *packs, *tables)


def join_kernel(*refs):
    refs[-1][...] = join([ref[...] for ref in refs[:-1]])[0]


def join_parts(parts):
    return pl.pallas_call(
        join_kernel,
        in_specs=[VMEM] * len(parts),
        out_specs=VMEM,
        out_shape=jax.ShapeDtypeStruct((parts[0].shape[0], QW), BF16),
        compiler_params=pltpu.CompilerParams(vmem_limit_bytes=16 << 20),
        name="join_parts",
    )(*parts)


def update_kernel(tokens, sets, off_ref, cache_hbm, near_ref, beside_ref, *refs):
    tables, (out_ref, cache_ref, sem) = refs[:KEY_SET], refs[-3:]
    load = pltpu.make_async_copy(cache_hbm.at[0], cache_ref, sem)
    load.start()
    ctx = cache_ref.shape[0]
    me = lax.axis_index(BLK)
    rows = [t[pl.ds(ctx, tokens), :] for t in tables]
    rows = jnp.concatenate(rows + [near_ref[...], beside_ref[...]], axis=0)
    count = rows.shape[0]
    index = lax.broadcasted_iota(jnp.int32, (1, count), 1)
    block = index // tokens
    half = sets * KEY_SET // 2
    far = block - KEY_SET
    inner = far % half
    distance = KEY_SET * (1 + inner % sets) + 2 * (inner // sets) + far // half
    token = (me ^ jnp.where(block < KEY_SET, block, distance)) * tokens + index % tokens
    wanted = me * ctx + lax.broadcasted_iota(jnp.int32, (ctx, 1), 0) - off_ref[:1, :1]
    picked = dot(jnp.where(wanted == token, 1.0, 0.0).astype(BF16), rows).astype(BF16)
    inside = jnp.broadcast_to((wanted >= 0) & (wanted < count), cache_ref.shape)
    load.wait()
    out_ref[0] = jnp.where(inside, picked, cache_ref[...])


def update_cache(offset, cache, near, beside, tables, tokens, sets):
    return pl.pallas_call(
        functools.partial(update_kernel, tokens, sets),
        in_specs=[VMEM, HBM] + [VMEM] * (2 + len(tables)),
        out_specs=VMEM,
        out_shape=jax.ShapeDtypeStruct(cache.shape, BF16),
        scratch_shapes=[pltpu.VMEM(cache.shape[1:], BF16), pltpu.SemaphoreType.DMA],
        compiler_params=pltpu.CompilerParams(vmem_limit_bytes=16 << 20),
        name="update_cache",
    )(offset, pltpu.with_memory_space_constraint(cache, pltpu.HBM), near, beside, *tables)


def route_kernel(count, route_ref, *refs):
    held, (pre_ref, dec_ref) = refs[:-2], refs[-2:]
    if len(held) < count:
        held = [held[0].at[j] for j in range(count)]
    tokens, slots = pre_ref.shape[1], dec_ref.shape[0]
    prefill = jnp.zeros(pre_ref.shape[1:], F32)
    decode = jnp.zeros(dec_ref.shape, F32)
    for j in range(count):
        flag = route_ref[j, pl.ds(slots, 1), pl.ds(0, 1)]
        prefill += flag * held[j][pl.ds(0, tokens), :].astype(F32)
        chosen = route_ref[j, pl.ds(0, slots), pl.ds(0, slots)].astype(BF16)
        decode += dot(chosen, held[j][pl.ds(tokens, slots), :])
    pre_ref[0] = prefill.astype(BF16)
    dec_ref[...] = decode.astype(BF16)


def route_outputs(route, held, tokens, slots):
    return pl.pallas_call(
        functools.partial(route_kernel, route.shape[0]),
        in_specs=[VMEM] * (1 + len(held)),
        out_specs=[VMEM] * 2,
        out_shape=[
            jax.ShapeDtypeStruct((1, tokens, QW), BF16),
            jax.ShapeDtypeStruct((slots, QW), BF16),
        ],
        compiler_params=pltpu.CompilerParams(vmem_limit_bytes=16 << 20),
        name="route_outputs",
    )(route, *held)


def per_device(
    prefill_queries,
    decode_queries,
    new_prefill,
    new_decode,
    prefill_cache,
    decode_cache,
    prefill_offsets,
    decode_lengths,
    dealing,
):
    blk = lax.axis_size(BLK)
    req = lax.axis_size("req")
    ctx = prefill_cache.shape[1]
    tokens = prefill_queries.shape[1]
    slots = decode_cache.shape[0]

    def swap(array, distance):
        return lax.ppermute(array, BLK, [(i, i ^ distance) for i in range(blk)])

    def after(array, *marks):
        return lax.optimization_barrier((array, *marks))[0]

    others = range(KEY_SET, blk, KEY_SET)
    packs = [swap(prefill_queries[0], k) for k in others]
    decode_cache_out, table, queries, route = decode_partials(
        decode_lengths,
        dealing,
        decode_queries,
        new_decode,
        decode_cache,
        prefill_queries,
        new_prefill,
        prefill_cache,
        req,
    )
    lanes = [table] + [swap(table, k) for k in range(2, KEY_SET, 2)]
    offset = jnp.full((8, HEAD_SIZE), prefill_offsets[0], jnp.int32)
    lanes[1], offset, *packs = lax.optimization_barrier((lanes[1], offset, *packs))
    for i in range(2, len(lanes)):
        lanes[i] = after(lanes[i], lanes[i - 1])
    tables = [t for lane in lanes for t in (lane, swap(lane, 1))]

    parts = prefill_partials(offset, [queries] + packs, tables, ctx, slots)
    attended = join_parts([parts[0]] + [swap(part, k * KEY_SET) for k, part in enumerate(parts) if k])

    own_rows = after(new_prefill[0], lanes[-1])
    far = jnp.concatenate([swap(own_rows, k) for k in others], axis=0)
    far = after(far, parts[0])
    for k in range(2, KEY_SET, 2):
        if k & (k - 1) == 0:
            far = jnp.concatenate([far, swap(far, k)], axis=0)
    prefill_cache_out = update_cache(
        offset, prefill_cache, far, swap(far, 1), tables, tokens, len(others)
    )

    if req == 2:
        held = [attended, lax.ppermute(attended, "req", [(0, 1), (1, 0)])]
    else:
        held = [lax.all_gather(attended, "req", axis=0)]
    held[-1], prefill_cache_out = lax.optimization_barrier((held[-1], prefill_cache_out))
    prefill_out, decode_out = route_outputs(route, held, tokens, slots)
    return (prefill_out, decode_out, prefill_cache_out, decode_cache_out)


def solution(mesh):
    blk, req = mesh.shape["blk"], mesh.shape["req"]
    mesh = jax.sharding.Mesh(mesh.devices.reshape(blk // QUAD, QUAD, req), ("hi", "quad", "req"))
    in_specs = (
        P("req", BLK, None),
        P("req", None),
        P("req", BLK, None),
        P("req", None),
        P("req", BLK, None),
        P("req", BLK, None),
        P("req"),
        P("req"),
        P(),
    )
    out_specs = (
        P("req", BLK, None),
        P("req", None),
        P("req", BLK, None),
        P("req", BLK, None),
    )
    return jax.shard_map(
        per_device, mesh=mesh, in_specs=in_specs, out_specs=out_specs, check_vma=False
    )
```

```python
import functools

import jax
import jax.numpy as jnp
from jax import lax
from jax.experimental import pallas as pl
from jax.experimental.pallas import tpu as pltpu
from jax.sharding import PartitionSpec as P

QUERY_HEADS = 8
KEY_VALUE_HEADS = 2
HEAD_SIZE = 128
GROUP = QUERY_HEADS // KEY_VALUE_HEADS
QW = QUERY_HEADS * HEAD_SIZE
KW = KEY_VALUE_HEADS * HEAD_SIZE
STATS = 128
QUAD = 4
KEY_SET = 8
PART_ROWS = KEY_VALUE_HEADS + 1
SCALE = HEAD_SIZE**-0.5
MASKED = -1e30
FLOOR = -1e20
F32 = jnp.float32
BF16 = jnp.bfloat16

KVW = 2 * KW
BLK = ("hi", "quad")
CHUNKS = 4
TILE = 16

HBM = pl.BlockSpec(memory_space=pltpu.HBM)
VMEM = pl.BlockSpec(memory_space=pltpu.VMEM)


def dot_t(a, b):
    return lax.dot_general(a, b, (((1,), (1,)), ((), ())), preferred_element_type=F32)


def dot(a, b):
    return lax.dot_general(a, b, (((1,), (0,)), ((), ())), preferred_element_type=F32)


def split3(value):
    high = value.astype(BF16).astype(F32)
    rest = value - high
    middle = rest.astype(BF16).astype(F32)
    return high, middle, rest - middle


def stats_block(columns, rows):
    lane = lax.broadcasted_iota(jnp.int32, (rows, STATS), 1)
    count = len(columns)
    out = jnp.zeros((rows, STATS), F32)
    for head, column in enumerate(columns):
        for term, part in enumerate(split3(column)):
            out = jnp.where(lane == term * count + head, part, out)
    return out.astype(BF16)


def spread_matrix(heads):
    lane = lax.broadcasted_iota(jnp.int32, (STATS, heads * HEAD_SIZE), 0)
    head = lax.broadcasted_iota(jnp.int32, (STATS, heads * HEAD_SIZE), 1) // HEAD_SIZE
    hit = (lane == head) | (lane == head + heads) | (lane == head + 2 * heads)
    return jnp.where(hit, 1.0, 0.0).astype(BF16)


def join(parts):
    spread = spread_matrix(QUERY_HEADS)
    logs = [dot(part[:, QW:], spread) for part in parts]
    top = functools.reduce(jnp.maximum, logs)
    scales = [jnp.exp(log - top) for log in logs]
    total = functools.reduce(jnp.add, scales)
    summed = functools.reduce(
        jnp.add, [scale * part[:, :QW].astype(F32) for scale, part in zip(scales, parts)]
    )
    return (summed / total).astype(BF16), top + jnp.log(total)


def source_group(j):
    return lax.axis_index("req") ^ j if lax.axis_size("req") == 2 else j


def decode_kernel(
    len_hbm,
    deal_hbm,
    q_hbm,
    new_hbm,
    cache_hbm,
    pre_q_hbm,
    out_hbm,
    part_ref,
    pre_q_ref,
    route_ref,
    lens,
    deal,
    query_ref,
    new_ref,
    table,
    sems,
):
    slots, ctx, _ = table.shape
    rows = GROUP * slots
    chunk = slots // CHUNKS
    base = lax.axis_index(BLK) * ctx
    small = [
        (len_hbm, lens),
        (deal_hbm, deal),
        (q_hbm, query_ref),
        (new_hbm, new_ref),
        (pre_q_hbm.at[0], pre_q_ref),
    ]
    small = [pltpu.make_async_copy(a, b, sems.at[i]) for i, (a, b) in enumerate(small)]
    loads, stores = [], []
    for c in range(CHUNKS):
        part = pl.ds(c * chunk, chunk)
        loads.append(pltpu.make_async_copy(cache_hbm.at[part], table.at[part], sems.at[5 + c]))
        stores.append(pltpu.make_async_copy(table.at[part], out_hbm.at[part], sems.at[5 + CHUNKS + c]))
    for copy in small + loads:
        copy.start()
    for copy in small:
        copy.wait()
    group = lax.axis_index("req")
    req = route_ref.shape[0]
    out_row = lax.broadcasted_iota(jnp.int32, (slots, HEAD_SIZE), 0)
    out_lane = lax.broadcasted_iota(jnp.int32, (slots, HEAD_SIZE), 1)
    for j in range(req):
        source = source_group(j)
        chosen = jnp.zeros((slots, HEAD_SIZE), F32)
        for s in range(slots):
            place = deal[req + source * slots + s] - group * slots
            chosen = jnp.where((out_lane == s) & (out_row == place), 1.0, chosen)
        route_ref[j, pl.ds(0, slots), :] = chosen
        mine = (deal[source] == group).astype(F32)
        route_ref[j, pl.ds(slots, 8), :] = jnp.full((8, HEAD_SIZE), mine, F32)
    row_slot = lax.broadcasted_iota(jnp.int32, (rows, ctx), 0) % slots
    column = lax.broadcasted_iota(jnp.int32, (rows, ctx), 1)
    in_tile = lax.broadcasted_iota(jnp.int32, (TILE, KVW), 0)
    limit = jnp.full((rows, ctx), -1, jnp.int32)
    queries = [
        jnp.concatenate(
            [query_ref[:, pl.ds((g * GROUP + h) * HEAD_SIZE, HEAD_SIZE)] for h in range(GROUP)], axis=0
        )
        for g in range(KEY_VALUE_HEADS)
    ]
    scores = [jnp.zeros((rows, ctx), F32) for _ in range(KEY_VALUE_HEADS)]
    for c in range(CHUNKS):
        loads[c].wait()
        for s in range(c * chunk, (c + 1) * chunk):
            relative = lens[s] - base
            limit = jnp.where(row_slot == s, relative, limit)

            @pl.when((relative >= 0) & (relative < ctx))
            def _():
                start = pl.multiple_of(relative // TILE * TILE, TILE)
                tile = table[s, pl.ds(start, TILE), :]
                table[s, pl.ds(start, TILE), :] = jnp.where(
                    in_tile == relative - start, new_ref[s : s + 1, :], tile
                )

        stores[c].start()
        for g in range(KEY_VALUE_HEADS):
            key = table[pl.ds(c * chunk, chunk), :, pl.ds(g * HEAD_SIZE, HEAD_SIZE)]
            wide = dot_t(queries[g], key.reshape(chunk * ctx, HEAD_SIZE))
            for s in range(chunk):
                part = wide[:, s * ctx : (s + 1) * ctx]
                scores[g] = jnp.where(row_slot == c * chunk + s, part, scores[g])
    visible = column <= limit
    columns = []
    for g in range(KEY_VALUE_HEADS):
        masked = jnp.where(visible, scores[g] * SCALE, MASKED)
        maxima = jnp.maximum(jnp.max(masked, axis=1, keepdims=True), FLOOR)
        weights = jnp.exp(masked - maxima)
        totals = jnp.sum(weights, axis=1, keepdims=True)
        summed = jnp.zeros((rows, HEAD_SIZE), F32)
        for c in range(CHUNKS):
            value = table[pl.ds(c * chunk, chunk), :, pl.ds(KW + g * HEAD_SIZE, HEAD_SIZE)]
            picked = [jnp.where(row_slot == c * chunk + s, weights, 0.0) for s in range(chunk)]
            picked = jnp.concatenate(picked, axis=1).astype(BF16)
            summed += dot(picked, value.reshape(chunk * ctx, HEAD_SIZE))
        seen = totals > 0.0
        safe = jnp.where(seen, totals, 1.0)
        normed = (summed / safe).astype(BF16)
        logs = jnp.where(seen, maxima + jnp.log(safe), MASKED)
        for h in range(GROUP):
            part = slice(h * slots, (h + 1) * slots)
            part_ref[pl.ds(g * slots, slots), pl.ds(h * HEAD_SIZE, HEAD_SIZE)] = normed[part]
            columns.append(logs[part])
    put_stats(part_ref, columns, slots)
    for copy in stores:
        copy.wait()


def decode_partials(lengths, dealing, queries, new_rows, cache, pre_queries, req):
    slots, ctx, width = cache.shape
    inputs = (lengths, dealing, queries, new_rows, cache, pre_queries)
    return pl.pallas_call(
        decode_kernel,
        in_specs=[HBM] * len(inputs),
        out_specs=[HBM, VMEM, VMEM, VMEM],
        out_shape=[
            pltpu.HBM(cache.shape, BF16),
            pltpu.VMEM((PART_ROWS * slots, KVW), BF16),
            pltpu.VMEM(pre_queries.shape[1:], BF16),
            pltpu.VMEM((req, slots + 8, HEAD_SIZE), F32),
        ],
        scratch_shapes=[
            pltpu.SMEM(lengths.shape, jnp.int32),
            pltpu.SMEM(dealing.shape, jnp.int32),
            pltpu.VMEM(queries.shape, BF16),
            pltpu.VMEM(new_rows.shape, BF16),
            pltpu.VMEM(cache.shape, BF16),
            pltpu.SemaphoreType.DMA((5 + 2 * CHUNKS,)),
        ],
        compiler_params=pltpu.CompilerParams(vmem_limit_bytes=16 << 20),
        cost_estimate=pl.CostEstimate(
            flops=4 * slots * ctx * QW, bytes_accessed=2 * cache.size * 2, transcendentals=slots * ctx * 8
        ),
        name="decode_partials",
    )(*[pltpu.with_memory_space_constraint(x, pltpu.HBM) for x in inputs])


def put_stats(ref, columns, slots):
    last = pl.ds(KEY_VALUE_HEADS * slots, slots)
    ref[last, pl.ds(0, STATS)] = stats_block(columns, slots)
    ref[last, pl.ds(STATS, KVW - STATS)] = jnp.zeros((slots, KVW - STATS), BF16)


def decode_part(ref, slots):
    blocks = [ref[pl.ds(g * slots, slots), :] for g in range(KEY_VALUE_HEADS)]
    return jnp.concatenate(blocks + [ref[pl.ds(KEY_VALUE_HEADS * slots, slots), pl.ds(0, STATS)]], axis=1)


def step_kernel(slots, own_ref, other_ref, *refs):
    joined, logs = join([decode_part(own_ref, slots), decode_part(other_ref, slots)])
    head = PART_ROWS * slots
    rest = own_ref.shape[0] - head
    out_ref = refs[0] if rest else refs[-1]
    for g in range(KEY_VALUE_HEADS):
        out_ref[pl.ds(g * slots, slots), :] = joined[:, g * KVW : (g + 1) * KVW]
    put_stats(out_ref, [logs[:, h * HEAD_SIZE : h * HEAD_SIZE + 1] for h in range(QUERY_HEADS)], slots)
    if not rest:
        far_ref = refs[0]
        out_ref[pl.ds(head, far_ref.shape[0]), :] = far_ref[...]
        return
    news_ref, at = (out_ref, head) if len(refs) == 1 else (refs[1], 0)
    news_ref[pl.ds(at, rest), :] = own_ref[pl.ds(head, rest), :]
    news_ref[pl.ds(at + rest, rest), :] = other_ref[pl.ds(head, rest), :]


def join_step(own, other, slots, shapes, name, *extra):
    return pl.pallas_call(
        functools.partial(step_kernel, slots),
        in_specs=[VMEM] * (2 + len(extra)),
        out_specs=[VMEM] * len(shapes),
        out_shape=[pltpu.VMEM((rows, KVW), BF16) for rows in shapes],
        compiler_params=pltpu.CompilerParams(vmem_limit_bytes=16 << 20),
        name=name,
    )(own, other, *extra)


def prefill_kernel(sets, ctx, off_ref, *refs):
    query_count = len(sets)
    packs, tables, outs = refs[:query_count], refs[query_count:-query_count], refs[-query_count:]
    tokens = packs[0].shape[0]
    span = ctx + tokens
    me = lax.axis_index(BLK)
    offset = off_ref[:1, :1]
    pieces = []
    for k in range(KEY_SET):
        holder = me ^ k
        index = lax.broadcasted_iota(jnp.int32, (1, span), 1)
        old = jnp.where(holder * ctx + index < offset, -1, 1 << 30)
        pieces.append(jnp.where(index < ctx, old, holder * tokens + index - ctx))
    key_mark = jnp.concatenate(pieces, axis=1)
    in_block = lax.broadcasted_iota(jnp.int32, (GROUP * tokens, 1), 0) % tokens
    lane = lax.broadcasted_iota(jnp.int32, (tokens, STATS), 1)
    stats = [jnp.zeros((tokens, STATS), F32) for _ in range(query_count)]
    for g in range(KEY_VALUE_HEADS):
        keys = jnp.concatenate([t[:, pl.ds(g * HEAD_SIZE, HEAD_SIZE)] for t in tables], axis=0)
        values = jnp.concatenate([t[:, pl.ds(KW + g * HEAD_SIZE, HEAD_SIZE)] for t in tables], axis=0)
        for k in range(query_count):
            token = (me ^ (sets[k] * KEY_SET)) * tokens + in_block
            query = jnp.concatenate(
                [packs[k][:, pl.ds((g * GROUP + h) * HEAD_SIZE, HEAD_SIZE)] for h in range(GROUP)], axis=0
            )
            scores = jnp.where(key_mark <= token, dot_t(query, keys) * SCALE, MASKED)
            maxima = jnp.maximum(jnp.max(scores, axis=1, keepdims=True), FLOOR)
            weights = jnp.exp(scores - maxima)
            totals = jnp.sum(weights, axis=1, keepdims=True)
            summed = dot(weights.astype(BF16), values)
            seen = totals > 0.0
            safe = jnp.where(seen, totals, 1.0)
            normed = (summed / safe).astype(BF16)
            logs = jnp.where(seen, maxima + jnp.log(safe), MASKED)
            for h in range(GROUP):
                part = slice(h * tokens, (h + 1) * tokens)
                outs[k][:, pl.ds((g * GROUP + h) * HEAD_SIZE, HEAD_SIZE)] = normed[part]
                for term, value in enumerate(split3(logs[part])):
                    stats[k] = jnp.where(lane == term * QUERY_HEADS + g * GROUP + h, value, stats[k])
    for k in range(query_count):
        outs[k][:, pl.ds(QW, STATS)] = stats[k].astype(BF16)


def prefill_partials(offset, packs, tables, ctx, sets):
    tokens = packs[0].shape[0]
    pairs = len(packs) * tokens * KEY_SET * (ctx + tokens)
    return pl.pallas_call(
        functools.partial(prefill_kernel, sets, ctx),
        in_specs=[VMEM] * (1 + len(packs) + len(tables)),
        out_specs=[VMEM] * len(packs),
        out_shape=[jax.ShapeDtypeStruct((tokens, QW + STATS), BF16)] * len(packs),
        compiler_params=pltpu.CompilerParams(vmem_limit_bytes=32 << 20),
        cost_estimate=pl.CostEstimate(
            flops=4 * pairs * QW, bytes_accessed=4 << 20, transcendentals=pairs * QUERY_HEADS
        ),
        name="prefill_partials",
    )(offset, *packs, *tables)


def join_kernel(count, slots, *refs):
    out_ref, tokens = refs[-1], refs[0].shape[0]
    out_ref[pl.ds(0, tokens), :] = join([ref[...] for ref in refs[:count]])[0]
    out_ref[pl.ds(tokens, slots), :] = join([decode_part(ref, slots) for ref in refs[count:-1]])[0]


def join_parts(parts, decodes, slots):
    return pl.pallas_call(
        functools.partial(join_kernel, len(parts), slots),
        in_specs=[VMEM] * (len(parts) + len(decodes)),
        out_specs=VMEM,
        out_shape=jax.ShapeDtypeStruct((parts[0].shape[0] + slots, QW), BF16),
        compiler_params=pltpu.CompilerParams(vmem_limit_bytes=16 << 20),
        name="join_parts",
    )(*parts, *decodes)


def update_kernel(tokens, sets, off_ref, cache_hbm, near_ref, beside_ref, *refs):
    tables, (out_ref, cache_ref, sem) = refs[:KEY_SET], refs[-3:]
    load = pltpu.make_async_copy(cache_hbm.at[0], cache_ref, sem)
    load.start()
    ctx = cache_ref.shape[0]
    me = lax.axis_index(BLK)
    rows = [t[pl.ds(ctx, tokens), :] for t in tables]
    rows = jnp.concatenate(rows + [near_ref[...], beside_ref[...]], axis=0)
    count = rows.shape[0]
    index = lax.broadcasted_iota(jnp.int32, (1, count), 1)
    block = index // tokens
    half = sets * KEY_SET // 2
    far = block - KEY_SET
    inner = far % half
    distance = KEY_SET * (1 + inner % sets) + 2 * (inner // sets) + far // half
    token = (me ^ jnp.where(block < KEY_SET, block, distance)) * tokens + index % tokens
    wanted = me * ctx + lax.broadcasted_iota(jnp.int32, (ctx, 1), 0) - off_ref[:1, :1]
    picked = dot(jnp.where(wanted == token, 1.0, 0.0).astype(BF16), rows).astype(BF16)
    inside = jnp.broadcast_to((wanted >= 0) & (wanted < count), cache_ref.shape)
    load.wait()
    out_ref[0] = jnp.where(inside, picked, cache_ref[...])


def update_cache(offset, cache, near, beside, tables, tokens, sets):
    return pl.pallas_call(
        functools.partial(update_kernel, tokens, sets),
        in_specs=[VMEM, HBM] + [VMEM] * (2 + len(tables)),
        out_specs=VMEM,
        out_shape=jax.ShapeDtypeStruct(cache.shape, BF16),
        scratch_shapes=[pltpu.VMEM(cache.shape[1:], BF16), pltpu.SemaphoreType.DMA],
        compiler_params=pltpu.CompilerParams(vmem_limit_bytes=16 << 20),
        name="update_cache",
    )(offset, pltpu.with_memory_space_constraint(cache, pltpu.HBM), near, beside, *tables)


def route_kernel(count, route_ref, *refs):
    held, (pre_ref, dec_ref) = refs[:-2], refs[-2:]
    if len(held) < count:
        held = [held[0].at[j] for j in range(count)]
    tokens, slots = pre_ref.shape[1], dec_ref.shape[0]
    prefill = jnp.zeros(pre_ref.shape[1:], F32)
    decode = jnp.zeros(dec_ref.shape, F32)
    for j in range(count):
        flag = route_ref[j, pl.ds(slots, 1), pl.ds(0, 1)]
        prefill += flag * held[j][pl.ds(0, tokens), :].astype(F32)
        chosen = route_ref[j, pl.ds(0, slots), pl.ds(0, slots)].astype(BF16)
        decode += dot(chosen, held[j][pl.ds(tokens, slots), :])
    pre_ref[0] = prefill.astype(BF16)
    dec_ref[...] = decode.astype(BF16)


def route_outputs(route, held, tokens, slots):
    return pl.pallas_call(
        functools.partial(route_kernel, route.shape[0]),
        in_specs=[VMEM] * (1 + len(held)),
        out_specs=[VMEM] * 2,
        out_shape=[
            jax.ShapeDtypeStruct((1, tokens, QW), BF16),
            jax.ShapeDtypeStruct((slots, QW), BF16),
        ],
        compiler_params=pltpu.CompilerParams(vmem_limit_bytes=16 << 20),
        name="route_outputs",
    )(route, *held)


def per_device(
    prefill_queries,
    decode_queries,
    new_prefill,
    new_decode,
    prefill_cache,
    decode_cache,
    prefill_offsets,
    decode_lengths,
    dealing,
):
    blk = lax.axis_size(BLK)
    req = lax.axis_size("req")
    ctx = prefill_cache.shape[1]
    tokens = prefill_queries.shape[1]
    slots = decode_cache.shape[0]

    def swap(array, distance):
        return lax.ppermute(array, BLK, [(i, i ^ distance) for i in range(blk)])

    def after(array, *marks):
        return lax.optimization_barrier((array, *marks))[0]

    others = range(KEY_SET, blk, KEY_SET)
    table = jnp.concatenate([prefill_cache[0], new_prefill[0]], axis=0)
    lanes = [table] + [swap(table, k) for k in range(2, KEY_SET, 2)]
    packs = [swap(prefill_queries[0], k) for k in others]
    far = jnp.concatenate([swap(new_prefill[0], k) for k in others], axis=0)

    decode_cache_out, part, queries, route = decode_partials(
        decode_lengths, dealing, decode_queries, new_decode, decode_cache, prefill_queries, req
    )
    head, rest = PART_ROWS * slots, far.shape[0]
    (part,) = join_step(part, swap(part, 1), slots, [head + rest], "join_core", far)
    part = after(part, *lanes[1:], *packs)
    (part,) = join_step(part, swap(part, 2), slots, [head + 2 * rest], "join_x")
    part, news = join_step(part, swap(part, 4), slots, [head, 4 * rest], "join_z")

    offset = jnp.full((8, HEAD_SIZE), prefill_offsets[0], jnp.int32)
    lanes[1], offset = lax.optimization_barrier((lanes[1], offset))
    for i in range(2, len(lanes)):
        lanes[i] = after(lanes[i], lanes[i - 1])
    tables = [t for lane in lanes for t in (lane, swap(lane, 1))]

    sent = prefill_partials(offset, packs, tables, ctx, [k // KEY_SET for k in others])
    queries = after(queries, sent[0])
    kept = prefill_partials(offset, [queries], tables, ctx, [0])
    attended = join_parts(
        [*kept] + [swap(p, k) for k, p in zip(others, sent)],
        [part] + [swap(part, k) for k in others],
        slots,
    )
    prefill_cache_out = update_cache(offset, prefill_cache, news, swap(news, 1), tables, tokens, len(others))

    if req == 2:
        held = [attended, lax.ppermute(attended, "req", [(0, 1), (1, 0)])]
    else:
        held = [lax.all_gather(attended, "req", axis=0)]
    held[-1], prefill_cache_out = lax.optimization_barrier((held[-1], prefill_cache_out))
    prefill_out, decode_out = route_outputs(route, held, tokens, slots)
    return (prefill_out, decode_out, prefill_cache_out, decode_cache_out)


def solution(mesh):
    blk, req = mesh.shape["blk"], mesh.shape["req"]
    mesh = jax.sharding.Mesh(mesh.devices.reshape(blk // QUAD, QUAD, req), ("hi", "quad", "req"))
    in_specs = (
        P("req", BLK, None),
        P("req", None),
        P("req", BLK, None),
        P("req", None),
        P("req", BLK, None),
        P("req", BLK, None),
        P("req"),
        P("req"),
        P(),
    )
    out_specs = (
        P("req", BLK, None),
        P("req", None),
        P("req", BLK, None),
        P("req", BLK, None),
    )
    return jax.shard_map(
        per_device, mesh=mesh, in_specs=in_specs, out_specs=out_specs, check_vma=False
    )
```

```python
import functools

import jax
import jax.numpy as jnp
from jax import lax
from jax.experimental import pallas as pl
from jax.experimental.pallas import tpu as pltpu
from jax.sharding import PartitionSpec as P

QUERY_HEADS = 8
KEY_VALUE_HEADS = 2
HEAD_SIZE = 128
GROUP = QUERY_HEADS // KEY_VALUE_HEADS
QW = QUERY_HEADS * HEAD_SIZE
KW = KEY_VALUE_HEADS * HEAD_SIZE
STATS = 128
QUAD = 4
KEY_SET = 8
PART_ROWS = KEY_VALUE_HEADS + 1
SCALE = HEAD_SIZE**-0.5
MASKED = -1e30
FLOOR = -1e20
F32 = jnp.float32
BF16 = jnp.bfloat16

KVW = 2 * KW
BLK = ("hi", "quad")
CHUNKS = 4
TILE = 16

HBM = pl.BlockSpec(memory_space=pltpu.HBM)
VMEM = pl.BlockSpec(memory_space=pltpu.VMEM)


def dot_t(a, b):
    return lax.dot_general(a, b, (((1,), (1,)), ((), ())), preferred_element_type=F32)


def dot(a, b):
    return lax.dot_general(a, b, (((1,), (0,)), ((), ())), preferred_element_type=F32)


def split3(value):
    high = value.astype(BF16).astype(F32)
    rest = value - high
    middle = rest.astype(BF16).astype(F32)
    return high, middle, rest - middle


def stats_block(columns, rows):
    lane = lax.broadcasted_iota(jnp.int32, (rows, STATS), 1)
    count = len(columns)
    out = jnp.zeros((rows, STATS), F32)
    for head, column in enumerate(columns):
        for term, part in enumerate(split3(column)):
            out = jnp.where(lane == term * count + head, part, out)
    return out.astype(BF16)


def spread_matrix(heads):
    lane = lax.broadcasted_iota(jnp.int32, (STATS, heads * HEAD_SIZE), 0)
    head = lax.broadcasted_iota(jnp.int32, (STATS, heads * HEAD_SIZE), 1) // HEAD_SIZE
    hit = (lane == head) | (lane == head + heads) | (lane == head + 2 * heads)
    return jnp.where(hit, 1.0, 0.0).astype(BF16)


def join(parts):
    spread = spread_matrix(QUERY_HEADS)
    logs = [dot(part[:, QW:], spread) for part in parts]
    top = functools.reduce(jnp.maximum, logs)
    scales = [jnp.exp(log - top) for log in logs]
    total = functools.reduce(jnp.add, scales)
    summed = functools.reduce(
        jnp.add, [scale * part[:, :QW].astype(F32) for scale, part in zip(scales, parts)]
    )
    return (summed / total).astype(BF16), top + jnp.log(total)


def source_group(j):
    return lax.axis_index("req") ^ j if lax.axis_size("req") == 2 else j


def decode_kernel(
    len_hbm,
    deal_hbm,
    q_hbm,
    new_hbm,
    cache_hbm,
    pre_q_hbm,
    out_hbm,
    part_ref,
    pre_q_ref,
    route_ref,
    lens,
    deal,
    query_ref,
    new_ref,
    table,
    sems,
):
    slots, ctx, _ = table.shape
    rows = GROUP * slots
    chunk = slots // CHUNKS
    base = lax.axis_index(BLK) * ctx
    small = [
        (len_hbm, lens),
        (deal_hbm, deal),
        (q_hbm, query_ref),
        (new_hbm, new_ref),
        (pre_q_hbm.at[0], pre_q_ref),
    ]
    small = [pltpu.make_async_copy(a, b, sems.at[i]) for i, (a, b) in enumerate(small)]
    loads, stores = [], []
    for c in range(CHUNKS):
        part = pl.ds(c * chunk, chunk)
        loads.append(pltpu.make_async_copy(cache_hbm.at[part], table.at[part], sems.at[5 + c]))
        stores.append(pltpu.make_async_copy(table.at[part], out_hbm.at[part], sems.at[5 + CHUNKS + c]))
    for copy in small + loads:
        copy.start()
    for copy in small:
        copy.wait()
    group = lax.axis_index("req")
    req = route_ref.shape[0]
    out_row = lax.broadcasted_iota(jnp.int32, (slots, HEAD_SIZE), 0)
    out_lane = lax.broadcasted_iota(jnp.int32, (slots, HEAD_SIZE), 1)
    for j in range(req):
        source = source_group(j)
        chosen = jnp.zeros((slots, HEAD_SIZE), F32)
        for s in range(slots):
            place = deal[req + source * slots + s] - group * slots
            chosen = jnp.where((out_lane == s) & (out_row == place), 1.0, chosen)
        route_ref[j, pl.ds(0, slots), :] = chosen
        mine = (deal[source] == group).astype(F32)
        route_ref[j, pl.ds(slots, 8), :] = jnp.full((8, HEAD_SIZE), mine, F32)
    row_slot = lax.broadcasted_iota(jnp.int32, (rows, ctx), 0) % slots
    column = lax.broadcasted_iota(jnp.int32, (rows, ctx), 1)
    in_tile = lax.broadcasted_iota(jnp.int32, (TILE, KVW), 0)
    limit = jnp.full((rows, ctx), -1, jnp.int32)
    queries = [
        jnp.concatenate(
            [query_ref[:, pl.ds((g * GROUP + h) * HEAD_SIZE, HEAD_SIZE)] for h in range(GROUP)], axis=0
        )
        for g in range(KEY_VALUE_HEADS)
    ]
    scores = [jnp.zeros((rows, ctx), F32) for _ in range(KEY_VALUE_HEADS)]
    for c in range(CHUNKS):
        loads[c].wait()
        for s in range(c * chunk, (c + 1) * chunk):
            relative = lens[s] - base
            limit = jnp.where(row_slot == s, relative, limit)

            @pl.when((relative >= 0) & (relative < ctx))
            def _():
                start = pl.multiple_of(relative // TILE * TILE, TILE)
                tile = table[s, pl.ds(start, TILE), :]
                table[s, pl.ds(start, TILE), :] = jnp.where(
                    in_tile == relative - start, new_ref[s : s + 1, :], tile
                )

        stores[c].start()
        for g in range(KEY_VALUE_HEADS):
            key = table[pl.ds(c * chunk, chunk), :, pl.ds(g * HEAD_SIZE, HEAD_SIZE)]
            wide = dot_t(queries[g], key.reshape(chunk * ctx, HEAD_SIZE))
            for s in range(chunk):
                part = wide[:, s * ctx : (s + 1) * ctx]
                scores[g] = jnp.where(row_slot == c * chunk + s, part, scores[g])
    visible = column <= limit
    columns = []
    for g in range(KEY_VALUE_HEADS):
        masked = jnp.where(visible, scores[g] * SCALE, MASKED)
        maxima = jnp.maximum(jnp.max(masked, axis=1, keepdims=True), FLOOR)
        weights = jnp.exp(masked - maxima)
        totals = jnp.sum(weights, axis=1, keepdims=True)
        summed = jnp.zeros((rows, HEAD_SIZE), F32)
        for c in range(CHUNKS):
            value = table[pl.ds(c * chunk, chunk), :, pl.ds(KW + g * HEAD_SIZE, HEAD_SIZE)]
            picked = [jnp.where(row_slot == c * chunk + s, weights, 0.0) for s in range(chunk)]
            picked = jnp.concatenate(picked, axis=1).astype(BF16)
            summed += dot(picked, value.reshape(chunk * ctx, HEAD_SIZE))
        seen = totals > 0.0
        safe = jnp.where(seen, totals, 1.0)
        normed = (summed / safe).astype(BF16)
        logs = jnp.where(seen, maxima + jnp.log(safe), MASKED)
        for h in range(GROUP):
            part = slice(h * slots, (h + 1) * slots)
            part_ref[pl.ds(g * slots, slots), pl.ds(h * HEAD_SIZE, HEAD_SIZE)] = normed[part]
            columns.append(logs[part])
    put_stats(part_ref, columns, slots)
    for copy in stores:
        copy.wait()


def decode_partials(lengths, dealing, queries, new_rows, cache, pre_queries, req):
    slots, ctx, width = cache.shape
    inputs = (lengths, dealing, queries, new_rows, cache, pre_queries)
    return pl.pallas_call(
        decode_kernel,
        in_specs=[HBM] * len(inputs),
        out_specs=[HBM, VMEM, VMEM, VMEM],
        out_shape=[
            pltpu.HBM(cache.shape, BF16),
            pltpu.VMEM((PART_ROWS * slots, KVW), BF16),
            pltpu.VMEM(pre_queries.shape[1:], BF16),
            pltpu.VMEM((req, slots + 8, HEAD_SIZE), F32),
        ],
        scratch_shapes=[
            pltpu.SMEM(lengths.shape, jnp.int32),
            pltpu.SMEM(dealing.shape, jnp.int32),
            pltpu.VMEM(queries.shape, BF16),
            pltpu.VMEM(new_rows.shape, BF16),
            pltpu.VMEM(cache.shape, BF16),
            pltpu.SemaphoreType.DMA((5 + 2 * CHUNKS,)),
        ],
        compiler_params=pltpu.CompilerParams(vmem_limit_bytes=16 << 20),
        cost_estimate=pl.CostEstimate(
            flops=4 * slots * ctx * QW, bytes_accessed=2 * cache.size * 2, transcendentals=slots * ctx * 8
        ),
        name="decode_partials",
    )(*[pltpu.with_memory_space_constraint(x, pltpu.HBM) for x in inputs])


def put_stats(ref, columns, slots):
    last = pl.ds(KEY_VALUE_HEADS * slots, slots)
    ref[last, pl.ds(0, STATS)] = stats_block(columns, slots)
    ref[last, pl.ds(STATS, KVW - STATS)] = jnp.zeros((slots, KVW - STATS), BF16)


def decode_part(ref, slots):
    blocks = [ref[pl.ds(g * slots, slots), :] for g in range(KEY_VALUE_HEADS)]
    return jnp.concatenate(blocks + [ref[pl.ds(KEY_VALUE_HEADS * slots, slots), pl.ds(0, STATS)]], axis=1)


def step_kernel(slots, own_ref, other_ref, *refs):
    joined, logs = join([decode_part(own_ref, slots), decode_part(other_ref, slots)])
    head = PART_ROWS * slots
    rest = own_ref.shape[0] - head
    out_ref = refs[0] if rest else refs[-1]
    for g in range(KEY_VALUE_HEADS):
        out_ref[pl.ds(g * slots, slots), :] = joined[:, g * KVW : (g + 1) * KVW]
    put_stats(out_ref, [logs[:, h * HEAD_SIZE : h * HEAD_SIZE + 1] for h in range(QUERY_HEADS)], slots)
    if not rest:
        far_ref = refs[0]
        out_ref[pl.ds(head, far_ref.shape[0]), :] = far_ref[...]
        return
    news_ref, at = (out_ref, head) if len(refs) == 1 else (refs[1], 0)
    news_ref[pl.ds(at, rest), :] = own_ref[pl.ds(head, rest), :]
    news_ref[pl.ds(at + rest, rest), :] = other_ref[pl.ds(head, rest), :]


def join_step(own, other, slots, shapes, name, *extra):
    return pl.pallas_call(
        functools.partial(step_kernel, slots),
        in_specs=[VMEM] * (2 + len(extra)),
        out_specs=[VMEM] * len(shapes),
        out_shape=[pltpu.VMEM((rows, KVW), BF16) for rows in shapes],
        compiler_params=pltpu.CompilerParams(vmem_limit_bytes=16 << 20),
        name=name,
    )(own, other, *extra)


def prefill_kernel(sets, ctx, off_ref, *refs):
    query_count = len(sets)
    packs, tables, outs = refs[:query_count], refs[query_count:-query_count], refs[-query_count:]
    tokens = packs[0].shape[0]
    span = ctx + tokens
    me = lax.axis_index(BLK)
    offset = off_ref[:1, :1]
    pieces = []
    for k in range(KEY_SET):
        holder = me ^ k
        index = lax.broadcasted_iota(jnp.int32, (1, span), 1)
        old = jnp.where(holder * ctx + index < offset, -1, 1 << 30)
        pieces.append(jnp.where(index < ctx, old, holder * tokens + index - ctx))
    key_mark = jnp.concatenate(pieces, axis=1)
    in_block = lax.broadcasted_iota(jnp.int32, (GROUP * tokens, 1), 0) % tokens
    lane = lax.broadcasted_iota(jnp.int32, (tokens, STATS), 1)
    stats = [jnp.zeros((tokens, STATS), F32) for _ in range(query_count)]
    for g in range(KEY_VALUE_HEADS):
        keys = jnp.concatenate([t[:, pl.ds(g * HEAD_SIZE, HEAD_SIZE)] for t in tables], axis=0)
        values = jnp.concatenate([t[:, pl.ds(KW + g * HEAD_SIZE, HEAD_SIZE)] for t in tables], axis=0)
        for k in range(query_count):
            token = (me ^ (sets[k] * KEY_SET)) * tokens + in_block
            query = jnp.concatenate(
                [packs[k][:, pl.ds((g * GROUP + h) * HEAD_SIZE, HEAD_SIZE)] for h in range(GROUP)], axis=0
            )
            scores = jnp.where(key_mark <= token, dot_t(query, keys) * SCALE, MASKED)
            maxima = jnp.maximum(jnp.max(scores, axis=1, keepdims=True), FLOOR)
            weights = jnp.exp(scores - maxima)
            totals = jnp.sum(weights, axis=1, keepdims=True)
            summed = dot(weights.astype(BF16), values)
            seen = totals > 0.0
            safe = jnp.where(seen, totals, 1.0)
            normed = (summed / safe).astype(BF16)
            logs = jnp.where(seen, maxima + jnp.log(safe), MASKED)
            for h in range(GROUP):
                part = slice(h * tokens, (h + 1) * tokens)
                outs[k][:, pl.ds((g * GROUP + h) * HEAD_SIZE, HEAD_SIZE)] = normed[part]
                for term, value in enumerate(split3(logs[part])):
                    stats[k] = jnp.where(lane == term * QUERY_HEADS + g * GROUP + h, value, stats[k])
    for k in range(query_count):
        outs[k][:, pl.ds(QW, STATS)] = stats[k].astype(BF16)


def prefill_partials(offset, packs, tables, ctx, sets):
    tokens = packs[0].shape[0]
    pairs = len(packs) * tokens * KEY_SET * (ctx + tokens)
    return pl.pallas_call(
        functools.partial(prefill_kernel, sets, ctx),
        in_specs=[VMEM] * (1 + len(packs) + len(tables)),
        out_specs=[VMEM] * len(packs),
        out_shape=[jax.ShapeDtypeStruct((tokens, QW + STATS), BF16)] * len(packs),
        compiler_params=pltpu.CompilerParams(vmem_limit_bytes=32 << 20),
        cost_estimate=pl.CostEstimate(
            flops=4 * pairs * QW, bytes_accessed=4 << 20, transcendentals=pairs * QUERY_HEADS
        ),
        name="prefill_partials",
    )(offset, *packs, *tables)


def join_kernel(count, slots, *refs):
    out_ref, tokens = refs[-1], refs[0].shape[0]
    out_ref[pl.ds(0, tokens), :] = join([ref[...] for ref in refs[:count]])[0]
    out_ref[pl.ds(tokens, slots), :] = join([decode_part(ref, slots) for ref in refs[count:-1]])[0]


def join_parts(parts, decodes, slots):
    return pl.pallas_call(
        functools.partial(join_kernel, len(parts), slots),
        in_specs=[VMEM] * (len(parts) + len(decodes)),
        out_specs=VMEM,
        out_shape=jax.ShapeDtypeStruct((parts[0].shape[0] + slots, QW), BF16),
        compiler_params=pltpu.CompilerParams(vmem_limit_bytes=16 << 20),
        name="join_parts",
    )(*parts, *decodes)


def update_kernel(tokens, sets, off_ref, cache_hbm, near_ref, beside_ref, *refs):
    tables, (out_ref, cache_ref, sem) = refs[:KEY_SET], refs[-3:]
    load = pltpu.make_async_copy(cache_hbm.at[0], cache_ref, sem)
    load.start()
    ctx = cache_ref.shape[0]
    me = lax.axis_index(BLK)
    rows = [t[pl.ds(ctx, tokens), :] for t in tables]
    rows = jnp.concatenate(rows + [near_ref[...], beside_ref[...]], axis=0)
    count = rows.shape[0]
    index = lax.broadcasted_iota(jnp.int32, (1, count), 1)
    block = index // tokens
    half = sets * KEY_SET // 2
    far = block - KEY_SET
    inner = far % half
    distance = KEY_SET * (1 + inner % sets) + 2 * (inner // sets) + far // half
    token = (me ^ jnp.where(block < KEY_SET, block, distance)) * tokens + index % tokens
    wanted = me * ctx + lax.broadcasted_iota(jnp.int32, (ctx, 1), 0) - off_ref[:1, :1]
    picked = dot(jnp.where(wanted == token, 1.0, 0.0).astype(BF16), rows).astype(BF16)
    inside = jnp.broadcast_to((wanted >= 0) & (wanted < count), cache_ref.shape)
    load.wait()
    out_ref[0] = jnp.where(inside, picked, cache_ref[...])


def update_cache(offset, cache, near, beside, tables, tokens, sets):
    return pl.pallas_call(
        functools.partial(update_kernel, tokens, sets),
        in_specs=[VMEM, HBM] + [VMEM] * (2 + len(tables)),
        out_specs=VMEM,
        out_shape=jax.ShapeDtypeStruct(cache.shape, BF16),
        scratch_shapes=[pltpu.VMEM(cache.shape[1:], BF16), pltpu.SemaphoreType.DMA],
        compiler_params=pltpu.CompilerParams(vmem_limit_bytes=16 << 20),
        name="update_cache",
    )(offset, pltpu.with_memory_space_constraint(cache, pltpu.HBM), near, beside, *tables)


def route_kernel(count, route_ref, *refs):
    held, (pre_ref, dec_ref) = refs[:-2], refs[-2:]
    if len(held) < count:
        held = [held[0].at[j] for j in range(count)]
    tokens, slots = pre_ref.shape[1], dec_ref.shape[0]
    prefill = jnp.zeros(pre_ref.shape[1:], F32)
    decode = jnp.zeros(dec_ref.shape, F32)
    for j in range(count):
        flag = route_ref[j, pl.ds(slots, 1), pl.ds(0, 1)]
        prefill += flag * held[j][pl.ds(0, tokens), :].astype(F32)
        chosen = route_ref[j, pl.ds(0, slots), pl.ds(0, slots)].astype(BF16)
        decode += dot(chosen, held[j][pl.ds(tokens, slots), :])
    pre_ref[0] = prefill.astype(BF16)
    dec_ref[...] = decode.astype(BF16)


def route_outputs(route, held, tokens, slots):
    return pl.pallas_call(
        functools.partial(route_kernel, route.shape[0]),
        in_specs=[VMEM] * (1 + len(held)),
        out_specs=[VMEM] * 2,
        out_shape=[
            jax.ShapeDtypeStruct((1, tokens, QW), BF16),
            jax.ShapeDtypeStruct((slots, QW), BF16),
        ],
        compiler_params=pltpu.CompilerParams(vmem_limit_bytes=16 << 20),
        name="route_outputs",
    )(route, *held)


def per_device(
    prefill_queries,
    decode_queries,
    new_prefill,
    new_decode,
    prefill_cache,
    decode_cache,
    prefill_offsets,
    decode_lengths,
    dealing,
):
    blk = lax.axis_size(BLK)
    req = lax.axis_size("req")
    ctx = prefill_cache.shape[1]
    tokens = prefill_queries.shape[1]
    slots = decode_cache.shape[0]

    def swap(array, distance):
        return lax.ppermute(array, BLK, [(i, i ^ distance) for i in range(blk)])

    def after(array, *marks):
        return lax.optimization_barrier((array, *marks))[0]

    others = range(KEY_SET, blk, KEY_SET)
    table = jnp.concatenate([prefill_cache[0], new_prefill[0]], axis=0)
    lanes = [table] + [swap(table, k) for k in range(2, KEY_SET, 2)]
    packs = [swap(prefill_queries[0], k) for k in others]
    far = jnp.concatenate([swap(new_prefill[0], k) for k in others], axis=0)

    decode_cache_out, part, queries, route = decode_partials(
        decode_lengths, dealing, decode_queries, new_decode, decode_cache, prefill_queries, req
    )
    head, rest = PART_ROWS * slots, far.shape[0]
    part, far = lax.optimization_barrier((part, far))
    beside = swap(part, 1)
    offset = jnp.full((8, HEAD_SIZE), prefill_offsets[0], jnp.int32)
    lanes[1], offset, _ = lax.optimization_barrier((lanes[1], offset, part))
    lanes[2], beside, _ = lax.optimization_barrier((lanes[2], beside, lanes[1]))
    lanes[3], packs, _ = lax.optimization_barrier((lanes[3], packs, lanes[2]))
    (part,) = join_step(part, beside, slots, [head + rest], "join_core", far)
    across = swap(part, 2)
    tables = [t for lane in lanes for t in (lane, swap(lane, 1))]

    sent = prefill_partials(offset, packs, tables, ctx, [k // KEY_SET for k in others])
    (part,) = join_step(part, after(across, sent[0]), slots, [head + 2 * rest], "join_x")
    part, news = join_step(part, swap(part, 4), slots, [head, 4 * rest], "join_z")

    queries = after(queries, sent[0])
    kept = prefill_partials(offset, [queries], tables, ctx, [0])
    attended = join_parts(
        [*kept] + [swap(p, k) for k, p in zip(others, sent)],
        [part] + [swap(part, k) for k in others],
        slots,
    )
    prefill_cache_out = update_cache(offset, prefill_cache, news, swap(news, 1), tables, tokens, len(others))

    if req == 2:
        held = [attended, lax.ppermute(attended, "req", [(0, 1), (1, 0)])]
    else:
        held = [lax.all_gather(attended, "req", axis=0)]
    held[-1], prefill_cache_out = lax.optimization_barrier((held[-1], prefill_cache_out))
    prefill_out, decode_out = route_outputs(route, held, tokens, slots)
    return (prefill_out, decode_out, prefill_cache_out, decode_cache_out)


def solution(mesh):
    blk, req = mesh.shape["blk"], mesh.shape["req"]
    mesh = jax.sharding.Mesh(mesh.devices.reshape(blk // QUAD, QUAD, req), ("hi", "quad", "req"))
    in_specs = (
        P("req", BLK, None),
        P("req", None),
        P("req", BLK, None),
        P("req", None),
        P("req", BLK, None),
        P("req", BLK, None),
        P("req"),
        P("req"),
        P(),
    )
    out_specs = (
        P("req", BLK, None),
        P("req", None),
        P("req", BLK, None),
        P("req", BLK, None),
    )
    return jax.shard_map(
        per_device, mesh=mesh, in_specs=in_specs, out_specs=out_specs, check_vma=False
    )
```

```python
import functools

import jax
import jax.numpy as jnp
from jax import lax
from jax.experimental import pallas as pl
from jax.experimental.pallas import tpu as pltpu
from jax.sharding import PartitionSpec as P

QUERY_HEADS = 8
KEY_VALUE_HEADS = 2
HEAD_SIZE = 128
GROUP = QUERY_HEADS // KEY_VALUE_HEADS
QW = QUERY_HEADS * HEAD_SIZE
KW = KEY_VALUE_HEADS * HEAD_SIZE
STATS = 128
QUAD = 4
KEY_SET = 8
PART_ROWS = KEY_VALUE_HEADS + 1
SCALE = HEAD_SIZE**-0.5
MASKED = -1e30
FLOOR = -1e20
F32 = jnp.float32
BF16 = jnp.bfloat16

KVW = 2 * KW
BLK = ("hi", "quad")
CHUNKS = 4
TILE = 16

HBM = pl.BlockSpec(memory_space=pltpu.HBM)
VMEM = pl.BlockSpec(memory_space=pltpu.VMEM)


def dot_t(a, b):
    return lax.dot_general(a, b, (((1,), (1,)), ((), ())), preferred_element_type=F32)


def dot(a, b):
    return lax.dot_general(a, b, (((1,), (0,)), ((), ())), preferred_element_type=F32)


def split3(value):
    high = value.astype(BF16).astype(F32)
    rest = value - high
    middle = rest.astype(BF16).astype(F32)
    return high, middle, rest - middle


def stats_block(columns, rows):
    lane = lax.broadcasted_iota(jnp.int32, (rows, STATS), 1)
    count = len(columns)
    out = jnp.zeros((rows, STATS), F32)
    for head, column in enumerate(columns):
        for term, part in enumerate(split3(column)):
            out = jnp.where(lane == term * count + head, part, out)
    return out.astype(BF16)


def spread_matrix(heads):
    lane = lax.broadcasted_iota(jnp.int32, (STATS, heads * HEAD_SIZE), 0)
    head = lax.broadcasted_iota(jnp.int32, (STATS, heads * HEAD_SIZE), 1) // HEAD_SIZE
    hit = (lane == head) | (lane == head + heads) | (lane == head + 2 * heads)
    return jnp.where(hit, 1.0, 0.0).astype(BF16)


def join(parts):
    spread = spread_matrix(QUERY_HEADS)
    logs = [dot(part[:, QW:], spread) for part in parts]
    top = functools.reduce(jnp.maximum, logs)
    scales = [jnp.exp(log - top) for log in logs]
    total = functools.reduce(jnp.add, scales)
    summed = functools.reduce(
        jnp.add, [scale * part[:, :QW].astype(F32) for scale, part in zip(scales, parts)]
    )
    return (summed / total).astype(BF16), top + jnp.log(total)


def source_group(j):
    return lax.axis_index("req") ^ j if lax.axis_size("req") == 2 else j


def decode_kernel(
    len_hbm,
    deal_hbm,
    q_hbm,
    new_hbm,
    cache_hbm,
    pre_q_hbm,
    out_hbm,
    part_ref,
    pre_q_ref,
    route_ref,
    lens,
    deal,
    query_ref,
    new_ref,
    table,
    sems,
):
    slots, ctx, _ = table.shape
    rows = GROUP * slots
    chunk = slots // CHUNKS
    base = lax.axis_index(BLK) * ctx
    small = [
        (len_hbm, lens),
        (deal_hbm, deal),
        (q_hbm, query_ref),
        (new_hbm, new_ref),
        (pre_q_hbm.at[0], pre_q_ref),
    ]
    small = [pltpu.make_async_copy(a, b, sems.at[i]) for i, (a, b) in enumerate(small)]
    loads, stores = [], []
    for c in range(CHUNKS):
        part = pl.ds(c * chunk, chunk)
        loads.append(pltpu.make_async_copy(cache_hbm.at[part], table.at[part], sems.at[5 + c]))
        stores.append(pltpu.make_async_copy(table.at[part], out_hbm.at[part], sems.at[5 + CHUNKS + c]))
    for copy in small + loads:
        copy.start()
    for copy in small:
        copy.wait()
    group = lax.axis_index("req")
    req = route_ref.shape[0]
    out_row = lax.broadcasted_iota(jnp.int32, (slots, HEAD_SIZE), 0)
    out_lane = lax.broadcasted_iota(jnp.int32, (slots, HEAD_SIZE), 1)
    for j in range(req):
        source = source_group(j)
        chosen = jnp.zeros((slots, HEAD_SIZE), F32)
        for s in range(slots):
            place = deal[req + source * slots + s] - group * slots
            chosen = jnp.where((out_lane == s) & (out_row == place), 1.0, chosen)
        route_ref[j, pl.ds(0, slots), :] = chosen
        mine = (deal[source] == group).astype(F32)
        route_ref[j, pl.ds(slots, 8), :] = jnp.full((8, HEAD_SIZE), mine, F32)
    row_slot = lax.broadcasted_iota(jnp.int32, (rows, ctx), 0) % slots
    column = lax.broadcasted_iota(jnp.int32, (rows, ctx), 1)
    in_tile = lax.broadcasted_iota(jnp.int32, (TILE, KVW), 0)
    limit = jnp.full((rows, ctx), -1, jnp.int32)
    queries = [
        jnp.concatenate(
            [query_ref[:, pl.ds((g * GROUP + h) * HEAD_SIZE, HEAD_SIZE)] for h in range(GROUP)], axis=0
        )
        for g in range(KEY_VALUE_HEADS)
    ]
    scores = [jnp.zeros((rows, ctx), F32) for _ in range(KEY_VALUE_HEADS)]
    for c in range(CHUNKS):
        loads[c].wait()
        for s in range(c * chunk, (c + 1) * chunk):
            relative = lens[s] - base
            limit = jnp.where(row_slot == s, relative, limit)

            @pl.when((relative >= 0) & (relative < ctx))
            def _():
                start = pl.multiple_of(relative // TILE * TILE, TILE)
                tile = table[s, pl.ds(start, TILE), :]
                table[s, pl.ds(start, TILE), :] = jnp.where(
                    in_tile == relative - start, new_ref[s : s + 1, :], tile
                )

        stores[c].start()
        for g in range(KEY_VALUE_HEADS):
            key = table[pl.ds(c * chunk, chunk), :, pl.ds(g * HEAD_SIZE, HEAD_SIZE)]
            wide = dot_t(queries[g], key.reshape(chunk * ctx, HEAD_SIZE))
            for s in range(chunk):
                part = wide[:, s * ctx : (s + 1) * ctx]
                scores[g] = jnp.where(row_slot == c * chunk + s, part, scores[g])
    visible = column <= limit
    columns = []
    for g in range(KEY_VALUE_HEADS):
        masked = jnp.where(visible, scores[g] * SCALE, MASKED)
        maxima = jnp.maximum(jnp.max(masked, axis=1, keepdims=True), FLOOR)
        weights = jnp.exp(masked - maxima)
        totals = jnp.sum(weights, axis=1, keepdims=True)
        summed = jnp.zeros((rows, HEAD_SIZE), F32)
        for c in range(CHUNKS):
            value = table[pl.ds(c * chunk, chunk), :, pl.ds(KW + g * HEAD_SIZE, HEAD_SIZE)]
            picked = [jnp.where(row_slot == c * chunk + s, weights, 0.0) for s in range(chunk)]
            picked = jnp.concatenate(picked, axis=1).astype(BF16)
            summed += dot(picked, value.reshape(chunk * ctx, HEAD_SIZE))
        seen = totals > 0.0
        safe = jnp.where(seen, totals, 1.0)
        normed = (summed / safe).astype(BF16)
        logs = jnp.where(seen, maxima + jnp.log(safe), MASKED)
        for h in range(GROUP):
            part = slice(h * slots, (h + 1) * slots)
            part_ref[pl.ds(g * slots, slots), pl.ds(h * HEAD_SIZE, HEAD_SIZE)] = normed[part]
            columns.append(logs[part])
    put_stats(part_ref, columns, slots)
    for copy in stores:
        copy.wait()


def decode_partials(lengths, dealing, queries, new_rows, cache, pre_queries, req):
    slots, ctx, width = cache.shape
    inputs = (lengths, dealing, queries, new_rows, cache, pre_queries)
    return pl.pallas_call(
        decode_kernel,
        in_specs=[HBM] * len(inputs),
        out_specs=[HBM, VMEM, VMEM, VMEM],
        out_shape=[
            pltpu.HBM(cache.shape, BF16),
            pltpu.VMEM((PART_ROWS * slots, KVW), BF16),
            pltpu.VMEM(pre_queries.shape[1:], BF16),
            pltpu.VMEM((req, slots + 8, HEAD_SIZE), F32),
        ],
        scratch_shapes=[
            pltpu.SMEM(lengths.shape, jnp.int32),
            pltpu.SMEM(dealing.shape, jnp.int32),
            pltpu.VMEM(queries.shape, BF16),
            pltpu.VMEM(new_rows.shape, BF16),
            pltpu.VMEM(cache.shape, BF16),
            pltpu.SemaphoreType.DMA((5 + 2 * CHUNKS,)),
        ],
        compiler_params=pltpu.CompilerParams(vmem_limit_bytes=16 << 20),
        cost_estimate=pl.CostEstimate(
            flops=4 * slots * ctx * QW, bytes_accessed=2 * cache.size * 2, transcendentals=slots * ctx * 8
        ),
        name="decode_partials",
    )(*[pltpu.with_memory_space_constraint(x, pltpu.HBM) for x in inputs])


def put_stats(ref, columns, slots):
    last = pl.ds(KEY_VALUE_HEADS * slots, slots)
    ref[last, pl.ds(0, STATS)] = stats_block(columns, slots)
    ref[last, pl.ds(STATS, KVW - STATS)] = jnp.zeros((slots, KVW - STATS), BF16)


def decode_part(ref, slots):
    blocks = [ref[pl.ds(g * slots, slots), :] for g in range(KEY_VALUE_HEADS)]
    return jnp.concatenate(blocks + [ref[pl.ds(KEY_VALUE_HEADS * slots, slots), pl.ds(0, STATS)]], axis=1)


def step_kernel(slots, appends, own_ref, other_ref, *refs):
    joined, logs = join([decode_part(own_ref, slots), decode_part(other_ref, slots)])
    head = PART_ROWS * slots
    rest = own_ref.shape[0] - head
    out_ref = refs[1] if appends else refs[0]
    for g in range(KEY_VALUE_HEADS):
        out_ref[pl.ds(g * slots, slots), :] = joined[:, g * KVW : (g + 1) * KVW]
    put_stats(out_ref, [logs[:, h * HEAD_SIZE : h * HEAD_SIZE + 1] for h in range(QUERY_HEADS)], slots)
    if appends:
        out_ref[pl.ds(head, refs[0].shape[0]), :] = refs[0][...]
    if rest:
        refs[1][pl.ds(0, rest), :] = own_ref[pl.ds(head, rest), :]
        refs[1][pl.ds(rest, rest), :] = other_ref[pl.ds(head, rest), :]


def join_step(own, other, slots, shapes, name, *extra):
    return pl.pallas_call(
        functools.partial(step_kernel, slots, bool(extra)),
        in_specs=[VMEM] * (2 + len(extra)),
        out_specs=[VMEM] * len(shapes),
        out_shape=[pltpu.VMEM((rows, KVW), BF16) for rows in shapes],
        compiler_params=pltpu.CompilerParams(vmem_limit_bytes=16 << 20),
        name=name,
    )(own, other, *extra)


def prefill_kernel(sets, ctx, off_ref, *refs):
    query_count = len(sets)
    packs, tables, outs = refs[:query_count], refs[query_count:-query_count], refs[-query_count:]
    tokens = packs[0].shape[0]
    span = ctx + tokens
    me = lax.axis_index(BLK)
    offset = off_ref[:1, :1]
    pieces = []
    for k in range(KEY_SET):
        holder = me ^ k
        index = lax.broadcasted_iota(jnp.int32, (1, span), 1)
        old = jnp.where(holder * ctx + index < offset, -1, 1 << 30)
        pieces.append(jnp.where(index < ctx, old, holder * tokens + index - ctx))
    key_mark = jnp.concatenate(pieces, axis=1)
    in_block = lax.broadcasted_iota(jnp.int32, (GROUP * tokens, 1), 0) % tokens
    lane = lax.broadcasted_iota(jnp.int32, (tokens, STATS), 1)
    stats = [jnp.zeros((tokens, STATS), F32) for _ in range(query_count)]
    for g in range(KEY_VALUE_HEADS):
        keys = jnp.concatenate([t[:, pl.ds(g * HEAD_SIZE, HEAD_SIZE)] for t in tables], axis=0)
        values = jnp.concatenate([t[:, pl.ds(KW + g * HEAD_SIZE, HEAD_SIZE)] for t in tables], axis=0)
        for k in range(query_count):
            token = (me ^ (sets[k] * KEY_SET)) * tokens + in_block
            query = jnp.concatenate(
                [packs[k][:, pl.ds((g * GROUP + h) * HEAD_SIZE, HEAD_SIZE)] for h in range(GROUP)], axis=0
            )
            scores = jnp.where(key_mark <= token, dot_t(query, keys) * SCALE, MASKED)
            maxima = jnp.maximum(jnp.max(scores, axis=1, keepdims=True), FLOOR)
            weights = jnp.exp(scores - maxima)
            totals = jnp.sum(weights, axis=1, keepdims=True)
            summed = dot(weights.astype(BF16), values)
            seen = totals > 0.0
            safe = jnp.where(seen, totals, 1.0)
            normed = (summed / safe).astype(BF16)
            logs = jnp.where(seen, maxima + jnp.log(safe), MASKED)
            for h in range(GROUP):
                part = slice(h * tokens, (h + 1) * tokens)
                outs[k][:, pl.ds((g * GROUP + h) * HEAD_SIZE, HEAD_SIZE)] = normed[part]
                for term, value in enumerate(split3(logs[part])):
                    stats[k] = jnp.where(lane == term * QUERY_HEADS + g * GROUP + h, value, stats[k])
    for k in range(query_count):
        outs[k][:, pl.ds(QW, STATS)] = stats[k].astype(BF16)


def prefill_partials(offset, packs, tables, ctx, sets):
    tokens = packs[0].shape[0]
    pairs = len(packs) * tokens * KEY_SET * (ctx + tokens)
    return pl.pallas_call(
        functools.partial(prefill_kernel, sets, ctx),
        in_specs=[VMEM] * (1 + len(packs) + len(tables)),
        out_specs=[VMEM] * len(packs),
        out_shape=[jax.ShapeDtypeStruct((tokens, QW + STATS), BF16)] * len(packs),
        compiler_params=pltpu.CompilerParams(vmem_limit_bytes=32 << 20),
        cost_estimate=pl.CostEstimate(
            flops=4 * pairs * QW, bytes_accessed=4 << 20, transcendentals=pairs * QUERY_HEADS
        ),
        name="prefill_partials",
    )(offset, *packs, *tables)


def join_kernel(count, slots, *refs):
    out_ref, tokens = refs[-1], refs[0].shape[0]
    out_ref[pl.ds(0, tokens), :] = join([ref[...] for ref in refs[:count]])[0]
    out_ref[pl.ds(tokens, slots), :] = join([decode_part(ref, slots) for ref in refs[count:-1]])[0]


def join_parts(parts, decodes, slots):
    return pl.pallas_call(
        functools.partial(join_kernel, len(parts), slots),
        in_specs=[VMEM] * (len(parts) + len(decodes)),
        out_specs=VMEM,
        out_shape=jax.ShapeDtypeStruct((parts[0].shape[0] + slots, QW), BF16),
        compiler_params=pltpu.CompilerParams(vmem_limit_bytes=16 << 20),
        name="join_parts",
    )(*parts, *decodes)


def update_kernel(tokens, sets, off_ref, cache_hbm, near_ref, beside_ref, *refs):
    tables, (out_ref, cache_ref, sem) = refs[:KEY_SET], refs[-3:]
    load = pltpu.make_async_copy(cache_hbm.at[0], cache_ref, sem)
    load.start()
    ctx = cache_ref.shape[0]
    me = lax.axis_index(BLK)
    rows = [t[pl.ds(ctx, tokens), :] for t in tables]
    rows = jnp.concatenate(rows + [near_ref[...], beside_ref[...]], axis=0)
    count = rows.shape[0]
    index = lax.broadcasted_iota(jnp.int32, (1, count), 1)
    block = index // tokens
    half = sets * KEY_SET // 2
    far = block - KEY_SET
    inner = far % half
    lane = inner // sets
    distance = KEY_SET * (1 + inner % sets) + lane % 2 * 4 + lane // 2 * 2 + far // half
    token = (me ^ jnp.where(block < KEY_SET, block, distance)) * tokens + index % tokens
    wanted = me * ctx + lax.broadcasted_iota(jnp.int32, (ctx, 1), 0) - off_ref[:1, :1]
    picked = dot(jnp.where(wanted == token, 1.0, 0.0).astype(BF16), rows).astype(BF16)
    inside = jnp.broadcast_to((wanted >= 0) & (wanted < count), cache_ref.shape)
    load.wait()
    out_ref[0] = jnp.where(inside, picked, cache_ref[...])


def update_cache(offset, cache, near, beside, tables, tokens, sets):
    return pl.pallas_call(
        functools.partial(update_kernel, tokens, sets),
        in_specs=[VMEM, HBM] + [VMEM] * (2 + len(tables)),
        out_specs=VMEM,
        out_shape=jax.ShapeDtypeStruct(cache.shape, BF16),
        scratch_shapes=[pltpu.VMEM(cache.shape[1:], BF16), pltpu.SemaphoreType.DMA],
        compiler_params=pltpu.CompilerParams(vmem_limit_bytes=16 << 20),
        name="update_cache",
    )(offset, pltpu.with_memory_space_constraint(cache, pltpu.HBM), near, beside, *tables)


def route_kernel(count, route_ref, *refs):
    held, (pre_ref, dec_ref) = refs[:-2], refs[-2:]
    if len(held) < count:
        held = [held[0].at[j] for j in range(count)]
    tokens, slots = pre_ref.shape[1], dec_ref.shape[0]
    prefill = jnp.zeros(pre_ref.shape[1:], F32)
    decode = jnp.zeros(dec_ref.shape, F32)
    for j in range(count):
        flag = route_ref[j, pl.ds(slots, 1), pl.ds(0, 1)]
        prefill += flag * held[j][pl.ds(0, tokens), :].astype(F32)
        chosen = route_ref[j, pl.ds(0, slots), pl.ds(0, slots)].astype(BF16)
        decode += dot(chosen, held[j][pl.ds(tokens, slots), :])
    pre_ref[0] = prefill.astype(BF16)
    dec_ref[...] = decode.astype(BF16)


def route_outputs(route, held, tokens, slots):
    return pl.pallas_call(
        functools.partial(route_kernel, route.shape[0]),
        in_specs=[VMEM] * (1 + len(held)),
        out_specs=[VMEM] * 2,
        out_shape=[
            jax.ShapeDtypeStruct((1, tokens, QW), BF16),
            jax.ShapeDtypeStruct((slots, QW), BF16),
        ],
        compiler_params=pltpu.CompilerParams(vmem_limit_bytes=16 << 20),
        name="route_outputs",
    )(route, *held)


def per_device(
    prefill_queries,
    decode_queries,
    new_prefill,
    new_decode,
    prefill_cache,
    decode_cache,
    prefill_offsets,
    decode_lengths,
    dealing,
):
    blk = lax.axis_size(BLK)
    req = lax.axis_size("req")
    ctx = prefill_cache.shape[1]
    tokens = prefill_queries.shape[1]
    slots = decode_cache.shape[0]

    def swap(array, distance):
        return lax.ppermute(array, BLK, [(i, i ^ distance) for i in range(blk)])

    def after(array, *marks):
        return lax.optimization_barrier((array, *marks))[0]

    others = range(KEY_SET, blk, KEY_SET)
    table = jnp.concatenate([prefill_cache[0], new_prefill[0]], axis=0)
    lanes = [table] + [swap(table, k) for k in range(2, KEY_SET, 2)]
    packs = [swap(prefill_queries[0], k) for k in others]
    far = jnp.concatenate([swap(new_prefill[0], k) for k in others], axis=0)

    decode_cache_out, part, queries, route = decode_partials(
        decode_lengths, dealing, decode_queries, new_decode, decode_cache, prefill_queries, req
    )
    head, rest = PART_ROWS * slots, far.shape[0]
    beside = swap(part, 1)
    offset = jnp.full((8, HEAD_SIZE), prefill_offsets[0], jnp.int32)
    lanes[1], offset, _ = lax.optimization_barrier((lanes[1], offset, part))
    lanes[2], beside, _ = lax.optimization_barrier((lanes[2], beside, lanes[1]))
    (part,) = join_step(part, beside, slots, [head], "join_core")
    across = swap(part, 2)
    lanes[3], packs, far, _ = lax.optimization_barrier((lanes[3], packs, far, lanes[2]))
    tables = [t for lane in lanes for t in (lane, swap(lane, 1))]

    sent = prefill_partials(offset, packs, tables, ctx, [k // KEY_SET for k in others])
    (part,) = join_step(part, after(across, sent[0]), slots, [head + rest], "join_x", far)
    queries = after(queries, sent[0])
    kept = prefill_partials(offset, [queries], tables, ctx, [0])
    part, news = join_step(part, after(swap(part, 4), kept[0]), slots, [head, 2 * rest], "join_z")
    attended = join_parts(
        [*kept] + [swap(p, k) for k, p in zip(others, sent)],
        [part] + [swap(part, k) for k in others],
        slots,
    )
    news = jnp.concatenate([news, swap(news, 2)], axis=0)
    prefill_cache_out = update_cache(offset, prefill_cache, news, swap(news, 1), tables, tokens, len(others))

    if req == 2:
        held = [attended, lax.ppermute(attended, "req", [(0, 1), (1, 0)])]
    else:
        held = [lax.all_gather(attended, "req", axis=0)]
    held[-1], prefill_cache_out = lax.optimization_barrier((held[-1], prefill_cache_out))
    prefill_out, decode_out = route_outputs(route, held, tokens, slots)
    return (prefill_out, decode_out, prefill_cache_out, decode_cache_out)


def solution(mesh):
    blk, req = mesh.shape["blk"], mesh.shape["req"]
    mesh = jax.sharding.Mesh(mesh.devices.reshape(blk // QUAD, QUAD, req), ("hi", "quad", "req"))
    in_specs = (
        P("req", BLK, None),
        P("req", None),
        P("req", BLK, None),
        P("req", None),
        P("req", BLK, None),
        P("req", BLK, None),
        P("req"),
        P("req"),
        P(),
    )
    out_specs = (
        P("req", BLK, None),
        P("req", None),
        P("req", BLK, None),
        P("req", BLK, None),
    )
    return jax.shard_map(
        per_device, mesh=mesh, in_specs=in_specs, out_specs=out_specs, check_vma=False
    )
```

```python
import functools

import jax
import jax.numpy as jnp
from jax import lax
from jax.experimental import pallas as pl
from jax.experimental.pallas import tpu as pltpu
from jax.sharding import PartitionSpec as P

QUERY_HEADS = 8
KEY_VALUE_HEADS = 2
HEAD_SIZE = 128
GROUP = QUERY_HEADS // KEY_VALUE_HEADS
QW = QUERY_HEADS * HEAD_SIZE
KW = KEY_VALUE_HEADS * HEAD_SIZE
STATS = 128
QUAD = 4
KEY_SET = 8
PART_ROWS = KEY_VALUE_HEADS + 1
SCALE = HEAD_SIZE**-0.5
MASKED = -1e30
FLOOR = -1e20
F32 = jnp.float32
BF16 = jnp.bfloat16

KVW = 2 * KW
BLK = ("hi", "quad")
CHUNKS = 4
TILE = 16

HBM = pl.BlockSpec(memory_space=pltpu.HBM)
VMEM = pl.BlockSpec(memory_space=pltpu.VMEM)


def dot_t(a, b):
    return lax.dot_general(a, b, (((1,), (1,)), ((), ())), preferred_element_type=F32)


def dot(a, b):
    return lax.dot_general(a, b, (((1,), (0,)), ((), ())), preferred_element_type=F32)


def split3(value):
    high = value.astype(BF16).astype(F32)
    rest = value - high
    middle = rest.astype(BF16).astype(F32)
    return high, middle, rest - middle


def stats_block(columns, rows):
    lane = lax.broadcasted_iota(jnp.int32, (rows, STATS), 1)
    count = len(columns)
    out = jnp.zeros((rows, STATS), F32)
    for head, column in enumerate(columns):
        for term, part in enumerate(split3(column)):
            out = jnp.where(lane == term * count + head, part, out)
    return out.astype(BF16)


def spread_matrix(heads):
    lane = lax.broadcasted_iota(jnp.int32, (STATS, heads * HEAD_SIZE), 0)
    head = lax.broadcasted_iota(jnp.int32, (STATS, heads * HEAD_SIZE), 1) // HEAD_SIZE
    hit = (lane == head) | (lane == head + heads) | (lane == head + 2 * heads)
    return jnp.where(hit, 1.0, 0.0).astype(BF16)


def join(parts):
    spread = spread_matrix(QUERY_HEADS)
    logs = [dot(part[:, QW:], spread) for part in parts]
    top = functools.reduce(jnp.maximum, logs)
    scales = [jnp.exp(log - top) for log in logs]
    total = functools.reduce(jnp.add, scales)
    summed = functools.reduce(
        jnp.add, [scale * part[:, :QW].astype(F32) for scale, part in zip(scales, parts)]
    )
    return (summed / total).astype(BF16), top + jnp.log(total)


def source_group(j):
    return lax.axis_index("req") ^ j if lax.axis_size("req") == 2 else j


def decode_kernel(
    len_hbm,
    deal_hbm,
    q_hbm,
    new_hbm,
    cache_hbm,
    pre_q_hbm,
    out_hbm,
    part_ref,
    pre_q_ref,
    route_ref,
    lens,
    deal,
    query_ref,
    new_ref,
    table,
    sems,
):
    slots, ctx, _ = table.shape
    rows = GROUP * slots
    chunk = slots // CHUNKS
    base = lax.axis_index(BLK) * ctx
    small = [
        (len_hbm, lens),
        (deal_hbm, deal),
        (q_hbm, query_ref),
        (new_hbm, new_ref),
        (pre_q_hbm.at[0], pre_q_ref),
    ]
    small = [pltpu.make_async_copy(a, b, sems.at[i]) for i, (a, b) in enumerate(small)]
    loads, stores = [], []
    for c in range(CHUNKS):
        part = pl.ds(c * chunk, chunk)
        loads.append(pltpu.make_async_copy(cache_hbm.at[part], table.at[part], sems.at[5 + c]))
        stores.append(pltpu.make_async_copy(table.at[part], out_hbm.at[part], sems.at[5 + CHUNKS + c]))
    for copy in small + loads:
        copy.start()
    for copy in small:
        copy.wait()
    group = lax.axis_index("req")
    req = route_ref.shape[0]
    out_row = lax.broadcasted_iota(jnp.int32, (slots, HEAD_SIZE), 0)
    out_lane = lax.broadcasted_iota(jnp.int32, (slots, HEAD_SIZE), 1)
    for j in range(req):
        source = source_group(j)
        chosen = jnp.zeros((slots, HEAD_SIZE), F32)
        for s in range(slots):
            place = deal[req + source * slots + s] - group * slots
            chosen = jnp.where((out_lane == s) & (out_row == place), 1.0, chosen)
        route_ref[j, pl.ds(0, slots), :] = chosen
        mine = (deal[source] == group).astype(F32)
        route_ref[j, pl.ds(slots, 8), :] = jnp.full((8, HEAD_SIZE), mine, F32)
    row_slot = lax.broadcasted_iota(jnp.int32, (rows, ctx), 0) % slots
    column = lax.broadcasted_iota(jnp.int32, (rows, ctx), 1)
    in_tile = lax.broadcasted_iota(jnp.int32, (TILE, KVW), 0)
    limit = jnp.full((rows, ctx), -1, jnp.int32)
    queries = [
        jnp.concatenate(
            [query_ref[:, pl.ds((g * GROUP + h) * HEAD_SIZE, HEAD_SIZE)] for h in range(GROUP)], axis=0
        )
        for g in range(KEY_VALUE_HEADS)
    ]
    scores = [jnp.zeros((rows, ctx), F32) for _ in range(KEY_VALUE_HEADS)]
    for c in range(CHUNKS):
        loads[c].wait()
        for s in range(c * chunk, (c + 1) * chunk):
            relative = lens[s] - base
            limit = jnp.where(row_slot == s, relative, limit)

            @pl.when((relative >= 0) & (relative < ctx))
            def _():
                start = pl.multiple_of(relative // TILE * TILE, TILE)
                tile = table[s, pl.ds(start, TILE), :]
                table[s, pl.ds(start, TILE), :] = jnp.where(
                    in_tile == relative - start, new_ref[s : s + 1, :], tile
                )

        stores[c].start()
        for g in range(KEY_VALUE_HEADS):
            key = table[pl.ds(c * chunk, chunk), :, pl.ds(g * HEAD_SIZE, HEAD_SIZE)]
            wide = dot_t(queries[g], key.reshape(chunk * ctx, HEAD_SIZE))
            for s in range(chunk):
                part = wide[:, s * ctx : (s + 1) * ctx]
                scores[g] = jnp.where(row_slot == c * chunk + s, part, scores[g])
    visible = column <= limit
    columns = []
    for g in range(KEY_VALUE_HEADS):
        masked = jnp.where(visible, scores[g] * SCALE, MASKED)
        maxima = jnp.maximum(jnp.max(masked, axis=1, keepdims=True), FLOOR)
        weights = jnp.exp(masked - maxima)
        totals = jnp.sum(weights, axis=1, keepdims=True)
        summed = jnp.zeros((rows, HEAD_SIZE), F32)
        for c in range(CHUNKS):
            value = table[pl.ds(c * chunk, chunk), :, pl.ds(KW + g * HEAD_SIZE, HEAD_SIZE)]
            picked = [jnp.where(row_slot == c * chunk + s, weights, 0.0) for s in range(chunk)]
            picked = jnp.concatenate(picked, axis=1).astype(BF16)
            summed += dot(picked, value.reshape(chunk * ctx, HEAD_SIZE))
        seen = totals > 0.0
        safe = jnp.where(seen, totals, 1.0)
        normed = (summed / safe).astype(BF16)
        logs = jnp.where(seen, maxima + jnp.log(safe), MASKED)
        for h in range(GROUP):
            part = slice(h * slots, (h + 1) * slots)
            part_ref[pl.ds(g * slots, slots), pl.ds(h * HEAD_SIZE, HEAD_SIZE)] = normed[part]
            columns.append(logs[part])
    put_stats(part_ref, columns, slots)
    for copy in stores:
        copy.wait()


def decode_partials(lengths, dealing, queries, new_rows, cache, pre_queries, req):
    slots, ctx, width = cache.shape
    inputs = (lengths, dealing, queries, new_rows, cache, pre_queries)
    return pl.pallas_call(
        decode_kernel,
        in_specs=[HBM] * len(inputs),
        out_specs=[HBM, VMEM, VMEM, VMEM],
        out_shape=[
            pltpu.HBM(cache.shape, BF16),
            pltpu.VMEM((PART_ROWS * slots, KVW), BF16),
            pltpu.VMEM(pre_queries.shape[1:], BF16),
            pltpu.VMEM((req, slots + 8, HEAD_SIZE), F32),
        ],
        scratch_shapes=[
            pltpu.SMEM(lengths.shape, jnp.int32),
            pltpu.SMEM(dealing.shape, jnp.int32),
            pltpu.VMEM(queries.shape, BF16),
            pltpu.VMEM(new_rows.shape, BF16),
            pltpu.VMEM(cache.shape, BF16),
            pltpu.SemaphoreType.DMA((5 + 2 * CHUNKS,)),
        ],
        compiler_params=pltpu.CompilerParams(vmem_limit_bytes=16 << 20),
        cost_estimate=pl.CostEstimate(
            flops=4 * slots * ctx * QW, bytes_accessed=2 * cache.size * 2, transcendentals=slots * ctx * 8
        ),
        name="decode_partials",
    )(*[pltpu.with_memory_space_constraint(x, pltpu.HBM) for x in inputs])


def put_stats(ref, columns, slots):
    last = pl.ds(KEY_VALUE_HEADS * slots, slots)
    ref[last, pl.ds(0, STATS)] = stats_block(columns, slots)
    ref[last, pl.ds(STATS, KVW - STATS)] = jnp.zeros((slots, KVW - STATS), BF16)


def decode_part(ref, slots):
    blocks = [ref[pl.ds(g * slots, slots), :] for g in range(KEY_VALUE_HEADS)]
    return jnp.concatenate(blocks + [ref[pl.ds(KEY_VALUE_HEADS * slots, slots), pl.ds(0, STATS)]], axis=1)


def step_kernel(slots, appends, own_ref, other_ref, *refs):
    joined, logs = join([decode_part(own_ref, slots), decode_part(other_ref, slots)])
    head = PART_ROWS * slots
    rest = own_ref.shape[0] - head
    out_ref = refs[1] if appends else refs[0]
    for g in range(KEY_VALUE_HEADS):
        out_ref[pl.ds(g * slots, slots), :] = joined[:, g * KVW : (g + 1) * KVW]
    put_stats(out_ref, [logs[:, h * HEAD_SIZE : h * HEAD_SIZE + 1] for h in range(QUERY_HEADS)], slots)
    if appends:
        out_ref[pl.ds(head, refs[0].shape[0]), :] = refs[0][...]
    if rest:
        refs[1][pl.ds(0, rest), :] = own_ref[pl.ds(head, rest), :]
        refs[1][pl.ds(rest, rest), :] = other_ref[pl.ds(head, rest), :]


def join_step(own, other, slots, shapes, name, *extra):
    return pl.pallas_call(
        functools.partial(step_kernel, slots, bool(extra)),
        in_specs=[VMEM] * (2 + len(extra)),
        out_specs=[VMEM] * len(shapes),
        out_shape=[pltpu.VMEM((rows, KVW), BF16) for rows in shapes],
        compiler_params=pltpu.CompilerParams(vmem_limit_bytes=16 << 20),
        name=name,
    )(own, other, *extra)


def prefill_kernel(sets, ctx, off_ref, *refs):
    query_count = len(sets)
    packs, tables, outs = refs[:query_count], refs[query_count:-query_count], refs[-query_count:]
    tokens = packs[0].shape[0]
    span = ctx + tokens
    me = lax.axis_index(BLK)
    offset = off_ref[:1, :1]
    pieces = []
    for k in range(KEY_SET):
        holder = me ^ k
        index = lax.broadcasted_iota(jnp.int32, (1, span), 1)
        old = jnp.where(holder * ctx + index < offset, -1, 1 << 30)
        pieces.append(jnp.where(index < ctx, old, holder * tokens + index - ctx))
    key_mark = jnp.concatenate(pieces, axis=1)
    in_block = lax.broadcasted_iota(jnp.int32, (GROUP * tokens, 1), 0) % tokens
    lane = lax.broadcasted_iota(jnp.int32, (tokens, STATS), 1)
    stats = [jnp.zeros((tokens, STATS), F32) for _ in range(query_count)]
    for g in range(KEY_VALUE_HEADS):
        keys = jnp.concatenate([t[:, pl.ds(g * HEAD_SIZE, HEAD_SIZE)] for t in tables], axis=0)
        values = jnp.concatenate([t[:, pl.ds(KW + g * HEAD_SIZE, HEAD_SIZE)] for t in tables], axis=0)
        for k in range(query_count):
            token = (me ^ (sets[k] * KEY_SET)) * tokens + in_block
            query = jnp.concatenate(
                [packs[k][:, pl.ds((g * GROUP + h) * HEAD_SIZE, HEAD_SIZE)] for h in range(GROUP)], axis=0
            )
            scores = jnp.where(key_mark <= token, dot_t(query, keys) * SCALE, MASKED)
            maxima = jnp.maximum(jnp.max(scores, axis=1, keepdims=True), FLOOR)
            weights = jnp.exp(scores - maxima)
            totals = jnp.sum(weights, axis=1, keepdims=True)
            summed = dot(weights.astype(BF16), values)
            seen = totals > 0.0
            safe = jnp.where(seen, totals, 1.0)
            normed = (summed / safe).astype(BF16)
            logs = jnp.where(seen, maxima + jnp.log(safe), MASKED)
            for h in range(GROUP):
                part = slice(h * tokens, (h + 1) * tokens)
                outs[k][:, pl.ds((g * GROUP + h) * HEAD_SIZE, HEAD_SIZE)] = normed[part]
                for term, value in enumerate(split3(logs[part])):
                    stats[k] = jnp.where(lane == term * QUERY_HEADS + g * GROUP + h, value, stats[k])
    for k in range(query_count):
        outs[k][:, pl.ds(QW, STATS)] = stats[k].astype(BF16)


def prefill_partials(offset, packs, tables, ctx, sets):
    tokens = packs[0].shape[0]
    pairs = len(packs) * tokens * KEY_SET * (ctx + tokens)
    return pl.pallas_call(
        functools.partial(prefill_kernel, sets, ctx),
        in_specs=[VMEM] * (1 + len(packs) + len(tables)),
        out_specs=[VMEM] * len(packs),
        out_shape=[jax.ShapeDtypeStruct((tokens, QW + STATS), BF16)] * len(packs),
        compiler_params=pltpu.CompilerParams(vmem_limit_bytes=32 << 20),
        cost_estimate=pl.CostEstimate(
            flops=4 * pairs * QW, bytes_accessed=4 << 20, transcendentals=pairs * QUERY_HEADS
        ),
        name="prefill_partials",
    )(offset, *packs, *tables)


def join_kernel(count, slots, *refs):
    out_ref, tokens = refs[-1], refs[0].shape[0]
    out_ref[pl.ds(0, tokens), :] = join([ref[...] for ref in refs[:count]])[0]
    out_ref[pl.ds(tokens, slots), :] = join([decode_part(ref, slots) for ref in refs[count:-1]])[0]


def join_parts(parts, decodes, slots):
    return pl.pallas_call(
        functools.partial(join_kernel, len(parts), slots),
        in_specs=[VMEM] * (len(parts) + len(decodes)),
        out_specs=VMEM,
        out_shape=jax.ShapeDtypeStruct((parts[0].shape[0] + slots, QW), BF16),
        compiler_params=pltpu.CompilerParams(vmem_limit_bytes=16 << 20),
        name="join_parts",
    )(*parts, *decodes)


def update_kernel(tokens, sets, off_ref, cache_hbm, near_ref, beside_ref, *refs):
    tables, (out_ref, cache_ref, sem) = refs[:KEY_SET], refs[-3:]
    load = pltpu.make_async_copy(cache_hbm.at[0], cache_ref, sem)
    load.start()
    ctx = cache_ref.shape[0]
    me = lax.axis_index(BLK)
    rows = [t[pl.ds(ctx, tokens), :] for t in tables]
    rows = jnp.concatenate(rows + [near_ref[...], beside_ref[...]], axis=0)
    count = rows.shape[0]
    index = lax.broadcasted_iota(jnp.int32, (1, count), 1)
    block = index // tokens
    half = sets * KEY_SET // 2
    far = block - KEY_SET
    inner = far % half
    distance = KEY_SET * (1 + inner % sets) + 2 * (inner // sets) + far // half
    token = (me ^ jnp.where(block < KEY_SET, block, distance)) * tokens + index % tokens
    wanted = me * ctx + lax.broadcasted_iota(jnp.int32, (ctx, 1), 0) - off_ref[:1, :1]
    picked = dot(jnp.where(wanted == token, 1.0, 0.0).astype(BF16), rows).astype(BF16)
    inside = jnp.broadcast_to((wanted >= 0) & (wanted < count), cache_ref.shape)
    load.wait()
    out_ref[0] = jnp.where(inside, picked, cache_ref[...])


def update_cache(offset, cache, near, beside, tables, tokens, sets):
    return pl.pallas_call(
        functools.partial(update_kernel, tokens, sets),
        in_specs=[VMEM, HBM] + [VMEM] * (2 + len(tables)),
        out_specs=VMEM,
        out_shape=jax.ShapeDtypeStruct(cache.shape, BF16),
        scratch_shapes=[pltpu.VMEM(cache.shape[1:], BF16), pltpu.SemaphoreType.DMA],
        compiler_params=pltpu.CompilerParams(vmem_limit_bytes=16 << 20),
        name="update_cache",
    )(offset, pltpu.with_memory_space_constraint(cache, pltpu.HBM), near, beside, *tables)


def route_kernel(count, route_ref, *refs):
    held, (pre_ref, dec_ref) = refs[:-2], refs[-2:]
    if len(held) < count:
        held = [held[0].at[j] for j in range(count)]
    tokens, slots = pre_ref.shape[1], dec_ref.shape[0]
    prefill = jnp.zeros(pre_ref.shape[1:], F32)
    decode = jnp.zeros(dec_ref.shape, F32)
    for j in range(count):
        flag = route_ref[j, pl.ds(slots, 1), pl.ds(0, 1)]
        prefill += flag * held[j][pl.ds(0, tokens), :].astype(F32)
        chosen = route_ref[j, pl.ds(0, slots), pl.ds(0, slots)].astype(BF16)
        decode += dot(chosen, held[j][pl.ds(tokens, slots), :])
    pre_ref[0] = prefill.astype(BF16)
    dec_ref[...] = decode.astype(BF16)


def route_outputs(route, held, tokens, slots):
    return pl.pallas_call(
        functools.partial(route_kernel, route.shape[0]),
        in_specs=[VMEM] * (1 + len(held)),
        out_specs=[VMEM] * 2,
        out_shape=[
            jax.ShapeDtypeStruct((1, tokens, QW), BF16),
            jax.ShapeDtypeStruct((slots, QW), BF16),
        ],
        compiler_params=pltpu.CompilerParams(vmem_limit_bytes=16 << 20),
        name="route_outputs",
    )(route, *held)


def per_device(
    prefill_queries,
    decode_queries,
    new_prefill,
    new_decode,
    prefill_cache,
    decode_cache,
    prefill_offsets,
    decode_lengths,
    dealing,
):
    blk = lax.axis_size(BLK)
    req = lax.axis_size("req")
    ctx = prefill_cache.shape[1]
    tokens = prefill_queries.shape[1]
    slots = decode_cache.shape[0]

    def swap(array, distance):
        return lax.ppermute(array, BLK, [(i, i ^ distance) for i in range(blk)])

    def after(array, *marks):
        return lax.optimization_barrier((array, *marks))[0]

    others = range(KEY_SET, blk, KEY_SET)
    table = jnp.concatenate([prefill_cache[0], new_prefill[0]], axis=0)
    lanes = [table] + [swap(table, k) for k in range(2, KEY_SET, 2)]
    packs = [swap(prefill_queries[0], k) for k in others]
    far = jnp.concatenate([swap(new_prefill[0], k) for k in others], axis=0)

    decode_cache_out, part, queries, route = decode_partials(
        decode_lengths, dealing, decode_queries, new_decode, decode_cache, prefill_queries, req
    )
    head, rest = PART_ROWS * slots, far.shape[0]
    beside = swap(part, 1)
    offset = jnp.full((8, HEAD_SIZE), prefill_offsets[0], jnp.int32)
    lanes[1], offset, _ = lax.optimization_barrier((lanes[1], offset, part))
    lanes[2], beside, far, _ = lax.optimization_barrier((lanes[2], beside, far, lanes[1]))
    (part,) = join_step(part, beside, slots, [head], "join_core")
    far_across = swap(far, 2)
    across = swap(part, 2)
    lanes[3], packs, across, _ = lax.optimization_barrier((lanes[3], packs, across, lanes[2]))
    tables = [t for lane in lanes for t in (lane, swap(lane, 1))]

    far = jnp.concatenate([far, far_across], axis=0)
    (part,) = join_step(part, across, slots, [head + 2 * rest], "join_x", far)
    packs, _ = lax.optimization_barrier((packs, part))
    sent = prefill_partials(offset, packs, tables, ctx, [k // KEY_SET for k in others])
    queries = after(queries, sent[0])
    kept = prefill_partials(offset, [queries], tables, ctx, [0])
    part, news = join_step(part, after(swap(part, 4), kept[0]), slots, [head, 4 * rest], "join_z")
    attended = join_parts(
        [*kept] + [swap(p, k) for k, p in zip(others, sent)],
        [part] + [swap(part, k) for k in others],
        slots,
    )
    prefill_cache_out = update_cache(offset, prefill_cache, news, swap(news, 1), tables, tokens, len(others))

    if req == 2:
        held = [attended, lax.ppermute(attended, "req", [(0, 1), (1, 0)])]
    else:
        held = [lax.all_gather(attended, "req", axis=0)]
    held[-1], prefill_cache_out = lax.optimization_barrier((held[-1], prefill_cache_out))
    prefill_out, decode_out = route_outputs(route, held, tokens, slots)
    return (prefill_out, decode_out, prefill_cache_out, decode_cache_out)


def solution(mesh):
    blk, req = mesh.shape["blk"], mesh.shape["req"]
    mesh = jax.sharding.Mesh(mesh.devices.reshape(blk // QUAD, QUAD, req), ("hi", "quad", "req"))
    in_specs = (
        P("req", BLK, None),
        P("req", None),
        P("req", BLK, None),
        P("req", None),
        P("req", BLK, None),
        P("req", BLK, None),
        P("req"),
        P("req"),
        P(),
    )
    out_specs = (
        P("req", BLK, None),
        P("req", None),
        P("req", BLK, None),
        P("req", BLK, None),
    )
    return jax.shard_map(
        per_device, mesh=mesh, in_specs=in_specs, out_specs=out_specs, check_vma=False
    )
```

```python
import functools

import jax
import jax.numpy as jnp
from jax import lax
from jax.experimental import pallas as pl
from jax.experimental.pallas import tpu as pltpu
from jax.sharding import PartitionSpec as P

QUERY_HEADS = 8
KEY_VALUE_HEADS = 2
HEAD_SIZE = 128
GROUP = QUERY_HEADS // KEY_VALUE_HEADS
QW = QUERY_HEADS * HEAD_SIZE
KW = KEY_VALUE_HEADS * HEAD_SIZE
STATS = 128
QUAD = 4
KEY_SET = 8
SCALE = HEAD_SIZE**-0.5
MASKED = -1e30
FLOOR = -1e20
F32 = jnp.float32
BF16 = jnp.bfloat16

KVW = 2 * KW
BLK = ("hi", "quad")
CHUNKS = 4
TILE = 16

HBM = pl.BlockSpec(memory_space=pltpu.HBM)
VMEM = pl.BlockSpec(memory_space=pltpu.VMEM)


def dot_t(a, b):
    return lax.dot_general(a, b, (((1,), (1,)), ((), ())), preferred_element_type=F32)


def dot(a, b):
    return lax.dot_general(a, b, (((1,), (0,)), ((), ())), preferred_element_type=F32)


def split3(value):
    high = value.astype(BF16).astype(F32)
    rest = value - high
    middle = rest.astype(BF16).astype(F32)
    return high, middle, rest - middle


def stats_block(columns, rows):
    lane = lax.broadcasted_iota(jnp.int32, (rows, STATS), 1)
    count = len(columns)
    out = jnp.zeros((rows, STATS), F32)
    for head, column in enumerate(columns):
        for term, part in enumerate(split3(column)):
            out = jnp.where(lane == term * count + head, part, out)
    return out.astype(BF16)


def spread_matrix(heads):
    lane = lax.broadcasted_iota(jnp.int32, (STATS, heads * HEAD_SIZE), 0)
    head = lax.broadcasted_iota(jnp.int32, (STATS, heads * HEAD_SIZE), 1) // HEAD_SIZE
    hit = (lane == head) | (lane == head + heads) | (lane == head + 2 * heads)
    return jnp.where(hit, 1.0, 0.0).astype(BF16)


def join(parts):
    spread = spread_matrix(QUERY_HEADS)
    logs = [dot(part[:, QW:], spread) for part in parts]
    top = functools.reduce(jnp.maximum, logs)
    scales = [jnp.exp(log - top) for log in logs]
    total = functools.reduce(jnp.add, scales)
    summed = functools.reduce(
        jnp.add, [scale * part[:, :QW].astype(F32) for scale, part in zip(scales, parts)]
    )
    return (summed / total).astype(BF16), top + jnp.log(total)


def source_group(j):
    return lax.axis_index("req") ^ j if lax.axis_size("req") == 2 else j


def decode_kernel(
    len_hbm,
    deal_hbm,
    q_hbm,
    new_hbm,
    cache_hbm,
    pre_q_hbm,
    pre_new_hbm,
    pre_cache_hbm,
    table,
    shared_ref,
    pre_q_ref,
    route_ref,
    lens,
    deal,
    query_ref,
    new_ref,
    sems,
):
    slots, ctx, _ = table.shape
    rows = GROUP * slots
    chunk = slots // CHUNKS
    base = lax.axis_index(BLK) * ctx
    tokens = pre_new_hbm.shape[1]
    first = ctx + tokens
    small = [
        (len_hbm, lens),
        (deal_hbm, deal),
        (q_hbm, query_ref),
        (new_hbm, new_ref),
        (pre_q_hbm.at[0], pre_q_ref),
        (pre_cache_hbm.at[0], shared_ref.at[pl.ds(0, ctx), :]),
        (pre_new_hbm.at[0], shared_ref.at[pl.ds(ctx, tokens), :]),
    ]
    small = [pltpu.make_async_copy(a, b, sems.at[i]) for i, (a, b) in enumerate(small)]
    loads = []
    for c in range(CHUNKS):
        part = pl.ds(c * chunk, chunk)
        loads.append(pltpu.make_async_copy(cache_hbm.at[part], table.at[part], sems.at[7 + c]))
    for copy in small + loads:
        copy.start()
    for copy in small:
        copy.wait()
    group = lax.axis_index("req")
    req = route_ref.shape[0]
    out_row = lax.broadcasted_iota(jnp.int32, (slots, HEAD_SIZE), 0)
    out_lane = lax.broadcasted_iota(jnp.int32, (slots, HEAD_SIZE), 1)
    for j in range(req):
        source = source_group(j)
        chosen = jnp.zeros((slots, HEAD_SIZE), F32)
        for s in range(slots):
            place = deal[req + source * slots + s] - group * slots
            chosen = jnp.where((out_lane == s) & (out_row == place), 1.0, chosen)
        route_ref[j, pl.ds(0, slots), :] = chosen
        mine = (deal[source] == group).astype(F32)
        route_ref[j, pl.ds(slots, 8), :] = jnp.full((8, HEAD_SIZE), mine, F32)
    row_slot = lax.broadcasted_iota(jnp.int32, (rows, ctx), 0) % slots
    column = lax.broadcasted_iota(jnp.int32, (rows, ctx), 1)
    in_tile = lax.broadcasted_iota(jnp.int32, (TILE, KVW), 0)
    limit = jnp.full((rows, ctx), -1, jnp.int32)
    queries = [
        jnp.concatenate(
            [query_ref[:, pl.ds((g * GROUP + h) * HEAD_SIZE, HEAD_SIZE)] for h in range(GROUP)], axis=0
        )
        for g in range(KEY_VALUE_HEADS)
    ]
    scores = [jnp.zeros((rows, ctx), F32) for _ in range(KEY_VALUE_HEADS)]
    for c in range(CHUNKS):
        loads[c].wait()
        for s in range(c * chunk, (c + 1) * chunk):
            relative = lens[s] - base
            limit = jnp.where(row_slot == s, relative, limit)

            @pl.when((relative >= 0) & (relative < ctx))
            def _():
                start = pl.multiple_of(relative // TILE * TILE, TILE)
                tile = table[s, pl.ds(start, TILE), :]
                table[s, pl.ds(start, TILE), :] = jnp.where(
                    in_tile == relative - start, new_ref[s : s + 1, :], tile
                )

        for g in range(KEY_VALUE_HEADS):
            key = table[pl.ds(c * chunk, chunk), :, pl.ds(g * HEAD_SIZE, HEAD_SIZE)]
            wide = dot_t(queries[g], key.reshape(chunk * ctx, HEAD_SIZE))
            for s in range(chunk):
                part = wide[:, s * ctx : (s + 1) * ctx]
                scores[g] = jnp.where(row_slot == c * chunk + s, part, scores[g])
    visible = column <= limit
    columns = []
    for g in range(KEY_VALUE_HEADS):
        masked = jnp.where(visible, scores[g] * SCALE, MASKED)
        maxima = jnp.maximum(jnp.max(masked, axis=1, keepdims=True), FLOOR)
        weights = jnp.exp(masked - maxima)
        totals = jnp.sum(weights, axis=1, keepdims=True)
        summed = jnp.zeros((rows, HEAD_SIZE), F32)
        for c in range(CHUNKS):
            value = table[pl.ds(c * chunk, chunk), :, pl.ds(KW + g * HEAD_SIZE, HEAD_SIZE)]
            picked = [jnp.where(row_slot == c * chunk + s, weights, 0.0) for s in range(chunk)]
            picked = jnp.concatenate(picked, axis=1).astype(BF16)
            summed += dot(picked, value.reshape(chunk * ctx, HEAD_SIZE))
        seen = totals > 0.0
        safe = jnp.where(seen, totals, 1.0)
        normed = (summed / safe).astype(BF16)
        logs = jnp.where(seen, maxima + jnp.log(safe), MASKED)
        for h in range(GROUP):
            part = slice(h * slots, (h + 1) * slots)
            shared_ref[pl.ds(first + g * slots, slots), pl.ds(h * HEAD_SIZE, HEAD_SIZE)] = normed[part]
            columns.append(logs[part])
    last = pl.ds(first + KEY_VALUE_HEADS * slots, slots)
    shared_ref[last, pl.ds(0, STATS)] = stats_block(columns, slots)
    shared_ref[last, pl.ds(STATS, KVW - STATS)] = jnp.zeros((slots, KVW - STATS), BF16)


def decode_partials(lengths, dealing, queries, new_rows, cache, pre_queries, pre_new, pre_cache, req):
    slots, ctx, width = cache.shape
    rows = ctx + pre_new.shape[1] + (KEY_VALUE_HEADS + 1) * slots
    inputs = (lengths, dealing, queries, new_rows, cache, pre_queries, pre_new, pre_cache)
    return pl.pallas_call(
        decode_kernel,
        in_specs=[HBM] * len(inputs),
        out_specs=[VMEM] * 4,
        out_shape=[
            pltpu.VMEM(cache.shape, BF16),
            pltpu.VMEM((rows, KVW), BF16),
            pltpu.VMEM(pre_queries.shape[1:], BF16),
            pltpu.VMEM((req, slots + 8, HEAD_SIZE), F32),
        ],
        scratch_shapes=[
            pltpu.SMEM(lengths.shape, jnp.int32),
            pltpu.SMEM(dealing.shape, jnp.int32),
            pltpu.VMEM(queries.shape, BF16),
            pltpu.VMEM(new_rows.shape, BF16),
            pltpu.SemaphoreType.DMA((7 + CHUNKS,)),
        ],
        compiler_params=pltpu.CompilerParams(vmem_limit_bytes=16 << 20),
        cost_estimate=pl.CostEstimate(
            flops=4 * slots * ctx * QW, bytes_accessed=2 * cache.size * 2, transcendentals=slots * ctx * 8
        ),
        name="decode_partials",
    )(*[pltpu.with_memory_space_constraint(x, pltpu.HBM) for x in inputs])


def store_kernel(cache_ref, out_hbm, sems):
    chunk = cache_ref.shape[0] // CHUNKS
    copies = []
    for c in range(CHUNKS):
        part = pl.ds(c * chunk, chunk)
        copies.append(pltpu.make_async_copy(cache_ref.at[part], out_hbm.at[part], sems.at[c]))
    for copy in copies:
        copy.start()
    for copy in copies:
        copy.wait()


def store_cache(cache):
    return pl.pallas_call(
        store_kernel,
        in_specs=[VMEM],
        out_specs=HBM,
        out_shape=pltpu.HBM(cache.shape, BF16),
        scratch_shapes=[pltpu.SemaphoreType.DMA((CHUNKS,))],
        compiler_params=pltpu.CompilerParams(vmem_limit_bytes=16 << 20),
        name="store_cache",
    )(pltpu.with_memory_space_constraint(cache, pltpu.VMEM))


def prefill_kernel(sets, ctx, slots, off_ref, *refs):
    query_count = len(sets)
    packs, tables, outs = refs[:query_count], refs[query_count:-query_count], refs[-query_count:]
    tokens = packs[0].shape[0]
    span = ctx + tokens
    me = lax.axis_index(BLK)
    offset = off_ref[:1, :1]
    pieces = []
    for k in range(KEY_SET):
        holder = me ^ k
        index = lax.broadcasted_iota(jnp.int32, (1, span), 1)
        old = jnp.where(holder * ctx + index < offset, -1, 1 << 30)
        pieces.append(jnp.where(index < ctx, old, holder * tokens + index - ctx))
    key_mark = jnp.concatenate(pieces, axis=1)
    in_block = lax.broadcasted_iota(jnp.int32, (GROUP * tokens, 1), 0) % tokens
    lane = lax.broadcasted_iota(jnp.int32, (tokens, STATS), 1)
    stats = [jnp.zeros((tokens, STATS), F32) for _ in range(query_count)]
    for g in range(KEY_VALUE_HEADS):
        keys = jnp.concatenate([t[pl.ds(0, span), pl.ds(g * HEAD_SIZE, HEAD_SIZE)] for t in tables], axis=0)
        values = jnp.concatenate([t[pl.ds(0, span), pl.ds(KW + g * HEAD_SIZE, HEAD_SIZE)] for t in tables], axis=0)
        for k in range(query_count):
            token = (me ^ (sets[k] * KEY_SET)) * tokens + in_block
            query = jnp.concatenate(
                [packs[k][:, pl.ds((g * GROUP + h) * HEAD_SIZE, HEAD_SIZE)] for h in range(GROUP)], axis=0
            )
            scores = jnp.where(key_mark <= token, dot_t(query, keys) * SCALE, MASKED)
            maxima = jnp.maximum(jnp.max(scores, axis=1, keepdims=True), FLOOR)
            weights = jnp.exp(scores - maxima)
            totals = jnp.sum(weights, axis=1, keepdims=True)
            summed = dot(weights.astype(BF16), values)
            seen = totals > 0.0
            safe = jnp.where(seen, totals, 1.0)
            normed = (summed / safe).astype(BF16)
            logs = jnp.where(seen, maxima + jnp.log(safe), MASKED)
            for h in range(GROUP):
                part = slice(h * tokens, (h + 1) * tokens)
                outs[k][pl.ds(0, tokens), pl.ds((g * GROUP + h) * HEAD_SIZE, HEAD_SIZE)] = normed[part]
                for term, value in enumerate(split3(logs[part])):
                    stats[k] = jnp.where(lane == term * QUERY_HEADS + g * GROUP + h, value, stats[k])
    for k in range(query_count):
        outs[k][pl.ds(0, tokens), pl.ds(QW, STATS)] = stats[k].astype(BF16)
    if outs[0].shape[0] == tokens:
        return
    decodes = [
        jnp.concatenate(
            [t[pl.ds(span + g * slots, slots), :] for g in range(KEY_VALUE_HEADS)]
            + [t[pl.ds(span + KEY_VALUE_HEADS * slots, slots), pl.ds(0, STATS)]],
            axis=1,
        )
        for t in tables
    ]
    joined, logs = join(decodes)
    joined_stats = stats_block([logs[:, h * HEAD_SIZE : h * HEAD_SIZE + 1] for h in range(QUERY_HEADS)], slots)
    for k in range(query_count):
        outs[k][pl.ds(tokens, slots), pl.ds(0, QW)] = joined
        outs[k][pl.ds(tokens, slots), pl.ds(QW, STATS)] = joined_stats


def prefill_partials(offset, packs, tables, ctx, slots, sets, with_decode):
    tokens = packs[0].shape[0]
    rows = tokens + slots if with_decode else tokens
    pairs = len(packs) * tokens * KEY_SET * (ctx + tokens)
    return pl.pallas_call(
        functools.partial(prefill_kernel, sets, ctx, slots),
        in_specs=[VMEM] * (1 + len(packs) + len(tables)),
        out_specs=[VMEM] * len(packs),
        out_shape=[pltpu.VMEM((rows, QW + STATS), BF16)] * len(packs),
        compiler_params=pltpu.CompilerParams(vmem_limit_bytes=32 << 20),
        cost_estimate=pl.CostEstimate(
            flops=4 * pairs * QW, bytes_accessed=4 << 20, transcendentals=pairs * QUERY_HEADS
        ),
        name="prefill_partials",
    )(offset, *packs, *tables)


def join_kernel(kept_ref, *refs):
    parts, out_ref = refs[:-1], refs[-1]
    tokens = kept_ref.shape[0]
    slots = out_ref.shape[0] - tokens
    out_ref[pl.ds(0, tokens), :] = join([kept_ref[...]] + [p[pl.ds(0, tokens), :] for p in parts[1:]])[0]
    out_ref[pl.ds(tokens, slots), :] = join([p[pl.ds(tokens, slots), :] for p in parts])[0]


def join_parts(kept, parts):
    return pl.pallas_call(
        join_kernel,
        in_specs=[VMEM] * (1 + len(parts)),
        out_specs=VMEM,
        out_shape=jax.ShapeDtypeStruct((parts[0].shape[0], QW), BF16),
        compiler_params=pltpu.CompilerParams(vmem_limit_bytes=16 << 20),
        name="join_parts",
    )(kept, *parts)


def update_kernel(tokens, sets, off_ref, cache_hbm, near_ref, beside_ref, *refs):
    tables, (out_ref, cache_ref, sem) = refs[:KEY_SET], refs[-3:]
    load = pltpu.make_async_copy(cache_hbm.at[0], cache_ref, sem)
    load.start()
    ctx = cache_ref.shape[0]
    me = lax.axis_index(BLK)
    rows = [t[pl.ds(ctx, tokens), :] for t in tables]
    rows = jnp.concatenate(rows + [near_ref[...], beside_ref[...]], axis=0)
    count = rows.shape[0]
    index = lax.broadcasted_iota(jnp.int32, (1, count), 1)
    block = index // tokens
    half = sets * KEY_SET // 2
    far = block - KEY_SET
    inner = far % half
    distance = KEY_SET * (1 + inner % sets) + 2 * (inner // sets) + far // half
    token = (me ^ jnp.where(block < KEY_SET, block, distance)) * tokens + index % tokens
    wanted = me * ctx + lax.broadcasted_iota(jnp.int32, (ctx, 1), 0) - off_ref[:1, :1]
    picked = dot(jnp.where(wanted == token, 1.0, 0.0).astype(BF16), rows).astype(BF16)
    inside = jnp.broadcast_to((wanted >= 0) & (wanted < count), cache_ref.shape)
    load.wait()
    out_ref[0] = jnp.where(inside, picked, cache_ref[...])


def update_cache(offset, cache, near, beside, tables, tokens, sets):
    return pl.pallas_call(
        functools.partial(update_kernel, tokens, sets),
        in_specs=[VMEM, HBM] + [VMEM] * (2 + len(tables)),
        out_specs=VMEM,
        out_shape=jax.ShapeDtypeStruct(cache.shape, BF16),
        scratch_shapes=[pltpu.VMEM(cache.shape[1:], BF16), pltpu.SemaphoreType.DMA],
        compiler_params=pltpu.CompilerParams(vmem_limit_bytes=16 << 20),
        name="update_cache",
    )(offset, pltpu.with_memory_space_constraint(cache, pltpu.HBM), near, beside, *tables)


def route_kernel(count, route_ref, *refs):
    held, (pre_ref, dec_ref) = refs[:-2], refs[-2:]
    if len(held) < count:
        held = [held[0].at[j] for j in range(count)]
    tokens, slots = pre_ref.shape[1], dec_ref.shape[0]
    prefill = jnp.zeros(pre_ref.shape[1:], F32)
    decode = jnp.zeros(dec_ref.shape, F32)
    for j in range(count):
        flag = route_ref[j, pl.ds(slots, 1), pl.ds(0, 1)]
        prefill += flag * held[j][pl.ds(0, tokens), :].astype(F32)
        chosen = route_ref[j, pl.ds(0, slots), pl.ds(0, slots)].astype(BF16)
        decode += dot(chosen, held[j][pl.ds(tokens, slots), :])
    pre_ref[0] = prefill.astype(BF16)
    dec_ref[...] = decode.astype(BF16)


def route_outputs(route, held, tokens, slots):
    return pl.pallas_call(
        functools.partial(route_kernel, route.shape[0]),
        in_specs=[VMEM] * (1 + len(held)),
        out_specs=[VMEM] * 2,
        out_shape=[
            jax.ShapeDtypeStruct((1, tokens, QW), BF16),
            jax.ShapeDtypeStruct((slots, QW), BF16),
        ],
        compiler_params=pltpu.CompilerParams(vmem_limit_bytes=16 << 20),
        name="route_outputs",
    )(route, *held)


def per_device(
    prefill_queries,
    decode_queries,
    new_prefill,
    new_decode,
    prefill_cache,
    decode_cache,
    prefill_offsets,
    decode_lengths,
    dealing,
):
    blk = lax.axis_size(BLK)
    req = lax.axis_size("req")
    ctx = prefill_cache.shape[1]
    tokens = prefill_queries.shape[1]
    slots = decode_cache.shape[0]

    def swap(array, distance):
        return lax.ppermute(array, BLK, [(i, i ^ distance) for i in range(blk)])

    def after(array, *marks):
        return lax.optimization_barrier((array, *marks))[0]

    others = range(KEY_SET, blk, KEY_SET)
    packs = [swap(prefill_queries[0], k) for k in others]
    far = jnp.concatenate([swap(new_prefill[0], k) for k in others], axis=0)
    decode_cache_out, table, queries, route = decode_partials(
        decode_lengths,
        dealing,
        decode_queries,
        new_decode,
        decode_cache,
        prefill_queries,
        new_prefill,
        prefill_cache,
        req,
    )
    lanes = [table] + [swap(table, k) for k in range(2, KEY_SET, 2)]
    offset = jnp.full((8, HEAD_SIZE), prefill_offsets[0], jnp.int32)
    decode_cache_out = store_cache(decode_cache_out)
    lanes[1], offset, far, _ = lax.optimization_barrier((lanes[1], offset, far, decode_cache_out))
    lanes[2] = after(lanes[2], lanes[1])
    far_across = swap(far, 2)
    lanes[3], packs, far_across, _ = lax.optimization_barrier((lanes[3], packs, far_across, lanes[2]))
    tables = [t for lane in lanes for t in (lane, swap(lane, 1))]

    sent = prefill_partials(offset, packs, tables, ctx, slots, [k // KEY_SET for k in others], True)
    queries = after(queries, sent[0])
    (kept,) = prefill_partials(offset, [queries], tables, ctx, slots, [0], False)
    attended = join_parts(kept, [sent[0]] + [swap(p, k) for k, p in zip(others, sent)])

    far = jnp.concatenate([far, far_across], axis=0)
    far = after(far, sent[0])
    far = jnp.concatenate([far, after(swap(far, 4), kept)], axis=0)
    prefill_cache_out = update_cache(
        offset, prefill_cache, far, swap(far, 1), tables, tokens, len(others)
    )

    if req == 2:
        held = [attended, lax.ppermute(attended, "req", [(0, 1), (1, 0)])]
    else:
        held = [lax.all_gather(attended, "req", axis=0)]
    held[-1], prefill_cache_out = lax.optimization_barrier((held[-1], prefill_cache_out))
    prefill_out, decode_out = route_outputs(route, held, tokens, slots)
    return (prefill_out, decode_out, prefill_cache_out, decode_cache_out)


def solution(mesh):
    blk, req = mesh.shape["blk"], mesh.shape["req"]
    mesh = jax.sharding.Mesh(mesh.devices.reshape(blk // QUAD, QUAD, req), ("hi", "quad", "req"))
    in_specs = (
        P("req", BLK, None),
        P("req", None),
        P("req", BLK, None),
        P("req", None),
        P("req", BLK, None),
        P("req", BLK, None),
        P("req"),
        P("req"),
        P(),
    )
    out_specs = (
        P("req", BLK, None),
        P("req", None),
        P("req", BLK, None),
        P("req", BLK, None),
    )
    return jax.shard_map(
        per_device, mesh=mesh, in_specs=in_specs, out_specs=out_specs, check_vma=False
    )
```

```python
import functools

import jax
import jax.numpy as jnp
from jax import lax
from jax.experimental import pallas as pl
from jax.experimental.pallas import tpu as pltpu
from jax.sharding import PartitionSpec as P

QUERY_HEADS = 8
KEY_VALUE_HEADS = 2
HEAD_SIZE = 128
GROUP = QUERY_HEADS // KEY_VALUE_HEADS
QW = QUERY_HEADS * HEAD_SIZE
KW = KEY_VALUE_HEADS * HEAD_SIZE
STATS = 128
QUAD = 4
KEY_SET = 8
PART_ROWS = KEY_VALUE_HEADS + 1
SCALE = HEAD_SIZE**-0.5
MASKED = -1e30
FLOOR = -1e20
F32 = jnp.float32
BF16 = jnp.bfloat16

KVW = 2 * KW
BLK = ("hi", "quad")
CHUNKS = 4
TILE = 16

HBM = pl.BlockSpec(memory_space=pltpu.HBM)
VMEM = pl.BlockSpec(memory_space=pltpu.VMEM)


def dot_t(a, b):
    return lax.dot_general(a, b, (((1,), (1,)), ((), ())), preferred_element_type=F32)


def dot(a, b):
    return lax.dot_general(a, b, (((1,), (0,)), ((), ())), preferred_element_type=F32)


def split3(value):
    high = value.astype(BF16).astype(F32)
    rest = value - high
    middle = rest.astype(BF16).astype(F32)
    return high, middle, rest - middle


def stats_block(columns, rows):
    lane = lax.broadcasted_iota(jnp.int32, (rows, STATS), 1)
    count = len(columns)
    out = jnp.zeros((rows, STATS), F32)
    for head, column in enumerate(columns):
        for term, part in enumerate(split3(column)):
            out = jnp.where(lane == term * count + head, part, out)
    return out.astype(BF16)


def spread_matrix(heads):
    lane = lax.broadcasted_iota(jnp.int32, (STATS, heads * HEAD_SIZE), 0)
    head = lax.broadcasted_iota(jnp.int32, (STATS, heads * HEAD_SIZE), 1) // HEAD_SIZE
    hit = (lane == head) | (lane == head + heads) | (lane == head + 2 * heads)
    return jnp.where(hit, 1.0, 0.0).astype(BF16)


def join(parts):
    spread = spread_matrix(QUERY_HEADS)
    logs = [dot(part[:, QW:], spread) for part in parts]
    top = functools.reduce(jnp.maximum, logs)
    scales = [jnp.exp(log - top) for log in logs]
    total = functools.reduce(jnp.add, scales)
    summed = functools.reduce(
        jnp.add, [scale * part[:, :QW].astype(F32) for scale, part in zip(scales, parts)]
    )
    return (summed / total).astype(BF16), top + jnp.log(total)


def source_group(j):
    return lax.axis_index("req") ^ j if lax.axis_size("req") == 2 else j


def decode_kernel(
    len_hbm,
    deal_hbm,
    q_hbm,
    new_hbm,
    cache_hbm,
    pre_q_hbm,
    pre_new_hbm,
    out_hbm,
    part_ref,
    pre_q_ref,
    route_ref,
    lens,
    deal,
    query_ref,
    new_ref,
    table,
    sems,
):
    slots, ctx, _ = table.shape
    rows = GROUP * slots
    chunk = slots // CHUNKS
    base = lax.axis_index(BLK) * ctx
    small = [
        (len_hbm, lens),
        (deal_hbm, deal),
        (q_hbm, query_ref),
        (new_hbm, new_ref),
        (pre_q_hbm.at[0], pre_q_ref),
        (pre_new_hbm.at[0], part_ref.at[pl.ds(PART_ROWS * slots, pre_new_hbm.shape[1]), :]),
    ]
    small = [pltpu.make_async_copy(a, b, sems.at[i]) for i, (a, b) in enumerate(small)]
    loads, stores = [], []
    for c in range(CHUNKS):
        part = pl.ds(c * chunk, chunk)
        loads.append(pltpu.make_async_copy(cache_hbm.at[part], table.at[part], sems.at[6 + c]))
        stores.append(pltpu.make_async_copy(table.at[part], out_hbm.at[part], sems.at[6 + CHUNKS + c]))
    for copy in small + loads:
        copy.start()
    for copy in small:
        copy.wait()
    group = lax.axis_index("req")
    req = route_ref.shape[0]
    out_row = lax.broadcasted_iota(jnp.int32, (slots, HEAD_SIZE), 0)
    out_lane = lax.broadcasted_iota(jnp.int32, (slots, HEAD_SIZE), 1)
    for j in range(req):
        source = source_group(j)
        chosen = jnp.zeros((slots, HEAD_SIZE), F32)
        for s in range(slots):
            place = deal[req + source * slots + s] - group * slots
            chosen = jnp.where((out_lane == s) & (out_row == place), 1.0, chosen)
        route_ref[j, pl.ds(0, slots), :] = chosen
        mine = (deal[source] == group).astype(F32)
        route_ref[j, pl.ds(slots, 8), :] = jnp.full((8, HEAD_SIZE), mine, F32)
    row_slot = lax.broadcasted_iota(jnp.int32, (rows, ctx), 0) % slots
    column = lax.broadcasted_iota(jnp.int32, (rows, ctx), 1)
    in_tile = lax.broadcasted_iota(jnp.int32, (TILE, KVW), 0)
    limit = jnp.full((rows, ctx), -1, jnp.int32)
    queries = [
        jnp.concatenate(
            [query_ref[:, pl.ds((g * GROUP + h) * HEAD_SIZE, HEAD_SIZE)] for h in range(GROUP)], axis=0
        )
        for g in range(KEY_VALUE_HEADS)
    ]
    scores = [jnp.zeros((rows, ctx), F32) for _ in range(KEY_VALUE_HEADS)]
    for c in range(CHUNKS):
        loads[c].wait()
        for s in range(c * chunk, (c + 1) * chunk):
            relative = lens[s] - base
            limit = jnp.where(row_slot == s, relative, limit)

            @pl.when((relative >= 0) & (relative < ctx))
            def _():
                start = pl.multiple_of(relative // TILE * TILE, TILE)
                tile = table[s, pl.ds(start, TILE), :]
                table[s, pl.ds(start, TILE), :] = jnp.where(
                    in_tile == relative - start, new_ref[s : s + 1, :], tile
                )

        stores[c].start()
        for g in range(KEY_VALUE_HEADS):
            key = table[pl.ds(c * chunk, chunk), :, pl.ds(g * HEAD_SIZE, HEAD_SIZE)]
            wide = dot_t(queries[g], key.reshape(chunk * ctx, HEAD_SIZE))
            for s in range(chunk):
                part = wide[:, s * ctx : (s + 1) * ctx]
                scores[g] = jnp.where(row_slot == c * chunk + s, part, scores[g])
    visible = column <= limit
    columns = []
    for g in range(KEY_VALUE_HEADS):
        masked = jnp.where(visible, scores[g] * SCALE, MASKED)
        maxima = jnp.maximum(jnp.max(masked, axis=1, keepdims=True), FLOOR)
        weights = jnp.exp(masked - maxima)
        totals = jnp.sum(weights, axis=1, keepdims=True)
        summed = jnp.zeros((rows, HEAD_SIZE), F32)
        for c in range(CHUNKS):
            value = table[pl.ds(c * chunk, chunk), :, pl.ds(KW + g * HEAD_SIZE, HEAD_SIZE)]
            picked = [jnp.where(row_slot == c * chunk + s, weights, 0.0) for s in range(chunk)]
            picked = jnp.concatenate(picked, axis=1).astype(BF16)
            summed += dot(picked, value.reshape(chunk * ctx, HEAD_SIZE))
        seen = totals > 0.0
        safe = jnp.where(seen, totals, 1.0)
        normed = (summed / safe).astype(BF16)
        logs = jnp.where(seen, maxima + jnp.log(safe), MASKED)
        for h in range(GROUP):
            part = slice(h * slots, (h + 1) * slots)
            part_ref[pl.ds(g * slots, slots), pl.ds(h * HEAD_SIZE, HEAD_SIZE)] = normed[part]
            columns.append(logs[part])
    put_stats(part_ref, columns, slots)
    for copy in stores:
        copy.wait()


def decode_partials(lengths, dealing, queries, new_rows, cache, pre_queries, pre_new, req):
    slots, ctx, width = cache.shape
    inputs = (lengths, dealing, queries, new_rows, cache, pre_queries, pre_new)
    return pl.pallas_call(
        decode_kernel,
        in_specs=[HBM] * len(inputs),
        out_specs=[HBM, VMEM, VMEM, VMEM],
        out_shape=[
            pltpu.HBM(cache.shape, BF16),
            pltpu.VMEM((PART_ROWS * slots + pre_new.shape[1], KVW), BF16),
            pltpu.VMEM(pre_queries.shape[1:], BF16),
            pltpu.VMEM((req, slots + 8, HEAD_SIZE), F32),
        ],
        scratch_shapes=[
            pltpu.SMEM(lengths.shape, jnp.int32),
            pltpu.SMEM(dealing.shape, jnp.int32),
            pltpu.VMEM(queries.shape, BF16),
            pltpu.VMEM(new_rows.shape, BF16),
            pltpu.VMEM(cache.shape, BF16),
            pltpu.SemaphoreType.DMA((6 + 2 * CHUNKS,)),
        ],
        compiler_params=pltpu.CompilerParams(vmem_limit_bytes=16 << 20),
        cost_estimate=pl.CostEstimate(
            flops=4 * slots * ctx * QW, bytes_accessed=2 * cache.size * 2, transcendentals=slots * ctx * 8
        ),
        name="decode_partials",
    )(*[pltpu.with_memory_space_constraint(x, pltpu.HBM) for x in inputs])


def put_stats(ref, columns, slots):
    last = pl.ds(KEY_VALUE_HEADS * slots, slots)
    ref[last, pl.ds(0, STATS)] = stats_block(columns, slots)
    ref[last, pl.ds(STATS, KVW - STATS)] = jnp.zeros((slots, KVW - STATS), BF16)


def decode_part(ref, slots):
    blocks = [ref[pl.ds(g * slots, slots), :] for g in range(KEY_VALUE_HEADS)]
    return jnp.concatenate(blocks + [ref[pl.ds(KEY_VALUE_HEADS * slots, slots), pl.ds(0, STATS)]], axis=1)


def step_kernel(slots, keep, *refs):
    parts, out_ref = refs[:-1], refs[-1]
    joined, logs = join([decode_part(ref, slots) for ref in parts])
    head = PART_ROWS * slots
    rest = parts[0].shape[0] - head
    for g in range(KEY_VALUE_HEADS):
        out_ref[pl.ds(g * slots, slots), :] = joined[:, g * KVW : (g + 1) * KVW]
    put_stats(out_ref, [logs[:, h * HEAD_SIZE : h * HEAD_SIZE + 1] for h in range(QUERY_HEADS)], slots)
    for i, ref in enumerate(parts if keep else parts[1:]):
        out_ref[pl.ds(head + i * rest, rest), :] = ref[pl.ds(head, rest), :]


def join_step(parts, slots, keep, name):
    head = PART_ROWS * slots
    rest = parts[0].shape[0] - head
    rows = head + rest * (len(parts) if keep else len(parts) - 1)
    return pl.pallas_call(
        functools.partial(step_kernel, slots, keep),
        in_specs=[VMEM] * len(parts),
        out_specs=VMEM,
        out_shape=pltpu.VMEM((rows, KVW), BF16),
        compiler_params=pltpu.CompilerParams(vmem_limit_bytes=16 << 20),
        name=name,
    )(*parts)


def prefill_kernel(sets, ctx, off_ref, *refs):
    query_count = len(sets)
    packs, tables, outs = refs[:query_count], refs[query_count:-query_count], refs[-query_count:]
    tokens = packs[0].shape[0]
    span = ctx + tokens
    me = lax.axis_index(BLK)
    offset = off_ref[:1, :1]
    pieces = []
    for k in range(KEY_SET):
        holder = me ^ k
        index = lax.broadcasted_iota(jnp.int32, (1, span), 1)
        old = jnp.where(holder * ctx + index < offset, -1, 1 << 30)
        pieces.append(jnp.where(index < ctx, old, holder * tokens + index - ctx))
    key_mark = jnp.concatenate(pieces, axis=1)
    in_block = lax.broadcasted_iota(jnp.int32, (GROUP * tokens, 1), 0) % tokens
    lane = lax.broadcasted_iota(jnp.int32, (tokens, STATS), 1)
    stats = [jnp.zeros((tokens, STATS), F32) for _ in range(query_count)]
    for g in range(KEY_VALUE_HEADS):
        keys = jnp.concatenate([t[:, pl.ds(g * HEAD_SIZE, HEAD_SIZE)] for t in tables], axis=0)
        values = jnp.concatenate([t[:, pl.ds(KW + g * HEAD_SIZE, HEAD_SIZE)] for t in tables], axis=0)
        for k in range(query_count):
            token = (me ^ (sets[k] * KEY_SET)) * tokens + in_block
            query = jnp.concatenate(
                [packs[k][:, pl.ds((g * GROUP + h) * HEAD_SIZE, HEAD_SIZE)] for h in range(GROUP)], axis=0
            )
            scores = jnp.where(key_mark <= token, dot_t(query, keys) * SCALE, MASKED)
            maxima = jnp.maximum(jnp.max(scores, axis=1, keepdims=True), FLOOR)
            weights = jnp.exp(scores - maxima)
            totals = jnp.sum(weights, axis=1, keepdims=True)
            summed = dot(weights.astype(BF16), values)
            seen = totals > 0.0
            safe = jnp.where(seen, totals, 1.0)
            normed = (summed / safe).astype(BF16)
            logs = jnp.where(seen, maxima + jnp.log(safe), MASKED)
            for h in range(GROUP):
                part = slice(h * tokens, (h + 1) * tokens)
                outs[k][:, pl.ds((g * GROUP + h) * HEAD_SIZE, HEAD_SIZE)] = normed[part]
                for term, value in enumerate(split3(logs[part])):
                    stats[k] = jnp.where(lane == term * QUERY_HEADS + g * GROUP + h, value, stats[k])
    for k in range(query_count):
        outs[k][:, pl.ds(QW, STATS)] = stats[k].astype(BF16)


def prefill_partials(offset, packs, tables, ctx, sets):
    tokens = packs[0].shape[0]
    pairs = len(packs) * tokens * KEY_SET * (ctx + tokens)
    return pl.pallas_call(
        functools.partial(prefill_kernel, sets, ctx),
        in_specs=[VMEM] * (1 + len(packs) + len(tables)),
        out_specs=[VMEM] * len(packs),
        out_shape=[jax.ShapeDtypeStruct((tokens, QW + STATS), BF16)] * len(packs),
        compiler_params=pltpu.CompilerParams(vmem_limit_bytes=32 << 20),
        cost_estimate=pl.CostEstimate(
            flops=4 * pairs * QW, bytes_accessed=4 << 20, transcendentals=pairs * QUERY_HEADS
        ),
        name="prefill_partials",
    )(offset, *packs, *tables)


def join_kernel(count, slots, *refs):
    out_ref, tokens = refs[-1], refs[0].shape[0]
    out_ref[pl.ds(0, tokens), :] = join([ref[...] for ref in refs[:count]])[0]
    out_ref[pl.ds(tokens, slots), :] = join([decode_part(ref, slots) for ref in refs[count:-1]])[0]


def join_parts(parts, decodes, slots):
    return pl.pallas_call(
        functools.partial(join_kernel, len(parts), slots),
        in_specs=[VMEM] * (len(parts) + len(decodes)),
        out_specs=VMEM,
        out_shape=jax.ShapeDtypeStruct((parts[0].shape[0] + slots, QW), BF16),
        compiler_params=pltpu.CompilerParams(vmem_limit_bytes=16 << 20),
        name="join_parts",
    )(*parts, *decodes)


def update_kernel(tokens, slots, off_ref, cache_hbm, near_ref, beside_ref, *refs):
    tables, (out_ref, cache_ref, sem) = refs[:KEY_SET], refs[-3:]
    load = pltpu.make_async_copy(cache_hbm.at[0], cache_ref, sem)
    load.start()
    ctx = cache_ref.shape[0]
    head = PART_ROWS * slots
    rest = near_ref.shape[0] - head
    me = lax.axis_index(BLK)
    rows = [t[pl.ds(ctx, tokens), :] for t in tables]
    rows = jnp.concatenate(rows + [r[pl.ds(head, rest), :] for r in (near_ref, beside_ref)], axis=0)
    count = rows.shape[0]
    index = lax.broadcasted_iota(jnp.int32, (1, count), 1)
    block = index // tokens
    half = rest // tokens
    sets = half * 2 // KEY_SET
    far = block - KEY_SET
    inner = far % half
    distance = KEY_SET * (1 + inner % sets) + 2 * (inner // sets) + far // half
    token = (me ^ jnp.where(block < KEY_SET, block, distance)) * tokens + index % tokens
    wanted = me * ctx + lax.broadcasted_iota(jnp.int32, (ctx, 1), 0) - off_ref[:1, :1]
    picked = dot(jnp.where(wanted == token, 1.0, 0.0).astype(BF16), rows).astype(BF16)
    inside = jnp.broadcast_to((wanted >= 0) & (wanted < count), cache_ref.shape)
    load.wait()
    out_ref[0] = jnp.where(inside, picked, cache_ref[...])


def update_cache(offset, cache, near, beside, tables, tokens, slots):
    return pl.pallas_call(
        functools.partial(update_kernel, tokens, slots),
        in_specs=[VMEM, HBM] + [VMEM] * (2 + len(tables)),
        out_specs=VMEM,
        out_shape=jax.ShapeDtypeStruct(cache.shape, BF16),
        scratch_shapes=[pltpu.VMEM(cache.shape[1:], BF16), pltpu.SemaphoreType.DMA],
        compiler_params=pltpu.CompilerParams(vmem_limit_bytes=16 << 20),
        name="update_cache",
    )(offset, pltpu.with_memory_space_constraint(cache, pltpu.HBM), near, beside, *tables)


def route_kernel(count, route_ref, *refs):
    held, (pre_ref, dec_ref) = refs[:-2], refs[-2:]
    if len(held) < count:
        held = [held[0].at[j] for j in range(count)]
    tokens, slots = pre_ref.shape[1], dec_ref.shape[0]
    prefill = jnp.zeros(pre_ref.shape[1:], F32)
    decode = jnp.zeros(dec_ref.shape, F32)
    for j in range(count):
        flag = route_ref[j, pl.ds(slots, 1), pl.ds(0, 1)]
        prefill += flag * held[j][pl.ds(0, tokens), :].astype(F32)
        chosen = route_ref[j, pl.ds(0, slots), pl.ds(0, slots)].astype(BF16)
        decode += dot(chosen, held[j][pl.ds(tokens, slots), :])
    pre_ref[0] = prefill.astype(BF16)
    dec_ref[...] = decode.astype(BF16)


def route_outputs(route, held, tokens, slots):
    return pl.pallas_call(
        functools.partial(route_kernel, route.shape[0]),
        in_specs=[VMEM] * (1 + len(held)),
        out_specs=[VMEM] * 2,
        out_shape=[
            jax.ShapeDtypeStruct((1, tokens, QW), BF16),
            jax.ShapeDtypeStruct((slots, QW), BF16),
        ],
        compiler_params=pltpu.CompilerParams(vmem_limit_bytes=16 << 20),
        name="route_outputs",
    )(route, *held)


def per_device(
    prefill_queries,
    decode_queries,
    new_prefill,
    new_decode,
    prefill_cache,
    decode_cache,
    prefill_offsets,
    decode_lengths,
    dealing,
):
    blk = lax.axis_size(BLK)
    req = lax.axis_size("req")
    ctx = prefill_cache.shape[1]
    tokens = prefill_queries.shape[1]
    slots = decode_cache.shape[0]

    def swap(array, distance):
        return lax.ppermute(array, BLK, [(i, i ^ distance) for i in range(blk)])

    def after(array, *marks):
        return lax.optimization_barrier((array, *marks))[0]

    others = range(KEY_SET, blk, KEY_SET)
    table = jnp.concatenate([prefill_cache[0], new_prefill[0]], axis=0)
    lanes = [table] + [swap(table, k) for k in range(2, KEY_SET, 2)]
    packs = [swap(prefill_queries[0], k) for k in others]

    decode_cache_out, part, queries, route = decode_partials(
        decode_lengths,
        dealing,
        decode_queries,
        new_decode,
        decode_cache,
        prefill_queries,
        new_prefill,
        req,
    )
    far = [swap(part, k) for k in others]
    offset = jnp.full((8, HEAD_SIZE), prefill_offsets[0], jnp.int32)
    lanes[1], offset, _ = lax.optimization_barrier((lanes[1], offset, part))
    lanes[2], packs, _ = lax.optimization_barrier((lanes[2], packs, lanes[1]))
    lanes[3], far, _ = lax.optimization_barrier((lanes[3], far, lanes[2]))
    part = join_step([part] + far, slots, False, "join_far")
    tables = [t for lane in lanes for t in (lane, swap(lane, 1))]
    across = swap(part, 2)

    sent = prefill_partials(offset, packs, tables, ctx, [k // KEY_SET for k in others])
    part = join_step([part, after(across, sent[0])], slots, True, "join_x")
    queries = after(queries, sent[0])
    kept = prefill_partials(offset, [queries], tables, ctx, [0])
    part = join_step([part, after(swap(part, 4), kept[0])], slots, True, "join_z")
    arrived = [swap(p, k) for k, p in zip(others, sent)]
    beside = swap(after(part, *arrived), 1)
    attended = join_parts([*kept] + arrived, [part, beside], slots)
    prefill_cache_out = update_cache(offset, prefill_cache, part, beside, tables, tokens, slots)

    if req == 2:
        held = [attended, lax.ppermute(attended, "req", [(0, 1), (1, 0)])]
    else:
        held = [lax.all_gather(attended, "req", axis=0)]
    held[-1], prefill_cache_out = lax.optimization_barrier((held[-1], prefill_cache_out))
    prefill_out, decode_out = route_outputs(route, held, tokens, slots)
    return (prefill_out, decode_out, prefill_cache_out, decode_cache_out)


def solution(mesh):
    blk, req = mesh.shape["blk"], mesh.shape["req"]
    mesh = jax.sharding.Mesh(mesh.devices.reshape(blk // QUAD, QUAD, req), ("hi", "quad", "req"))
    in_specs = (
        P("req", BLK, None),
        P("req", None),
        P("req", BLK, None),
        P("req", None),
        P("req", BLK, None),
        P("req", BLK, None),
        P("req"),
        P("req"),
        P(),
    )
    out_specs = (
        P("req", BLK, None),
        P("req", None),
        P("req", BLK, None),
        P("req", BLK, None),
    )
    return jax.shard_map(
        per_device, mesh=mesh, in_specs=in_specs, out_specs=out_specs, check_vma=False
    )
```

```python
import functools

import jax
import jax.numpy as jnp
from jax import lax
from jax.experimental import pallas as pl
from jax.experimental.pallas import tpu as pltpu
from jax.sharding import PartitionSpec as P

QUERY_HEADS = 8
KEY_VALUE_HEADS = 2
HEAD_SIZE = 128
GROUP = QUERY_HEADS // KEY_VALUE_HEADS
QW = QUERY_HEADS * HEAD_SIZE
KW = KEY_VALUE_HEADS * HEAD_SIZE
STATS = 128
QUAD = 4
KEY_SET = 8
PART_ROWS = KEY_VALUE_HEADS + 1
SCALE = HEAD_SIZE**-0.5
MASKED = -1e30
FLOOR = -1e20
F32 = jnp.float32
BF16 = jnp.bfloat16

KVW = 2 * KW
BLK = ("hi", "quad")
CHUNKS = 4
TILE = 16

HBM = pl.BlockSpec(memory_space=pltpu.HBM)
VMEM = pl.BlockSpec(memory_space=pltpu.VMEM)


def dot_t(a, b):
    return lax.dot_general(a, b, (((1,), (1,)), ((), ())), preferred_element_type=F32)


def dot(a, b):
    return lax.dot_general(a, b, (((1,), (0,)), ((), ())), preferred_element_type=F32)


def split3(value):
    high = value.astype(BF16).astype(F32)
    rest = value - high
    middle = rest.astype(BF16).astype(F32)
    return high, middle, rest - middle


def stats_block(columns, rows):
    lane = lax.broadcasted_iota(jnp.int32, (rows, STATS), 1)
    count = len(columns)
    out = jnp.zeros((rows, STATS), F32)
    for head, column in enumerate(columns):
        for term, part in enumerate(split3(column)):
            out = jnp.where(lane == term * count + head, part, out)
    return out.astype(BF16)


def spread_matrix(heads):
    lane = lax.broadcasted_iota(jnp.int32, (STATS, heads * HEAD_SIZE), 0)
    head = lax.broadcasted_iota(jnp.int32, (STATS, heads * HEAD_SIZE), 1) // HEAD_SIZE
    hit = (lane == head) | (lane == head + heads) | (lane == head + 2 * heads)
    return jnp.where(hit, 1.0, 0.0).astype(BF16)


def join(parts):
    spread = spread_matrix(QUERY_HEADS)
    logs = [dot(part[:, QW:], spread) for part in parts]
    top = functools.reduce(jnp.maximum, logs)
    scales = [jnp.exp(log - top) for log in logs]
    total = functools.reduce(jnp.add, scales)
    summed = functools.reduce(
        jnp.add, [scale * part[:, :QW].astype(F32) for scale, part in zip(scales, parts)]
    )
    return (summed / total).astype(BF16), top + jnp.log(total)


def source_group(j):
    return lax.axis_index("req") ^ j if lax.axis_size("req") == 2 else j


def decode_kernel(
    len_hbm,
    deal_hbm,
    q_hbm,
    new_hbm,
    cache_hbm,
    pre_q_hbm,
    pre_new_hbm,
    out_hbm,
    part_ref,
    pre_q_ref,
    route_ref,
    lens,
    deal,
    query_ref,
    new_ref,
    table,
    sems,
):
    slots, ctx, _ = table.shape
    rows = GROUP * slots
    chunk = slots // CHUNKS
    base = lax.axis_index(BLK) * ctx
    small = [
        (len_hbm, lens),
        (deal_hbm, deal),
        (q_hbm, query_ref),
        (new_hbm, new_ref),
        (pre_q_hbm.at[0], pre_q_ref),
        (pre_new_hbm.at[0], part_ref.at[pl.ds(PART_ROWS * slots, pre_new_hbm.shape[1]), :]),
    ]
    small = [pltpu.make_async_copy(a, b, sems.at[i]) for i, (a, b) in enumerate(small)]
    loads, stores = [], []
    for c in range(CHUNKS):
        part = pl.ds(c * chunk, chunk)
        loads.append(pltpu.make_async_copy(cache_hbm.at[part], table.at[part], sems.at[6 + c]))
        stores.append(pltpu.make_async_copy(table.at[part], out_hbm.at[part], sems.at[6 + CHUNKS + c]))
    for copy in small + loads:
        copy.start()
    for copy in small:
        copy.wait()
    group = lax.axis_index("req")
    req = route_ref.shape[0]
    out_row = lax.broadcasted_iota(jnp.int32, (slots, HEAD_SIZE), 0)
    out_lane = lax.broadcasted_iota(jnp.int32, (slots, HEAD_SIZE), 1)
    for j in range(req):
        source = source_group(j)
        chosen = jnp.zeros((slots, HEAD_SIZE), F32)
        for s in range(slots):
            place = deal[req + source * slots + s] - group * slots
            chosen = jnp.where((out_lane == s) & (out_row == place), 1.0, chosen)
        route_ref[j, pl.ds(0, slots), :] = chosen
        mine = (deal[source] == group).astype(F32)
        route_ref[j, pl.ds(slots, 8), :] = jnp.full((8, HEAD_SIZE), mine, F32)
    row_slot = lax.broadcasted_iota(jnp.int32, (rows, ctx), 0) % slots
    column = lax.broadcasted_iota(jnp.int32, (rows, ctx), 1)
    in_tile = lax.broadcasted_iota(jnp.int32, (TILE, KVW), 0)
    limit = jnp.full((rows, ctx), -1, jnp.int32)
    queries = [
        jnp.concatenate(
            [query_ref[:, pl.ds((g * GROUP + h) * HEAD_SIZE, HEAD_SIZE)] for h in range(GROUP)], axis=0
        )
        for g in range(KEY_VALUE_HEADS)
    ]
    scores = [jnp.zeros((rows, ctx), F32) for _ in range(KEY_VALUE_HEADS)]
    for c in range(CHUNKS):
        loads[c].wait()
        for s in range(c * chunk, (c + 1) * chunk):
            relative = lens[s] - base
            limit = jnp.where(row_slot == s, relative, limit)

            @pl.when((relative >= 0) & (relative < ctx))
            def _():
                start = pl.multiple_of(relative // TILE * TILE, TILE)
                tile = table[s, pl.ds(start, TILE), :]
                table[s, pl.ds(start, TILE), :] = jnp.where(
                    in_tile == relative - start, new_ref[s : s + 1, :], tile
                )

        stores[c].start()
        for g in range(KEY_VALUE_HEADS):
            key = table[pl.ds(c * chunk, chunk), :, pl.ds(g * HEAD_SIZE, HEAD_SIZE)]
            wide = dot_t(queries[g], key.reshape(chunk * ctx, HEAD_SIZE))
            for s in range(chunk):
                part = wide[:, s * ctx : (s + 1) * ctx]
                scores[g] = jnp.where(row_slot == c * chunk + s, part, scores[g])
    visible = column <= limit
    columns = []
    for g in range(KEY_VALUE_HEADS):
        masked = jnp.where(visible, scores[g] * SCALE, MASKED)
        maxima = jnp.maximum(jnp.max(masked, axis=1, keepdims=True), FLOOR)
        weights = jnp.exp(masked - maxima)
        totals = jnp.sum(weights, axis=1, keepdims=True)
        summed = jnp.zeros((rows, HEAD_SIZE), F32)
        for c in range(CHUNKS):
            value = table[pl.ds(c * chunk, chunk), :, pl.ds(KW + g * HEAD_SIZE, HEAD_SIZE)]
            picked = [jnp.where(row_slot == c * chunk + s, weights, 0.0) for s in range(chunk)]
            picked = jnp.concatenate(picked, axis=1).astype(BF16)
            summed += dot(picked, value.reshape(chunk * ctx, HEAD_SIZE))
        seen = totals > 0.0
        safe = jnp.where(seen, totals, 1.0)
        normed = (summed / safe).astype(BF16)
        logs = jnp.where(seen, maxima + jnp.log(safe), MASKED)
        for h in range(GROUP):
            part = slice(h * slots, (h + 1) * slots)
            part_ref[pl.ds(g * slots, slots), pl.ds(h * HEAD_SIZE, HEAD_SIZE)] = normed[part]
            columns.append(logs[part])
    put_stats(part_ref, columns, slots)
    for copy in stores:
        copy.wait()


def decode_partials(lengths, dealing, queries, new_rows, cache, pre_queries, pre_new, req):
    slots, ctx, width = cache.shape
    inputs = (lengths, dealing, queries, new_rows, cache, pre_queries, pre_new)
    return pl.pallas_call(
        decode_kernel,
        in_specs=[HBM] * len(inputs),
        out_specs=[HBM, VMEM, VMEM, VMEM],
        out_shape=[
            pltpu.HBM(cache.shape, BF16),
            pltpu.VMEM((PART_ROWS * slots + pre_new.shape[1], KVW), BF16),
            pltpu.VMEM(pre_queries.shape[1:], BF16),
            pltpu.VMEM((req, slots + 8, HEAD_SIZE), F32),
        ],
        scratch_shapes=[
            pltpu.SMEM(lengths.shape, jnp.int32),
            pltpu.SMEM(dealing.shape, jnp.int32),
            pltpu.VMEM(queries.shape, BF16),
            pltpu.VMEM(new_rows.shape, BF16),
            pltpu.VMEM(cache.shape, BF16),
            pltpu.SemaphoreType.DMA((6 + 2 * CHUNKS,)),
        ],
        compiler_params=pltpu.CompilerParams(vmem_limit_bytes=16 << 20),
        cost_estimate=pl.CostEstimate(
            flops=4 * slots * ctx * QW, bytes_accessed=2 * cache.size * 2, transcendentals=slots * ctx * 8
        ),
        name="decode_partials",
    )(*[pltpu.with_memory_space_constraint(x, pltpu.HBM) for x in inputs])


def put_stats(ref, columns, slots):
    last = pl.ds(KEY_VALUE_HEADS * slots, slots)
    ref[last, pl.ds(0, STATS)] = stats_block(columns, slots)
    ref[last, pl.ds(STATS, KVW - STATS)] = jnp.zeros((slots, KVW - STATS), BF16)


def decode_part(ref, slots):
    blocks = [ref[pl.ds(g * slots, slots), :] for g in range(KEY_VALUE_HEADS)]
    return jnp.concatenate(blocks + [ref[pl.ds(KEY_VALUE_HEADS * slots, slots), pl.ds(0, STATS)]], axis=1)


def step_kernel(slots, keep, *refs):
    parts, out_ref = refs[:-1], refs[-1]
    joined, logs = join([decode_part(ref, slots) for ref in parts])
    head = PART_ROWS * slots
    rest = parts[0].shape[0] - head
    for g in range(KEY_VALUE_HEADS):
        out_ref[pl.ds(g * slots, slots), :] = joined[:, g * KVW : (g + 1) * KVW]
    put_stats(out_ref, [logs[:, h * HEAD_SIZE : h * HEAD_SIZE + 1] for h in range(QUERY_HEADS)], slots)
    for i, ref in enumerate(parts if keep else parts[1:]):
        out_ref[pl.ds(head + i * rest, rest), :] = ref[pl.ds(head, rest), :]


def join_step(parts, slots, keep, name):
    head = PART_ROWS * slots
    rest = parts[0].shape[0] - head
    rows = head + rest * (len(parts) if keep else len(parts) - 1)
    return pl.pallas_call(
        functools.partial(step_kernel, slots, keep),
        in_specs=[VMEM] * len(parts),
        out_specs=VMEM,
        out_shape=pltpu.VMEM((rows, KVW), BF16),
        compiler_params=pltpu.CompilerParams(vmem_limit_bytes=16 << 20),
        name=name,
    )(*parts)


def prefill_kernel(sets, ctx, off_ref, *refs):
    query_count = len(sets)
    packs, tables, outs = refs[:query_count], refs[query_count:-query_count], refs[-query_count:]
    tokens = packs[0].shape[0]
    span = ctx + tokens
    me = lax.axis_index(BLK)
    offset = off_ref[:1, :1]
    pieces = []
    for k in range(KEY_SET):
        holder = me ^ k
        index = lax.broadcasted_iota(jnp.int32, (1, span), 1)
        old = jnp.where(holder * ctx + index < offset, -1, 1 << 30)
        pieces.append(jnp.where(index < ctx, old, holder * tokens + index - ctx))
    key_mark = jnp.concatenate(pieces, axis=1)
    in_block = lax.broadcasted_iota(jnp.int32, (GROUP * tokens, 1), 0) % tokens
    lane = lax.broadcasted_iota(jnp.int32, (tokens, STATS), 1)
    stats = [jnp.zeros((tokens, STATS), F32) for _ in range(query_count)]
    for g in range(KEY_VALUE_HEADS):
        keys = jnp.concatenate([t[:, pl.ds(g * HEAD_SIZE, HEAD_SIZE)] for t in tables], axis=0)
        values = jnp.concatenate([t[:, pl.ds(KW + g * HEAD_SIZE, HEAD_SIZE)] for t in tables], axis=0)
        for k in range(query_count):
            token = (me ^ (sets[k] * KEY_SET)) * tokens + in_block
            query = jnp.concatenate(
                [packs[k][:, pl.ds((g * GROUP + h) * HEAD_SIZE, HEAD_SIZE)] for h in range(GROUP)], axis=0
            )
            scores = jnp.where(key_mark <= token, dot_t(query, keys) * SCALE, MASKED)
            maxima = jnp.maximum(jnp.max(scores, axis=1, keepdims=True), FLOOR)
            weights = jnp.exp(scores - maxima)
            totals = jnp.sum(weights, axis=1, keepdims=True)
            summed = dot(weights.astype(BF16), values)
            seen = totals > 0.0
            safe = jnp.where(seen, totals, 1.0)
            normed = (summed / safe).astype(BF16)
            logs = jnp.where(seen, maxima + jnp.log(safe), MASKED)
            for h in range(GROUP):
                part = slice(h * tokens, (h + 1) * tokens)
                outs[k][:, pl.ds((g * GROUP + h) * HEAD_SIZE, HEAD_SIZE)] = normed[part]
                for term, value in enumerate(split3(logs[part])):
                    stats[k] = jnp.where(lane == term * QUERY_HEADS + g * GROUP + h, value, stats[k])
    for k in range(query_count):
        outs[k][:, pl.ds(QW, STATS)] = stats[k].astype(BF16)


def prefill_partials(offset, packs, tables, ctx, sets):
    tokens = packs[0].shape[0]
    pairs = len(packs) * tokens * KEY_SET * (ctx + tokens)
    return pl.pallas_call(
        functools.partial(prefill_kernel, sets, ctx),
        in_specs=[VMEM] * (1 + len(packs) + len(tables)),
        out_specs=[VMEM] * len(packs),
        out_shape=[jax.ShapeDtypeStruct((tokens, QW + STATS), BF16)] * len(packs),
        compiler_params=pltpu.CompilerParams(vmem_limit_bytes=32 << 20),
        cost_estimate=pl.CostEstimate(
            flops=4 * pairs * QW, bytes_accessed=4 << 20, transcendentals=pairs * QUERY_HEADS
        ),
        name="prefill_partials",
    )(offset, *packs, *tables)


def join_kernel(count, slots, *refs):
    out_ref, tokens = refs[-1], refs[0].shape[0]
    out_ref[pl.ds(0, tokens), :] = join([ref[...] for ref in refs[:count]])[0]
    out_ref[pl.ds(tokens, slots), :] = join([decode_part(ref, slots) for ref in refs[count:-1]])[0]


def join_parts(parts, decodes, slots):
    return pl.pallas_call(
        functools.partial(join_kernel, len(parts), slots),
        in_specs=[VMEM] * (len(parts) + len(decodes)),
        out_specs=VMEM,
        out_shape=jax.ShapeDtypeStruct((parts[0].shape[0] + slots, QW), BF16),
        compiler_params=pltpu.CompilerParams(vmem_limit_bytes=16 << 20),
        name="join_parts",
    )(*parts, *decodes)


def update_kernel(tokens, slots, off_ref, cache_hbm, near_ref, beside_ref, *refs):
    tables, (out_ref, cache_ref, sem) = refs[:KEY_SET], refs[-3:]
    load = pltpu.make_async_copy(cache_hbm.at[0], cache_ref, sem)
    load.start()
    ctx = cache_ref.shape[0]
    head = PART_ROWS * slots
    rest = near_ref.shape[0] - head
    me = lax.axis_index(BLK)
    rows = [t[pl.ds(ctx, tokens), :] for t in tables]
    rows = jnp.concatenate(rows + [r[pl.ds(head, rest), :] for r in (near_ref, beside_ref)], axis=0)
    count = rows.shape[0]
    index = lax.broadcasted_iota(jnp.int32, (1, count), 1)
    block = index // tokens
    half = rest // tokens
    sets = half * 2 // KEY_SET
    far = block - KEY_SET
    inner = far % half
    distance = KEY_SET * (1 + inner % sets) + 2 * (inner // sets) + far // half
    token = (me ^ jnp.where(block < KEY_SET, block, distance)) * tokens + index % tokens
    wanted = me * ctx + lax.broadcasted_iota(jnp.int32, (ctx, 1), 0) - off_ref[:1, :1]
    picked = dot(jnp.where(wanted == token, 1.0, 0.0).astype(BF16), rows).astype(BF16)
    inside = jnp.broadcast_to((wanted >= 0) & (wanted < count), cache_ref.shape)
    load.wait()
    out_ref[0] = jnp.where(inside, picked, cache_ref[...])


def update_cache(offset, cache, near, beside, tables, tokens, slots):
    return pl.pallas_call(
        functools.partial(update_kernel, tokens, slots),
        in_specs=[VMEM, HBM] + [VMEM] * (2 + len(tables)),
        out_specs=VMEM,
        out_shape=jax.ShapeDtypeStruct(cache.shape, BF16),
        scratch_shapes=[pltpu.VMEM(cache.shape[1:], BF16), pltpu.SemaphoreType.DMA],
        compiler_params=pltpu.CompilerParams(vmem_limit_bytes=16 << 20),
        name="update_cache",
    )(offset, pltpu.with_memory_space_constraint(cache, pltpu.HBM), near, beside, *tables)


def route_kernel(count, route_ref, *refs):
    held, (pre_ref, dec_ref) = refs[:-2], refs[-2:]
    if len(held) < count:
        held = [held[0].at[j] for j in range(count)]
    tokens, slots = pre_ref.shape[1], dec_ref.shape[0]
    prefill = jnp.zeros(pre_ref.shape[1:], F32)
    decode = jnp.zeros(dec_ref.shape, F32)
    for j in range(count):
        flag = route_ref[j, pl.ds(slots, 1), pl.ds(0, 1)]
        prefill += flag * held[j][pl.ds(0, tokens), :].astype(F32)
        chosen = route_ref[j, pl.ds(0, slots), pl.ds(0, slots)].astype(BF16)
        decode += dot(chosen, held[j][pl.ds(tokens, slots), :])
    pre_ref[0] = prefill.astype(BF16)
    dec_ref[...] = decode.astype(BF16)


def route_outputs(route, held, tokens, slots):
    return pl.pallas_call(
        functools.partial(route_kernel, route.shape[0]),
        in_specs=[VMEM] * (1 + len(held)),
        out_specs=[VMEM] * 2,
        out_shape=[
            jax.ShapeDtypeStruct((1, tokens, QW), BF16),
            jax.ShapeDtypeStruct((slots, QW), BF16),
        ],
        compiler_params=pltpu.CompilerParams(vmem_limit_bytes=16 << 20),
        name="route_outputs",
    )(route, *held)


def per_device(
    prefill_queries,
    decode_queries,
    new_prefill,
    new_decode,
    prefill_cache,
    decode_cache,
    prefill_offsets,
    decode_lengths,
    dealing,
):
    blk = lax.axis_size(BLK)
    req = lax.axis_size("req")
    ctx = prefill_cache.shape[1]
    tokens = prefill_queries.shape[1]
    slots = decode_cache.shape[0]

    def swap(array, distance):
        return lax.ppermute(array, BLK, [(i, i ^ distance) for i in range(blk)])

    def after(array, *marks):
        return lax.optimization_barrier((array, *marks))[0]

    others = range(KEY_SET, blk, KEY_SET)
    table = jnp.concatenate([prefill_cache[0], new_prefill[0]], axis=0)
    lanes = [table] + [swap(table, k) for k in range(2, KEY_SET, 2)]
    packs = [swap(prefill_queries[0], k) for k in others]

    decode_cache_out, part, queries, route = decode_partials(
        decode_lengths,
        dealing,
        decode_queries,
        new_decode,
        decode_cache,
        prefill_queries,
        new_prefill,
        req,
    )
    part = after(part, *packs)
    far = [swap(part, k) for k in others]
    offset = jnp.full((8, HEAD_SIZE), prefill_offsets[0], jnp.int32)
    lanes[1], offset, _ = lax.optimization_barrier((lanes[1], offset, part))
    lanes[2] = after(lanes[2], lanes[1])
    lanes[3], far, _ = lax.optimization_barrier((lanes[3], far, lanes[2]))
    part = join_step([part] + far, slots, False, "join_far")
    tables = [t for lane in lanes for t in (lane, swap(lane, 1))]
    around = [swap(part, k) for k in range(2, KEY_SET, 2)]

    sent = prefill_partials(offset, packs, tables, ctx, [k // KEY_SET for k in others])
    queries = after(queries, sent[0])
    kept = prefill_partials(offset, [queries], tables, ctx, [0])
    around[0] = after(around[0], kept[0])
    part = join_step([part] + around, slots, True, "join_lanes")
    arrived = [swap(p, k) for k, p in zip(others, sent)]
    beside = swap(after(part, *arrived), 1)
    attended = join_parts([*kept] + arrived, [part, beside], slots)
    prefill_cache_out = update_cache(offset, prefill_cache, part, beside, tables, tokens, slots)

    if req == 2:
        held = [attended, lax.ppermute(attended, "req", [(0, 1), (1, 0)])]
    else:
        held = [lax.all_gather(attended, "req", axis=0)]
    held[-1], prefill_cache_out = lax.optimization_barrier((held[-1], prefill_cache_out))
    prefill_out, decode_out = route_outputs(route, held, tokens, slots)
    return (prefill_out, decode_out, prefill_cache_out, decode_cache_out)


def solution(mesh):
    blk, req = mesh.shape["blk"], mesh.shape["req"]
    mesh = jax.sharding.Mesh(mesh.devices.reshape(blk // QUAD, QUAD, req), ("hi", "quad", "req"))
    in_specs = (
        P("req", BLK, None),
        P("req", None),
        P("req", BLK, None),
        P("req", None),
        P("req", BLK, None),
        P("req", BLK, None),
        P("req"),
        P("req"),
        P(),
    )
    out_specs = (
        P("req", BLK, None),
        P("req", None),
        P("req", BLK, None),
        P("req", BLK, None),
    )
    return jax.shard_map(
        per_device, mesh=mesh, in_specs=in_specs, out_specs=out_specs, check_vma=False
    )
```

```python
import functools

import jax
import jax.numpy as jnp
from jax import lax
from jax.experimental import pallas as pl
from jax.experimental.pallas import tpu as pltpu
from jax.sharding import PartitionSpec as P

QUERY_HEADS = 8
KEY_VALUE_HEADS = 2
HEAD_SIZE = 128
GROUP = QUERY_HEADS // KEY_VALUE_HEADS
QW = QUERY_HEADS * HEAD_SIZE
KW = KEY_VALUE_HEADS * HEAD_SIZE
STATS = 128
QUAD = 4
KEY_SET = 8
PART_ROWS = KEY_VALUE_HEADS + 1
SCALE = HEAD_SIZE**-0.5
MASKED = -1e30
FLOOR = -1e20
F32 = jnp.float32
BF16 = jnp.bfloat16

KVW = 2 * KW
BLK = ("hi", "quad")
CHUNKS = 4
TILE = 16

HBM = pl.BlockSpec(memory_space=pltpu.HBM)
VMEM = pl.BlockSpec(memory_space=pltpu.VMEM)


def dot_t(a, b):
    return lax.dot_general(a, b, (((1,), (1,)), ((), ())), preferred_element_type=F32)


def dot(a, b):
    return lax.dot_general(a, b, (((1,), (0,)), ((), ())), preferred_element_type=F32)


def split3(value):
    high = value.astype(BF16).astype(F32)
    rest = value - high
    middle = rest.astype(BF16).astype(F32)
    return high, middle, rest - middle


def stats_block(columns, rows):
    lane = lax.broadcasted_iota(jnp.int32, (rows, STATS), 1)
    count = len(columns)
    out = jnp.zeros((rows, STATS), F32)
    for head, column in enumerate(columns):
        for term, part in enumerate(split3(column)):
            out = jnp.where(lane == term * count + head, part, out)
    return out.astype(BF16)


def spread_matrix(heads):
    lane = lax.broadcasted_iota(jnp.int32, (STATS, heads * HEAD_SIZE), 0)
    head = lax.broadcasted_iota(jnp.int32, (STATS, heads * HEAD_SIZE), 1) // HEAD_SIZE
    hit = (lane == head) | (lane == head + heads) | (lane == head + 2 * heads)
    return jnp.where(hit, 1.0, 0.0).astype(BF16)


def join(parts):
    spread = spread_matrix(QUERY_HEADS)
    logs = [dot(part[:, QW:], spread) for part in parts]
    top = functools.reduce(jnp.maximum, logs)
    scales = [jnp.exp(log - top) for log in logs]
    total = functools.reduce(jnp.add, scales)
    summed = functools.reduce(
        jnp.add, [scale * part[:, :QW].astype(F32) for scale, part in zip(scales, parts)]
    )
    return (summed / total).astype(BF16), top + jnp.log(total)


def source_group(j):
    return lax.axis_index("req") ^ j if lax.axis_size("req") == 2 else j


def decode_kernel(
    len_hbm,
    deal_hbm,
    q_hbm,
    new_hbm,
    cache_hbm,
    pre_q_hbm,
    pre_new_hbm,
    out_hbm,
    part_ref,
    pre_q_ref,
    route_ref,
    lens,
    deal,
    query_ref,
    new_ref,
    table,
    sems,
):
    slots, ctx, _ = table.shape
    rows = GROUP * slots
    chunk = slots // CHUNKS
    base = lax.axis_index(BLK) * ctx
    small = [
        (len_hbm, lens),
        (deal_hbm, deal),
        (q_hbm, query_ref),
        (new_hbm, new_ref),
        (pre_q_hbm.at[0], pre_q_ref),
        (pre_new_hbm.at[0], part_ref.at[pl.ds(PART_ROWS * slots, pre_new_hbm.shape[1]), :]),
    ]
    small = [pltpu.make_async_copy(a, b, sems.at[i]) for i, (a, b) in enumerate(small)]
    loads, stores = [], []
    for c in range(CHUNKS):
        part = pl.ds(c * chunk, chunk)
        loads.append(pltpu.make_async_copy(cache_hbm.at[part], table.at[part], sems.at[6 + c]))
        stores.append(pltpu.make_async_copy(table.at[part], out_hbm.at[part], sems.at[6 + CHUNKS + c]))
    for copy in small + loads:
        copy.start()
    for copy in small:
        copy.wait()
    group = lax.axis_index("req")
    req = route_ref.shape[0]
    out_row = lax.broadcasted_iota(jnp.int32, (slots, HEAD_SIZE), 0)
    out_lane = lax.broadcasted_iota(jnp.int32, (slots, HEAD_SIZE), 1)
    for j in range(req):
        source = source_group(j)
        chosen = jnp.zeros((slots, HEAD_SIZE), F32)
        for s in range(slots):
            place = deal[req + source * slots + s] - group * slots
            chosen = jnp.where((out_lane == s) & (out_row == place), 1.0, chosen)
        route_ref[j, pl.ds(0, slots), :] = chosen
        mine = (deal[source] == group).astype(F32)
        route_ref[j, pl.ds(slots, 8), :] = jnp.full((8, HEAD_SIZE), mine, F32)
    row_slot = lax.broadcasted_iota(jnp.int32, (rows, ctx), 0) % slots
    column = lax.broadcasted_iota(jnp.int32, (rows, ctx), 1)
    in_tile = lax.broadcasted_iota(jnp.int32, (TILE, KVW), 0)
    limit = jnp.full((rows, ctx), -1, jnp.int32)
    queries = [
        jnp.concatenate(
            [query_ref[:, pl.ds((g * GROUP + h) * HEAD_SIZE, HEAD_SIZE)] for h in range(GROUP)], axis=0
        )
        for g in range(KEY_VALUE_HEADS)
    ]
    scores = [jnp.zeros((rows, ctx), F32) for _ in range(KEY_VALUE_HEADS)]
    for c in range(CHUNKS):
        loads[c].wait()
        for s in range(c * chunk, (c + 1) * chunk):
            relative = lens[s] - base
            limit = jnp.where(row_slot == s, relative, limit)

            @pl.when((relative >= 0) & (relative < ctx))
            def _():
                start = pl.multiple_of(relative // TILE * TILE, TILE)
                tile = table[s, pl.ds(start, TILE), :]
                table[s, pl.ds(start, TILE), :] = jnp.where(
                    in_tile == relative - start, new_ref[s : s + 1, :], tile
                )

        stores[c].start()
        for g in range(KEY_VALUE_HEADS):
            key = table[pl.ds(c * chunk, chunk), :, pl.ds(g * HEAD_SIZE, HEAD_SIZE)]
            wide = dot_t(queries[g], key.reshape(chunk * ctx, HEAD_SIZE))
            for s in range(chunk):
                part = wide[:, s * ctx : (s + 1) * ctx]
                scores[g] = jnp.where(row_slot == c * chunk + s, part, scores[g])
    visible = column <= limit
    columns = []
    for g in range(KEY_VALUE_HEADS):
        masked = jnp.where(visible, scores[g] * SCALE, MASKED)
        maxima = jnp.maximum(jnp.max(masked, axis=1, keepdims=True), FLOOR)
        weights = jnp.exp(masked - maxima)
        totals = jnp.sum(weights, axis=1, keepdims=True)
        summed = jnp.zeros((rows, HEAD_SIZE), F32)
        for c in range(CHUNKS):
            value = table[pl.ds(c * chunk, chunk), :, pl.ds(KW + g * HEAD_SIZE, HEAD_SIZE)]
            picked = [jnp.where(row_slot == c * chunk + s, weights, 0.0) for s in range(chunk)]
            picked = jnp.concatenate(picked, axis=1).astype(BF16)
            summed += dot(picked, value.reshape(chunk * ctx, HEAD_SIZE))
        seen = totals > 0.0
        safe = jnp.where(seen, totals, 1.0)
        normed = (summed / safe).astype(BF16)
        logs = jnp.where(seen, maxima + jnp.log(safe), MASKED)
        for h in range(GROUP):
            part = slice(h * slots, (h + 1) * slots)
            part_ref[pl.ds(g * slots, slots), pl.ds(h * HEAD_SIZE, HEAD_SIZE)] = normed[part]
            columns.append(logs[part])
    put_stats(part_ref, columns, slots)
    for copy in stores:
        copy.wait()


def decode_partials(lengths, dealing, queries, new_rows, cache, pre_queries, pre_new, req):
    slots, ctx, width = cache.shape
    inputs = (lengths, dealing, queries, new_rows, cache, pre_queries, pre_new)
    return pl.pallas_call(
        decode_kernel,
        in_specs=[HBM] * len(inputs),
        out_specs=[HBM, VMEM, VMEM, VMEM],
        out_shape=[
            pltpu.HBM(cache.shape, BF16),
            pltpu.VMEM((PART_ROWS * slots + pre_new.shape[1], KVW), BF16),
            pltpu.VMEM(pre_queries.shape[1:], BF16),
            pltpu.VMEM((req, slots + 8, HEAD_SIZE), F32),
        ],
        scratch_shapes=[
            pltpu.SMEM(lengths.shape, jnp.int32),
            pltpu.SMEM(dealing.shape, jnp.int32),
            pltpu.VMEM(queries.shape, BF16),
            pltpu.VMEM(new_rows.shape, BF16),
            pltpu.VMEM(cache.shape, BF16),
            pltpu.SemaphoreType.DMA((6 + 2 * CHUNKS,)),
        ],
        compiler_params=pltpu.CompilerParams(vmem_limit_bytes=16 << 20),
        cost_estimate=pl.CostEstimate(
            flops=4 * slots * ctx * QW, bytes_accessed=2 * cache.size * 2, transcendentals=slots * ctx * 8
        ),
        name="decode_partials",
    )(*[pltpu.with_memory_space_constraint(x, pltpu.HBM) for x in inputs])


def put_stats(ref, columns, slots):
    last = pl.ds(KEY_VALUE_HEADS * slots, slots)
    ref[last, pl.ds(0, STATS)] = stats_block(columns, slots)
    ref[last, pl.ds(STATS, KVW - STATS)] = jnp.zeros((slots, KVW - STATS), BF16)


def decode_part(ref, slots):
    blocks = [ref[pl.ds(g * slots, slots), :] for g in range(KEY_VALUE_HEADS)]
    return jnp.concatenate(blocks + [ref[pl.ds(KEY_VALUE_HEADS * slots, slots), pl.ds(0, STATS)]], axis=1)


def step_kernel(slots, count, *refs):
    out_ref = refs[-1]
    joined, logs = join([decode_part(ref, slots) for ref in refs[:count]])
    head = PART_ROWS * slots
    for g in range(KEY_VALUE_HEADS):
        out_ref[pl.ds(g * slots, slots), :] = joined[:, g * KVW : (g + 1) * KVW]
    put_stats(out_ref, [logs[:, h * HEAD_SIZE : h * HEAD_SIZE + 1] for h in range(QUERY_HEADS)], slots)
    at = head
    for ref in refs[count:-1]:
        rest = ref.shape[0] - head
        out_ref[pl.ds(at, rest), :] = ref[pl.ds(head, rest), :]
        at += rest


def join_step(parts, carriers, slots, name):
    head = PART_ROWS * slots
    rows = head + sum(c.shape[0] - head for c in carriers)
    return pl.pallas_call(
        functools.partial(step_kernel, slots, len(parts)),
        in_specs=[VMEM] * (len(parts) + len(carriers)),
        out_specs=VMEM,
        out_shape=pltpu.VMEM((rows, KVW), BF16),
        compiler_params=pltpu.CompilerParams(vmem_limit_bytes=16 << 20),
        name=name,
    )(*parts, *carriers)


def prefill_kernel(sets, ctx, off_ref, *refs):
    query_count = len(sets)
    packs, tables, outs = refs[:query_count], refs[query_count:-query_count], refs[-query_count:]
    tokens = packs[0].shape[0]
    span = ctx + tokens
    me = lax.axis_index(BLK)
    offset = off_ref[:1, :1]
    pieces = []
    for k in range(KEY_SET):
        holder = me ^ k
        index = lax.broadcasted_iota(jnp.int32, (1, span), 1)
        old = jnp.where(holder * ctx + index < offset, -1, 1 << 30)
        pieces.append(jnp.where(index < ctx, old, holder * tokens + index - ctx))
    key_mark = jnp.concatenate(pieces, axis=1)
    in_block = lax.broadcasted_iota(jnp.int32, (GROUP * tokens, 1), 0) % tokens
    lane = lax.broadcasted_iota(jnp.int32, (tokens, STATS), 1)
    stats = [jnp.zeros((tokens, STATS), F32) for _ in range(query_count)]
    for g in range(KEY_VALUE_HEADS):
        keys = jnp.concatenate([t[:, pl.ds(g * HEAD_SIZE, HEAD_SIZE)] for t in tables], axis=0)
        values = jnp.concatenate([t[:, pl.ds(KW + g * HEAD_SIZE, HEAD_SIZE)] for t in tables], axis=0)
        for k in range(query_count):
            token = (me ^ (sets[k] * KEY_SET)) * tokens + in_block
            query = jnp.concatenate(
                [packs[k][:, pl.ds((g * GROUP + h) * HEAD_SIZE, HEAD_SIZE)] for h in range(GROUP)], axis=0
            )
            scores = jnp.where(key_mark <= token, dot_t(query, keys) * SCALE, MASKED)
            maxima = jnp.maximum(jnp.max(scores, axis=1, keepdims=True), FLOOR)
            weights = jnp.exp(scores - maxima)
            totals = jnp.sum(weights, axis=1, keepdims=True)
            summed = dot(weights.astype(BF16), values)
            seen = totals > 0.0
            safe = jnp.where(seen, totals, 1.0)
            normed = (summed / safe).astype(BF16)
            logs = jnp.where(seen, maxima + jnp.log(safe), MASKED)
            for h in range(GROUP):
                part = slice(h * tokens, (h + 1) * tokens)
                outs[k][:, pl.ds((g * GROUP + h) * HEAD_SIZE, HEAD_SIZE)] = normed[part]
                for term, value in enumerate(split3(logs[part])):
                    stats[k] = jnp.where(lane == term * QUERY_HEADS + g * GROUP + h, value, stats[k])
    for k in range(query_count):
        outs[k][:, pl.ds(QW, STATS)] = stats[k].astype(BF16)


def prefill_partials(offset, packs, tables, ctx, sets):
    tokens = packs[0].shape[0]
    pairs = len(packs) * tokens * KEY_SET * (ctx + tokens)
    return pl.pallas_call(
        functools.partial(prefill_kernel, sets, ctx),
        in_specs=[VMEM] * (1 + len(packs) + len(tables)),
        out_specs=[VMEM] * len(packs),
        out_shape=[jax.ShapeDtypeStruct((tokens, QW + STATS), BF16)] * len(packs),
        compiler_params=pltpu.CompilerParams(vmem_limit_bytes=32 << 20),
        cost_estimate=pl.CostEstimate(
            flops=4 * pairs * QW, bytes_accessed=4 << 20, transcendentals=pairs * QUERY_HEADS
        ),
        name="prefill_partials",
    )(offset, *packs, *tables)


def join_kernel(*refs):
    refs[-1][...] = join([ref[...] for ref in refs[:-1]])[0]


def join_parts(parts):
    return pl.pallas_call(
        join_kernel,
        in_specs=[VMEM] * len(parts),
        out_specs=VMEM,
        out_shape=pltpu.VMEM((parts[0].shape[0], QW), BF16),
        compiler_params=pltpu.CompilerParams(vmem_limit_bytes=16 << 20),
        name="join_parts",
    )(*parts)


def finish_kernel(slots, prefill_ref, *refs):
    decodes, out_ref = refs[:-1], refs[-1]
    tokens = prefill_ref.shape[0]
    out_ref[pl.ds(0, tokens), :] = prefill_ref[...]
    out_ref[pl.ds(tokens, slots), :] = join([decode_part(ref, slots) for ref in decodes])[0]


def finish(prefill, decodes, slots):
    return pl.pallas_call(
        functools.partial(finish_kernel, slots),
        in_specs=[VMEM] * (1 + len(decodes)),
        out_specs=VMEM,
        out_shape=pltpu.VMEM((prefill.shape[0] + slots, QW), BF16),
        compiler_params=pltpu.CompilerParams(vmem_limit_bytes=16 << 20),
        name="finish",
    )(prefill, *decodes)


def update_kernel(tokens, sets, off_ref, cache_hbm, near_ref, beside_ref, *refs):
    tables, (out_ref, cache_ref, sem) = refs[:KEY_SET], refs[-3:]
    load = pltpu.make_async_copy(cache_hbm.at[0], cache_ref, sem)
    load.start()
    ctx = cache_ref.shape[0]
    me = lax.axis_index(BLK)
    rows = [t[pl.ds(ctx, tokens), :] for t in tables]
    rows = jnp.concatenate(rows + [near_ref[...], beside_ref[...]], axis=0)
    count = rows.shape[0]
    index = lax.broadcasted_iota(jnp.int32, (1, count), 1)
    block = index // tokens
    half = sets * KEY_SET // 2
    far = block - KEY_SET
    inner = far % half
    distance = KEY_SET * (1 + inner % sets) + 2 * (inner // sets) + far // half
    token = (me ^ jnp.where(block < KEY_SET, block, distance)) * tokens + index % tokens
    wanted = me * ctx + lax.broadcasted_iota(jnp.int32, (ctx, 1), 0) - off_ref[:1, :1]
    picked = dot(jnp.where(wanted == token, 1.0, 0.0).astype(BF16), rows).astype(BF16)
    inside = jnp.broadcast_to((wanted >= 0) & (wanted < count), cache_ref.shape)
    load.wait()
    out_ref[0] = jnp.where(inside, picked, cache_ref[...])


def update_cache(offset, cache, near, beside, tables, tokens, sets):
    return pl.pallas_call(
        functools.partial(update_kernel, tokens, sets),
        in_specs=[VMEM, HBM] + [VMEM] * (2 + len(tables)),
        out_specs=VMEM,
        out_shape=jax.ShapeDtypeStruct(cache.shape, BF16),
        scratch_shapes=[pltpu.VMEM(cache.shape[1:], BF16), pltpu.SemaphoreType.DMA],
        compiler_params=pltpu.CompilerParams(vmem_limit_bytes=16 << 20),
        name="update_cache",
    )(offset, pltpu.with_memory_space_constraint(cache, pltpu.HBM), near, beside, *tables)


def route_kernel(count, route_ref, *refs):
    held, (pre_ref, dec_ref) = refs[:-2], refs[-2:]
    if len(held) < count:
        held = [held[0].at[j] for j in range(count)]
    tokens, slots = pre_ref.shape[1], dec_ref.shape[0]
    prefill = jnp.zeros(pre_ref.shape[1:], F32)
    decode = jnp.zeros(dec_ref.shape, F32)
    for j in range(count):
        flag = route_ref[j, pl.ds(slots, 1), pl.ds(0, 1)]
        prefill += flag * held[j][pl.ds(0, tokens), :].astype(F32)
        chosen = route_ref[j, pl.ds(0, slots), pl.ds(0, slots)].astype(BF16)
        decode += dot(chosen, held[j][pl.ds(tokens, slots), :])
    pre_ref[0] = prefill.astype(BF16)
    dec_ref[...] = decode.astype(BF16)


def route_outputs(route, held, tokens, slots):
    return pl.pallas_call(
        functools.partial(route_kernel, route.shape[0]),
        in_specs=[VMEM] * (1 + len(held)),
        out_specs=[VMEM] * 2,
        out_shape=[
            jax.ShapeDtypeStruct((1, tokens, QW), BF16),
            jax.ShapeDtypeStruct((slots, QW), BF16),
        ],
        compiler_params=pltpu.CompilerParams(vmem_limit_bytes=16 << 20),
        name="route_outputs",
    )(route, *held)


def per_device(
    prefill_queries,
    decode_queries,
    new_prefill,
    new_decode,
    prefill_cache,
    decode_cache,
    prefill_offsets,
    decode_lengths,
    dealing,
):
    blk = lax.axis_size(BLK)
    req = lax.axis_size("req")
    ctx = prefill_cache.shape[1]
    tokens = prefill_queries.shape[1]
    slots = decode_cache.shape[0]

    def swap(array, distance):
        return lax.ppermute(array, BLK, [(i, i ^ distance) for i in range(blk)])

    def after(array, *marks):
        return lax.optimization_barrier((array, *marks))[0]

    others = range(KEY_SET, blk, KEY_SET)
    table = jnp.concatenate([prefill_cache[0], new_prefill[0]], axis=0)
    lanes = [table] + [swap(table, k) for k in range(2, KEY_SET, 2)]
    packs = [swap(prefill_queries[0], k) for k in others]

    decode_cache_out, part, queries, route = decode_partials(
        decode_lengths,
        dealing,
        decode_queries,
        new_decode,
        decode_cache,
        prefill_queries,
        new_prefill,
        req,
    )
    far = [swap(part, k) for k in others]
    offset = jnp.full((8, HEAD_SIZE), prefill_offsets[0], jnp.int32)
    lanes[2], offset, _ = lax.optimization_barrier((lanes[2], offset, part))
    lanes[3], far, _ = lax.optimization_barrier((lanes[3], far, lanes[2]))
    lanes[1], packs, _ = lax.optimization_barrier((lanes[1], packs, lanes[2]))
    part = join_step([part] + far, [], slots, "join_far")
    tables = [t for lane in lanes for t in (lane, swap(lane, 1))]
    beside = swap(part, 1)

    sent = prefill_partials(offset, packs, tables, ctx, [k // KEY_SET for k in others])
    arrived = [swap(p, k) for k, p in zip(others, sent)]
    queries = after(queries, sent[0])
    kept = prefill_partials(offset, [queries], tables, ctx, [0])
    part = join_step([part, after(beside, sent[0])], far, slots, "join_core")
    around = [part] + [swap(part, k) for k in range(2, KEY_SET, 2)]
    attended = join_parts([*kept] + arrived)
    attended = finish(attended, around, slots)
    around[0], attended = lax.optimization_barrier((around[0], attended))
    news = jnp.concatenate([after(a, attended)[PART_ROWS * slots :] for a in around], axis=0)
    prefill_cache_out = update_cache(offset, prefill_cache, news, swap(news, 1), tables, tokens, len(others))

    if req == 2:
        held = [attended, lax.ppermute(attended, "req", [(0, 1), (1, 0)])]
    else:
        held = [lax.all_gather(attended, "req", axis=0)]
    held[-1], prefill_cache_out = lax.optimization_barrier((held[-1], prefill_cache_out))
    prefill_out, decode_out = route_outputs(route, held, tokens, slots)
    return (prefill_out, decode_out, prefill_cache_out, decode_cache_out)


def solution(mesh):
    blk, req = mesh.shape["blk"], mesh.shape["req"]
    mesh = jax.sharding.Mesh(mesh.devices.reshape(blk // QUAD, QUAD, req), ("hi", "quad", "req"))
    in_specs = (
        P("req", BLK, None),
        P("req", None),
        P("req", BLK, None),
        P("req", None),
        P("req", BLK, None),
        P("req", BLK, None),
        P("req"),
        P("req"),
        P(),
    )
    out_specs = (
        P("req", BLK, None),
        P("req", None),
        P("req", BLK, None),
        P("req", BLK, None),
    )
    return jax.shard_map(
        per_device, mesh=mesh, in_specs=in_specs, out_specs=out_specs, check_vma=False
    )
```

```python
import functools

import jax
import jax.numpy as jnp
from jax import lax
from jax.experimental import pallas as pl
from jax.experimental.pallas import tpu as pltpu
from jax.sharding import PartitionSpec as P

QUERY_HEADS = 8
KEY_VALUE_HEADS = 2
HEAD_SIZE = 128
GROUP = QUERY_HEADS // KEY_VALUE_HEADS
QW = QUERY_HEADS * HEAD_SIZE
KW = KEY_VALUE_HEADS * HEAD_SIZE
STATS = 128
QUAD = 4
KEY_SET = 8
PART_ROWS = KEY_VALUE_HEADS + 1
SCALE = HEAD_SIZE**-0.5
MASKED = -1e30
FLOOR = -1e20
F32 = jnp.float32
BF16 = jnp.bfloat16

KVW = 2 * KW
BLK = ("hi", "quad")
CHUNKS = 4
TILE = 16

HBM = pl.BlockSpec(memory_space=pltpu.HBM)
VMEM = pl.BlockSpec(memory_space=pltpu.VMEM)


def dot_t(a, b):
    return lax.dot_general(a, b, (((1,), (1,)), ((), ())), preferred_element_type=F32)


def dot(a, b):
    return lax.dot_general(a, b, (((1,), (0,)), ((), ())), preferred_element_type=F32)


def split3(value):
    high = value.astype(BF16).astype(F32)
    rest = value - high
    middle = rest.astype(BF16).astype(F32)
    return high, middle, rest - middle


def stats_block(columns, rows):
    lane = lax.broadcasted_iota(jnp.int32, (rows, STATS), 1)
    count = len(columns)
    out = jnp.zeros((rows, STATS), F32)
    for head, column in enumerate(columns):
        for term, part in enumerate(split3(column)):
            out = jnp.where(lane == term * count + head, part, out)
    return out.astype(BF16)


def spread_matrix(heads):
    lane = lax.broadcasted_iota(jnp.int32, (STATS, heads * HEAD_SIZE), 0)
    head = lax.broadcasted_iota(jnp.int32, (STATS, heads * HEAD_SIZE), 1) // HEAD_SIZE
    hit = (lane == head) | (lane == head + heads) | (lane == head + 2 * heads)
    return jnp.where(hit, 1.0, 0.0).astype(BF16)


def join(parts):
    spread = spread_matrix(QUERY_HEADS)
    logs = [dot(part[:, QW:], spread) for part in parts]
    top = functools.reduce(jnp.maximum, logs)
    scales = [jnp.exp(log - top) for log in logs]
    total = functools.reduce(jnp.add, scales)
    summed = functools.reduce(
        jnp.add, [scale * part[:, :QW].astype(F32) for scale, part in zip(scales, parts)]
    )
    return (summed / total).astype(BF16), top + jnp.log(total)


def source_group(j):
    return lax.axis_index("req") ^ j if lax.axis_size("req") == 2 else j


def decode_kernel(
    len_hbm,
    deal_hbm,
    q_hbm,
    new_hbm,
    cache_hbm,
    pre_q_hbm,
    pre_new_hbm,
    out_hbm,
    part_ref,
    pre_q_ref,
    route_ref,
    lens,
    deal,
    query_ref,
    new_ref,
    table,
    sems,
):
    slots, ctx, _ = table.shape
    rows = GROUP * slots
    chunk = slots // CHUNKS
    base = lax.axis_index(BLK) * ctx
    small = [
        (len_hbm, lens),
        (deal_hbm, deal),
        (q_hbm, query_ref),
        (new_hbm, new_ref),
        (pre_q_hbm.at[0], pre_q_ref),
        (pre_new_hbm.at[0], part_ref.at[pl.ds(PART_ROWS * slots, pre_new_hbm.shape[1]), :]),
    ]
    small = [pltpu.make_async_copy(a, b, sems.at[i]) for i, (a, b) in enumerate(small)]
    loads, stores = [], []
    for c in range(CHUNKS):
        part = pl.ds(c * chunk, chunk)
        loads.append(pltpu.make_async_copy(cache_hbm.at[part], table.at[part], sems.at[6 + c]))
        stores.append(pltpu.make_async_copy(table.at[part], out_hbm.at[part], sems.at[6 + CHUNKS + c]))
    for copy in small + loads:
        copy.start()
    for copy in small:
        copy.wait()
    group = lax.axis_index("req")
    req = route_ref.shape[0]
    out_row = lax.broadcasted_iota(jnp.int32, (slots, HEAD_SIZE), 0)
    out_lane = lax.broadcasted_iota(jnp.int32, (slots, HEAD_SIZE), 1)
    for j in range(req):
        source = source_group(j)
        chosen = jnp.zeros((slots, HEAD_SIZE), F32)
        for s in range(slots):
            place = deal[req + source * slots + s] - group * slots
            chosen = jnp.where((out_lane == s) & (out_row == place), 1.0, chosen)
        route_ref[j, pl.ds(0, slots), :] = chosen
        mine = (deal[source] == group).astype(F32)
        route_ref[j, pl.ds(slots, 8), :] = jnp.full((8, HEAD_SIZE), mine, F32)
    row_slot = lax.broadcasted_iota(jnp.int32, (rows, ctx), 0) % slots
    column = lax.broadcasted_iota(jnp.int32, (rows, ctx), 1)
    in_tile = lax.broadcasted_iota(jnp.int32, (TILE, KVW), 0)
    limit = jnp.full((rows, ctx), -1, jnp.int32)
    queries = [
        jnp.concatenate(
            [query_ref[:, pl.ds((g * GROUP + h) * HEAD_SIZE, HEAD_SIZE)] for h in range(GROUP)], axis=0
        )
        for g in range(KEY_VALUE_HEADS)
    ]
    scores = [jnp.zeros((rows, ctx), F32) for _ in range(KEY_VALUE_HEADS)]
    for c in range(CHUNKS):
        loads[c].wait()
        for s in range(c * chunk, (c + 1) * chunk):
            relative = lens[s] - base
            limit = jnp.where(row_slot == s, relative, limit)

            @pl.when((relative >= 0) & (relative < ctx))
            def _():
                start = pl.multiple_of(relative // TILE * TILE, TILE)
                tile = table[s, pl.ds(start, TILE), :]
                table[s, pl.ds(start, TILE), :] = jnp.where(
                    in_tile == relative - start, new_ref[s : s + 1, :], tile
                )

        stores[c].start()
        for g in range(KEY_VALUE_HEADS):
            key = table[pl.ds(c * chunk, chunk), :, pl.ds(g * HEAD_SIZE, HEAD_SIZE)]
            wide = dot_t(queries[g], key.reshape(chunk * ctx, HEAD_SIZE))
            for s in range(chunk):
                part = wide[:, s * ctx : (s + 1) * ctx]
                scores[g] = jnp.where(row_slot == c * chunk + s, part, scores[g])
    visible = column <= limit
    columns = []
    for g in range(KEY_VALUE_HEADS):
        masked = jnp.where(visible, scores[g] * SCALE, MASKED)
        maxima = jnp.maximum(jnp.max(masked, axis=1, keepdims=True), FLOOR)
        weights = jnp.exp(masked - maxima)
        totals = jnp.sum(weights, axis=1, keepdims=True)
        summed = jnp.zeros((rows, HEAD_SIZE), F32)
        for c in range(CHUNKS):
            value = table[pl.ds(c * chunk, chunk), :, pl.ds(KW + g * HEAD_SIZE, HEAD_SIZE)]
            picked = [jnp.where(row_slot == c * chunk + s, weights, 0.0) for s in range(chunk)]
            picked = jnp.concatenate(picked, axis=1).astype(BF16)
            summed += dot(picked, value.reshape(chunk * ctx, HEAD_SIZE))
        seen = totals > 0.0
        safe = jnp.where(seen, totals, 1.0)
        normed = (summed / safe).astype(BF16)
        logs = jnp.where(seen, maxima + jnp.log(safe), MASKED)
        for h in range(GROUP):
            part = slice(h * slots, (h + 1) * slots)
            part_ref[pl.ds(g * slots, slots), pl.ds(h * HEAD_SIZE, HEAD_SIZE)] = normed[part]
            columns.append(logs[part])
    put_stats(part_ref, columns, slots)
    for copy in stores:
        copy.wait()


def decode_partials(lengths, dealing, queries, new_rows, cache, pre_queries, pre_new, req):
    slots, ctx, width = cache.shape
    inputs = (lengths, dealing, queries, new_rows, cache, pre_queries, pre_new)
    return pl.pallas_call(
        decode_kernel,
        in_specs=[HBM] * len(inputs),
        out_specs=[HBM, VMEM, VMEM, VMEM],
        out_shape=[
            pltpu.HBM(cache.shape, BF16),
            pltpu.VMEM((PART_ROWS * slots + pre_new.shape[1], KVW), BF16),
            pltpu.VMEM(pre_queries.shape[1:], BF16),
            pltpu.VMEM((req, slots + 8, HEAD_SIZE), F32),
        ],
        scratch_shapes=[
            pltpu.SMEM(lengths.shape, jnp.int32),
            pltpu.SMEM(dealing.shape, jnp.int32),
            pltpu.VMEM(queries.shape, BF16),
            pltpu.VMEM(new_rows.shape, BF16),
            pltpu.VMEM(cache.shape, BF16),
            pltpu.SemaphoreType.DMA((6 + 2 * CHUNKS,)),
        ],
        compiler_params=pltpu.CompilerParams(vmem_limit_bytes=16 << 20),
        cost_estimate=pl.CostEstimate(
            flops=4 * slots * ctx * QW, bytes_accessed=2 * cache.size * 2, transcendentals=slots * ctx * 8
        ),
        name="decode_partials",
    )(*[pltpu.with_memory_space_constraint(x, pltpu.HBM) for x in inputs])


def put_stats(ref, columns, slots):
    last = pl.ds(KEY_VALUE_HEADS * slots, slots)
    ref[last, pl.ds(0, STATS)] = stats_block(columns, slots)
    ref[last, pl.ds(STATS, KVW - STATS)] = jnp.zeros((slots, KVW - STATS), BF16)


def decode_part(ref, slots):
    blocks = [ref[pl.ds(g * slots, slots), :] for g in range(KEY_VALUE_HEADS)]
    return jnp.concatenate(blocks + [ref[pl.ds(KEY_VALUE_HEADS * slots, slots), pl.ds(0, STATS)]], axis=1)


def step_kernel(slots, count, *refs):
    out_ref = refs[-1]
    joined, logs = join([decode_part(ref, slots) for ref in refs[:count]])
    head = PART_ROWS * slots
    for g in range(KEY_VALUE_HEADS):
        out_ref[pl.ds(g * slots, slots), :] = joined[:, g * KVW : (g + 1) * KVW]
    put_stats(out_ref, [logs[:, h * HEAD_SIZE : h * HEAD_SIZE + 1] for h in range(QUERY_HEADS)], slots)
    at = head
    for ref in refs[count:-1]:
        rest = ref.shape[0] - head
        out_ref[pl.ds(at, rest), :] = ref[pl.ds(head, rest), :]
        at += rest


def join_step(parts, carriers, slots, name):
    head = PART_ROWS * slots
    rows = head + sum(c.shape[0] - head for c in carriers)
    return pl.pallas_call(
        functools.partial(step_kernel, slots, len(parts)),
        in_specs=[VMEM] * (len(parts) + len(carriers)),
        out_specs=VMEM,
        out_shape=pltpu.VMEM((rows, KVW), BF16),
        compiler_params=pltpu.CompilerParams(vmem_limit_bytes=16 << 20),
        name=name,
    )(*parts, *carriers)


def prefill_kernel(sets, ctx, off_ref, *refs):
    query_count = len(sets)
    packs, tables, outs = refs[:query_count], refs[query_count:-query_count], refs[-query_count:]
    tokens = packs[0].shape[0]
    span = ctx + tokens
    me = lax.axis_index(BLK)
    offset = off_ref[:1, :1]
    pieces = []
    for k in range(KEY_SET):
        holder = me ^ k
        index = lax.broadcasted_iota(jnp.int32, (1, span), 1)
        old = jnp.where(holder * ctx + index < offset, -1, 1 << 30)
        pieces.append(jnp.where(index < ctx, old, holder * tokens + index - ctx))
    key_mark = jnp.concatenate(pieces, axis=1)
    in_block = lax.broadcasted_iota(jnp.int32, (GROUP * tokens, 1), 0) % tokens
    lane = lax.broadcasted_iota(jnp.int32, (tokens, STATS), 1)
    stats = [jnp.zeros((tokens, STATS), F32) for _ in range(query_count)]
    for g in range(KEY_VALUE_HEADS):
        keys = jnp.concatenate([t[:, pl.ds(g * HEAD_SIZE, HEAD_SIZE)] for t in tables], axis=0)
        values = jnp.concatenate([t[:, pl.ds(KW + g * HEAD_SIZE, HEAD_SIZE)] for t in tables], axis=0)
        for k in range(query_count):
            token = (me ^ (sets[k] * KEY_SET)) * tokens + in_block
            query = jnp.concatenate(
                [packs[k][:, pl.ds((g * GROUP + h) * HEAD_SIZE, HEAD_SIZE)] for h in range(GROUP)], axis=0
            )
            scores = jnp.where(key_mark <= token, dot_t(query, keys) * SCALE, MASKED)
            maxima = jnp.maximum(jnp.max(scores, axis=1, keepdims=True), FLOOR)
            weights = jnp.exp(scores - maxima)
            totals = jnp.sum(weights, axis=1, keepdims=True)
            summed = dot(weights.astype(BF16), values)
            seen = totals > 0.0
            safe = jnp.where(seen, totals, 1.0)
            normed = (summed / safe).astype(BF16)
            logs = jnp.where(seen, maxima + jnp.log(safe), MASKED)
            for h in range(GROUP):
                part = slice(h * tokens, (h + 1) * tokens)
                outs[k][:, pl.ds((g * GROUP + h) * HEAD_SIZE, HEAD_SIZE)] = normed[part]
                for term, value in enumerate(split3(logs[part])):
                    stats[k] = jnp.where(lane == term * QUERY_HEADS + g * GROUP + h, value, stats[k])
    for k in range(query_count):
        outs[k][:, pl.ds(QW, STATS)] = stats[k].astype(BF16)


def prefill_partials(offset, packs, tables, ctx, sets):
    tokens = packs[0].shape[0]
    pairs = len(packs) * tokens * KEY_SET * (ctx + tokens)
    return pl.pallas_call(
        functools.partial(prefill_kernel, sets, ctx),
        in_specs=[VMEM] * (1 + len(packs) + len(tables)),
        out_specs=[VMEM] * len(packs),
        out_shape=[jax.ShapeDtypeStruct((tokens, QW + STATS), BF16)] * len(packs),
        compiler_params=pltpu.CompilerParams(vmem_limit_bytes=32 << 20),
        cost_estimate=pl.CostEstimate(
            flops=4 * pairs * QW, bytes_accessed=4 << 20, transcendentals=pairs * QUERY_HEADS
        ),
        name="prefill_partials",
    )(offset, *packs, *tables)


def join_kernel(*refs):
    refs[-1][...] = join([ref[...] for ref in refs[:-1]])[0]


def join_parts(parts):
    return pl.pallas_call(
        join_kernel,
        in_specs=[VMEM] * len(parts),
        out_specs=VMEM,
        out_shape=pltpu.VMEM((parts[0].shape[0], QW), BF16),
        compiler_params=pltpu.CompilerParams(vmem_limit_bytes=16 << 20),
        name="join_parts",
    )(*parts)


def finish_kernel(slots, prefill_ref, *refs):
    decodes, out_ref = refs[:-1], refs[-1]
    tokens = prefill_ref.shape[0]
    out_ref[pl.ds(0, tokens), :] = prefill_ref[...]
    out_ref[pl.ds(tokens, slots), :] = join([decode_part(ref, slots) for ref in decodes])[0]


def finish(prefill, decodes, slots):
    return pl.pallas_call(
        functools.partial(finish_kernel, slots),
        in_specs=[VMEM] * (1 + len(decodes)),
        out_specs=VMEM,
        out_shape=pltpu.VMEM((prefill.shape[0] + slots, QW), BF16),
        compiler_params=pltpu.CompilerParams(vmem_limit_bytes=16 << 20),
        name="finish",
    )(prefill, *decodes)


def update_kernel(tokens, sets, off_ref, cache_hbm, near_ref, beside_ref, *refs):
    tables, (out_ref, cache_ref, sem) = refs[:KEY_SET], refs[-3:]
    load = pltpu.make_async_copy(cache_hbm.at[0], cache_ref, sem)
    load.start()
    ctx = cache_ref.shape[0]
    me = lax.axis_index(BLK)
    rows = [t[pl.ds(ctx, tokens), :] for t in tables]
    rows = jnp.concatenate(rows + [near_ref[...], beside_ref[...]], axis=0)
    count = rows.shape[0]
    index = lax.broadcasted_iota(jnp.int32, (1, count), 1)
    block = index // tokens
    half = sets * KEY_SET // 2
    far = block - KEY_SET
    inner = far % half
    distance = KEY_SET * (1 + inner % sets) + 2 * (inner // sets) + far // half
    token = (me ^ jnp.where(block < KEY_SET, block, distance)) * tokens + index % tokens
    wanted = me * ctx + lax.broadcasted_iota(jnp.int32, (ctx, 1), 0) - off_ref[:1, :1]
    picked = dot(jnp.where(wanted == token, 1.0, 0.0).astype(BF16), rows).astype(BF16)
    inside = jnp.broadcast_to((wanted >= 0) & (wanted < count), cache_ref.shape)
    load.wait()
    out_ref[0] = jnp.where(inside, picked, cache_ref[...])


def update_cache(offset, cache, near, beside, tables, tokens, sets):
    return pl.pallas_call(
        functools.partial(update_kernel, tokens, sets),
        in_specs=[VMEM, HBM] + [VMEM] * (2 + len(tables)),
        out_specs=VMEM,
        out_shape=jax.ShapeDtypeStruct(cache.shape, BF16),
        scratch_shapes=[pltpu.VMEM(cache.shape[1:], BF16), pltpu.SemaphoreType.DMA],
        compiler_params=pltpu.CompilerParams(vmem_limit_bytes=16 << 20),
        name="update_cache",
    )(offset, pltpu.with_memory_space_constraint(cache, pltpu.HBM), near, beside, *tables)


def route_kernel(count, route_ref, *refs):
    held, (pre_ref, dec_ref) = refs[:-2], refs[-2:]
    if len(held) < count:
        held = [held[0].at[j] for j in range(count)]
    tokens, slots = pre_ref.shape[1], dec_ref.shape[0]
    prefill = jnp.zeros(pre_ref.shape[1:], F32)
    decode = jnp.zeros(dec_ref.shape, F32)
    for j in range(count):
        flag = route_ref[j, pl.ds(slots, 1), pl.ds(0, 1)]
        prefill += flag * held[j][pl.ds(0, tokens), :].astype(F32)
        chosen = route_ref[j, pl.ds(0, slots), pl.ds(0, slots)].astype(BF16)
        decode += dot(chosen, held[j][pl.ds(tokens, slots), :])
    pre_ref[0] = prefill.astype(BF16)
    dec_ref[...] = decode.astype(BF16)


def route_outputs(route, held, tokens, slots):
    return pl.pallas_call(
        functools.partial(route_kernel, route.shape[0]),
        in_specs=[VMEM] * (1 + len(held)),
        out_specs=[VMEM] * 2,
        out_shape=[
            jax.ShapeDtypeStruct((1, tokens, QW), BF16),
            jax.ShapeDtypeStruct((slots, QW), BF16),
        ],
        compiler_params=pltpu.CompilerParams(vmem_limit_bytes=16 << 20),
        name="route_outputs",
    )(route, *held)


def per_device(
    prefill_queries,
    decode_queries,
    new_prefill,
    new_decode,
    prefill_cache,
    decode_cache,
    prefill_offsets,
    decode_lengths,
    dealing,
):
    blk = lax.axis_size(BLK)
    req = lax.axis_size("req")
    ctx = prefill_cache.shape[1]
    tokens = prefill_queries.shape[1]
    slots = decode_cache.shape[0]

    def swap(array, distance):
        return lax.ppermute(array, BLK, [(i, i ^ distance) for i in range(blk)])

    def after(array, *marks):
        return lax.optimization_barrier((array, *marks))[0]

    others = range(KEY_SET, blk, KEY_SET)
    table = jnp.concatenate([prefill_cache[0], new_prefill[0]], axis=0)
    lanes = [table] + [swap(table, k) for k in range(2, KEY_SET, 2)]
    packs = [swap(prefill_queries[0], k) for k in others]

    decode_cache_out, part, queries, route = decode_partials(
        decode_lengths,
        dealing,
        decode_queries,
        new_decode,
        decode_cache,
        prefill_queries,
        new_prefill,
        req,
    )
    far = [swap(part, k) for k in others]
    offset = jnp.full((8, HEAD_SIZE), prefill_offsets[0], jnp.int32)
    lanes[1], offset, _ = lax.optimization_barrier((lanes[1], offset, part))
    lanes[2] = after(lanes[2], lanes[1])
    lanes[3], far, packs, _ = lax.optimization_barrier((lanes[3], far, packs, lanes[2]))
    part = join_step([part] + far, [], slots, "join_far")
    tables = [t for lane in lanes for t in (lane, swap(lane, 1))]
    beside = swap(part, 1)

    sent = prefill_partials(offset, packs, tables, ctx, [k // KEY_SET for k in others])
    arrived = [swap(p, k) for k, p in zip(others, sent)]
    queries = after(queries, sent[0])
    kept = prefill_partials(offset, [queries], tables, ctx, [0])
    part = join_step([part, after(beside, sent[0])], far, slots, "join_core")
    around = [part] + [swap(part, k) for k in range(2, KEY_SET, 2)]
    attended = join_parts([*kept] + arrived)
    attended = finish(attended, around, slots)
    news = jnp.concatenate([a[PART_ROWS * slots :] for a in around], axis=0)
    prefill_cache_out = update_cache(offset, prefill_cache, news, swap(news, 1), tables, tokens, len(others))

    if req == 2:
        held = [attended, lax.ppermute(attended, "req", [(0, 1), (1, 0)])]
    else:
        held = [lax.all_gather(attended, "req", axis=0)]
    held[-1], prefill_cache_out = lax.optimization_barrier((held[-1], prefill_cache_out))
    prefill_out, decode_out = route_outputs(route, held, tokens, slots)
    return (prefill_out, decode_out, prefill_cache_out, decode_cache_out)


def solution(mesh):
    blk, req = mesh.shape["blk"], mesh.shape["req"]
    mesh = jax.sharding.Mesh(mesh.devices.reshape(blk // QUAD, QUAD, req), ("hi", "quad", "req"))
    in_specs = (
        P("req", BLK, None),
        P("req", None),
        P("req", BLK, None),
        P("req", None),
        P("req", BLK, None),
        P("req", BLK, None),
        P("req"),
        P("req"),
        P(),
    )
    out_specs = (
        P("req", BLK, None),
        P("req", None),
        P("req", BLK, None),
        P("req", BLK, None),
    )
    return jax.shard_map(
        per_device, mesh=mesh, in_specs=in_specs, out_specs=out_specs, check_vma=False
    )
```

```python
import functools

import jax
import jax.numpy as jnp
from jax import lax
from jax.experimental import pallas as pl
from jax.experimental.pallas import tpu as pltpu
from jax.sharding import PartitionSpec as P

QUERY_HEADS = 8
KEY_VALUE_HEADS = 2
HEAD_SIZE = 128
GROUP = QUERY_HEADS // KEY_VALUE_HEADS
QW = QUERY_HEADS * HEAD_SIZE
KW = KEY_VALUE_HEADS * HEAD_SIZE
STATS = 128
QUAD = 4
KEY_SET = 8
PART_ROWS = KEY_VALUE_HEADS + 1
SCALE = HEAD_SIZE**-0.5
MASKED = -1e30
FLOOR = -1e20
F32 = jnp.float32
BF16 = jnp.bfloat16

KVW = 2 * KW
BLK = ("hi", "quad")
CHUNKS = 4
TILE = 16

HBM = pl.BlockSpec(memory_space=pltpu.HBM)
VMEM = pl.BlockSpec(memory_space=pltpu.VMEM)


def dot_t(a, b):
    return lax.dot_general(a, b, (((1,), (1,)), ((), ())), preferred_element_type=F32)


def dot(a, b):
    return lax.dot_general(a, b, (((1,), (0,)), ((), ())), preferred_element_type=F32)


def split3(value):
    high = value.astype(BF16).astype(F32)
    rest = value - high
    middle = rest.astype(BF16).astype(F32)
    return high, middle, rest - middle


def stats_block(columns, rows):
    lane = lax.broadcasted_iota(jnp.int32, (rows, STATS), 1)
    count = len(columns)
    out = jnp.zeros((rows, STATS), F32)
    for head, column in enumerate(columns):
        for term, part in enumerate(split3(column)):
            out = jnp.where(lane == term * count + head, part, out)
    return out.astype(BF16)


def spread_matrix(heads):
    lane = lax.broadcasted_iota(jnp.int32, (STATS, heads * HEAD_SIZE), 0)
    head = lax.broadcasted_iota(jnp.int32, (STATS, heads * HEAD_SIZE), 1) // HEAD_SIZE
    hit = (lane == head) | (lane == head + heads) | (lane == head + 2 * heads)
    return jnp.where(hit, 1.0, 0.0).astype(BF16)


def join(parts):
    spread = spread_matrix(QUERY_HEADS)
    logs = [dot(part[:, QW:], spread) for part in parts]
    top = functools.reduce(jnp.maximum, logs)
    scales = [jnp.exp(log - top) for log in logs]
    total = functools.reduce(jnp.add, scales)
    summed = functools.reduce(
        jnp.add, [scale * part[:, :QW].astype(F32) for scale, part in zip(scales, parts)]
    )
    return (summed / total).astype(BF16), top + jnp.log(total)


def source_group(j):
    return lax.axis_index("req") ^ j if lax.axis_size("req") == 2 else j


def decode_kernel(
    len_hbm,
    deal_hbm,
    q_hbm,
    new_hbm,
    cache_hbm,
    pre_q_hbm,
    pre_new_hbm,
    out_hbm,
    part_ref,
    pre_q_ref,
    route_ref,
    lens,
    deal,
    query_ref,
    new_ref,
    table,
    sems,
):
    slots, ctx, _ = table.shape
    rows = GROUP * slots
    chunk = slots // CHUNKS
    base = lax.axis_index(BLK) * ctx
    small = [
        (len_hbm, lens),
        (deal_hbm, deal),
        (q_hbm, query_ref),
        (new_hbm, new_ref),
        (pre_q_hbm.at[0], pre_q_ref),
        (pre_new_hbm.at[0], part_ref.at[pl.ds(PART_ROWS * slots, pre_new_hbm.shape[1]), :]),
    ]
    small = [pltpu.make_async_copy(a, b, sems.at[i]) for i, (a, b) in enumerate(small)]
    loads, stores = [], []
    for c in range(CHUNKS):
        part = pl.ds(c * chunk, chunk)
        loads.append(pltpu.make_async_copy(cache_hbm.at[part], table.at[part], sems.at[6 + c]))
        stores.append(pltpu.make_async_copy(table.at[part], out_hbm.at[part], sems.at[6 + CHUNKS + c]))
    for copy in small + loads:
        copy.start()
    for copy in small:
        copy.wait()
    group = lax.axis_index("req")
    req = route_ref.shape[0]
    out_row = lax.broadcasted_iota(jnp.int32, (slots, HEAD_SIZE), 0)
    out_lane = lax.broadcasted_iota(jnp.int32, (slots, HEAD_SIZE), 1)
    for j in range(req):
        source = source_group(j)
        chosen = jnp.zeros((slots, HEAD_SIZE), F32)
        for s in range(slots):
            place = deal[req + source * slots + s] - group * slots
            chosen = jnp.where((out_lane == s) & (out_row == place), 1.0, chosen)
        route_ref[j, pl.ds(0, slots), :] = chosen
        mine = (deal[source] == group).astype(F32)
        route_ref[j, pl.ds(slots, 8), :] = jnp.full((8, HEAD_SIZE), mine, F32)
    row_slot = lax.broadcasted_iota(jnp.int32, (rows, ctx), 0) % slots
    column = lax.broadcasted_iota(jnp.int32, (rows, ctx), 1)
    in_tile = lax.broadcasted_iota(jnp.int32, (TILE, KVW), 0)
    limit = jnp.full((rows, ctx), -1, jnp.int32)
    queries = [
        jnp.concatenate(
            [query_ref[:, pl.ds((g * GROUP + h) * HEAD_SIZE, HEAD_SIZE)] for h in range(GROUP)], axis=0
        )
        for g in range(KEY_VALUE_HEADS)
    ]
    scores = [jnp.zeros((rows, ctx), F32) for _ in range(KEY_VALUE_HEADS)]
    for c in range(CHUNKS):
        loads[c].wait()
        for s in range(c * chunk, (c + 1) * chunk):
            relative = lens[s] - base
            limit = jnp.where(row_slot == s, relative, limit)

            @pl.when((relative >= 0) & (relative < ctx))
            def _():
                start = pl.multiple_of(relative // TILE * TILE, TILE)
                tile = table[s, pl.ds(start, TILE), :]
                table[s, pl.ds(start, TILE), :] = jnp.where(
                    in_tile == relative - start, new_ref[s : s + 1, :], tile
                )

        stores[c].start()
        for g in range(KEY_VALUE_HEADS):
            key = table[pl.ds(c * chunk, chunk), :, pl.ds(g * HEAD_SIZE, HEAD_SIZE)]
            wide = dot_t(queries[g], key.reshape(chunk * ctx, HEAD_SIZE))
            for s in range(chunk):
                part = wide[:, s * ctx : (s + 1) * ctx]
                scores[g] = jnp.where(row_slot == c * chunk + s, part, scores[g])
    visible = column <= limit
    columns = []
    for g in range(KEY_VALUE_HEADS):
        masked = jnp.where(visible, scores[g] * SCALE, MASKED)
        maxima = jnp.maximum(jnp.max(masked, axis=1, keepdims=True), FLOOR)
        weights = jnp.exp(masked - maxima)
        totals = jnp.sum(weights, axis=1, keepdims=True)
        summed = jnp.zeros((rows, HEAD_SIZE), F32)
        for c in range(CHUNKS):
            value = table[pl.ds(c * chunk, chunk), :, pl.ds(KW + g * HEAD_SIZE, HEAD_SIZE)]
            picked = [jnp.where(row_slot == c * chunk + s, weights, 0.0) for s in range(chunk)]
            picked = jnp.concatenate(picked, axis=1).astype(BF16)
            summed += dot(picked, value.reshape(chunk * ctx, HEAD_SIZE))
        seen = totals > 0.0
        safe = jnp.where(seen, totals, 1.0)
        normed = (summed / safe).astype(BF16)
        logs = jnp.where(seen, maxima + jnp.log(safe), MASKED)
        for h in range(GROUP):
            part = slice(h * slots, (h + 1) * slots)
            part_ref[pl.ds(g * slots, slots), pl.ds(h * HEAD_SIZE, HEAD_SIZE)] = normed[part]
            columns.append(logs[part])
    put_stats(part_ref, columns, slots)
    for copy in stores:
        copy.wait()


def decode_partials(lengths, dealing, queries, new_rows, cache, pre_queries, pre_new, req):
    slots, ctx, width = cache.shape
    inputs = (lengths, dealing, queries, new_rows, cache, pre_queries, pre_new)
    return pl.pallas_call(
        decode_kernel,
        in_specs=[HBM] * len(inputs),
        out_specs=[HBM, VMEM, VMEM, VMEM],
        out_shape=[
            pltpu.HBM(cache.shape, BF16),
            pltpu.VMEM((PART_ROWS * slots + pre_new.shape[1], KVW), BF16),
            pltpu.VMEM(pre_queries.shape[1:], BF16),
            pltpu.VMEM((req, slots + 8, HEAD_SIZE), F32),
        ],
        scratch_shapes=[
            pltpu.SMEM(lengths.shape, jnp.int32),
            pltpu.SMEM(dealing.shape, jnp.int32),
            pltpu.VMEM(queries.shape, BF16),
            pltpu.VMEM(new_rows.shape, BF16),
            pltpu.VMEM(cache.shape, BF16),
            pltpu.SemaphoreType.DMA((6 + 2 * CHUNKS,)),
        ],
        compiler_params=pltpu.CompilerParams(vmem_limit_bytes=16 << 20),
        cost_estimate=pl.CostEstimate(
            flops=4 * slots * ctx * QW, bytes_accessed=2 * cache.size * 2, transcendentals=slots * ctx * 8
        ),
        name="decode_partials",
    )(*[pltpu.with_memory_space_constraint(x, pltpu.HBM) for x in inputs])


def put_stats(ref, columns, slots):
    last = pl.ds(KEY_VALUE_HEADS * slots, slots)
    ref[last, pl.ds(0, STATS)] = stats_block(columns, slots)
    ref[last, pl.ds(STATS, KVW - STATS)] = jnp.zeros((slots, KVW - STATS), BF16)


def decode_part(ref, slots):
    blocks = [ref[pl.ds(g * slots, slots), :] for g in range(KEY_VALUE_HEADS)]
    return jnp.concatenate(blocks + [ref[pl.ds(KEY_VALUE_HEADS * slots, slots), pl.ds(0, STATS)]], axis=1)


def step_kernel(slots, count, *refs):
    out_ref = refs[-1]
    joined, logs = join([decode_part(ref, slots) for ref in refs[:count]])
    head = PART_ROWS * slots
    for g in range(KEY_VALUE_HEADS):
        out_ref[pl.ds(g * slots, slots), :] = joined[:, g * KVW : (g + 1) * KVW]
    put_stats(out_ref, [logs[:, h * HEAD_SIZE : h * HEAD_SIZE + 1] for h in range(QUERY_HEADS)], slots)
    at = head
    for ref in refs[count:-1]:
        rest = ref.shape[0] - head
        out_ref[pl.ds(at, rest), :] = ref[pl.ds(head, rest), :]
        at += rest


def join_step(parts, carriers, slots, name):
    head = PART_ROWS * slots
    rows = head + sum(c.shape[0] - head for c in carriers)
    return pl.pallas_call(
        functools.partial(step_kernel, slots, len(parts)),
        in_specs=[VMEM] * (len(parts) + len(carriers)),
        out_specs=VMEM,
        out_shape=pltpu.VMEM((rows, KVW), BF16),
        compiler_params=pltpu.CompilerParams(vmem_limit_bytes=16 << 20),
        name=name,
    )(*parts, *carriers)


def prefill_kernel(sets, ctx, off_ref, *refs):
    query_count = len(sets)
    packs, tables, outs = refs[:query_count], refs[query_count:-query_count], refs[-query_count:]
    tokens = packs[0].shape[0]
    span = ctx + tokens
    me = lax.axis_index(BLK)
    offset = off_ref[:1, :1]
    pieces = []
    for k in range(KEY_SET):
        holder = me ^ k
        index = lax.broadcasted_iota(jnp.int32, (1, span), 1)
        old = jnp.where(holder * ctx + index < offset, -1, 1 << 30)
        pieces.append(jnp.where(index < ctx, old, holder * tokens + index - ctx))
    key_mark = jnp.concatenate(pieces, axis=1)
    in_block = lax.broadcasted_iota(jnp.int32, (GROUP * tokens, 1), 0) % tokens
    lane = lax.broadcasted_iota(jnp.int32, (tokens, STATS), 1)
    stats = [jnp.zeros((tokens, STATS), F32) for _ in range(query_count)]
    for g in range(KEY_VALUE_HEADS):
        keys = jnp.concatenate([t[:, pl.ds(g * HEAD_SIZE, HEAD_SIZE)] for t in tables], axis=0)
        values = jnp.concatenate([t[:, pl.ds(KW + g * HEAD_SIZE, HEAD_SIZE)] for t in tables], axis=0)
        for k in range(query_count):
            token = (me ^ (sets[k] * KEY_SET)) * tokens + in_block
            query = jnp.concatenate(
                [packs[k][:, pl.ds((g * GROUP + h) * HEAD_SIZE, HEAD_SIZE)] for h in range(GROUP)], axis=0
            )
            scores = jnp.where(key_mark <= token, dot_t(query, keys) * SCALE, MASKED)
            maxima = jnp.maximum(jnp.max(scores, axis=1, keepdims=True), FLOOR)
            weights = jnp.exp(scores - maxima)
            totals = jnp.sum(weights, axis=1, keepdims=True)
            summed = dot(weights.astype(BF16), values)
            seen = totals > 0.0
            safe = jnp.where(seen, totals, 1.0)
            normed = (summed / safe).astype(BF16)
            logs = jnp.where(seen, maxima + jnp.log(safe), MASKED)
            for h in range(GROUP):
                part = slice(h * tokens, (h + 1) * tokens)
                outs[k][:, pl.ds((g * GROUP + h) * HEAD_SIZE, HEAD_SIZE)] = normed[part]
                for term, value in enumerate(split3(logs[part])):
                    stats[k] = jnp.where(lane == term * QUERY_HEADS + g * GROUP + h, value, stats[k])
    for k in range(query_count):
        outs[k][:, pl.ds(QW, STATS)] = stats[k].astype(BF16)


def prefill_partials(offset, packs, tables, ctx, sets):
    tokens = packs[0].shape[0]
    pairs = len(packs) * tokens * KEY_SET * (ctx + tokens)
    return pl.pallas_call(
        functools.partial(prefill_kernel, sets, ctx),
        in_specs=[VMEM] * (1 + len(packs) + len(tables)),
        out_specs=[VMEM] * len(packs),
        out_shape=[jax.ShapeDtypeStruct((tokens, QW + STATS), BF16)] * len(packs),
        compiler_params=pltpu.CompilerParams(vmem_limit_bytes=32 << 20),
        cost_estimate=pl.CostEstimate(
            flops=4 * pairs * QW, bytes_accessed=4 << 20, transcendentals=pairs * QUERY_HEADS
        ),
        name="prefill_partials",
    )(offset, *packs, *tables)


def join_kernel(count, slots, *refs):
    parts, decodes, out_ref = refs[:count], refs[count:-1], refs[-1]
    tokens = parts[0].shape[0]
    out_ref[pl.ds(0, tokens), :] = join([ref[...] for ref in parts])[0]
    out_ref[pl.ds(tokens, slots), :] = join([decode_part(ref, slots) for ref in decodes])[0]


def join_parts(parts, decodes, slots):
    return pl.pallas_call(
        functools.partial(join_kernel, len(parts), slots),
        in_specs=[VMEM] * (len(parts) + len(decodes)),
        out_specs=VMEM,
        out_shape=pltpu.VMEM((parts[0].shape[0] + slots, QW), BF16),
        compiler_params=pltpu.CompilerParams(vmem_limit_bytes=16 << 20),
        name="join_parts",
    )(*parts, *decodes)


def update_kernel(tokens, sets, off_ref, cache_hbm, near_ref, beside_ref, *refs):
    tables, (out_ref, cache_ref, sem) = refs[:KEY_SET], refs[-3:]
    load = pltpu.make_async_copy(cache_hbm.at[0], cache_ref, sem)
    load.start()
    ctx = cache_ref.shape[0]
    me = lax.axis_index(BLK)
    rows = [t[pl.ds(ctx, tokens), :] for t in tables]
    rows = jnp.concatenate(rows + [near_ref[...], beside_ref[...]], axis=0)
    count = rows.shape[0]
    index = lax.broadcasted_iota(jnp.int32, (1, count), 1)
    block = index // tokens
    half = sets * KEY_SET // 2
    far = block - KEY_SET
    inner = far % half
    distance = KEY_SET * (1 + inner % sets) + 2 * (inner // sets) + far // half
    token = (me ^ jnp.where(block < KEY_SET, block, distance)) * tokens + index % tokens
    wanted = me * ctx + lax.broadcasted_iota(jnp.int32, (ctx, 1), 0) - off_ref[:1, :1]
    picked = dot(jnp.where(wanted == token, 1.0, 0.0).astype(BF16), rows).astype(BF16)
    inside = jnp.broadcast_to((wanted >= 0) & (wanted < count), cache_ref.shape)
    load.wait()
    out_ref[0] = jnp.where(inside, picked, cache_ref[...])


def update_cache(offset, cache, near, beside, tables, tokens, sets):
    return pl.pallas_call(
        functools.partial(update_kernel, tokens, sets),
        in_specs=[VMEM, HBM] + [VMEM] * (2 + len(tables)),
        out_specs=VMEM,
        out_shape=jax.ShapeDtypeStruct(cache.shape, BF16),
        scratch_shapes=[pltpu.VMEM(cache.shape[1:], BF16), pltpu.SemaphoreType.DMA],
        compiler_params=pltpu.CompilerParams(vmem_limit_bytes=16 << 20),
        name="update_cache",
    )(offset, pltpu.with_memory_space_constraint(cache, pltpu.HBM), near, beside, *tables)


def route_kernel(count, route_ref, *refs):
    held, (pre_ref, dec_ref) = refs[:-2], refs[-2:]
    if len(held) < count:
        held = [held[0].at[j] for j in range(count)]
    tokens, slots = pre_ref.shape[1], dec_ref.shape[0]
    prefill = jnp.zeros(pre_ref.shape[1:], F32)
    decode = jnp.zeros(dec_ref.shape, F32)
    for j in range(count):
        flag = route_ref[j, pl.ds(slots, 1), pl.ds(0, 1)]
        prefill += flag * held[j][pl.ds(0, tokens), :].astype(F32)
        chosen = route_ref[j, pl.ds(0, slots), pl.ds(0, slots)].astype(BF16)
        decode += dot(chosen, held[j][pl.ds(tokens, slots), :])
    pre_ref[0] = prefill.astype(BF16)
    dec_ref[...] = decode.astype(BF16)


def route_outputs(route, held, tokens, slots):
    return pl.pallas_call(
        functools.partial(route_kernel, route.shape[0]),
        in_specs=[VMEM] * (1 + len(held)),
        out_specs=[VMEM] * 2,
        out_shape=[
            jax.ShapeDtypeStruct((1, tokens, QW), BF16),
            jax.ShapeDtypeStruct((slots, QW), BF16),
        ],
        compiler_params=pltpu.CompilerParams(vmem_limit_bytes=16 << 20),
        name="route_outputs",
    )(route, *held)


def per_device(
    prefill_queries,
    decode_queries,
    new_prefill,
    new_decode,
    prefill_cache,
    decode_cache,
    prefill_offsets,
    decode_lengths,
    dealing,
):
    blk = lax.axis_size(BLK)
    req = lax.axis_size("req")
    ctx = prefill_cache.shape[1]
    tokens = prefill_queries.shape[1]
    slots = decode_cache.shape[0]

    def swap(array, distance):
        return lax.ppermute(array, BLK, [(i, i ^ distance) for i in range(blk)])

    def after(array, *marks):
        return lax.optimization_barrier((array, *marks))[0]

    others = range(KEY_SET, blk, KEY_SET)
    table = jnp.concatenate([prefill_cache[0], new_prefill[0]], axis=0)
    lanes = [table] + [swap(table, k) for k in range(2, KEY_SET, 2)]
    packs = [swap(prefill_queries[0], k) for k in others]

    decode_cache_out, part, queries, route = decode_partials(
        decode_lengths,
        dealing,
        decode_queries,
        new_decode,
        decode_cache,
        prefill_queries,
        new_prefill,
        req,
    )
    far = [swap(part, k) for k in others]
    offset = jnp.full((8, HEAD_SIZE), prefill_offsets[0], jnp.int32)
    lanes[2], offset, _ = lax.optimization_barrier((lanes[2], offset, part))
    lanes[3], far, _ = lax.optimization_barrier((lanes[3], far, lanes[2]))
    lanes[1], packs, _ = lax.optimization_barrier((lanes[1], packs, lanes[2]))
    part = join_step([part] + far, [], slots, "join_far")
    tables = [t for lane in lanes for t in (lane, swap(lane, 1))]
    beside = swap(part, 1)

    sent = prefill_partials(offset, packs, tables, ctx, [k // KEY_SET for k in others])
    arrived = [swap(p, k) for k, p in zip(others, sent)]
    queries = after(queries, sent[0])
    kept = prefill_partials(offset, [queries], tables, ctx, [0])
    part = join_step([part, after(beside, sent[0])], far, slots, "join_core")
    around = [part] + [swap(part, k) for k in range(2, KEY_SET, 2)]
    attended = join_parts([*kept] + arrived, around, slots)
    news = jnp.concatenate([a[PART_ROWS * slots :] for a in around], axis=0)
    prefill_cache_out = update_cache(offset, prefill_cache, news, swap(news, 1), tables, tokens, len(others))

    if req == 2:
        held = [attended, lax.ppermute(attended, "req", [(0, 1), (1, 0)])]
    else:
        held = [lax.all_gather(attended, "req", axis=0)]
    held[-1], prefill_cache_out = lax.optimization_barrier((held[-1], prefill_cache_out))
    prefill_out, decode_out = route_outputs(route, held, tokens, slots)
    return (prefill_out, decode_out, prefill_cache_out, decode_cache_out)


def solution(mesh):
    blk, req = mesh.shape["blk"], mesh.shape["req"]
    mesh = jax.sharding.Mesh(mesh.devices.reshape(blk // QUAD, QUAD, req), ("hi", "quad", "req"))
    in_specs = (
        P("req", BLK, None),
        P("req", None),
        P("req", BLK, None),
        P("req", None),
        P("req", BLK, None),
        P("req", BLK, None),
        P("req"),
        P("req"),
        P(),
    )
    out_specs = (
        P("req", BLK, None),
        P("req", None),
        P("req", BLK, None),
        P("req", BLK, None),
    )
    return jax.shard_map(
        per_device, mesh=mesh, in_specs=in_specs, out_specs=out_specs, check_vma=False
    )
```

```python
import functools

import jax
import jax.numpy as jnp
from jax import lax
from jax.experimental import pallas as pl
from jax.experimental.pallas import tpu as pltpu
from jax.sharding import PartitionSpec as P

QUERY_HEADS = 8
KEY_VALUE_HEADS = 2
HEAD_SIZE = 128
GROUP = QUERY_HEADS // KEY_VALUE_HEADS
QW = QUERY_HEADS * HEAD_SIZE
KW = KEY_VALUE_HEADS * HEAD_SIZE
STATS = 128
QUAD = 4
KEY_SET = 8
PART_ROWS = KEY_VALUE_HEADS + 1
SCALE = HEAD_SIZE**-0.5
MASKED = -1e30
FLOOR = -1e20
F32 = jnp.float32
BF16 = jnp.bfloat16

KVW = 2 * KW
BLK = ("hi", "quad")
CHUNKS = 4
TILE = 16

HBM = pl.BlockSpec(memory_space=pltpu.HBM)
VMEM = pl.BlockSpec(memory_space=pltpu.VMEM)


def dot_t(a, b):
    return lax.dot_general(a, b, (((1,), (1,)), ((), ())), preferred_element_type=F32)


def dot(a, b):
    return lax.dot_general(a, b, (((1,), (0,)), ((), ())), preferred_element_type=F32)


def split3(value):
    high = value.astype(BF16).astype(F32)
    rest = value - high
    middle = rest.astype(BF16).astype(F32)
    return high, middle, rest - middle


def stats_block(columns, rows):
    lane = lax.broadcasted_iota(jnp.int32, (rows, STATS), 1)
    count = len(columns)
    out = jnp.zeros((rows, STATS), F32)
    for head, column in enumerate(columns):
        for term, part in enumerate(split3(column)):
            out = jnp.where(lane == term * count + head, part, out)
    return out.astype(BF16)


def spread_matrix(heads):
    lane = lax.broadcasted_iota(jnp.int32, (STATS, heads * HEAD_SIZE), 0)
    head = lax.broadcasted_iota(jnp.int32, (STATS, heads * HEAD_SIZE), 1) // HEAD_SIZE
    hit = (lane == head) | (lane == head + heads) | (lane == head + 2 * heads)
    return jnp.where(hit, 1.0, 0.0).astype(BF16)


def join(parts):
    spread = spread_matrix(QUERY_HEADS)
    logs = [dot(part[:, QW:], spread) for part in parts]
    top = functools.reduce(jnp.maximum, logs)
    scales = [jnp.exp(log - top) for log in logs]
    total = functools.reduce(jnp.add, scales)
    summed = functools.reduce(
        jnp.add, [scale * part[:, :QW].astype(F32) for scale, part in zip(scales, parts)]
    )
    return (summed / total).astype(BF16), top + jnp.log(total)


def source_group(j):
    return lax.axis_index("req") ^ j if lax.axis_size("req") == 2 else j


def decode_kernel(
    len_hbm,
    deal_hbm,
    q_hbm,
    new_hbm,
    cache_hbm,
    pre_q_hbm,
    pre_new_hbm,
    out_hbm,
    part_ref,
    pre_q_ref,
    route_ref,
    lens,
    deal,
    query_ref,
    new_ref,
    table,
    sems,
):
    slots, ctx, _ = table.shape
    rows = GROUP * slots
    chunk = slots // CHUNKS
    base = lax.axis_index(BLK) * ctx
    small = [
        (len_hbm, lens),
        (deal_hbm, deal),
        (q_hbm, query_ref),
        (new_hbm, new_ref),
        (pre_q_hbm.at[0], pre_q_ref),
        (pre_new_hbm.at[0], part_ref.at[pl.ds(PART_ROWS * slots, pre_new_hbm.shape[1]), :]),
    ]
    small = [pltpu.make_async_copy(a, b, sems.at[i]) for i, (a, b) in enumerate(small)]
    loads, stores = [], []
    for c in range(CHUNKS):
        part = pl.ds(c * chunk, chunk)
        loads.append(pltpu.make_async_copy(cache_hbm.at[part], table.at[part], sems.at[6 + c]))
        stores.append(pltpu.make_async_copy(table.at[part], out_hbm.at[part], sems.at[6 + CHUNKS + c]))
    for copy in small + loads:
        copy.start()
    for copy in small:
        copy.wait()
    group = lax.axis_index("req")
    req = route_ref.shape[0]
    out_row = lax.broadcasted_iota(jnp.int32, (slots, HEAD_SIZE), 0)
    out_lane = lax.broadcasted_iota(jnp.int32, (slots, HEAD_SIZE), 1)
    for j in range(req):
        source = source_group(j)
        chosen = jnp.zeros((slots, HEAD_SIZE), F32)
        for s in range(slots):
            place = deal[req + source * slots + s] - group * slots
            chosen = jnp.where((out_lane == s) & (out_row == place), 1.0, chosen)
        route_ref[j, pl.ds(0, slots), :] = chosen
        mine = (deal[source] == group).astype(F32)
        route_ref[j, pl.ds(slots, 8), :] = jnp.full((8, HEAD_SIZE), mine, F32)
    row_slot = lax.broadcasted_iota(jnp.int32, (rows, ctx), 0) % slots
    column = lax.broadcasted_iota(jnp.int32, (rows, ctx), 1)
    in_tile = lax.broadcasted_iota(jnp.int32, (TILE, KVW), 0)
    limit = jnp.full((rows, ctx), -1, jnp.int32)
    queries = [
        jnp.concatenate(
            [query_ref[:, pl.ds((g * GROUP + h) * HEAD_SIZE, HEAD_SIZE)] for h in range(GROUP)], axis=0
        )
        for g in range(KEY_VALUE_HEADS)
    ]
    scores = [jnp.zeros((rows, ctx), F32) for _ in range(KEY_VALUE_HEADS)]
    for c in range(CHUNKS):
        loads[c].wait()
        for s in range(c * chunk, (c + 1) * chunk):
            relative = lens[s] - base
            limit = jnp.where(row_slot == s, relative, limit)

            @pl.when((relative >= 0) & (relative < ctx))
            def _():
                start = pl.multiple_of(relative // TILE * TILE, TILE)
                tile = table[s, pl.ds(start, TILE), :]
                table[s, pl.ds(start, TILE), :] = jnp.where(
                    in_tile == relative - start, new_ref[s : s + 1, :], tile
                )

        stores[c].start()
        for g in range(KEY_VALUE_HEADS):
            key = table[pl.ds(c * chunk, chunk), :, pl.ds(g * HEAD_SIZE, HEAD_SIZE)]
            wide = dot_t(queries[g], key.reshape(chunk * ctx, HEAD_SIZE))
            for s in range(chunk):
                part = wide[:, s * ctx : (s + 1) * ctx]
                scores[g] = jnp.where(row_slot == c * chunk + s, part, scores[g])
    visible = column <= limit
    columns = []
    for g in range(KEY_VALUE_HEADS):
        masked = jnp.where(visible, scores[g] * SCALE, MASKED)
        maxima = jnp.maximum(jnp.max(masked, axis=1, keepdims=True), FLOOR)
        weights = jnp.exp(masked - maxima)
        totals = jnp.sum(weights, axis=1, keepdims=True)
        summed = jnp.zeros((rows, HEAD_SIZE), F32)
        for c in range(CHUNKS):
            value = table[pl.ds(c * chunk, chunk), :, pl.ds(KW + g * HEAD_SIZE, HEAD_SIZE)]
            picked = [jnp.where(row_slot == c * chunk + s, weights, 0.0) for s in range(chunk)]
            picked = jnp.concatenate(picked, axis=1).astype(BF16)
            summed += dot(picked, value.reshape(chunk * ctx, HEAD_SIZE))
        seen = totals > 0.0
        safe = jnp.where(seen, totals, 1.0)
        normed = (summed / safe).astype(BF16)
        logs = jnp.where(seen, maxima + jnp.log(safe), MASKED)
        for h in range(GROUP):
            part = slice(h * slots, (h + 1) * slots)
            part_ref[pl.ds(g * slots, slots), pl.ds(h * HEAD_SIZE, HEAD_SIZE)] = normed[part]
            columns.append(logs[part])
    put_stats(part_ref, columns, slots)
    for copy in stores:
        copy.wait()


def decode_partials(lengths, dealing, queries, new_rows, cache, pre_queries, pre_new, req):
    slots, ctx, width = cache.shape
    inputs = (lengths, dealing, queries, new_rows, cache, pre_queries, pre_new)
    return pl.pallas_call(
        decode_kernel,
        in_specs=[HBM] * len(inputs),
        out_specs=[HBM, VMEM, VMEM, VMEM],
        out_shape=[
            pltpu.HBM(cache.shape, BF16),
            pltpu.VMEM((PART_ROWS * slots + pre_new.shape[1], KVW), BF16),
            pltpu.VMEM(pre_queries.shape[1:], BF16),
            pltpu.VMEM((req, slots + 8, HEAD_SIZE), F32),
        ],
        scratch_shapes=[
            pltpu.SMEM(lengths.shape, jnp.int32),
            pltpu.SMEM(dealing.shape, jnp.int32),
            pltpu.VMEM(queries.shape, BF16),
            pltpu.VMEM(new_rows.shape, BF16),
            pltpu.VMEM(cache.shape, BF16),
            pltpu.SemaphoreType.DMA((6 + 2 * CHUNKS,)),
        ],
        compiler_params=pltpu.CompilerParams(vmem_limit_bytes=16 << 20),
        cost_estimate=pl.CostEstimate(
            flops=4 * slots * ctx * QW, bytes_accessed=2 * cache.size * 2, transcendentals=slots * ctx * 8
        ),
        name="decode_partials",
    )(*[pltpu.with_memory_space_constraint(x, pltpu.HBM) for x in inputs])


def put_stats(ref, columns, slots):
    last = pl.ds(KEY_VALUE_HEADS * slots, slots)
    ref[last, pl.ds(0, STATS)] = stats_block(columns, slots)
    ref[last, pl.ds(STATS, KVW - STATS)] = jnp.zeros((slots, KVW - STATS), BF16)


def decode_part(ref, slots):
    blocks = [ref[pl.ds(g * slots, slots), :] for g in range(KEY_VALUE_HEADS)]
    return jnp.concatenate(blocks + [ref[pl.ds(KEY_VALUE_HEADS * slots, slots), pl.ds(0, STATS)]], axis=1)


def step_kernel(slots, count, *refs):
    out_ref = refs[-1]
    joined, logs = join([decode_part(ref, slots) for ref in refs[:count]])
    head = PART_ROWS * slots
    for g in range(KEY_VALUE_HEADS):
        out_ref[pl.ds(g * slots, slots), :] = joined[:, g * KVW : (g + 1) * KVW]
    put_stats(out_ref, [logs[:, h * HEAD_SIZE : h * HEAD_SIZE + 1] for h in range(QUERY_HEADS)], slots)
    at = head
    for ref in refs[count:-1]:
        rest = ref.shape[0] - head
        out_ref[pl.ds(at, rest), :] = ref[pl.ds(head, rest), :]
        at += rest


def join_step(parts, carriers, slots, name):
    head = PART_ROWS * slots
    rows = head + sum(c.shape[0] - head for c in carriers)
    return pl.pallas_call(
        functools.partial(step_kernel, slots, len(parts)),
        in_specs=[VMEM] * (len(parts) + len(carriers)),
        out_specs=VMEM,
        out_shape=pltpu.VMEM((rows, KVW), BF16),
        compiler_params=pltpu.CompilerParams(vmem_limit_bytes=16 << 20),
        name=name,
    )(*parts, *carriers)


def prefill_kernel(sets, ctx, off_ref, *refs):
    query_count = len(sets)
    packs, tables, outs = refs[:query_count], refs[query_count:-query_count], refs[-query_count:]
    tokens = packs[0].shape[0]
    span = ctx + tokens
    me = lax.axis_index(BLK)
    offset = off_ref[:1, :1]
    pieces = []
    for k in range(KEY_SET):
        holder = me ^ k
        index = lax.broadcasted_iota(jnp.int32, (1, span), 1)
        old = jnp.where(holder * ctx + index < offset, -1, 1 << 30)
        pieces.append(jnp.where(index < ctx, old, holder * tokens + index - ctx))
    key_mark = jnp.concatenate(pieces, axis=1)
    in_block = lax.broadcasted_iota(jnp.int32, (GROUP * tokens, 1), 0) % tokens
    lane = lax.broadcasted_iota(jnp.int32, (tokens, STATS), 1)
    stats = [jnp.zeros((tokens, STATS), F32) for _ in range(query_count)]
    for g in range(KEY_VALUE_HEADS):
        keys = jnp.concatenate([t[:, pl.ds(g * HEAD_SIZE, HEAD_SIZE)] for t in tables], axis=0)
        values = jnp.concatenate([t[:, pl.ds(KW + g * HEAD_SIZE, HEAD_SIZE)] for t in tables], axis=0)
        for k in range(query_count):
            token = (me ^ (sets[k] * KEY_SET)) * tokens + in_block
            query = jnp.concatenate(
                [packs[k][:, pl.ds((g * GROUP + h) * HEAD_SIZE, HEAD_SIZE)] for h in range(GROUP)], axis=0
            )
            scores = jnp.where(key_mark <= token, dot_t(query, keys) * SCALE, MASKED)
            maxima = jnp.maximum(jnp.max(scores, axis=1, keepdims=True), FLOOR)
            weights = jnp.exp(scores - maxima)
            totals = jnp.sum(weights, axis=1, keepdims=True)
            summed = dot(weights.astype(BF16), values)
            seen = totals > 0.0
            safe = jnp.where(seen, totals, 1.0)
            normed = (summed / safe).astype(BF16)
            logs = jnp.where(seen, maxima + jnp.log(safe), MASKED)
            for h in range(GROUP):
                part = slice(h * tokens, (h + 1) * tokens)
                outs[k][:, pl.ds((g * GROUP + h) * HEAD_SIZE, HEAD_SIZE)] = normed[part]
                for term, value in enumerate(split3(logs[part])):
                    stats[k] = jnp.where(lane == term * QUERY_HEADS + g * GROUP + h, value, stats[k])
    for k in range(query_count):
        outs[k][:, pl.ds(QW, STATS)] = stats[k].astype(BF16)


def prefill_partials(offset, packs, tables, ctx, sets):
    tokens = packs[0].shape[0]
    pairs = len(packs) * tokens * KEY_SET * (ctx + tokens)
    return pl.pallas_call(
        functools.partial(prefill_kernel, sets, ctx),
        in_specs=[VMEM] * (1 + len(packs) + len(tables)),
        out_specs=[VMEM] * len(packs),
        out_shape=[jax.ShapeDtypeStruct((tokens, QW + STATS), BF16)] * len(packs),
        compiler_params=pltpu.CompilerParams(vmem_limit_bytes=32 << 20),
        cost_estimate=pl.CostEstimate(
            flops=4 * pairs * QW, bytes_accessed=4 << 20, transcendentals=pairs * QUERY_HEADS
        ),
        name="prefill_partials",
    )(offset, *packs, *tables)


def join_kernel(count, slots, *refs):
    parts, decodes, out_ref = refs[:count], refs[count:-1], refs[-1]
    tokens = parts[0].shape[0]
    out_ref[pl.ds(0, tokens), :] = join([ref[...] for ref in parts])[0]
    out_ref[pl.ds(tokens, slots), :] = join([decode_part(ref, slots) for ref in decodes])[0]


def join_parts(parts, decodes, slots):
    return pl.pallas_call(
        functools.partial(join_kernel, len(parts), slots),
        in_specs=[VMEM] * (len(parts) + len(decodes)),
        out_specs=VMEM,
        out_shape=pltpu.VMEM((parts[0].shape[0] + slots, QW), BF16),
        compiler_params=pltpu.CompilerParams(vmem_limit_bytes=16 << 20),
        name="join_parts",
    )(*parts, *decodes)


def update_kernel(tokens, sets, off_ref, cache_hbm, near_ref, beside_ref, *refs):
    tables, (out_ref, cache_ref, sem) = refs[:KEY_SET], refs[-3:]
    load = pltpu.make_async_copy(cache_hbm.at[0], cache_ref, sem)
    load.start()
    ctx = cache_ref.shape[0]
    me = lax.axis_index(BLK)
    rows = [t[pl.ds(ctx, tokens), :] for t in tables]
    rows = jnp.concatenate(rows + [near_ref[...], beside_ref[...]], axis=0)
    count = rows.shape[0]
    index = lax.broadcasted_iota(jnp.int32, (1, count), 1)
    block = index // tokens
    half = sets * KEY_SET // 2
    far = block - KEY_SET
    inner = far % half
    distance = KEY_SET * (1 + inner % sets) + 2 * (inner // sets) + far // half
    token = (me ^ jnp.where(block < KEY_SET, block, distance)) * tokens + index % tokens
    wanted = me * ctx + lax.broadcasted_iota(jnp.int32, (ctx, 1), 0) - off_ref[:1, :1]
    picked = dot(jnp.where(wanted == token, 1.0, 0.0).astype(BF16), rows).astype(BF16)
    inside = jnp.broadcast_to((wanted >= 0) & (wanted < count), cache_ref.shape)
    load.wait()
    out_ref[0] = jnp.where(inside, picked, cache_ref[...])


def update_cache(offset, cache, near, beside, tables, tokens, sets):
    return pl.pallas_call(
        functools.partial(update_kernel, tokens, sets),
        in_specs=[VMEM, HBM] + [VMEM] * (2 + len(tables)),
        out_specs=VMEM,
        out_shape=jax.ShapeDtypeStruct(cache.shape, BF16),
        scratch_shapes=[pltpu.VMEM(cache.shape[1:], BF16), pltpu.SemaphoreType.DMA],
        compiler_params=pltpu.CompilerParams(vmem_limit_bytes=16 << 20),
        name="update_cache",
    )(offset, pltpu.with_memory_space_constraint(cache, pltpu.HBM), near, beside, *tables)


def route_kernel(count, route_ref, *refs):
    held, (pre_ref, dec_ref) = refs[:-2], refs[-2:]
    if len(held) < count:
        held = [held[0].at[j] for j in range(count)]
    tokens, slots = pre_ref.shape[1], dec_ref.shape[0]
    prefill = jnp.zeros(pre_ref.shape[1:], F32)
    decode = jnp.zeros(dec_ref.shape, F32)
    for j in range(count):
        flag = route_ref[j, pl.ds(slots, 1), pl.ds(0, 1)]
        prefill += flag * held[j][pl.ds(0, tokens), :].astype(F32)
        chosen = route_ref[j, pl.ds(0, slots), pl.ds(0, slots)].astype(BF16)
        decode += dot(chosen, held[j][pl.ds(tokens, slots), :])
    pre_ref[0] = prefill.astype(BF16)
    dec_ref[...] = decode.astype(BF16)


def route_outputs(route, held, tokens, slots):
    return pl.pallas_call(
        functools.partial(route_kernel, route.shape[0]),
        in_specs=[VMEM] * (1 + len(held)),
        out_specs=[VMEM] * 2,
        out_shape=[
            jax.ShapeDtypeStruct((1, tokens, QW), BF16),
            jax.ShapeDtypeStruct((slots, QW), BF16),
        ],
        compiler_params=pltpu.CompilerParams(vmem_limit_bytes=16 << 20),
        name="route_outputs",
    )(route, *held)


def per_device(
    prefill_queries,
    decode_queries,
    new_prefill,
    new_decode,
    prefill_cache,
    decode_cache,
    prefill_offsets,
    decode_lengths,
    dealing,
):
    blk = lax.axis_size(BLK)
    req = lax.axis_size("req")
    ctx = prefill_cache.shape[1]
    tokens = prefill_queries.shape[1]
    slots = decode_cache.shape[0]

    def swap(array, distance):
        return lax.ppermute(array, BLK, [(i, i ^ distance) for i in range(blk)])

    def after(array, *marks):
        return lax.optimization_barrier((array, *marks))[0]

    others = range(KEY_SET, blk, KEY_SET)
    table = jnp.concatenate([prefill_cache[0], new_prefill[0]], axis=0)
    lanes = [table] + [swap(table, k) for k in range(2, KEY_SET, 2)]
    packs = [swap(prefill_queries[0], k) for k in others]

    decode_cache_out, part, queries, route = decode_partials(
        decode_lengths,
        dealing,
        decode_queries,
        new_decode,
        decode_cache,
        prefill_queries,
        new_prefill,
        req,
    )
    far = [swap(part, k) for k in others]
    offset = jnp.full((8, HEAD_SIZE), prefill_offsets[0], jnp.int32)
    lanes[2], offset, _ = lax.optimization_barrier((lanes[2], offset, part))
    lanes[3], far, _ = lax.optimization_barrier((lanes[3], far, lanes[2]))
    lanes[1], packs, _ = lax.optimization_barrier((lanes[1], packs, lanes[2]))
    part = join_step([part] + far, [], slots, "join_far")
    tables = [t for lane in lanes for t in (lane, swap(lane, 1))]
    beside = swap(part, 1)

    part = join_step([part, beside], far, slots, "join_core")
    offset = after(offset, part)
    sent = prefill_partials(offset, packs, tables, ctx, [k // KEY_SET for k in others])
    arrived = [swap(p, k) for k, p in zip(others, sent)]
    part = after(part, sent[0])
    around = [part] + [swap(part, k) for k in range(2, KEY_SET, 2)]
    queries = after(queries, sent[0])
    kept = prefill_partials(offset, [queries], tables, ctx, [0])
    attended = join_parts([*kept] + arrived, around, slots)
    news = jnp.concatenate([a[PART_ROWS * slots :] for a in around], axis=0)
    prefill_cache_out = update_cache(offset, prefill_cache, news, swap(news, 1), tables, tokens, len(others))

    if req == 2:
        held = [attended, lax.ppermute(attended, "req", [(0, 1), (1, 0)])]
    else:
        held = [lax.all_gather(attended, "req", axis=0)]
    held[-1], prefill_cache_out = lax.optimization_barrier((held[-1], prefill_cache_out))
    prefill_out, decode_out = route_outputs(route, held, tokens, slots)
    return (prefill_out, decode_out, prefill_cache_out, decode_cache_out)


def solution(mesh):
    blk, req = mesh.shape["blk"], mesh.shape["req"]
    mesh = jax.sharding.Mesh(mesh.devices.reshape(blk // QUAD, QUAD, req), ("hi", "quad", "req"))
    in_specs = (
        P("req", BLK, None),
        P("req", None),
        P("req", BLK, None),
        P("req", None),
        P("req", BLK, None),
        P("req", BLK, None),
        P("req"),
        P("req"),
        P(),
    )
    out_specs = (
        P("req", BLK, None),
        P("req", None),
        P("req", BLK, None),
        P("req", BLK, None),
    )
    return jax.shard_map(
        per_device, mesh=mesh, in_specs=in_specs, out_specs=out_specs, check_vma=False
    )
```

```python
import functools

import jax
import jax.numpy as jnp
from jax import lax
from jax.experimental import pallas as pl
from jax.experimental.pallas import tpu as pltpu
from jax.sharding import PartitionSpec as P

QUERY_HEADS = 8
KEY_VALUE_HEADS = 2
HEAD_SIZE = 128
GROUP = QUERY_HEADS // KEY_VALUE_HEADS
QW = QUERY_HEADS * HEAD_SIZE
KW = KEY_VALUE_HEADS * HEAD_SIZE
STATS = 128
QUAD = 4
KEY_SET = 8
PART_ROWS = KEY_VALUE_HEADS + 1
SCALE = HEAD_SIZE**-0.5
MASKED = -1e30
FLOOR = -1e20
F32 = jnp.float32
BF16 = jnp.bfloat16

KVW = 2 * KW
BLK = ("hi", "quad")
CHUNKS = 4
TILE = 16

HBM = pl.BlockSpec(memory_space=pltpu.HBM)
VMEM = pl.BlockSpec(memory_space=pltpu.VMEM)


def dot_t(a, b):
    return lax.dot_general(a, b, (((1,), (1,)), ((), ())), preferred_element_type=F32)


def dot(a, b):
    return lax.dot_general(a, b, (((1,), (0,)), ((), ())), preferred_element_type=F32)


def split3(value):
    high = value.astype(BF16).astype(F32)
    rest = value - high
    middle = rest.astype(BF16).astype(F32)
    return high, middle, rest - middle


def stats_block(columns, rows):
    lane = lax.broadcasted_iota(jnp.int32, (rows, STATS), 1)
    count = len(columns)
    out = jnp.zeros((rows, STATS), F32)
    for head, column in enumerate(columns):
        for term, part in enumerate(split3(column)):
            out = jnp.where(lane == term * count + head, part, out)
    return out.astype(BF16)


def spread_matrix(heads):
    lane = lax.broadcasted_iota(jnp.int32, (STATS, heads * HEAD_SIZE), 0)
    head = lax.broadcasted_iota(jnp.int32, (STATS, heads * HEAD_SIZE), 1) // HEAD_SIZE
    hit = (lane == head) | (lane == head + heads) | (lane == head + 2 * heads)
    return jnp.where(hit, 1.0, 0.0).astype(BF16)


def join(parts):
    spread = spread_matrix(QUERY_HEADS)
    logs = [dot(part[:, QW:], spread) for part in parts]
    top = functools.reduce(jnp.maximum, logs)
    scales = [jnp.exp(log - top) for log in logs]
    total = functools.reduce(jnp.add, scales)
    summed = functools.reduce(
        jnp.add, [scale * part[:, :QW].astype(F32) for scale, part in zip(scales, parts)]
    )
    return (summed / total).astype(BF16), top + jnp.log(total)


def source_group(j):
    return lax.axis_index("req") ^ j if lax.axis_size("req") == 2 else j


def decode_kernel(
    len_hbm,
    deal_hbm,
    q_hbm,
    new_hbm,
    cache_hbm,
    pre_q_hbm,
    pre_new_hbm,
    out_hbm,
    part_ref,
    pre_q_ref,
    route_ref,
    lens,
    deal,
    query_ref,
    new_ref,
    table,
    sems,
):
    slots, ctx, _ = table.shape
    rows = GROUP * slots
    chunk = slots // CHUNKS
    base = lax.axis_index(BLK) * ctx
    small = [
        (len_hbm, lens),
        (deal_hbm, deal),
        (q_hbm, query_ref),
        (new_hbm, new_ref),
        (pre_q_hbm.at[0], pre_q_ref),
        (pre_new_hbm.at[0], part_ref.at[pl.ds(PART_ROWS * slots, pre_new_hbm.shape[1]), :]),
    ]
    small = [pltpu.make_async_copy(a, b, sems.at[i]) for i, (a, b) in enumerate(small)]
    loads, stores = [], []
    for c in range(CHUNKS):
        part = pl.ds(c * chunk, chunk)
        loads.append(pltpu.make_async_copy(cache_hbm.at[part], table.at[part], sems.at[6 + c]))
        stores.append(pltpu.make_async_copy(table.at[part], out_hbm.at[part], sems.at[6 + CHUNKS + c]))
    for copy in small + loads:
        copy.start()
    for copy in small:
        copy.wait()
    group = lax.axis_index("req")
    req = route_ref.shape[0]
    out_row = lax.broadcasted_iota(jnp.int32, (slots, HEAD_SIZE), 0)
    out_lane = lax.broadcasted_iota(jnp.int32, (slots, HEAD_SIZE), 1)
    for j in range(req):
        source = source_group(j)
        chosen = jnp.zeros((slots, HEAD_SIZE), F32)
        for s in range(slots):
            place = deal[req + source * slots + s] - group * slots
            chosen = jnp.where((out_lane == s) & (out_row == place), 1.0, chosen)
        route_ref[j, pl.ds(0, slots), :] = chosen
        mine = (deal[source] == group).astype(F32)
        route_ref[j, pl.ds(slots, 8), :] = jnp.full((8, HEAD_SIZE), mine, F32)
    row_slot = lax.broadcasted_iota(jnp.int32, (rows, ctx), 0) % slots
    column = lax.broadcasted_iota(jnp.int32, (rows, ctx), 1)
    in_tile = lax.broadcasted_iota(jnp.int32, (TILE, KVW), 0)
    limit = jnp.full((rows, ctx), -1, jnp.int32)
    queries = [
        jnp.concatenate(
            [query_ref[:, pl.ds((g * GROUP + h) * HEAD_SIZE, HEAD_SIZE)] for h in range(GROUP)], axis=0
        )
        for g in range(KEY_VALUE_HEADS)
    ]
    scores = [jnp.zeros((rows, ctx), F32) for _ in range(KEY_VALUE_HEADS)]
    for c in range(CHUNKS):
        loads[c].wait()
        for s in range(c * chunk, (c + 1) * chunk):
            relative = lens[s] - base
            limit = jnp.where(row_slot == s, relative, limit)

            @pl.when((relative >= 0) & (relative < ctx))
            def _():
                start = pl.multiple_of(relative // TILE * TILE, TILE)
                tile = table[s, pl.ds(start, TILE), :]
                table[s, pl.ds(start, TILE), :] = jnp.where(
                    in_tile == relative - start, new_ref[s : s + 1, :], tile
                )

        stores[c].start()
        for g in range(KEY_VALUE_HEADS):
            key = table[pl.ds(c * chunk, chunk), :, pl.ds(g * HEAD_SIZE, HEAD_SIZE)]
            wide = dot_t(queries[g], key.reshape(chunk * ctx, HEAD_SIZE))
            for s in range(chunk):
                part = wide[:, s * ctx : (s + 1) * ctx]
                scores[g] = jnp.where(row_slot == c * chunk + s, part, scores[g])
    visible = column <= limit
    columns = []
    for g in range(KEY_VALUE_HEADS):
        masked = jnp.where(visible, scores[g] * SCALE, MASKED)
        maxima = jnp.maximum(jnp.max(masked, axis=1, keepdims=True), FLOOR)
        weights = jnp.exp(masked - maxima)
        totals = jnp.sum(weights, axis=1, keepdims=True)
        summed = jnp.zeros((rows, HEAD_SIZE), F32)
        for c in range(CHUNKS):
            value = table[pl.ds(c * chunk, chunk), :, pl.ds(KW + g * HEAD_SIZE, HEAD_SIZE)]
            picked = [jnp.where(row_slot == c * chunk + s, weights, 0.0) for s in range(chunk)]
            picked = jnp.concatenate(picked, axis=1).astype(BF16)
            summed += dot(picked, value.reshape(chunk * ctx, HEAD_SIZE))
        seen = totals > 0.0
        safe = jnp.where(seen, totals, 1.0)
        normed = (summed / safe).astype(BF16)
        logs = jnp.where(seen, maxima + jnp.log(safe), MASKED)
        for h in range(GROUP):
            part = slice(h * slots, (h + 1) * slots)
            part_ref[pl.ds(g * slots, slots), pl.ds(h * HEAD_SIZE, HEAD_SIZE)] = normed[part]
            columns.append(logs[part])
    put_stats(part_ref, columns, slots)
    for copy in stores:
        copy.wait()


def decode_partials(lengths, dealing, queries, new_rows, cache, pre_queries, pre_new, req):
    slots, ctx, width = cache.shape
    inputs = (lengths, dealing, queries, new_rows, cache, pre_queries, pre_new)
    return pl.pallas_call(
        decode_kernel,
        in_specs=[HBM] * len(inputs),
        out_specs=[HBM, VMEM, VMEM, VMEM],
        out_shape=[
            pltpu.HBM(cache.shape, BF16),
            pltpu.VMEM((PART_ROWS * slots + pre_new.shape[1], KVW), BF16),
            pltpu.VMEM(pre_queries.shape[1:], BF16),
            pltpu.VMEM((req, slots + 8, HEAD_SIZE), F32),
        ],
        scratch_shapes=[
            pltpu.SMEM(lengths.shape, jnp.int32),
            pltpu.SMEM(dealing.shape, jnp.int32),
            pltpu.VMEM(queries.shape, BF16),
            pltpu.VMEM(new_rows.shape, BF16),
            pltpu.VMEM(cache.shape, BF16),
            pltpu.SemaphoreType.DMA((6 + 2 * CHUNKS,)),
        ],
        compiler_params=pltpu.CompilerParams(vmem_limit_bytes=16 << 20),
        cost_estimate=pl.CostEstimate(
            flops=4 * slots * ctx * QW, bytes_accessed=2 * cache.size * 2, transcendentals=slots * ctx * 8
        ),
        name="decode_partials",
    )(*[pltpu.with_memory_space_constraint(x, pltpu.HBM) for x in inputs])


def put_stats(ref, columns, slots):
    last = pl.ds(KEY_VALUE_HEADS * slots, slots)
    ref[last, pl.ds(0, STATS)] = stats_block(columns, slots)
    ref[last, pl.ds(STATS, KVW - STATS)] = jnp.zeros((slots, KVW - STATS), BF16)


def decode_part(ref, slots):
    blocks = [ref[pl.ds(g * slots, slots), :] for g in range(KEY_VALUE_HEADS)]
    return jnp.concatenate(blocks + [ref[pl.ds(KEY_VALUE_HEADS * slots, slots), pl.ds(0, STATS)]], axis=1)


def step_kernel(slots, count, *refs):
    out_ref = refs[-1]
    joined, logs = join([decode_part(ref, slots) for ref in refs[:count]])
    head = PART_ROWS * slots
    for g in range(KEY_VALUE_HEADS):
        out_ref[pl.ds(g * slots, slots), :] = joined[:, g * KVW : (g + 1) * KVW]
    put_stats(out_ref, [logs[:, h * HEAD_SIZE : h * HEAD_SIZE + 1] for h in range(QUERY_HEADS)], slots)
    at = head
    for ref in refs[count:-1]:
        rest = ref.shape[0] - head
        out_ref[pl.ds(at, rest), :] = ref[pl.ds(head, rest), :]
        at += rest


def join_step(parts, carriers, slots, name):
    head = PART_ROWS * slots
    rows = head + sum(c.shape[0] - head for c in carriers)
    return pl.pallas_call(
        functools.partial(step_kernel, slots, len(parts)),
        in_specs=[VMEM] * (len(parts) + len(carriers)),
        out_specs=VMEM,
        out_shape=pltpu.VMEM((rows, KVW), BF16),
        compiler_params=pltpu.CompilerParams(vmem_limit_bytes=16 << 20),
        name=name,
    )(*parts, *carriers)


def prefill_kernel(sets, ctx, off_ref, *refs):
    query_count = len(sets)
    packs, tables, outs = refs[:query_count], refs[query_count:-query_count], refs[-query_count:]
    tokens = packs[0].shape[0]
    span = ctx + tokens
    me = lax.axis_index(BLK)
    offset = off_ref[:1, :1]
    pieces = []
    for k in range(KEY_SET):
        holder = me ^ k
        index = lax.broadcasted_iota(jnp.int32, (1, span), 1)
        old = jnp.where(holder * ctx + index < offset, -1, 1 << 30)
        pieces.append(jnp.where(index < ctx, old, holder * tokens + index - ctx))
    key_mark = jnp.concatenate(pieces, axis=1)
    in_block = lax.broadcasted_iota(jnp.int32, (GROUP * tokens, 1), 0) % tokens
    lane = lax.broadcasted_iota(jnp.int32, (tokens, STATS), 1)
    stats = [jnp.zeros((tokens, STATS), F32) for _ in range(query_count)]
    for g in range(KEY_VALUE_HEADS):
        keys = jnp.concatenate([t[:, pl.ds(g * HEAD_SIZE, HEAD_SIZE)] for t in tables], axis=0)
        values = jnp.concatenate([t[:, pl.ds(KW + g * HEAD_SIZE, HEAD_SIZE)] for t in tables], axis=0)
        for k in range(query_count):
            token = (me ^ (sets[k] * KEY_SET)) * tokens + in_block
            query = jnp.concatenate(
                [packs[k][:, pl.ds((g * GROUP + h) * HEAD_SIZE, HEAD_SIZE)] for h in range(GROUP)], axis=0
            )
            scores = jnp.where(key_mark <= token, dot_t(query, keys) * SCALE, MASKED)
            maxima = jnp.maximum(jnp.max(scores, axis=1, keepdims=True), FLOOR)
            weights = jnp.exp(scores - maxima)
            totals = jnp.sum(weights, axis=1, keepdims=True)
            summed = dot(weights.astype(BF16), values)
            seen = totals > 0.0
            safe = jnp.where(seen, totals, 1.0)
            normed = (summed / safe).astype(BF16)
            logs = jnp.where(seen, maxima + jnp.log(safe), MASKED)
            for h in range(GROUP):
                part = slice(h * tokens, (h + 1) * tokens)
                outs[k][:, pl.ds((g * GROUP + h) * HEAD_SIZE, HEAD_SIZE)] = normed[part]
                for term, value in enumerate(split3(logs[part])):
                    stats[k] = jnp.where(lane == term * QUERY_HEADS + g * GROUP + h, value, stats[k])
    for k in range(query_count):
        outs[k][:, pl.ds(QW, STATS)] = stats[k].astype(BF16)


def prefill_partials(offset, packs, tables, ctx, sets):
    tokens = packs[0].shape[0]
    pairs = len(packs) * tokens * KEY_SET * (ctx + tokens)
    return pl.pallas_call(
        functools.partial(prefill_kernel, sets, ctx),
        in_specs=[VMEM] * (1 + len(packs) + len(tables)),
        out_specs=[VMEM] * len(packs),
        out_shape=[jax.ShapeDtypeStruct((tokens, QW + STATS), BF16)] * len(packs),
        compiler_params=pltpu.CompilerParams(vmem_limit_bytes=32 << 20),
        cost_estimate=pl.CostEstimate(
            flops=4 * pairs * QW, bytes_accessed=4 << 20, transcendentals=pairs * QUERY_HEADS
        ),
        name="prefill_partials",
    )(offset, *packs, *tables)


def join_kernel(count, slots, *refs):
    parts, decodes, out_ref = refs[:count], refs[count:-1], refs[-1]
    tokens = parts[0].shape[0]
    out_ref[pl.ds(0, tokens), :] = join([ref[...] for ref in parts])[0]
    out_ref[pl.ds(tokens, slots), :] = join([decode_part(ref, slots) for ref in decodes])[0]


def join_parts(parts, decodes, slots):
    return pl.pallas_call(
        functools.partial(join_kernel, len(parts), slots),
        in_specs=[VMEM] * (len(parts) + len(decodes)),
        out_specs=VMEM,
        out_shape=pltpu.VMEM((parts[0].shape[0] + slots, QW), BF16),
        compiler_params=pltpu.CompilerParams(vmem_limit_bytes=16 << 20),
        name="join_parts",
    )(*parts, *decodes)


def update_kernel(tokens, sets, off_ref, cache_hbm, near_ref, beside_ref, *refs):
    tables, (out_ref, cache_ref, sem) = refs[:KEY_SET], refs[-3:]
    load = pltpu.make_async_copy(cache_hbm.at[0], cache_ref, sem)
    load.start()
    ctx = cache_ref.shape[0]
    me = lax.axis_index(BLK)
    rows = [t[pl.ds(ctx, tokens), :] for t in tables]
    rows = jnp.concatenate(rows + [near_ref[...], beside_ref[...]], axis=0)
    count = rows.shape[0]
    index = lax.broadcasted_iota(jnp.int32, (1, count), 1)
    block = index // tokens
    half = sets * KEY_SET // 2
    far = block - KEY_SET
    inner = far % half
    distance = KEY_SET * (1 + inner % sets) + 2 * (inner // sets) + far // half
    token = (me ^ jnp.where(block < KEY_SET, block, distance)) * tokens + index % tokens
    wanted = me * ctx + lax.broadcasted_iota(jnp.int32, (ctx, 1), 0) - off_ref[:1, :1]
    picked = dot(jnp.where(wanted == token, 1.0, 0.0).astype(BF16), rows).astype(BF16)
    inside = jnp.broadcast_to((wanted >= 0) & (wanted < count), cache_ref.shape)
    load.wait()
    out_ref[0] = jnp.where(inside, picked, cache_ref[...])


def update_cache(offset, cache, near, beside, tables, tokens, sets):
    return pl.pallas_call(
        functools.partial(update_kernel, tokens, sets),
        in_specs=[VMEM, HBM] + [VMEM] * (2 + len(tables)),
        out_specs=VMEM,
        out_shape=jax.ShapeDtypeStruct(cache.shape, BF16),
        scratch_shapes=[pltpu.VMEM(cache.shape[1:], BF16), pltpu.SemaphoreType.DMA],
        compiler_params=pltpu.CompilerParams(vmem_limit_bytes=16 << 20),
        name="update_cache",
    )(offset, pltpu.with_memory_space_constraint(cache, pltpu.HBM), near, beside, *tables)


def route_kernel(count, route_ref, *refs):
    held, (pre_ref, dec_ref) = refs[:-2], refs[-2:]
    if len(held) < count:
        held = [held[0].at[j] for j in range(count)]
    tokens, slots = pre_ref.shape[1], dec_ref.shape[0]
    prefill = jnp.zeros(pre_ref.shape[1:], F32)
    decode = jnp.zeros(dec_ref.shape, F32)
    for j in range(count):
        flag = route_ref[j, pl.ds(slots, 1), pl.ds(0, 1)]
        prefill += flag * held[j][pl.ds(0, tokens), :].astype(F32)
        chosen = route_ref[j, pl.ds(0, slots), pl.ds(0, slots)].astype(BF16)
        decode += dot(chosen, held[j][pl.ds(tokens, slots), :])
    pre_ref[0] = prefill.astype(BF16)
    dec_ref[...] = decode.astype(BF16)


def route_outputs(route, held, tokens, slots):
    return pl.pallas_call(
        functools.partial(route_kernel, route.shape[0]),
        in_specs=[VMEM] * (1 + len(held)),
        out_specs=[VMEM] * 2,
        out_shape=[
            jax.ShapeDtypeStruct((1, tokens, QW), BF16),
            jax.ShapeDtypeStruct((slots, QW), BF16),
        ],
        compiler_params=pltpu.CompilerParams(vmem_limit_bytes=16 << 20),
        name="route_outputs",
    )(route, *held)


def per_device(
    prefill_queries,
    decode_queries,
    new_prefill,
    new_decode,
    prefill_cache,
    decode_cache,
    prefill_offsets,
    decode_lengths,
    dealing,
):
    blk = lax.axis_size(BLK)
    req = lax.axis_size("req")
    ctx = prefill_cache.shape[1]
    tokens = prefill_queries.shape[1]
    slots = decode_cache.shape[0]

    def swap(array, distance):
        return lax.ppermute(array, BLK, [(i, i ^ distance) for i in range(blk)])

    def after(array, *marks):
        return lax.optimization_barrier((array, *marks))[0]

    others = range(KEY_SET, blk, KEY_SET)
    table = jnp.concatenate([prefill_cache[0], new_prefill[0]], axis=0)
    lanes = [table] + [swap(table, k) for k in range(2, KEY_SET, 2)]
    packs = [swap(prefill_queries[0], k) for k in others]

    decode_cache_out, part, queries, route = decode_partials(
        decode_lengths,
        dealing,
        decode_queries,
        new_decode,
        decode_cache,
        prefill_queries,
        new_prefill,
        req,
    )
    far = [swap(part, k) for k in others]
    offset = jnp.full((8, HEAD_SIZE), prefill_offsets[0], jnp.int32)
    lanes[2], offset, _ = lax.optimization_barrier((lanes[2], offset, part))
    lanes[3], far, _ = lax.optimization_barrier((lanes[3], far, lanes[2]))
    lanes[1], packs, _ = lax.optimization_barrier((lanes[1], packs, lanes[2]))
    part = join_step([part] + far, [], slots, "join_far")
    tables = [t for lane in lanes for t in (lane, swap(lane, 1))]
    beside = swap(part, 1)

    part = join_step([part, beside], far, slots, "join_core")
    offset = after(offset, part)
    sent = prefill_partials(offset, packs, tables, ctx, [k // KEY_SET for k in others])
    arrived = [swap(p, k) for k, p in zip(others, sent)]
    part = after(part, sent[0])
    around = [part] + [swap(part, k) for k in range(2, KEY_SET, 2)]
    queries = after(queries, sent[0])
    kept = prefill_partials(offset, [queries], tables, ctx, [0])
    around = [part] + [after(a, *kept) for a in around[1:]]
    attended = join_parts([*kept] + arrived, around, slots)
    news = jnp.concatenate([a[PART_ROWS * slots :] for a in around], axis=0)
    prefill_cache_out = update_cache(offset, prefill_cache, news, swap(news, 1), tables, tokens, len(others))

    if req == 2:
        held = [attended, lax.ppermute(attended, "req", [(0, 1), (1, 0)])]
    else:
        held = [lax.all_gather(attended, "req", axis=0)]
    held[-1], prefill_cache_out = lax.optimization_barrier((held[-1], prefill_cache_out))
    prefill_out, decode_out = route_outputs(route, held, tokens, slots)
    return (prefill_out, decode_out, prefill_cache_out, decode_cache_out)


def solution(mesh):
    blk, req = mesh.shape["blk"], mesh.shape["req"]
    mesh = jax.sharding.Mesh(mesh.devices.reshape(blk // QUAD, QUAD, req), ("hi", "quad", "req"))
    in_specs = (
        P("req", BLK, None),
        P("req", None),
        P("req", BLK, None),
        P("req", None),
        P("req", BLK, None),
        P("req", BLK, None),
        P("req"),
        P("req"),
        P(),
    )
    out_specs = (
        P("req", BLK, None),
        P("req", None),
        P("req", BLK, None),
        P("req", BLK, None),
    )
    return jax.shard_map(
        per_device, mesh=mesh, in_specs=in_specs, out_specs=out_specs, check_vma=False
    )
```

```python
import functools

import jax
import jax.numpy as jnp
from jax import lax
from jax.experimental import pallas as pl
from jax.experimental.pallas import tpu as pltpu
from jax.sharding import PartitionSpec as P

QUERY_HEADS = 8
KEY_VALUE_HEADS = 2
HEAD_SIZE = 128
GROUP = QUERY_HEADS // KEY_VALUE_HEADS
QW = QUERY_HEADS * HEAD_SIZE
KW = KEY_VALUE_HEADS * HEAD_SIZE
STATS = 128
QUAD = 4
KEY_SET = 8
PART_ROWS = KEY_VALUE_HEADS + 1
SCALE = HEAD_SIZE**-0.5
MASKED = -1e30
FLOOR = -1e20
F32 = jnp.float32
BF16 = jnp.bfloat16

KVW = 2 * KW
BLK = ("hi", "quad")
CHUNKS = 2
TILE = 16

HBM = pl.BlockSpec(memory_space=pltpu.HBM)
VMEM = pl.BlockSpec(memory_space=pltpu.VMEM)


def dot_t(a, b):
    return lax.dot_general(a, b, (((1,), (1,)), ((), ())), preferred_element_type=F32)


def dot(a, b):
    return lax.dot_general(a, b, (((1,), (0,)), ((), ())), preferred_element_type=F32)


def split3(value):
    high = value.astype(BF16).astype(F32)
    rest = value - high
    middle = rest.astype(BF16).astype(F32)
    return high, middle, rest - middle


def stats_block(columns, rows):
    lane = lax.broadcasted_iota(jnp.int32, (rows, STATS), 1)
    count = len(columns)
    out = jnp.zeros((rows, STATS), F32)
    for head, column in enumerate(columns):
        for term, part in enumerate(split3(column)):
            out = jnp.where(lane == term * count + head, part, out)
    return out.astype(BF16)


def spread_matrix(heads):
    lane = lax.broadcasted_iota(jnp.int32, (STATS, heads * HEAD_SIZE), 0)
    head = lax.broadcasted_iota(jnp.int32, (STATS, heads * HEAD_SIZE), 1) // HEAD_SIZE
    hit = (lane == head) | (lane == head + heads) | (lane == head + 2 * heads)
    return jnp.where(hit, 1.0, 0.0).astype(BF16)


def join(parts):
    spread = spread_matrix(QUERY_HEADS)
    logs = [dot(part[:, QW:], spread) for part in parts]
    top = functools.reduce(jnp.maximum, logs)
    scales = [jnp.exp(log - top) for log in logs]
    total = functools.reduce(jnp.add, scales)
    summed = functools.reduce(
        jnp.add, [scale * part[:, :QW].astype(F32) for scale, part in zip(scales, parts)]
    )
    return (summed / total).astype(BF16), top + jnp.log(total)


def source_group(j):
    return lax.axis_index("req") ^ j if lax.axis_size("req") == 2 else j


def decode_kernel(
    len_hbm,
    deal_hbm,
    q_hbm,
    new_hbm,
    cache_hbm,
    pre_q_hbm,
    pre_new_hbm,
    out_hbm,
    part_ref,
    pre_q_ref,
    route_ref,
    lens,
    deal,
    query_ref,
    new_ref,
    table,
    sems,
):
    slots, ctx, _ = table.shape
    rows = GROUP * slots
    chunk = slots // CHUNKS
    base = lax.axis_index(BLK) * ctx
    small = [
        (len_hbm, lens),
        (deal_hbm, deal),
        (q_hbm, query_ref),
        (new_hbm, new_ref),
        (pre_q_hbm.at[0], pre_q_ref),
        (pre_new_hbm.at[0], part_ref.at[pl.ds(PART_ROWS * slots, pre_new_hbm.shape[1]), :]),
    ]
    small = [pltpu.make_async_copy(a, b, sems.at[i]) for i, (a, b) in enumerate(small)]
    loads, stores = [], []
    for c in range(CHUNKS):
        part = pl.ds(c * chunk, chunk)
        loads.append(pltpu.make_async_copy(cache_hbm.at[part], table.at[part], sems.at[6 + c]))
        stores.append(pltpu.make_async_copy(table.at[part], out_hbm.at[part], sems.at[6 + CHUNKS + c]))
    for copy in small + loads:
        copy.start()
    for copy in small:
        copy.wait()
    group = lax.axis_index("req")
    req = route_ref.shape[0]
    out_row = lax.broadcasted_iota(jnp.int32, (slots, HEAD_SIZE), 0)
    out_lane = lax.broadcasted_iota(jnp.int32, (slots, HEAD_SIZE), 1)
    for j in range(req):
        source = source_group(j)
        chosen = jnp.zeros((slots, HEAD_SIZE), F32)
        for s in range(slots):
            place = deal[req + source * slots + s] - group * slots
            chosen = jnp.where((out_lane == s) & (out_row == place), 1.0, chosen)
        route_ref[j, pl.ds(0, slots), :] = chosen
        mine = (deal[source] == group).astype(F32)
        route_ref[j, pl.ds(slots, 8), :] = jnp.full((8, HEAD_SIZE), mine, F32)
    row_slot = lax.broadcasted_iota(jnp.int32, (rows, ctx), 0) % slots
    column = lax.broadcasted_iota(jnp.int32, (rows, ctx), 1)
    in_tile = lax.broadcasted_iota(jnp.int32, (TILE, KVW), 0)
    limit = jnp.full((rows, ctx), -1, jnp.int32)
    queries = [
        jnp.concatenate(
            [query_ref[:, pl.ds((g * GROUP + h) * HEAD_SIZE, HEAD_SIZE)] for h in range(GROUP)], axis=0
        )
        for g in range(KEY_VALUE_HEADS)
    ]
    scores = [jnp.zeros((rows, ctx), F32) for _ in range(KEY_VALUE_HEADS)]
    for c in range(CHUNKS):
        loads[c].wait()
        for s in range(c * chunk, (c + 1) * chunk):
            relative = lens[s] - base
            limit = jnp.where(row_slot == s, relative, limit)

            @pl.when((relative >= 0) & (relative < ctx))
            def _():
                start = pl.multiple_of(relative // TILE * TILE, TILE)
                tile = table[s, pl.ds(start, TILE), :]
                table[s, pl.ds(start, TILE), :] = jnp.where(
                    in_tile == relative - start, new_ref[s : s + 1, :], tile
                )

        stores[c].start()
        for g in range(KEY_VALUE_HEADS):
            key = table[pl.ds(c * chunk, chunk), :, pl.ds(g * HEAD_SIZE, HEAD_SIZE)]
            wide = dot_t(queries[g], key.reshape(chunk * ctx, HEAD_SIZE))
            for s in range(chunk):
                part = wide[:, s * ctx : (s + 1) * ctx]
                scores[g] = jnp.where(row_slot == c * chunk + s, part, scores[g])
    visible = column <= limit
    columns = []
    for g in range(KEY_VALUE_HEADS):
        masked = jnp.where(visible, scores[g] * SCALE, MASKED)
        maxima = jnp.maximum(jnp.max(masked, axis=1, keepdims=True), FLOOR)
        weights = jnp.exp(masked - maxima)
        totals = jnp.sum(weights, axis=1, keepdims=True)
        summed = jnp.zeros((rows, HEAD_SIZE), F32)
        for c in range(CHUNKS):
            value = table[pl.ds(c * chunk, chunk), :, pl.ds(KW + g * HEAD_SIZE, HEAD_SIZE)]
            picked = [jnp.where(row_slot == c * chunk + s, weights, 0.0) for s in range(chunk)]
            picked = jnp.concatenate(picked, axis=1).astype(BF16)
            summed += dot(picked, value.reshape(chunk * ctx, HEAD_SIZE))
        seen = totals > 0.0
        safe = jnp.where(seen, totals, 1.0)
        normed = (summed / safe).astype(BF16)
        logs = jnp.where(seen, maxima + jnp.log(safe), MASKED)
        for h in range(GROUP):
            part = slice(h * slots, (h + 1) * slots)
            part_ref[pl.ds(g * slots, slots), pl.ds(h * HEAD_SIZE, HEAD_SIZE)] = normed[part]
            columns.append(logs[part])
    put_stats(part_ref, columns, slots)
    for copy in stores:
        copy.wait()


def decode_partials(lengths, dealing, queries, new_rows, cache, pre_queries, pre_new, req):
    slots, ctx, width = cache.shape
    inputs = (lengths, dealing, queries, new_rows, cache, pre_queries, pre_new)
    return pl.pallas_call(
        decode_kernel,
        in_specs=[HBM] * len(inputs),
        out_specs=[HBM, VMEM, VMEM, VMEM],
        out_shape=[
            pltpu.HBM(cache.shape, BF16),
            pltpu.VMEM((PART_ROWS * slots + pre_new.shape[1], KVW), BF16),
            pltpu.VMEM(pre_queries.shape[1:], BF16),
            pltpu.VMEM((req, slots + 8, HEAD_SIZE), F32),
        ],
        scratch_shapes=[
            pltpu.SMEM(lengths.shape, jnp.int32),
            pltpu.SMEM(dealing.shape, jnp.int32),
            pltpu.VMEM(queries.shape, BF16),
            pltpu.VMEM(new_rows.shape, BF16),
            pltpu.VMEM(cache.shape, BF16),
            pltpu.SemaphoreType.DMA((6 + 2 * CHUNKS,)),
        ],
        compiler_params=pltpu.CompilerParams(vmem_limit_bytes=16 << 20),
        cost_estimate=pl.CostEstimate(
            flops=4 * slots * ctx * QW, bytes_accessed=2 * cache.size * 2, transcendentals=slots * ctx * 8
        ),
        name="decode_partials",
    )(*[pltpu.with_memory_space_constraint(x, pltpu.HBM) for x in inputs])


def put_stats(ref, columns, slots):
    last = pl.ds(KEY_VALUE_HEADS * slots, slots)
    ref[last, pl.ds(0, STATS)] = stats_block(columns, slots)
    ref[last, pl.ds(STATS, KVW - STATS)] = jnp.zeros((slots, KVW - STATS), BF16)


def decode_part(ref, slots):
    blocks = [ref[pl.ds(g * slots, slots), :] for g in range(KEY_VALUE_HEADS)]
    return jnp.concatenate(blocks + [ref[pl.ds(KEY_VALUE_HEADS * slots, slots), pl.ds(0, STATS)]], axis=1)


def step_kernel(slots, count, *refs):
    out_ref = refs[-1]
    joined, logs = join([decode_part(ref, slots) for ref in refs[:count]])
    head = PART_ROWS * slots
    for g in range(KEY_VALUE_HEADS):
        out_ref[pl.ds(g * slots, slots), :] = joined[:, g * KVW : (g + 1) * KVW]
    put_stats(out_ref, [logs[:, h * HEAD_SIZE : h * HEAD_SIZE + 1] for h in range(QUERY_HEADS)], slots)
    at = head
    for ref in refs[count:-1]:
        rest = ref.shape[0] - head
        out_ref[pl.ds(at, rest), :] = ref[pl.ds(head, rest), :]
        at += rest


def join_step(parts, carriers, slots, name):
    head = PART_ROWS * slots
    rows = head + sum(c.shape[0] - head for c in carriers)
    return pl.pallas_call(
        functools.partial(step_kernel, slots, len(parts)),
        in_specs=[VMEM] * (len(parts) + len(carriers)),
        out_specs=VMEM,
        out_shape=pltpu.VMEM((rows, KVW), BF16),
        compiler_params=pltpu.CompilerParams(vmem_limit_bytes=16 << 20),
        name=name,
    )(*parts, *carriers)


def prefill_kernel(sets, ctx, off_ref, *refs):
    query_count = len(sets)
    packs, tables, outs = refs[:query_count], refs[query_count:-query_count], refs[-query_count:]
    tokens = packs[0].shape[0]
    span = ctx + tokens
    me = lax.axis_index(BLK)
    offset = off_ref[:1, :1]
    pieces = []
    for k in range(KEY_SET):
        holder = me ^ k
        index = lax.broadcasted_iota(jnp.int32, (1, span), 1)
        old = jnp.where(holder * ctx + index < offset, -1, 1 << 30)
        pieces.append(jnp.where(index < ctx, old, holder * tokens + index - ctx))
    key_mark = jnp.concatenate(pieces, axis=1)
    in_block = lax.broadcasted_iota(jnp.int32, (GROUP * tokens, 1), 0) % tokens
    lane = lax.broadcasted_iota(jnp.int32, (tokens, STATS), 1)
    stats = [jnp.zeros((tokens, STATS), F32) for _ in range(query_count)]
    for g in range(KEY_VALUE_HEADS):
        keys = jnp.concatenate([t[:, pl.ds(g * HEAD_SIZE, HEAD_SIZE)] for t in tables], axis=0)
        values = jnp.concatenate([t[:, pl.ds(KW + g * HEAD_SIZE, HEAD_SIZE)] for t in tables], axis=0)
        for k in range(query_count):
            token = (me ^ (sets[k] * KEY_SET)) * tokens + in_block
            query = jnp.concatenate(
                [packs[k][:, pl.ds((g * GROUP + h) * HEAD_SIZE, HEAD_SIZE)] for h in range(GROUP)], axis=0
            )
            scores = jnp.where(key_mark <= token, dot_t(query, keys) * SCALE, MASKED)
            maxima = jnp.maximum(jnp.max(scores, axis=1, keepdims=True), FLOOR)
            weights = jnp.exp(scores - maxima)
            totals = jnp.sum(weights, axis=1, keepdims=True)
            summed = dot(weights.astype(BF16), values)
            seen = totals > 0.0
            safe = jnp.where(seen, totals, 1.0)
            normed = (summed / safe).astype(BF16)
            logs = jnp.where(seen, maxima + jnp.log(safe), MASKED)
            for h in range(GROUP):
                part = slice(h * tokens, (h + 1) * tokens)
                outs[k][:, pl.ds((g * GROUP + h) * HEAD_SIZE, HEAD_SIZE)] = normed[part]
                for term, value in enumerate(split3(logs[part])):
                    stats[k] = jnp.where(lane == term * QUERY_HEADS + g * GROUP + h, value, stats[k])
    for k in range(query_count):
        outs[k][:, pl.ds(QW, STATS)] = stats[k].astype(BF16)


def prefill_partials(offset, packs, tables, ctx, sets):
    tokens = packs[0].shape[0]
    pairs = len(packs) * tokens * KEY_SET * (ctx + tokens)
    return pl.pallas_call(
        functools.partial(prefill_kernel, sets, ctx),
        in_specs=[VMEM] * (1 + len(packs) + len(tables)),
        out_specs=[VMEM] * len(packs),
        out_shape=[jax.ShapeDtypeStruct((tokens, QW + STATS), BF16)] * len(packs),
        compiler_params=pltpu.CompilerParams(vmem_limit_bytes=32 << 20),
        cost_estimate=pl.CostEstimate(
            flops=4 * pairs * QW, bytes_accessed=4 << 20, transcendentals=pairs * QUERY_HEADS
        ),
        name="prefill_partials",
    )(offset, *packs, *tables)


def join_kernel(count, slots, *refs):
    parts, decodes, out_ref = refs[:count], refs[count:-1], refs[-1]
    tokens = parts[0].shape[0]
    out_ref[pl.ds(0, tokens), :] = join([ref[...] for ref in parts])[0]
    out_ref[pl.ds(tokens, slots), :] = join([decode_part(ref, slots) for ref in decodes])[0]


def join_parts(parts, decodes, slots):
    return pl.pallas_call(
        functools.partial(join_kernel, len(parts), slots),
        in_specs=[VMEM] * (len(parts) + len(decodes)),
        out_specs=VMEM,
        out_shape=pltpu.VMEM((parts[0].shape[0] + slots, QW), BF16),
        compiler_params=pltpu.CompilerParams(vmem_limit_bytes=16 << 20),
        name="join_parts",
    )(*parts, *decodes)


def update_kernel(tokens, sets, off_ref, cache_hbm, near_ref, beside_ref, *refs):
    tables, (out_ref, cache_ref, sem) = refs[:KEY_SET], refs[-3:]
    load = pltpu.make_async_copy(cache_hbm.at[0], cache_ref, sem)
    load.start()
    ctx = cache_ref.shape[0]
    me = lax.axis_index(BLK)
    rows = [t[pl.ds(ctx, tokens), :] for t in tables]
    rows = jnp.concatenate(rows + [near_ref[...], beside_ref[...]], axis=0)
    count = rows.shape[0]
    index = lax.broadcasted_iota(jnp.int32, (1, count), 1)
    block = index // tokens
    half = sets * KEY_SET // 2
    far = block - KEY_SET
    inner = far % half
    distance = KEY_SET * (1 + inner % sets) + 2 * (inner // sets) + far // half
    token = (me ^ jnp.where(block < KEY_SET, block, distance)) * tokens + index % tokens
    wanted = me * ctx + lax.broadcasted_iota(jnp.int32, (ctx, 1), 0) - off_ref[:1, :1]
    picked = dot(jnp.where(wanted == token, 1.0, 0.0).astype(BF16), rows).astype(BF16)
    inside = jnp.broadcast_to((wanted >= 0) & (wanted < count), cache_ref.shape)
    load.wait()
    out_ref[0] = jnp.where(inside, picked, cache_ref[...])


def update_cache(offset, cache, near, beside, tables, tokens, sets):
    return pl.pallas_call(
        functools.partial(update_kernel, tokens, sets),
        in_specs=[VMEM, HBM] + [VMEM] * (2 + len(tables)),
        out_specs=VMEM,
        out_shape=jax.ShapeDtypeStruct(cache.shape, BF16),
        scratch_shapes=[pltpu.VMEM(cache.shape[1:], BF16), pltpu.SemaphoreType.DMA],
        compiler_params=pltpu.CompilerParams(vmem_limit_bytes=16 << 20),
        name="update_cache",
    )(offset, pltpu.with_memory_space_constraint(cache, pltpu.HBM), near, beside, *tables)


def route_kernel(count, route_ref, *refs):
    held, (pre_ref, dec_ref) = refs[:-2], refs[-2:]
    if len(held) < count:
        held = [held[0].at[j] for j in range(count)]
    tokens, slots = pre_ref.shape[1], dec_ref.shape[0]
    prefill = jnp.zeros(pre_ref.shape[1:], F32)
    decode = jnp.zeros(dec_ref.shape, F32)
    for j in range(count):
        flag = route_ref[j, pl.ds(slots, 1), pl.ds(0, 1)]
        prefill += flag * held[j][pl.ds(0, tokens), :].astype(F32)
        chosen = route_ref[j, pl.ds(0, slots), pl.ds(0, slots)].astype(BF16)
        decode += dot(chosen, held[j][pl.ds(tokens, slots), :])
    pre_ref[0] = prefill.astype(BF16)
    dec_ref[...] = decode.astype(BF16)


def route_outputs(route, held, tokens, slots):
    return pl.pallas_call(
        functools.partial(route_kernel, route.shape[0]),
        in_specs=[VMEM] * (1 + len(held)),
        out_specs=[VMEM] * 2,
        out_shape=[
            jax.ShapeDtypeStruct((1, tokens, QW), BF16),
            jax.ShapeDtypeStruct((slots, QW), BF16),
        ],
        compiler_params=pltpu.CompilerParams(vmem_limit_bytes=16 << 20),
        name="route_outputs",
    )(route, *held)


def per_device(
    prefill_queries,
    decode_queries,
    new_prefill,
    new_decode,
    prefill_cache,
    decode_cache,
    prefill_offsets,
    decode_lengths,
    dealing,
):
    blk = lax.axis_size(BLK)
    req = lax.axis_size("req")
    ctx = prefill_cache.shape[1]
    tokens = prefill_queries.shape[1]
    slots = decode_cache.shape[0]

    def swap(array, distance):
        return lax.ppermute(array, BLK, [(i, i ^ distance) for i in range(blk)])

    def after(array, *marks):
        return lax.optimization_barrier((array, *marks))[0]

    others = range(KEY_SET, blk, KEY_SET)
    table = jnp.concatenate([prefill_cache[0], new_prefill[0]], axis=0)
    lanes = [table] + [swap(table, k) for k in range(2, KEY_SET, 2)]
    packs = [swap(prefill_queries[0], k) for k in others]

    decode_cache_out, part, queries, route = decode_partials(
        decode_lengths,
        dealing,
        decode_queries,
        new_decode,
        decode_cache,
        prefill_queries,
        new_prefill,
        req,
    )
    far = [swap(part, k) for k in others]
    offset = jnp.full((8, HEAD_SIZE), prefill_offsets[0], jnp.int32)
    lanes[2], offset, _ = lax.optimization_barrier((lanes[2], offset, part))
    lanes[3], far, _ = lax.optimization_barrier((lanes[3], far, lanes[2]))
    lanes[1], packs, _ = lax.optimization_barrier((lanes[1], packs, lanes[2]))
    part = join_step([part] + far, [], slots, "join_far")
    tables = [t for lane in lanes for t in (lane, swap(lane, 1))]
    beside = swap(part, 1)

    part = join_step([part, beside], far, slots, "join_core")
    offset = after(offset, part)
    sent = prefill_partials(offset, packs, tables, ctx, [k // KEY_SET for k in others])
    arrived = [swap(p, k) for k, p in zip(others, sent)]
    part = after(part, sent[0])
    around = [part] + [swap(part, k) for k in range(2, KEY_SET, 2)]
    queries = after(queries, sent[0])
    kept = prefill_partials(offset, [queries], tables, ctx, [0])
    around = [part] + [after(a, *kept) for a in around[1:]]
    attended = join_parts([*kept] + arrived, around, slots)
    news = jnp.concatenate([a[PART_ROWS * slots :] for a in around], axis=0)
    prefill_cache_out = update_cache(offset, prefill_cache, news, swap(news, 1), tables, tokens, len(others))

    if req == 2:
        held = [attended, lax.ppermute(attended, "req", [(0, 1), (1, 0)])]
    else:
        held = [lax.all_gather(attended, "req", axis=0)]
    held[-1], prefill_cache_out = lax.optimization_barrier((held[-1], prefill_cache_out))
    prefill_out, decode_out = route_outputs(route, held, tokens, slots)
    return (prefill_out, decode_out, prefill_cache_out, decode_cache_out)


def solution(mesh):
    blk, req = mesh.shape["blk"], mesh.shape["req"]
    mesh = jax.sharding.Mesh(mesh.devices.reshape(blk // QUAD, QUAD, req), ("hi", "quad", "req"))
    in_specs = (
        P("req", BLK, None),
        P("req", None),
        P("req", BLK, None),
        P("req", None),
        P("req", BLK, None),
        P("req", BLK, None),
        P("req"),
        P("req"),
        P(),
    )
    out_specs = (
        P("req", BLK, None),
        P("req", None),
        P("req", BLK, None),
        P("req", BLK, None),
    )
    return jax.shard_map(
        per_device, mesh=mesh, in_specs=in_specs, out_specs=out_specs, check_vma=False
    )
```
